32 devices in a mesh: seq: 8 (over y, x, core), fsdp: 4 (over z).
Axes of the slice: x: 2, y: 2, z: 4, core: 2. Of those that a mesh axis runs over, the one named last changes fastest.
Arguments:
- tokens: bfloat16 [8, 4096, 640], P('fsdp', 'seq'), may hold values from -6 to 6
- doc_starts: int32 [8, 4096], P('fsdp', 'seq'), may hold values from 0 to 1, as said below
- w_query: bfloat16 [640, 1024], P('fsdp'), may hold values from -0.25 to 0.25
- w_key: bfloat16 [640, 256], P('fsdp'), may hold values from -0.25 to 0.25
- w_value: bfloat16 [640, 256], P('fsdp'), may hold values from -0.25 to 0.25
- w_out: bfloat16 [1024, 640], P('fsdp'), may hold values from -1.5 to 1.5
- w_gate: bfloat16 [640, 2048], P('fsdp'), may hold values from -0.25 to 0.25
- w_up: bfloat16 [640, 2048], P('fsdp'), may hold values from -0.25 to 0.25
- w_down: bfloat16 [2048, 640], P('fsdp'), may hold values from -0.125 to 0.125
- pre_attn: float32 [640], replicated, may hold values from 0.25 to 1.75
- post_attn: float32 [640], replicated, may hold values from 0.25 to 1.75
- pre_ffn: float32 [640], replicated, may hold values from 0.25 to 1.75
- post_ffn: float32 [640], replicated, may hold values from 0.25 to 1.75
- query_norm: float32 [256], replicated, may hold values from 0.25 to 1.75
- key_norm: float32 [256], replicated, may hold values from 0.25 to 1.75
- cotangent: bfloat16 [8, 4096, 640], P('fsdp', 'seq'), may hold values from -6 to 6
Outputs:
- layer_out: bfloat16 [8, 4096, 640], P('fsdp', 'seq')
- dtokens: bfloat16 [8, 4096, 640], P('fsdp', 'seq')
- dw_query: float32 [640, 1024], P('fsdp', 'seq')
- dw_key: float32 [640, 256], P('fsdp', 'seq')
- dw_value: float32 [640, 256], P('fsdp', 'seq')
- dw_out: float32 [1024, 640], P('fsdp', 'seq')
- dw_gate: float32 [640, 2048], P('fsdp', 'seq')
- dw_up: float32 [640, 2048], P('fsdp', 'seq')
- dw_down: float32 [2048, 640], P('fsdp', 'seq')
- dpre_attn: float32 [640], replicated
- dpost_attn: float32 [640], replicated
- dpre_ffn: float32 [640], replicated
- dpost_ffn: float32 [640], replicated
- dquery_norm: float32 [256], replicated
- dkey_norm: float32 [256], replicated
The draws below stay inside these ranges and needn't reach their ends.
Inputs may be any that keep to these rules, and one draw needn't show every extreme that they name: `doc_starts`: 1 marks the first token of a document, 0 any other token; the first token of every sequence is 1.
All inputs are finite; a program needn't handle non-finite values.
Results may differ from the reference program's by a relative error of at most 0.022.
Values may be sent and summed in bfloat16 or wider, within the bound.
No kernel may reach another device: no remote copies, remote signals or barrier semaphores. Data moves between devices by JAX's collectives and lax.ppermute only.
A program may use at most 192 MiB of HBM per device.

```python
import jax
import jax.numpy as jnp
from jax import lax

D = 640
FF = 2048
H = 4
HD = 256
WINDOW = 512
BLOCK = 512
SEQ_DEV = 2
SEQS = 8
LEN = 4096


def draw_doc_starts(key, part):
    key = jax.random.fold_in(key, 11)
    key_pick, key_first, key_last, key_rand, key_tail = jax.random.split(key, 5)
    indices = jnp.arange(LEN, dtype=jnp.int32)[None, :]
    picked = jax.random.randint(key_pick, (SEQS // SEQ_DEV,), 0, SEQ_DEV)
    chosen = jnp.repeat(picked, SEQ_DEV)
    slot_ids = jnp.arange(SEQS, dtype=jnp.int32) % SEQ_DEV
    long_doc = (slot_ids == chosen)[:, None]
    first_cut = jax.random.randint(key_first, (SEQS, 1), 1, BLOCK)
    last_cut = LEN - jax.random.randint(key_last, (SEQS, 1), 1, BLOCK + 1)
    spanning = (indices == 0) | (indices == first_cut) | (indices == last_cut)
    tail_hi = max(2, min(BLOCK, WINDOW) // 2 + 1)
    tail_back = jax.random.randint(key_tail, (SEQS, LEN // BLOCK), 1, tail_hi)
    tail_back = jnp.repeat(tail_back, BLOCK, axis=1)
    late_start = indices % BLOCK == BLOCK - tail_back
    scattered = (jax.random.randint(key_rand, (SEQS, LEN), 0, 300) == 0) | (indices == 0) | late_start
    return jnp.where(long_doc, spanning, scattered).astype(jnp.int32)


def with_spikes(entries, own_key, source, target, parts, factor):
    owner, partner = [(jnp.arange(entries.shape[position]) // (entries.shape[position] // parts)).reshape([-1 if axis == position else 1 for axis in range(entries.ndim)]) for position in (source, target)]
    chosen = jax.random.permutation(own_key, parts)[partner]
    strong = (owner == chosen) | (owner == (partner + parts // 2) % parts)
    return jnp.where(strong, factor * entries, entries)


def block_scale(stream_key, extent, cuts, smallest, high):
    loudness = 1.0
    for dim, blocks in cuts:
        steps = jax.random.uniform(jax.random.fold_in(jax.random.fold_in(stream_key, 6), dim), (blocks,), jnp.float32, smallest / len(cuts), high / len(cuts))
        loudness = loudness * jnp.repeat(jnp.exp(steps), extent[dim] // blocks).reshape((-1,) + (1,) * (len(extent) - 1 - dim))
    return loudness


def normal_values(rng, shape, scale, limit, shards=(), held_as=jnp.bfloat16):
    entries = scale * jax.random.normal(rng, shape, jnp.float32)
    if shards:
        entries = entries * block_scale(rng, shape, shards, -0.22, 0.18)
    return jnp.clip(entries, -limit, limit).astype(held_as)


def gaussian_with(rng, dims, scale, reach, cuts, heavy, kind=jnp.bfloat16):
    values = scale * jax.random.normal(rng, dims, jnp.float32)
    if cuts:
        values = values * block_scale(rng, dims, cuts, -0.22, 0.18)
    return jnp.clip(with_spikes(values, jax.random.fold_in(rng, 3), *heavy), -reach, reach).astype(kind)


def setup_inputs(seed: int = 0) -> dict:
    seeds = jax.random.split(jax.random.key(seed), 17)
    tokens = normal_values(seeds[0], (SEQS, LEN, D), 1.0, 6.0, ((0, 4), (1, 8)))
    doc_starts = draw_doc_starts(jax.random.fold_in(seeds[16], 71), 0)
    w_query = normal_values(seeds[2], (D, H * HD), D ** -0.5, 0.25, ((0, 4),))
    w_key = normal_values(seeds[3], (D, HD), D ** -0.5, 0.25, ((0, 4),))
    w_value = normal_values(seeds[4], (D, HD), D ** -0.5, 0.25, ((0, 4),))
    w_out = normal_values(seeds[5], (H * HD, D), 16 ** -0.5, 1.5, ((0, 4),))
    w_gate = normal_values(seeds[6], (D, FF), D ** -0.5, 0.25, ((0, 4),))
    w_up = normal_values(seeds[7], (D, FF), D ** -0.5, 0.25, ((0, 4),))
    w_down = normal_values(seeds[8], (FF, D), FF ** -0.5, 0.125, ((0, 4),))
    pre_attn = jnp.clip(1.0 + 0.15 * jax.random.normal(seeds[9], (D,), jnp.float32), 0.25, 1.75)
    post_attn = jnp.clip(1.0 + 0.15 * jax.random.normal(seeds[10], (D,), jnp.float32), 0.25, 1.75)
    pre_ffn = jnp.clip(1.0 + 0.15 * jax.random.normal(seeds[11], (D,), jnp.float32), 0.25, 1.75)
    post_ffn = jnp.clip(1.0 + 0.15 * jax.random.normal(seeds[12], (D,), jnp.float32), 0.25, 1.75)
    query_norm = jnp.clip(1.0 + 0.15 * jax.random.normal(seeds[13], (HD,), jnp.float32), 0.25, 1.75)
    key_norm = jnp.clip(1.0 + 0.15 * jax.random.normal(seeds[14], (HD,), jnp.float32), 0.25, 1.75)
    cotangent = gaussian_with(seeds[15], (SEQS, LEN, D), 1.0, 6.0, ((0, 4), (1, 8)), (1, 2, 8, 2.0))
    return dict(tokens=tokens, doc_starts=doc_starts, w_query=w_query, w_key=w_key, w_value=w_value, w_out=w_out, w_gate=w_gate, w_up=w_up, w_down=w_down, pre_attn=pre_attn, post_attn=post_attn, pre_ffn=pre_ffn, post_ffn=post_ffn, query_norm=query_norm, key_norm=key_norm, cotangent=cotangent)


@jax.custom_vjp
def low(v):
    return lax.optimization_barrier(v.astype(jnp.bfloat16)).astype(jnp.float32)

@jax.custom_vjp
def low_back(v):
    return v

def low_keep(v):
    return (low(v), None)

def low_pass(kept, grad):
    return (grad,)

def back_keep(v):
    return (v, None)

def back_low(kept, grad):
    return (low(grad),)
low.defvjp(low_keep, low_pass)
low_back.defvjp(back_keep, back_low)
epsilon = 1e-06
NEG_FILL = -1e+30
ROPE_BASE = 10000.0

def matmul_high(left, right):
    return jnp.dot(left, right, precision=lax.Precision.HIGHEST, preferred_element_type=jnp.float32)

def norm_rows(vector, gain_vec):
    return vector * lax.rsqrt(lax.optimization_barrier(jnp.mean(vector * vector, axis=-1, keepdims=True)) + epsilon) * gain_vec

def rotate(vector, cosine, sine_tab):
    half_width = vector.shape[-1] // 2
    first_half = vector[..., :half_width]
    second_half = vector[..., half_width:]
    turned = jnp.concatenate([-second_half, first_half], axis=-1)
    return vector * cosine + turned * sine_tab

def tables(positions, head_dim):
    half_width = head_dim // 2
    frequency = ROPE_BASE ** (-(jnp.arange(half_width, dtype=jnp.float32) * 2.0) / head_dim)
    angles = positions.astype(jnp.float32)[..., None] * frequency
    angles = jnp.concatenate([angles, angles], axis=-1)
    return (jnp.cos(angles), jnp.sin(angles))

def gated_unit(gate_proj, up_proj):
    return jax.nn.gelu(gate_proj, approximate=True) * up_proj

def attention(query_rot, key_rot, value_low, positions):
    length, head_count, head_dim = query_rot.shape
    span_rows = min(512, length)
    scaling = head_dim ** (-0.5)
    key_pad = jnp.concatenate([jnp.zeros((WINDOW, head_dim), key_rot.dtype), key_rot], axis=0)
    value_pad = jnp.concatenate([jnp.zeros((WINDOW, head_dim), value_low.dtype), value_low], axis=0)
    row_ids = jnp.arange(span_rows, dtype=jnp.int32)
    col_ids = jnp.arange(span_rows + WINDOW, dtype=jnp.int32)
    distance = WINDOW + row_ids[:, None] - col_ids[None, :]

    def one_block(start_row):
        query_part = lax.dynamic_slice_in_dim(query_rot, start_row, span_rows, 0)
        key_part = lax.dynamic_slice_in_dim(key_pad, start_row, span_rows + WINDOW, 0)
        value_part = lax.dynamic_slice_in_dim(value_pad, start_row, span_rows + WINDOW, 0)
        pos_part = lax.dynamic_slice_in_dim(positions, start_row, span_rows, 0)
        raw_dot = jnp.einsum('qhd,kd->hqk', query_part, key_part, precision=lax.Precision.HIGHEST, preferred_element_type=jnp.float32)
        scores = low_back(raw_dot * scaling)
        allowed = (distance >= 0) & (distance <= jnp.minimum(pos_part, WINDOW - 1)[:, None])
        scores = jnp.where(allowed[None], scores, NEG_FILL)
        largest = lax.optimization_barrier(jnp.max(scores, axis=-1, keepdims=True))
        exponent = jnp.exp(scores - largest)
        probs_full = exponent / lax.optimization_barrier(jnp.sum(exponent, axis=-1, keepdims=True))
        context = jnp.einsum('hqk,kd->qhd', low(probs_full), value_part, precision=lax.Precision.HIGHEST, preferred_element_type=jnp.float32)
        return context.reshape(span_rows, head_count * head_dim)
    starts = jnp.arange(length // span_rows, dtype=jnp.int32) * span_rows
    blocks = lax.map(jax.checkpoint(one_block), starts)
    return blocks.reshape(length, head_count * head_dim)

def layer_fn(tokens_f, positions, w_query, w_key, w_value, w_out, w_gate, w_up, w_down, pre_attn, post_attn, pre_ffn, post_ffn, query_norm, key_norm):
    length = tokens_f.shape[0]
    head_dim = w_key.shape[1]
    head_count = w_query.shape[1] // head_dim
    cosine, sine_tab = tables(positions, head_dim)
    attn_low = low(norm_rows(tokens_f, pre_attn))
    query_raw = low_back(matmul_high(attn_low, w_query)).reshape(length, head_count, head_dim)
    key_raw = low_back(matmul_high(attn_low, w_key))
    value_raw = low_back(matmul_high(attn_low, w_value))
    query_rot = low(rotate(norm_rows(query_raw, query_norm), cosine[:, None, :], sine_tab[:, None, :]))
    key_rot = low(rotate(norm_rows(key_raw, key_norm), cosine, sine_tab))
    value_low = low(value_raw)
    context = attention(query_rot, key_rot, value_low, positions)
    context_low = low(low_back(context))
    attn_branch = low_back(matmul_high(context_low, w_out))
    residual = tokens_f + norm_rows(attn_branch, post_attn)
    ffn_low = low(norm_rows(residual, pre_ffn))
    gate_proj = low_back(matmul_high(ffn_low, w_gate))
    up_proj = low_back(matmul_high(ffn_low, w_up))
    hidden_low = low(gated_unit(gate_proj, up_proj))
    ffn_branch = low_back(matmul_high(hidden_low, w_down))
    return residual + norm_rows(ffn_branch, post_ffn)

def reference(tokens, doc_starts, w_query, w_key, w_value, w_out, w_gate, w_up, w_down, pre_attn, post_attn, pre_ffn, post_ffn, query_norm, key_norm, cotangent):
    indices = jnp.arange(LEN, dtype=jnp.int32)
    marked = jnp.where(doc_starts == 1, indices[None, :], 0).astype(jnp.int32)
    positions = (indices[None, :] - lax.cummax(marked, axis=1)).astype(jnp.int32)
    params = (tokens.astype(jnp.float32), w_query.astype(jnp.float32), w_key.astype(jnp.float32), w_value.astype(jnp.float32), w_out.astype(jnp.float32), w_gate.astype(jnp.float32), w_up.astype(jnp.float32), w_down.astype(jnp.float32), pre_attn.astype(jnp.float32), post_attn.astype(jnp.float32), pre_ffn.astype(jnp.float32), post_ffn.astype(jnp.float32), query_norm.astype(jnp.float32), key_norm.astype(jnp.float32))

    def forward(tokens_f, wq_full, wk_full, wv_full, wo_full, wg_full, wu_full, wd_full, gain_one, gain_two, gain_three, gain_four, gain_query, gain_key):

        def per_sequence(pair_args):
            seq_tokens, seq_pos = pair_args
            return layer_fn(seq_tokens, seq_pos, wq_full, wk_full, wv_full, wo_full, wg_full, wu_full, wd_full, gain_one, gain_two, gain_three, gain_four, gain_query, gain_key)
        return lax.map(jax.checkpoint(per_sequence), (tokens_f, positions))
    result_out, pullback = jax.vjp(forward, *params)
    gradients = pullback(cotangent.astype(jnp.float32))
    return (result_out.astype(jnp.bfloat16), gradients[0].astype(jnp.bfloat16), gradients[1], gradients[2], gradients[3], gradients[4], gradients[5], gradients[6], gradients[7], gradients[8], gradients[9], gradients[10], gradients[11], gradients[12], gradients[13])
```

```python
import functools

import jax
import jax.numpy as jnp
from jax import lax
from jax.experimental import pallas as pl
from jax.experimental.pallas import tpu as pltpu
from jax.sharding import PartitionSpec as P

WINDOW = 512
TILE = 128
FF_TILE = 256
FFN_ROWS = 256

epsilon = 1e-06
NEG_FILL = -1e30
ROPE_BASE = 10000.0
GELU_C = 0.7978845608028654
GELU_K = 0.044715

f32 = jnp.float32
bf16 = jnp.bfloat16

NN = (((1,), (0,)), ((), ()))
NT = (((1,), (1,)), ((), ()))
TN = (((0,), (0,)), ((), ()))


def mm(left, right, dims=NN):
    return lax.dot_general(left, right, dims, preferred_element_type=f32)


def inv_rms(vector):
    return lax.rsqrt(jnp.mean(vector * vector, axis=-1, keepdims=True) + epsilon)


def norm_back(vector, inv, gain, grad):
    unit = vector * inv
    scaled = gain * grad
    back = inv * (scaled - unit * jnp.mean(unit * scaled, axis=-1, keepdims=True))
    return back, grad * unit


def rope(vector, cosine, sine):
    half = vector.shape[-1] // 2
    one, two = vector[:, :half], vector[:, half:]
    return jnp.concatenate([one * cosine - two * sine, two * cosine + one * sine], axis=1)


def rope_back(vector, cosine, sine):
    half = vector.shape[-1] // 2
    one, two = vector[:, :half], vector[:, half:]
    return jnp.concatenate([one * cosine + two * sine, two * cosine - one * sine], axis=1)


def params(limit_mib=56):
    return pltpu.CompilerParams(vmem_limit_bytes=limit_mib * 1024 * 1024)


def whole(shape):
    return pl.BlockSpec(shape, lambda *_: (0,) * len(shape))


def rows(count, width):
    return pl.BlockSpec((count, width), lambda i: (i, 0))


def shaped(shape, dtype):
    return jax.ShapeDtypeStruct(shape, dtype)


def qkv_kernel(
    tok_ref, far_ref, cos_ref, sin_ref, fcos_ref, fsin_ref, pack_ref, pre_ref, qn_ref, kn_ref,
    attn_ref, qraw_ref, qrot_ref, kraw_ref, key_ref, val_ref, wq_ref, wkv_ref, wot_ref,
):
    head_dim = kn_ref.shape[1]
    head_count = wq_ref.shape[1] // head_dim
    width = tok_ref.shape[1]
    block = tok_ref.shape[0]
    pieces, chunks, chunk_rows, _ = pack_ref.shape

    @pl.when(pl.program_id(0) == 0)
    def _():
        for s in range(pieces):
            wq_ref[:, s * 128 : (s + 1) * 128] = pack_ref[s, :, :, :128].reshape(width, 128)
        for s in range(0, pieces, 2):
            both = jnp.concatenate(
                [pack_ref[s + i, :, :, 256:320].reshape(width, 64) for i in range(2)], axis=1
            )
            wkv_ref[:, s * 64 : (s + 2) * 64] = both
        half = chunk_rows // 2
        for z in range(chunks):
            for i in range(2):
                part = pack_ref[:, z, i * half : (i + 1) * half, 128:256].reshape(width, 128)
                wot_ref[:, z * 256 + i * 128 : z * 256 + (i + 1) * 128] = part

    pre = pre_ref[...]
    kgain = kn_ref[...]
    token = tok_ref[...].astype(f32)
    low = (token * inv_rms(token) * pre).astype(bf16)
    attn_ref[...] = low
    query = mm(low, wq_ref[...])
    qraw_ref[...] = query
    cosine, sine = cos_ref[...], sin_ref[...]
    scaling = head_dim ** (-0.5)
    for h in range(head_count):
        part = query[:, h * head_dim : (h + 1) * head_dim]
        normed = part * inv_rms(part) * qn_ref[...]
        qrot_ref[:, h * head_dim : (h + 1) * head_dim] = (
            rope(normed, cosine, sine).astype(bf16) * jnp.asarray(scaling, bf16)
        )
    both = mm(low, wkv_ref[...])
    key = both[:, :head_dim]
    kraw_ref[...] = key
    key_ref[0, block:, :] = rope(key * inv_rms(key) * kgain, cosine, sine).astype(bf16)
    val_ref[0, block:, :] = both[:, head_dim:].astype(bf16)
    token = far_ref[...].astype(f32)
    low = (token * inv_rms(token) * pre).astype(bf16)
    both = mm(low, wkv_ref[...])
    key = both[:, :head_dim]
    key_ref[0, :block, :] = rope(key * inv_rms(key) * kgain, fcos_ref[...], fsin_ref[...]).astype(
        bf16
    )
    val_ref[0, :block, :] = both[:, head_dim:].astype(bf16)


def stacked(ref, tile, head_count, head_dim):
    return jnp.concatenate(
        [
            ref[tile * TILE : (tile + 1) * TILE, h * head_dim : (h + 1) * head_dim]
            for h in range(head_count)
        ],
        axis=0,
    )


def mask_of(pos_ref, tile, span):
    reach = jnp.minimum(pos_ref[tile * TILE : (tile + 1) * TILE, :], WINDOW - 1)
    row = lax.broadcasted_iota(jnp.int32, (TILE, span), 0)
    col = lax.broadcasted_iota(jnp.int32, (TILE, span), 1)
    distance = WINDOW + row - col
    return jnp.where((distance >= 0) & (distance <= reach), 0.0, NEG_FILL)


def attn_kernel(
    q_ref, key_ref, val_ref, pos_ref, tok_ref, wot_ref, post_ref, pre_ref,
    ctx_ref, lse_ref, branch_ref, res_ref, fin_ref,
):
    head_dim = key_ref.shape[2]
    head_count = q_ref.shape[1] // head_dim
    span = WINDOW + TILE
    lane = lax.broadcasted_iota(jnp.int32, (TILE, 128), 1)
    for tile in range(q_ref.shape[0] // TILE):
        query = stacked(q_ref, tile, head_count, head_dim)
        key = key_ref[0, tile * TILE : tile * TILE + span, :]
        value = val_ref[0, tile * TILE : tile * TILE + span, :]
        score = mm(query, key, NT).reshape(head_count, TILE, span) + mask_of(pos_ref, tile, span)
        largest = jnp.max(score, axis=-1, keepdims=True)
        expo = jnp.exp(score - largest)
        total = jnp.sum(expo, axis=-1, keepdims=True)
        low = expo.astype(bf16).reshape(head_count * TILE, span)
        context = mm(low, value).reshape(head_count, TILE, head_dim) / total
        log_total = largest + jnp.log(total)
        kept = jnp.zeros((TILE, 128), f32)
        for h in range(head_count):
            ctx_ref[tile * TILE : (tile + 1) * TILE, h * head_dim : (h + 1) * head_dim] = context[
                h
            ].astype(bf16)
            kept = jnp.where(lane == h, log_total[h], kept)
        lse_ref[tile * TILE : (tile + 1) * TILE, :] = kept
    branch = mm(ctx_ref[...], wot_ref[...], NT)
    branch_ref[...] = branch
    residual = tok_ref[...].astype(f32) + branch * inv_rms(branch) * post_ref[...]
    res_ref[...] = residual
    fin_ref[...] = (residual * inv_rms(residual) * pre_ref[...]).astype(bf16)


def ffn_kernel(
    res_ref, fin_ref, cot_ref, branch_ref, wf_ref, wot_ref, postf_ref, pref_ref, posta_ref,
    out_ref, hid_ref, gg_ref, gu_ref, gffn_ref, gres_ref, gattn_ref, gctx_ref, gain_ref,
    slope_ref, act_ref,
):
    pieces, chunks, _, _ = wf_ref.shape
    width = res_ref.shape[1]
    quarter = width // chunks
    strip = width // pieces

    def gate_block(j):
        return wf_ref[j, :, :quarter, :].reshape(width, FF_TILE)

    def up_block(j):
        return wf_ref[j, :, quarter : 2 * quarter, :].reshape(width, FF_TILE)

    def down_block(j):
        start = 2 * quarter + (j % 2) * strip
        return wf_ref[:, j // 2, start : start + strip, :].reshape(width, FF_TILE)

    @pl.when(pl.program_id(0) == 0)
    def _():
        gain_ref[...] = jnp.zeros_like(gain_ref)

    ffn_in = fin_ref[...]
    branch = jnp.zeros(res_ref.shape, f32)
    for j in range(pieces):
        cols = slice(j * FF_TILE, (j + 1) * FF_TILE)
        gate = mm(ffn_in, gate_block(j))
        up = mm(ffn_in, up_block(j))
        square = gate * gate
        bent = jnp.tanh(GELU_C * gate * (1.0 + GELU_K * square))
        half = 0.5 * (1.0 + bent)
        act = gate * half
        slope = half + 0.5 * gate * (1.0 - bent * bent) * (
            GELU_C * (1.0 + 3.0 * GELU_K * square)
        )
        act_ref[:, cols] = act
        slope_ref[:, cols] = slope * up
        hidden = (act * up).astype(bf16)
        hid_ref[:, cols] = hidden
        branch += mm(hidden, down_block(j), NT)
    residual = res_ref[...]
    cot = cot_ref[...].astype(f32)
    inv = inv_rms(branch)
    out_ref[...] = (residual + branch * inv * postf_ref[...]).astype(bf16)
    g_ffn, gain_post = norm_back(branch, inv, postf_ref[...], cot)
    g_low = g_ffn.astype(bf16)
    gffn_ref[...] = g_low
    g_in = jnp.zeros(res_ref.shape, f32)
    for j in range(pieces):
        cols = slice(j * FF_TILE, (j + 1) * FF_TILE)
        g_hidden = mm(g_low, down_block(j))
        g_gate = (g_hidden * slope_ref[:, cols]).astype(bf16)
        g_up = (g_hidden * act_ref[:, cols]).astype(bf16)
        gg_ref[:, cols] = g_gate
        gu_ref[:, cols] = g_up
        g_in += mm(g_gate, gate_block(j), NT) + mm(g_up, up_block(j), NT)
    back, gain_pre = norm_back(residual, inv_rms(residual), pref_ref[...], g_in)
    g_res = cot + back
    gres_ref[...] = g_res
    attn_branch = branch_ref[...]
    g_attn, gain_attn = norm_back(attn_branch, inv_rms(attn_branch), posta_ref[...], g_res)
    g_attn = g_attn.astype(bf16)
    gattn_ref[...] = g_attn
    gctx_ref[...] = mm(g_attn, wot_ref[...]).astype(bf16)
    gain_ref[0:1, :] += jnp.sum(gain_post, axis=0, keepdims=True)
    gain_ref[1:2, :] += jnp.sum(gain_pre, axis=0, keepdims=True)
    gain_ref[2:3, :] += jnp.sum(gain_attn, axis=0, keepdims=True)


def down_kernel(gffn_ref, hid_ref, out_ref, left_ref):
    @pl.when(pl.program_id(0) == 0)
    def _():
        left_ref[...] = gffn_ref[...].T

    part = mm(left_ref[...], hid_ref[...]).astype(bf16)
    out_ref[...] = part.reshape(out_ref.shape)


def gate_kernel(fin_ref, gg_ref, gu_ref, out_ref, left_ref):
    @pl.when(pl.program_id(0) == 0)
    def _():
        left_ref[...] = fin_ref[...].T

    chunks, double, tile = out_ref.shape[1:]
    quarter = double // 2
    part = mm(left_ref[...], gg_ref[...]).astype(bf16)
    out_ref[0, :, :quarter, :] = part.reshape(chunks, quarter, tile)
    part = mm(left_ref[...], gu_ref[...]).astype(bf16)
    out_ref[0, :, quarter:, :] = part.reshape(chunks, quarter, tile)


def attn_back_kernel(
    q_ref, gctx_ref, key_ref, val_ref, pos_ref, lse_ref, qraw_ref, cos_ref, sin_ref, qn_ref,
    gq_ref, far_ref, near_ref, gain_ref, gkey_ref, gval_ref,
):
    head_dim = key_ref.shape[2]
    head_count = q_ref.shape[1] // head_dim
    block = q_ref.shape[0]
    span = WINDOW + TILE
    scaling = head_dim ** (-0.5)

    @pl.when(pl.program_id(0) == 0)
    def _():
        gain_ref[...] = jnp.zeros_like(gain_ref)

    gkey_ref[...] = jnp.zeros_like(gkey_ref)
    gval_ref[...] = jnp.zeros_like(gval_ref)
    gain = jnp.zeros((1, head_dim), f32)
    for tile in range(block // TILE):
        own = slice(tile * TILE, (tile + 1) * TILE)
        reach = slice(tile * TILE, tile * TILE + span)
        query = stacked(q_ref, tile, head_count, head_dim)
        g_ctx = stacked(gctx_ref, tile, head_count, head_dim)
        key = key_ref[0, reach, :]
        value = val_ref[0, reach, :]
        log_total = jnp.stack([lse_ref[own, h : h + 1] for h in range(head_count)])
        score = mm(query, key, NT).reshape(head_count, TILE, span) + mask_of(pos_ref, tile, span)
        probs = jnp.exp(score - log_total)
        g_probs = mm(g_ctx, value, NT).reshape(head_count, TILE, span)
        spread = jnp.sum(g_probs * probs, axis=-1, keepdims=True)
        g_score = (probs * (g_probs - spread)).astype(bf16).reshape(head_count * TILE, span)
        low = probs.astype(bf16).reshape(head_count * TILE, span)
        gkey_ref[reach, :] += mm(g_score, query, TN)
        gval_ref[reach, :] += mm(low, g_ctx, TN)
        g_rot = mm(g_score, key) * scaling
        cosine, sine = cos_ref[own, :], sin_ref[own, :]
        for h in range(head_count):
            cols = slice(h * head_dim, (h + 1) * head_dim)
            raw = qraw_ref[own, cols]
            back, share = norm_back(
                raw,
                inv_rms(raw),
                qn_ref[...],
                rope_back(g_rot[h * TILE : (h + 1) * TILE], cosine, sine),
            )
            gq_ref[own, cols] = back.astype(bf16)
            gain += jnp.sum(share, axis=0, keepdims=True)
    gain_ref[0:1, :] += gain
    far_ref[0, :, :head_dim] = gkey_ref[:block, :].astype(bf16)
    far_ref[0, :, head_dim:] = gval_ref[:block, :].astype(bf16)
    near_ref[0, :, :head_dim] = gkey_ref[block:, :]
    near_ref[0, :, head_dim:] = gval_ref[block:, :]


def input_kernel(
    near_ref, recv_ref, kraw_ref, cos_ref, sin_ref, gq_ref, wq_ref, wkv_ref, tok_ref, gres_ref,
    kn_ref, pre_ref,
    dtok_ref, gkv_ref, kgain_ref, gain_ref,
):
    head_dim = kn_ref.shape[1]

    @pl.when(pl.program_id(0) == 0)
    def _():
        gain_ref[...] = jnp.zeros_like(gain_ref)
        kgain_ref[...] = jnp.zeros_like(kgain_ref)

    both = near_ref[0] + recv_ref[0].astype(f32)
    raw = kraw_ref[...]
    g_key, share = norm_back(
        raw, inv_rms(raw), kn_ref[...], rope_back(both[:, :head_dim], cos_ref[...], sin_ref[...])
    )
    kgain_ref[0:1, :] += jnp.sum(share, axis=0, keepdims=True)
    gkv_ref[:, :head_dim] = g_key.astype(bf16)
    gkv_ref[:, head_dim:] = both[:, head_dim:].astype(bf16)
    g_in = mm(gq_ref[...], wq_ref[...], NT) + mm(gkv_ref[...], wkv_ref[...], NT)
    token = tok_ref[...].astype(f32)
    back, share = norm_back(token, inv_rms(token), pre_ref[...], g_in)
    dtok_ref[...] = (gres_ref[...] + back).astype(bf16)
    gain_ref[0:1, :] += jnp.sum(share, axis=0, keepdims=True)


def query_kernel(attn_ref, gq_ref, out_ref, left_ref):
    @pl.when(pl.program_id(0) == 0)
    def _():
        left_ref[...] = attn_ref[...].T

    part = mm(left_ref[...], gq_ref[...]).astype(bf16)
    for i in range(out_ref.shape[0]):
        out_ref[i] = part[:, i * 128 : (i + 1) * 128].reshape(out_ref.shape[1:])


def kv_kernel(attn_ref, gkv_ref, out_ref):
    out_ref[...] = mm(attn_ref[...].T, gkv_ref[...]).astype(bf16)


def carried_in(value, axis, join, neutral):
    count, mine = (lax.axis_size(axis), lax.axis_index(axis))
    pieces = lax.all_gather(value, axis)
    subtotal = jnp.full_like(value, 0) + jnp.asarray(neutral, value.dtype)

    def step(position, subtotal):
        longer = join(subtotal, pieces[position])
        return jnp.where(position < mine, longer, subtotal)

    return lax.fori_loop(0, count - 1, step, subtotal)


def passed_along(shard, axis, by):
    length = lax.axis_size(axis)
    pairs = [(i, i + by) for i in range(length) if 0 <= i + by < length]
    return lax.ppermute(shard, axis, pairs)


def tables(positions, head_dim):
    half_width = head_dim // 2
    frequency = ROPE_BASE ** (-(jnp.arange(half_width, dtype=f32) * 2.0) / head_dim)
    angles = positions.astype(f32)[..., None] * frequency
    return (jnp.cos(angles), jnp.sin(angles))


def column_piece(array, axis_name, parts):
    wide = array.shape[1] // parts
    return lax.dynamic_slice_in_dim(array, lax.axis_index(axis_name) * wide, wide, 1)


def gathered(piece):
    return lax.all_gather(piece, ("seq", "fsdp"), axis=0, tiled=False)


def scattered(parts):
    over_seq = lax.psum_scatter(parts, "seq", scatter_dimension=0, tiled=True)
    return lax.psum_scatter(over_seq[0], "fsdp", scatter_dimension=0, tiled=True)[0]


def scattered_plain(part):
    columns = lax.psum_scatter(part, "seq", scatter_dimension=1, tiled=True)
    return lax.psum_scatter(columns, "fsdp", scatter_dimension=0, tiled=True).astype(f32)


def gather_weights(w_query, w_key, w_value, w_out, w_gate, w_up, w_down, seqs, chunks):
    pieces = w_gate.shape[1] // FF_TILE
    width = w_out.shape[1]
    if pieces == seqs and w_down.shape[0] == 2 * FF_TILE:
        both = jnp.concatenate([w_key, w_value], axis=1)
        out = column_piece(w_out, "seq", seqs).T
        out = jnp.concatenate([out[:, :128], out[:, 128:]], axis=0)
        attn = jnp.concatenate(
            [column_piece(w_query, "seq", seqs), out, column_piece(both, "seq", seqs)], axis=1
        )
        down = column_piece(w_down, "seq", seqs).T
        ffn = jnp.concatenate(
            [
                column_piece(w_gate, "seq", seqs),
                column_piece(w_up, "seq", seqs),
                down[:, :FF_TILE],
                down[:, FF_TILE:],
            ],
            axis=0,
        )
        shape = (seqs, chunks)
        attn = gathered(attn)
        attn, ffn = lax.optimization_barrier((attn, ffn))
        ffn = gathered(ffn)
        return attn.reshape(shape + attn.shape[1:]), ffn.reshape(shape + ffn.shape[1:])
    w_query, w_key, w_value, w_out, w_gate, w_up, w_down = [
        lax.all_gather(w, "fsdp", axis=0, tiled=True)
        for w in (w_query, w_key, w_value, w_out, w_gate, w_up, w_down)
    ]
    chunks = w_down.shape[0] // (2 * FF_TILE)
    quarter, strip = width // chunks, width // pieces

    def columns(weight):
        return weight.reshape(chunks, quarter, pieces, -1).transpose(2, 0, 1, 3)

    def turned(weight):
        shape = (pieces, strip, chunks, 2, weight.shape[0] // (2 * chunks))
        turned_part = weight.T.reshape(shape).transpose(0, 2, 3, 1, 4)
        return turned_part.reshape(pieces, chunks, 2 * strip, -1)

    both = jnp.concatenate([w_key, w_value], axis=1)
    attn = jnp.concatenate([columns(w_query), turned(w_out), columns(both)], axis=3)
    ffn = jnp.concatenate([columns(w_gate), columns(w_up), turned(w_down)], axis=2)
    return attn, ffn


def scatter_gradients(part_gate, part_down, part_out, part_query, part_kv, seqs, chunks):
    pieces, quarters, _, _ = part_gate.shape
    width = part_kv.shape[0]
    quarter, strip = width // quarters, width // pieces
    head_dim = part_kv.shape[1] // 2
    if pieces == seqs and quarters == chunks:
        both = part_kv.reshape(quarters, quarter, 2, pieces, head_dim // pieces)
        both = both.transpose(3, 0, 1, 2, 4).reshape(pieces, quarters, quarter, -1)
        part_attn = jnp.concatenate([part_query, both], axis=3)
        down = scattered(part_down)
        out = scattered(part_out)
        gate = scattered(part_gate)
        attn = scattered(part_attn)
        down = jnp.concatenate([down[:strip], down[strip:]], axis=1)
        return (
            attn[:, :128].astype(f32),
            attn[:, 128 : 128 + head_dim // pieces].astype(f32),
            attn[:, 128 + head_dim // pieces :].astype(f32),
            out.astype(f32).T,
            gate[:quarter].astype(f32),
            gate[quarter:].astype(f32),
            down.astype(f32).T,
        )

    def columns(parts):
        return parts.transpose(1, 2, 0, 3).reshape(width, -1)

    down = part_down.reshape(pieces, quarters, 2, strip, FF_TILE).transpose(1, 2, 4, 0, 3)
    out = part_out.transpose(1, 3, 0, 2)
    return tuple(
        scattered_plain(part)
        for part in (
            columns(part_query),
            part_kv[:, :head_dim],
            part_kv[:, head_dim:],
            out.reshape(-1, width),
            columns(part_gate[:, :, :quarter]),
            columns(part_gate[:, :, quarter:]),
            down.reshape(-1, width),
        )
    )


def body(
    tokens, doc_starts, w_query, w_key, w_value, w_out, w_gate, w_up, w_down,
    pre_attn, post_attn, pre_ffn, post_ffn, query_norm, key_norm, cotangent,
):
    seq_dev, block, width = tokens.shape
    head_dim = w_key.shape[1]
    inner = w_query.shape[1]
    hidden_dim = w_gate.shape[1]
    count = seq_dev * block
    seqs, chunks = lax.axis_size("seq"), lax.axis_size("fsdp")
    offset = lax.axis_index("seq") * block
    indices = offset + jnp.arange(block, dtype=jnp.int32)
    marked = jnp.where(doc_starts == 1, indices[None, :], -1)
    before = carried_in(
        jnp.max(marked, axis=1), "seq", jnp.maximum, jnp.full((seq_dev,), -1, jnp.int32)
    )
    latest = jnp.maximum(lax.cummax(marked, axis=1), before[:, None])
    positions = indices[None, :] - latest
    far_tokens = passed_along(tokens, "seq", 1).reshape(count, width)
    far_positions = passed_along(positions, "seq", 1)
    cosine, sine = tables(positions.reshape(count), head_dim)
    far_cosine, far_sine = tables(far_positions.reshape(count), head_dim)
    pos_column = positions.reshape(count, 1)

    pack, ffn_pack = gather_weights(
        w_query, w_key, w_value, w_out, w_gate, w_up, w_down, seqs, chunks
    )
    pieces, quarters = ffn_pack.shape[:2]
    quarter, strip = width // quarters, width // pieces
    gains = [g.reshape(1, -1) for g in (pre_attn, post_attn, pre_ffn, post_ffn)]
    pre_attn, post_attn, pre_ffn, post_ffn = gains
    query_norm, key_norm = query_norm.reshape(1, -1), key_norm.reshape(1, -1)
    tokens_2d = tokens.reshape(count, width)
    cot_2d = cotangent.reshape(count, width)

    tok_spec = rows(block, width)
    half_spec = rows(block, head_dim // 2)
    key_spec = pl.BlockSpec((1, 2 * block, head_dim), lambda i: (i, 0, 0))
    gain_w, gain_h = whole((1, width)), whole((1, head_dim))
    wq_spec, wkv_spec, wot_spec = (
        whole((width, inner)),
        whole((width, 2 * head_dim)),
        whole((width, inner)),
    )
    attn_low, query_raw, query_rot, key_raw, keys, values, full_q, full_kv, full_ot = (
        pl.pallas_call(
            qkv_kernel,
            grid=(seq_dev,),
            in_specs=[tok_spec, tok_spec, half_spec, half_spec, half_spec, half_spec]
            + [whole(pack.shape), gain_w, gain_h, gain_h],
            out_specs=[
                tok_spec,
                rows(block, inner),
                rows(block, inner),
                rows(block, head_dim),
                key_spec,
                key_spec,
                wq_spec,
                wkv_spec,
                wot_spec,
            ],
            out_shape=[
                shaped((count, width), bf16),
                shaped((count, inner), f32),
                shaped((count, inner), bf16),
                shaped((count, head_dim), f32),
                shaped((seq_dev, 2 * block, head_dim), bf16),
                shaped((seq_dev, 2 * block, head_dim), bf16),
                shaped((width, inner), bf16),
                shaped((width, 2 * head_dim), bf16),
                shaped((width, inner), bf16),
            ],
            compiler_params=params(),
            name="project_rotate",
        )(
            tokens_2d, far_tokens, cosine, sine, far_cosine, far_sine, pack,
            pre_attn, query_norm, key_norm,
        )
    )
    context, log_total, attn_branch, residual, ffn_in = pl.pallas_call(
        attn_kernel,
        grid=(seq_dev,),
        in_specs=[rows(block, inner), key_spec, key_spec, rows(block, 1), tok_spec]
        + [wot_spec, gain_w, gain_w],
        out_specs=[rows(block, inner), rows(block, 128), tok_spec, tok_spec, tok_spec],
        out_shape=[
            shaped((count, inner), bf16),
            shaped((count, 128), f32),
            shaped((count, width), f32),
            shaped((count, width), f32),
            shaped((count, width), bf16),
        ],
        compiler_params=params(),
        name="window_attention",
    )(query_rot, keys, values, pos_column, tokens_2d, full_ot, post_attn, pre_ffn)

    small = rows(FFN_ROWS, width)
    wide = rows(FFN_ROWS, hidden_dim)
    layer_out, hidden, g_gate, g_up, g_ffn, g_res, g_attn, g_ctx, ffn_gains = pl.pallas_call(
        ffn_kernel,
        grid=(count // FFN_ROWS,),
        in_specs=[small, small, small, small, whole(ffn_pack.shape), wot_spec]
        + [gain_w, gain_w, gain_w],
        out_specs=[small, wide, wide, wide, small, small, small, rows(FFN_ROWS, inner)]
        + [whole((8, width))],
        out_shape=[
            shaped((count, width), bf16),
            shaped((count, hidden_dim), bf16),
            shaped((count, hidden_dim), bf16),
            shaped((count, hidden_dim), bf16),
            shaped((count, width), bf16),
            shaped((count, width), f32),
            shaped((count, width), bf16),
            shaped((count, inner), bf16),
            shaped((8, width), f32),
        ],
        scratch_shapes=[
            pltpu.VMEM((FFN_ROWS, hidden_dim), f32),
            pltpu.VMEM((FFN_ROWS, hidden_dim), f32),
        ],
        compiler_params=params(),
        name="feed_forward",
    )(residual, ffn_in, cot_2d, attn_branch, ffn_pack, full_ot, post_ffn, pre_ffn, post_attn)

    full_rows = whole((count, width))
    ff_cols = pl.BlockSpec((count, FF_TILE), lambda j: (0, j))
    left_scratch = [pltpu.VMEM((width, count), bf16)]
    part_down = pl.pallas_call(
        down_kernel,
        grid=(pieces,),
        in_specs=[full_rows, ff_cols],
        out_specs=pl.BlockSpec((pieces, 1, strip, FF_TILE), lambda j: (0, j // 2, j % 2, 0)),
        out_shape=shaped((pieces, quarters, 2 * strip, FF_TILE), bf16),
        scratch_shapes=left_scratch,
        compiler_params=params(),
        name="down_gradient",
    )(g_ffn, hidden)
    part_gate = pl.pallas_call(
        gate_kernel,
        grid=(pieces,),
        in_specs=[full_rows, ff_cols, ff_cols],
        out_specs=pl.BlockSpec((1, quarters, 2 * quarter, FF_TILE), lambda j: (j, 0, 0, 0)),
        out_shape=shaped((pieces, quarters, 2 * quarter, FF_TILE), bf16),
        scratch_shapes=left_scratch,
        compiler_params=params(),
        name="gate_up_gradient",
    )(ffn_in, g_gate, g_up)
    part_out = pl.pallas_call(
        down_kernel,
        grid=(quarters,),
        in_specs=[full_rows, ff_cols],
        out_specs=pl.BlockSpec((pieces, 1, strip, FF_TILE), lambda j: (0, j, 0, 0)),
        out_shape=shaped((pieces, quarters, strip, FF_TILE), bf16),
        scratch_shapes=left_scratch,
        compiler_params=params(),
        name="out_gradient",
    )(g_attn, context)

    kv_spec = pl.BlockSpec((1, block, 2 * head_dim), lambda i: (i, 0, 0))
    g_query, g_far, g_near, query_gain = pl.pallas_call(
        attn_back_kernel,
        grid=(seq_dev,),
        in_specs=[rows(block, inner), rows(block, inner), key_spec, key_spec, rows(block, 1)]
        + [rows(block, 128), rows(block, inner), half_spec, half_spec, gain_h],
        out_specs=[rows(block, inner), kv_spec, kv_spec, whole((8, head_dim))],
        out_shape=[
            shaped((count, inner), bf16),
            shaped((seq_dev, block, 2 * head_dim), bf16),
            shaped((seq_dev, block, 2 * head_dim), f32),
            shaped((8, head_dim), f32),
        ],
        scratch_shapes=[
            pltpu.VMEM((2 * block, head_dim), f32),
            pltpu.VMEM((2 * block, head_dim), f32),
        ],
        compiler_params=params(),
        name="attention_gradient",
    )(
        query_rot, g_ctx, keys, values, pos_column, log_total, query_raw, cosine, sine, query_norm
    )
    g_recv = passed_along(g_far, "seq", -1)
    part_query = pl.pallas_call(
        query_kernel,
        grid=(inner // 256,),
        in_specs=[full_rows, ff_cols],
        out_specs=pl.BlockSpec((2, quarters, quarter, 128), lambda j: (j, 0, 0, 0)),
        out_shape=shaped((inner // 128, quarters, quarter, 128), bf16),
        scratch_shapes=left_scratch,
        compiler_params=params(),
        name="query_gradient",
    )(attn_low, g_query)
    dtokens, g_kv, key_gain, attn_gain = pl.pallas_call(
        input_kernel,
        grid=(seq_dev,),
        in_specs=[kv_spec, kv_spec, rows(block, head_dim), half_spec, half_spec]
        + [rows(block, inner), wq_spec, wkv_spec, tok_spec, tok_spec, gain_h, gain_w],
        out_specs=[tok_spec, rows(block, 2 * head_dim), whole((8, head_dim)), whole((8, width))],
        out_shape=[
            shaped((count, width), bf16),
            shaped((count, 2 * head_dim), bf16),
            shaped((8, head_dim), f32),
            shaped((8, width), f32),
        ],
        compiler_params=params(),
        name="input_gradient",
    )(
        g_near, g_recv, key_raw, cosine, sine, g_query, full_q, full_kv, tokens_2d, g_res,
        key_norm, pre_attn,
    )
    part_kv = pl.pallas_call(
        kv_kernel,
        out_shape=shaped((width, 2 * head_dim), bf16),
        compiler_params=params(),
        name="key_value_gradient",
    )(attn_low, g_kv)

    weights = scatter_gradients(
        part_gate, part_down, part_out, part_query, part_kv, seqs, chunks
    )
    sums = lax.psum(
        jnp.concatenate(
            [attn_gain[0], ffn_gains[2], ffn_gains[1], ffn_gains[0], query_gain[0], key_gain[0]]
        ),
        ("seq", "fsdp"),
    )
    cuts = [0, width, 2 * width, 3 * width, 4 * width, 4 * width + head_dim]
    cuts.append(cuts[-1] + head_dim)
    gain_sums = tuple(sums[a:b] for a, b in zip(cuts[:-1], cuts[1:]))
    shape = (seq_dev, block, width)
    return (layer_out.reshape(shape), dtokens.reshape(shape)) + weights + gain_sums


def solution(mesh):
    sharded = P("fsdp", "seq", None)
    weight = P("fsdp", None)
    in_specs = (sharded, P("fsdp", "seq")) + (weight,) * 7 + (P(),) * 6 + (sharded,)
    out_specs = (sharded, sharded) + (P("fsdp", "seq"),) * 7 + (P(),) * 6
    return jax.shard_map(body, mesh=mesh, in_specs=in_specs, out_specs=out_specs, check_vma=False)
```

```python
import jax
import jax.numpy as jnp
import numpy as np
from jax import lax
from jax.experimental import pallas as pl
from jax.experimental.pallas import tpu as pltpu
from jax.sharding import PartitionSpec as P

WINDOW = 512
TILE = 128
FF_TILE = 256
FFN_ROWS = 256

epsilon = 1e-06
NEG_FILL = -1e30
ROPE_BASE = 10000.0
GELU_C = 0.7978845608028654
GELU_K = 0.044715

f32 = jnp.float32
bf16 = jnp.bfloat16

NN = (((1,), (0,)), ((), ()))
NT = (((1,), (1,)), ((), ()))
TN = (((0,), (0,)), ((), ()))


def mm(left, right, dims=NN):
    return lax.dot_general(left, right, dims, preferred_element_type=f32)


def inv_rms(vector):
    return lax.rsqrt(jnp.mean(vector * vector, axis=-1, keepdims=True) + epsilon)


def norm_back(vector, inv, gain, grad):
    unit = vector * inv
    scaled = gain * grad
    back = inv * (scaled - unit * jnp.mean(unit * scaled, axis=-1, keepdims=True))
    return back, grad * unit


def rope(vector, cosine, sine):
    half = vector.shape[-1] // 2
    one, two = vector[:, :half], vector[:, half:]
    return jnp.concatenate([one * cosine - two * sine, two * cosine + one * sine], axis=1)


def rope_back(vector, cosine, sine):
    half = vector.shape[-1] // 2
    one, two = vector[:, :half], vector[:, half:]
    return jnp.concatenate([one * cosine + two * sine, two * cosine - one * sine], axis=1)


def params(limit_mib=56):
    return pltpu.CompilerParams(vmem_limit_bytes=limit_mib * 1024 * 1024)


def whole(shape):
    return pl.BlockSpec(shape, lambda *_: (0,) * len(shape))


def rows(count, width):
    return pl.BlockSpec((count, width), lambda i: (i, 0))


def shaped(shape, dtype):
    return jax.ShapeDtypeStruct(shape, dtype)


def qkv_kernel(
    place_ref, tok_ref, far_ref, cos_ref, sin_ref, pack_ref, pre_ref, qn_ref, kn_ref,
    attn_ref, qraw_ref, qrot_ref, kraw_ref, key_ref, val_ref, wq_ref, wkv_ref, wot_ref,
):
    head_dim = kn_ref.shape[1]
    head_count = wq_ref.shape[1] // head_dim
    block, width = tok_ref.shape
    pieces, chunks, chunk_rows, _ = pack_ref.shape

    @pl.when(pl.program_id(0) == 0)
    def _():
        def part(s, z, begin, end):
            return pack_ref[place_ref[s], place_ref[pieces + z], :, begin:end]

        half = chunk_rows // 2
        for z in range(chunks):
            own = slice(z * chunk_rows, (z + 1) * chunk_rows)
            for s in range(pieces):
                wq_ref[own, s * 128 : (s + 1) * 128] = part(s, z, 0, 128)
                turned = part(s, z, 128, 256)
                for i in range(2):
                    wot_ref[
                        s * half : (s + 1) * half, z * 256 + i * 128 : z * 256 + (i + 1) * 128
                    ] = turned[i * half : (i + 1) * half]
            for s in range(0, pieces, 2):
                wkv_ref[own, s * 64 : (s + 2) * 64] = jnp.concatenate(
                    [part(s, z, 256, 320), part(s + 1, z, 256, 320)], axis=1
                )

    pre = pre_ref[...]
    kgain = kn_ref[...]
    token = tok_ref[...].astype(f32)
    low = (token * inv_rms(token) * pre).astype(bf16)
    attn_ref[...] = low
    query = mm(low, wq_ref[...])
    qraw_ref[...] = query
    cosine, sine = cos_ref[block:, :], sin_ref[block:, :]
    scaling = head_dim ** (-0.5)
    for h in range(head_count):
        part = query[:, h * head_dim : (h + 1) * head_dim]
        normed = part * inv_rms(part) * qn_ref[...]
        qrot_ref[:, h * head_dim : (h + 1) * head_dim] = (
            rope(normed, cosine, sine).astype(bf16) * jnp.asarray(scaling, bf16)
        )
    both = mm(low, wkv_ref[...])
    key = both[:, :head_dim]
    kraw_ref[...] = key
    key_ref[0, block:, :] = rope(key * inv_rms(key) * kgain, cosine, sine).astype(bf16)
    val_ref[0, block:, :] = both[:, head_dim:].astype(bf16)
    token = far_ref[...].astype(f32)
    low = (token * inv_rms(token) * pre).astype(bf16)
    both = mm(low, wkv_ref[...])
    key = both[:, :head_dim]
    key_ref[0, :block, :] = rope(
        key * inv_rms(key) * kgain, cos_ref[:block, :], sin_ref[:block, :]
    ).astype(bf16)
    val_ref[0, :block, :] = both[:, head_dim:].astype(bf16)


def stacked(ref, tile, head_count, head_dim):
    return jnp.concatenate(
        [
            ref[tile * TILE : (tile + 1) * TILE, h * head_dim : (h + 1) * head_dim]
            for h in range(head_count)
        ],
        axis=0,
    )


def mask_of(pos_ref, tile, span):
    reach = pos_ref[tile * TILE : (tile + 1) * TILE, :]
    row = lax.broadcasted_iota(jnp.int32, (TILE, span), 0)
    col = lax.broadcasted_iota(jnp.int32, (TILE, span), 1)
    distance = WINDOW + row - col
    return jnp.where((distance >= 0) & (distance <= reach), 0.0, NEG_FILL)


def attn_kernel(
    q_ref, key_ref, val_ref, pos_ref, tok_ref, wot_ref, post_ref, pre_ref,
    ctx_ref, lse_ref, branch_ref, res_ref, fin_ref,
):
    head_dim = key_ref.shape[2]
    head_count = q_ref.shape[1] // head_dim
    span = WINDOW + TILE
    lane = lax.broadcasted_iota(jnp.int32, (TILE, 128), 1)
    for tile in range(q_ref.shape[0] // TILE):
        query = stacked(q_ref, tile, head_count, head_dim)
        key = key_ref[0, tile * TILE : tile * TILE + span, :]
        value = val_ref[0, tile * TILE : tile * TILE + span, :]
        score = mm(query, key, NT).reshape(head_count, TILE, span) + mask_of(pos_ref, tile, span)
        largest = jnp.max(score, axis=-1, keepdims=True)
        expo = jnp.exp(score - largest)
        total = jnp.sum(expo, axis=-1, keepdims=True)
        low = expo.astype(bf16).reshape(head_count * TILE, span)
        context = mm(low, value).reshape(head_count, TILE, head_dim) / total
        log_total = largest + jnp.log(total)
        kept = jnp.zeros((TILE, 128), f32)
        for h in range(head_count):
            ctx_ref[tile * TILE : (tile + 1) * TILE, h * head_dim : (h + 1) * head_dim] = context[
                h
            ].astype(bf16)
            kept = jnp.where(lane == h, log_total[h], kept)
        lse_ref[tile * TILE : (tile + 1) * TILE, :] = kept
    branch = mm(ctx_ref[...], wot_ref[...], NT)
    branch_ref[...] = branch
    residual = tok_ref[...].astype(f32) + branch * inv_rms(branch) * post_ref[...]
    res_ref[...] = residual
    fin_ref[...] = (residual * inv_rms(residual) * pre_ref[...]).astype(bf16)


def ffn_kernel(
    res_ref, fin_ref, cot_ref, branch_ref, wf_ref, wot_ref, postf_ref, pref_ref, posta_ref,
    out_ref, hid_ref, gg_ref, gu_ref, gffn_ref, gres_ref, gattn_ref, gctx_ref, gain_ref,
    slope_ref, act_ref,
):
    pieces, chunks, _, _ = wf_ref.shape
    width = res_ref.shape[1]
    quarter = width // chunks
    strip = width // pieces

    def gate_block(j):
        return wf_ref[j, :, :quarter, :].reshape(width, FF_TILE)

    def up_block(j):
        return wf_ref[j, :, quarter : 2 * quarter, :].reshape(width, FF_TILE)

    def down_block(j):
        start = 2 * quarter + (j % 2) * strip
        return wf_ref[:, j // 2, start : start + strip, :].reshape(width, FF_TILE)

    @pl.when(pl.program_id(0) == 0)
    def _():
        gain_ref[...] = jnp.zeros_like(gain_ref)

    ffn_in = fin_ref[...]
    branch = jnp.zeros(res_ref.shape, f32)
    for j in range(pieces):
        cols = slice(j * FF_TILE, (j + 1) * FF_TILE)
        gate = mm(ffn_in, gate_block(j))
        up = mm(ffn_in, up_block(j))
        square = gate * gate
        bent = jnp.tanh(GELU_C * gate * (1.0 + GELU_K * square))
        half = 0.5 * (1.0 + bent)
        act = gate * half
        slope = half + 0.5 * gate * (1.0 - bent * bent) * (
            GELU_C * (1.0 + 3.0 * GELU_K * square)
        )
        act_ref[:, cols] = act
        slope_ref[:, cols] = slope * up
        hidden = (act * up).astype(bf16)
        hid_ref[:, cols] = hidden
        branch += mm(hidden, down_block(j), NT)
    residual = res_ref[...]
    cot = cot_ref[...].astype(f32)
    inv = inv_rms(branch)
    out_ref[...] = (residual + branch * inv * postf_ref[...]).astype(bf16)
    g_ffn, gain_post = norm_back(branch, inv, postf_ref[...], cot)
    g_low = g_ffn.astype(bf16)
    gffn_ref[...] = g_low
    g_in = jnp.zeros(res_ref.shape, f32)
    for j in range(pieces):
        cols = slice(j * FF_TILE, (j + 1) * FF_TILE)
        g_hidden = mm(g_low, down_block(j))
        g_gate = (g_hidden * slope_ref[:, cols]).astype(bf16)
        g_up = (g_hidden * act_ref[:, cols]).astype(bf16)
        gg_ref[:, cols] = g_gate
        gu_ref[:, cols] = g_up
        g_in += mm(g_gate, gate_block(j), NT) + mm(g_up, up_block(j), NT)
    back, gain_pre = norm_back(residual, inv_rms(residual), pref_ref[...], g_in)
    g_res = cot + back
    gres_ref[...] = g_res
    attn_branch = branch_ref[...]
    g_attn, gain_attn = norm_back(attn_branch, inv_rms(attn_branch), posta_ref[...], g_res)
    g_attn = g_attn.astype(bf16)
    gattn_ref[...] = g_attn
    gctx_ref[...] = mm(g_attn, wot_ref[...]).astype(bf16)
    gain_ref[0:1, :] += jnp.sum(gain_post, axis=0, keepdims=True)
    gain_ref[1:2, :] += jnp.sum(gain_pre, axis=0, keepdims=True)
    gain_ref[2:3, :] += jnp.sum(gain_attn, axis=0, keepdims=True)


def turn_strips(left_ref, source, strip, where, count):
    left_ref[1] = source.T
    for m in range(count):
        begin = pl.multiple_of(where(m) * strip, 16)
        left_ref[0, m * strip : (m + 1) * strip, :] = left_ref[1, pl.ds(begin, strip), :]


def ffn_grad_kernel(
    base, order_ref, fin_ref, gffn_ref, gattn_ref, gg_ref, gu_ref, hid_ref, ctx_ref, *refs
):
    recv_ref = refs[0] if base else None
    outs = refs[1:3] if base else refs[:1]
    in_left, ffn_left, attn_left = refs[-3:]
    held, chunks, _, tile = outs[0].shape
    width = fin_ref.shape[1]
    pieces = order_ref.shape[0] - chunks
    quarter, strip = width // chunks, width // pieces
    half = pieces // 2
    j = pl.program_id(0)

    @pl.when(j == 0)
    def _():
        turn_strips(in_left, fin_ref[...], quarter, lambda m: order_ref[pieces + m], chunks)
        turn_strips(ffn_left, gffn_ref[...], strip, lambda m: order_ref[base + m], half)
        turn_strips(attn_left, gattn_ref[...], strip, lambda m: order_ref[base + m], half)

    def put(piece, chunk, begin, value):
        end = begin + value.shape[0]
        if base:
            value = value + recv_ref[piece, chunk, begin:end, :].astype(f32)
        for i, out in enumerate(outs):
            if len(outs) == 1:
                out[piece, chunk, begin:end, :] = value.astype(bf16)
            elif isinstance(piece, int):
                if piece // held == i:
                    out[piece % held, chunk, begin:end, :] = value.astype(bf16)
            else:

                @pl.when(piece // held == i)
                def _(out=out):
                    out[piece % held, chunk, begin:end, :] = value.astype(bf16)

    for i, ref in enumerate((gg_ref, gu_ref)):
        part = mm(in_left[0], ref[...])
        for z in range(chunks):
            put(j, z, i * quarter, part[z * quarter : (z + 1) * quarter])
    part = mm(ffn_left[0, : half * strip, :], hid_ref[...])
    for m in range(half):
        for i in range(2):
            put(
                m, j, 2 * quarter + i * strip,
                part[m * strip : (m + 1) * strip, i * tile : (i + 1) * tile],
            )
    part = mm(attn_left[0, : half * strip, :], ctx_ref[...])
    for m in range(half):
        put(m, j, 2 * quarter + 2 * strip, part[m * strip : (m + 1) * strip])


def attn_grad_kernel(base, order_ref, attn_ref, gq_ref, gkv_ref, sort_ref, *refs):
    recv_ref = refs[0] if base else None
    outs = refs[1:3] if base else refs[:1]
    left = refs[-1]
    held, chunks, quarter, _ = outs[0].shape
    width = attn_ref.shape[1]
    pieces = order_ref.shape[0] - chunks
    half = pieces // 2
    turn_strips(left, attn_ref[...], quarter, lambda m: order_ref[pieces + m], chunks)
    sorted_kv = mm(gkv_ref[...], sort_ref[...]).astype(bf16)
    part_kv = mm(left[0], sorted_kv)
    wide = part_kv.shape[1] // half
    for pair in range(0, half, 2):
        both = jnp.concatenate(
            [
                gq_ref[:, pl.ds(pl.multiple_of(order_ref[base + pair + i] * 128, 128), 128)]
                for i in range(2)
            ],
            axis=1,
        )
        part = mm(left[0], both)
        for i in range(2):
            m = pair + i
            value = part[:, i * 128 : (i + 1) * 128].reshape(chunks, quarter, 128)
            value_kv = part_kv[:, m * wide : (m + 1) * wide].reshape(chunks, quarter, wide)
            if base:
                value = value + recv_ref[m, :, :, :128].astype(f32)
                value_kv = value_kv + recv_ref[m, :, :, 128:].astype(f32)
            out = outs[m // held]
            out[m % held, :, :, :128] = value.astype(bf16)
            out[m % held, :, :, 128:] = value_kv.astype(bf16)


def attn_back_kernel(
    q_ref, gctx_ref, key_ref, val_ref, pos_ref, lse_ref, qraw_ref, cos_ref, sin_ref, qn_ref,
    gq_ref, far_ref, near_ref, gain_ref, gkey_ref, gval_ref,
):
    head_dim = key_ref.shape[2]
    head_count = q_ref.shape[1] // head_dim
    block = q_ref.shape[0]
    span = WINDOW + TILE
    scaling = head_dim ** (-0.5)

    @pl.when(pl.program_id(0) == 0)
    def _():
        gain_ref[...] = jnp.zeros_like(gain_ref)

    gkey_ref[...] = jnp.zeros_like(gkey_ref)
    gval_ref[...] = jnp.zeros_like(gval_ref)
    gain = jnp.zeros((1, head_dim), f32)
    for tile in range(block // TILE):
        own = slice(tile * TILE, (tile + 1) * TILE)
        reach = slice(tile * TILE, tile * TILE + span)
        query = stacked(q_ref, tile, head_count, head_dim)
        g_ctx = stacked(gctx_ref, tile, head_count, head_dim)
        key = key_ref[0, reach, :]
        value = val_ref[0, reach, :]
        log_total = jnp.stack([lse_ref[own, h : h + 1] for h in range(head_count)])
        score = mm(query, key, NT).reshape(head_count, TILE, span) + mask_of(pos_ref, tile, span)
        probs = jnp.exp(score - log_total)
        g_probs = mm(g_ctx, value, NT).reshape(head_count, TILE, span)
        spread = jnp.sum(g_probs * probs, axis=-1, keepdims=True)
        g_score = (probs * (g_probs - spread)).astype(bf16).reshape(head_count * TILE, span)
        low = probs.astype(bf16).reshape(head_count * TILE, span)
        gkey_ref[reach, :] += mm(g_score, query, TN)
        gval_ref[reach, :] += mm(low, g_ctx, TN)
        g_rot = mm(g_score, key) * scaling
        turned = slice(block + tile * TILE, block + (tile + 1) * TILE)
        cosine, sine = cos_ref[turned, :], sin_ref[turned, :]
        for h in range(head_count):
            cols = slice(h * head_dim, (h + 1) * head_dim)
            raw = qraw_ref[own, cols]
            back, share = norm_back(
                raw,
                inv_rms(raw),
                qn_ref[...],
                rope_back(g_rot[h * TILE : (h + 1) * TILE], cosine, sine),
            )
            gq_ref[own, cols] = back.astype(bf16)
            gain += jnp.sum(share, axis=0, keepdims=True)
    gain_ref[0:1, :] += gain
    far_ref[0, :, :head_dim] = rope_back(
        gkey_ref[:block, :], cos_ref[:block, :], sin_ref[:block, :]
    ).astype(bf16)
    far_ref[0, :, head_dim:] = gval_ref[:block, :].astype(bf16)
    near_ref[0, :, :head_dim] = gkey_ref[block:, :]
    near_ref[0, :, head_dim:] = gval_ref[block:, :]


def kv_back_kernel(
    near_ref, recv_ref, kraw_ref, cos_ref, sin_ref, kn_ref, gkv_ref, kgain_ref
):
    head_dim = kn_ref.shape[1]

    @pl.when(pl.program_id(0) == 0)
    def _():
        kgain_ref[...] = jnp.zeros_like(kgain_ref)

    near, far = near_ref[0], recv_ref[0].astype(f32)
    raw = kraw_ref[...]
    g_normed = rope_back(near[:, :head_dim], cos_ref[...], sin_ref[...]) + far[:, :head_dim]
    g_key, share = norm_back(raw, inv_rms(raw), kn_ref[...], g_normed)
    kgain_ref[0:1, :] += jnp.sum(share, axis=0, keepdims=True)
    gkv_ref[:, :head_dim] = g_key.astype(bf16)
    gkv_ref[:, head_dim:] = (near[:, head_dim:] + far[:, head_dim:]).astype(bf16)


def input_kernel(
    gq_ref, gkv_ref, wq_ref, wkv_ref, tok_ref, gres_ref, pre_ref, dtok_ref, gain_ref
):
    @pl.when(pl.program_id(0) == 0)
    def _():
        gain_ref[...] = jnp.zeros_like(gain_ref)

    g_in = mm(gq_ref[...], wq_ref[...], NT) + mm(gkv_ref[...], wkv_ref[...], NT)
    token = tok_ref[...].astype(f32)
    back, share = norm_back(token, inv_rms(token), pre_ref[...], g_in)
    dtok_ref[...] = (gres_ref[...] + back).astype(bf16)
    gain_ref[0:1, :] += jnp.sum(share, axis=0, keepdims=True)


def passed_along(shard, axis, by):
    length = lax.axis_size(axis)
    pairs = [(i, i + by) for i in range(length) if 0 <= i + by < length]
    return lax.ppermute(shard, axis, pairs)


def swapped(array, axis, even, odd):
    length = lax.axis_size(axis)
    return lax.ppermute(array, axis, [(i, i ^ (odd if i % 2 else even)) for i in range(length)])


def tables(block, head_dim):
    half_width = head_dim // 2
    frequency = ROPE_BASE ** (-(np.arange(half_width) * 2.0) / head_dim)
    angles = np.arange(-block, block)[:, None] * frequency
    return np.cos(angles).astype(np.float32), np.sin(angles).astype(np.float32)


def column_piece(array, axis_name, parts):
    wide = array.shape[1] // parts
    return lax.dynamic_slice_in_dim(array, lax.axis_index(axis_name) * wide, wide, 1)


def added(left, right):
    return left.astype(f32) + right.astype(f32)


class Exchange:
    def __init__(self, seqs, chunks):
        self.direct = seqs == 8 and chunks == 4
        if not self.direct:
            self.order = jnp.arange(12, dtype=jnp.int32) % 8
            self.place = self.order
            return
        s, z = lax.axis_index("seq"), lax.axis_index("fsdp")
        odd = s % 2 == 1
        one, two = jnp.where(odd, 4, 2), jnp.where(odd, 2, 4)
        zero = jnp.zeros_like(s)
        sent = [one | two | 1, two | 1, one | 1, zero | 1]
        kept = [one | two, one, two, zero]
        order = [s ^ k for k in sent + kept] + [z ^ k for k in (3, 1, 2, 0)]
        self.order = jnp.stack(order).astype(jnp.int32)
        held = [zero, two, one, one | two, zero | 1, one | 1, two | 1, one | two | 1]
        held = jnp.stack([s ^ k for k in held])
        held_z = jnp.stack([z ^ k for k in (0, 2, 1, 3)])
        place = jnp.sum(
            jnp.where(held[None] == jnp.arange(8)[:, None], jnp.arange(8)[None], 0), axis=1
        )
        place_z = jnp.sum(
            jnp.where(held_z[None] == jnp.arange(4)[:, None], jnp.arange(4)[None], 0), axis=1
        )
        self.place = jnp.concatenate([place, place_z]).astype(jnp.int32)

    def gather(self, piece):
        held = piece[None]
        for bits in (2, 1):
            held = jnp.concatenate([held, swapped(held, "fsdp", bits, bits)], axis=0)
        held = held[None]
        for even, odd in ((4, 2), (2, 4), (1, 1)):
            held = jnp.concatenate([held, swapped(held, "seq", even, odd)], axis=0)
        return held

    def swap_cores(self, parts):
        return swapped(parts, "seq", 1, 1)

    def reduce(self, send, keep):
        got = swapped(send, "seq", 2, 4)
        send, keep = added(keep[0], got[0]).astype(bf16), added(keep[1], got[1]).astype(bf16)
        got = swapped(send, "seq", 4, 2)
        send = added(keep[:2], got[:2]).astype(bf16)
        keep = added(keep[2:], got[2:]).astype(bf16)
        got = swapped(send, "fsdp", 1, 1)
        send, keep = added(keep[0], got[0]).astype(bf16), added(keep[1], got[1]).astype(bf16)
        return added(keep, swapped(send, "fsdp", 2, 2))

    def total(self, value):
        if not self.direct:
            return lax.psum(value, ("seq", "fsdp"))
        for axis, bits in (("seq", 1), ("seq", 2), ("seq", 4), ("fsdp", 1), ("fsdp", 2)):
            value = value + swapped(value, axis, bits, bits)
        return value


def scattered_plain(part):
    columns = lax.psum_scatter(part, "seq", scatter_dimension=1, tiled=True)
    return lax.psum_scatter(columns, "fsdp", scatter_dimension=0, tiled=True).astype(f32)


def gather_weights(w_query, w_key, w_value, w_out, w_gate, w_up, w_down, exchange):
    pieces = w_gate.shape[1] // FF_TILE
    width = w_out.shape[1]
    if exchange.direct:
        down = column_piece(w_down, "seq", pieces).T
        ffn = jnp.concatenate(
            [
                column_piece(w_gate, "seq", pieces),
                column_piece(w_up, "seq", pieces),
                down[:, :FF_TILE],
                down[:, FF_TILE:],
            ],
            axis=0,
        )
        ffn = lax.all_gather(ffn, "fsdp", axis=0, tiled=False)
        ffn = lax.all_gather(ffn, "seq", axis=0, tiled=False)
        both = jnp.concatenate([w_key, w_value], axis=1)
        out = column_piece(w_out, "seq", pieces).T
        out = jnp.concatenate([out[:, :128], out[:, 128:]], axis=0)
        attn = jnp.concatenate(
            [column_piece(w_query, "seq", pieces), out, column_piece(both, "seq", pieces)], axis=1
        )
        return exchange.gather(attn), ffn
    w_query, w_key, w_value, w_out, w_gate, w_up, w_down = [
        lax.all_gather(w, "fsdp", axis=0, tiled=True)
        for w in (w_query, w_key, w_value, w_out, w_gate, w_up, w_down)
    ]
    chunks = w_down.shape[0] // (2 * FF_TILE)
    quarter, strip = width // chunks, width // pieces

    def columns(weight):
        return weight.reshape(chunks, quarter, pieces, -1).transpose(2, 0, 1, 3)

    def turned(weight):
        shape = (pieces, strip, chunks, 2, weight.shape[0] // (2 * chunks))
        turned_part = weight.T.reshape(shape).transpose(0, 2, 3, 1, 4)
        return turned_part.reshape(pieces, chunks, 2 * strip, -1)

    both = jnp.concatenate([w_key, w_value], axis=1)
    attn = jnp.concatenate([columns(w_query), turned(w_out), columns(both)], axis=3)
    ffn = jnp.concatenate([columns(w_gate), columns(w_up), turned(w_down)], axis=2)
    return attn, ffn


def plain_gradients(part_ffn, part_attn):
    pieces, quarters = part_ffn.shape[:2]
    quarter = part_attn.shape[2]
    width = quarters * quarter
    strip = width // pieces
    down_end = 2 * quarter + 2 * strip

    def columns(parts):
        return parts.transpose(1, 2, 0, 3).reshape(width, -1)

    def turned(parts):
        parts = parts.reshape(pieces, quarters, -1, strip, FF_TILE).transpose(1, 2, 4, 0, 3)
        return parts.reshape(-1, width)

    each = part_attn.shape[3] - (part_attn.shape[3] - 128) // 2
    return tuple(
        scattered_plain(part)
        for part in (
            columns(part_attn[..., :128]),
            columns(part_attn[..., 128:each]),
            columns(part_attn[..., each:]),
            turned(part_ffn[:, :, down_end:]),
            columns(part_ffn[:, :, :quarter]),
            columns(part_ffn[:, :, quarter : 2 * quarter]),
            turned(part_ffn[:, :, 2 * quarter : down_end]),
        )
    )


def split_gradients(ffn, attn):
    quarter = attn.shape[0]
    strip = (ffn.shape[0] - 2 * quarter) // 3
    each = attn.shape[1] - (attn.shape[1] - 128) // 2
    down = ffn[2 * quarter :]
    return (
        attn[:, :128],
        attn[:, 128:each],
        attn[:, each:],
        down[2 * strip :].T,
        ffn[:quarter],
        ffn[quarter : 2 * quarter],
        jnp.concatenate([down[:strip].T, down[strip : 2 * strip].T], axis=0),
    )


def body(
    tokens, doc_starts, w_query, w_key, w_value, w_out, w_gate, w_up, w_down,
    pre_attn, post_attn, pre_ffn, post_ffn, query_norm, key_norm, cotangent,
):
    seq_dev, block, width = tokens.shape
    head_dim = w_key.shape[1]
    inner = w_query.shape[1]
    hidden_dim = w_gate.shape[1]
    count = seq_dev * block
    seqs, chunks = lax.axis_size("seq"), lax.axis_size("fsdp")
    exchange = Exchange(seqs, chunks)
    far_tokens = passed_along(tokens, "seq", 1).reshape(count, width)
    starts = jnp.concatenate([passed_along(doc_starts, "seq", 1), doc_starts], axis=1)
    indices = jnp.arange(2 * block, dtype=jnp.int32)
    latest = lax.cummax(jnp.where(starts == 1, indices[None, :], -WINDOW), axis=1)
    reach = jnp.minimum(indices[None, :] - latest, WINDOW - 1)[:, block:]
    pos_column = reach.reshape(count, 1)
    cosine, sine = tables(block, head_dim)
    own_cosine, own_sine = cosine[block:], sine[block:]

    pack, ffn_pack = gather_weights(
        w_query, w_key, w_value, w_out, w_gate, w_up, w_down, exchange
    )
    pieces, quarters = ffn_pack.shape[:2]
    quarter, strip = width // quarters, width // pieces
    gains = [g.reshape(1, -1) for g in (pre_attn, post_attn, pre_ffn, post_ffn)]
    pre_attn, post_attn, pre_ffn, post_ffn = gains
    query_norm, key_norm = query_norm.reshape(1, -1), key_norm.reshape(1, -1)
    tokens_2d = tokens.reshape(count, width)
    cot_2d = cotangent.reshape(count, width)

    tok_spec = rows(block, width)
    table_spec = whole((2 * block, head_dim // 2))
    half_spec = whole((block, head_dim // 2))
    key_spec = pl.BlockSpec((1, 2 * block, head_dim), lambda i: (i, 0, 0))
    gain_w, gain_h = whole((1, width)), whole((1, head_dim))
    wq_spec, wkv_spec, wot_spec = (
        whole((width, inner)),
        whole((width, 2 * head_dim)),
        whole((width, inner)),
    )
    smem = pl.BlockSpec(memory_space=pltpu.SMEM)
    attn_low, query_raw, query_rot, key_raw, keys, values, full_q, full_kv, full_ot = (
        pl.pallas_call(
            qkv_kernel,
            grid=(seq_dev,),
            in_specs=[smem, tok_spec, tok_spec, table_spec, table_spec]
            + [whole(pack.shape), gain_w, gain_h, gain_h],
            out_specs=[
                tok_spec,
                rows(block, inner),
                rows(block, inner),
                rows(block, head_dim),
                key_spec,
                key_spec,
                wq_spec,
                wkv_spec,
                wot_spec,
            ],
            out_shape=[
                shaped((count, width), bf16),
                shaped((count, inner), f32),
                shaped((count, inner), bf16),
                shaped((count, head_dim), f32),
                shaped((seq_dev, 2 * block, head_dim), bf16),
                shaped((seq_dev, 2 * block, head_dim), bf16),
                shaped((width, inner), bf16),
                shaped((width, 2 * head_dim), bf16),
                shaped((width, inner), bf16),
            ],
            compiler_params=params(),
            name="project_rotate",
        )(
            exchange.place, tokens_2d, far_tokens, cosine, sine, pack,
            pre_attn, query_norm, key_norm,
        )
    )
    context, log_total, attn_branch, residual, ffn_in = pl.pallas_call(
        attn_kernel,
        grid=(seq_dev,),
        in_specs=[rows(block, inner), key_spec, key_spec, rows(block, 1), tok_spec]
        + [wot_spec, gain_w, gain_w],
        out_specs=[rows(block, inner), rows(block, 128), tok_spec, tok_spec, tok_spec],
        out_shape=[
            shaped((count, inner), bf16),
            shaped((count, 128), f32),
            shaped((count, width), f32),
            shaped((count, width), f32),
            shaped((count, width), bf16),
        ],
        compiler_params=params(),
        name="window_attention",
    )(query_rot, keys, values, pos_column, tokens_2d, full_ot, post_attn, pre_ffn)

    small = rows(FFN_ROWS, width)
    wide = rows(FFN_ROWS, hidden_dim)
    layer_out, hidden, g_gate, g_up, g_ffn, g_res, g_attn, g_ctx, ffn_gains = pl.pallas_call(
        ffn_kernel,
        grid=(count // FFN_ROWS,),
        in_specs=[small, small, small, small, whole(ffn_pack.shape), wot_spec]
        + [gain_w, gain_w, gain_w],
        out_specs=[small, wide, wide, wide, small, small, small, rows(FFN_ROWS, inner)]
        + [whole((8, width))],
        out_shape=[
            shaped((count, width), bf16),
            shaped((count, hidden_dim), bf16),
            shaped((count, hidden_dim), bf16),
            shaped((count, hidden_dim), bf16),
            shaped((count, width), bf16),
            shaped((count, width), f32),
            shaped((count, width), bf16),
            shaped((count, inner), bf16),
            shaped((8, width), f32),
        ],
        scratch_shapes=[
            pltpu.VMEM((FFN_ROWS, hidden_dim), f32),
            pltpu.VMEM((FFN_ROWS, hidden_dim), f32),
        ],
        compiler_params=params(),
        name="feed_forward",
    )(residual, ffn_in, cot_2d, attn_branch, ffn_pack, full_ot, post_ffn, pre_ffn, post_attn)

    half = pieces // 2
    full_rows = whole((count, width))

    def ffn_parts(base, extra):
        shape = (half, quarters, 2 * quarter + 3 * strip, FF_TILE)
        sent = (half // 2,) + shape[1:]
        outs = [shape] if base == 0 else [sent, sent]
        turned = pltpu.VMEM((2, width, count), bf16)
        by_piece = pl.BlockSpec((count, FF_TILE), lambda j, order: (0, order[base + j]))
        wide = pl.BlockSpec((count, 2 * FF_TILE), lambda j, order: (0, order[pieces + j]))
        by_chunk = pl.BlockSpec((count, FF_TILE), lambda j, order: (0, order[pieces + j]))
        return pl.pallas_call(
            lambda *refs: ffn_grad_kernel(base, *refs),
            grid_spec=pltpu.PrefetchScalarGridSpec(
                num_scalar_prefetch=1,
                grid=(half,),
                in_specs=[full_rows, full_rows, full_rows, by_piece, by_piece, wide, by_chunk]
                + [whole(e.shape) for e in extra],
                out_specs=[whole(o) for o in outs],
                scratch_shapes=[turned, turned, turned],
            ),
            out_shape=[shaped(o, bf16) for o in outs],
            compiler_params=params(),
            name="ffn_gradients_kept" if base else "ffn_gradients_sent",
        )(exchange.order, ffn_in, g_ffn, g_attn, g_gate, g_up, hidden, context, *extra)

    (ffn_sent,) = ffn_parts(0, [])
    ffn_got = exchange.swap_cores(ffn_sent) if exchange.direct else jnp.zeros_like(ffn_sent)
    ffn_parts_kept = ffn_parts(half, [ffn_got])

    kv_spec = pl.BlockSpec((1, block, 2 * head_dim), lambda i: (i, 0, 0))
    g_query, g_far, g_near, query_gain = pl.pallas_call(
        attn_back_kernel,
        grid=(seq_dev,),
        in_specs=[rows(block, inner), rows(block, inner), key_spec, key_spec, rows(block, 1)]
        + [rows(block, 128), rows(block, inner), table_spec, table_spec, gain_h],
        out_specs=[rows(block, inner), kv_spec, kv_spec, whole((8, head_dim))],
        out_shape=[
            shaped((count, inner), bf16),
            shaped((seq_dev, block, 2 * head_dim), bf16),
            shaped((seq_dev, block, 2 * head_dim), f32),
            shaped((8, head_dim), f32),
        ],
        scratch_shapes=[
            pltpu.VMEM((2 * block, head_dim), f32),
            pltpu.VMEM((2 * block, head_dim), f32),
        ],
        compiler_params=params(),
        name="attention_gradient",
    )(
        query_rot, g_ctx, keys, values, pos_column, log_total, query_raw, cosine, sine,
        query_norm,
    )
    g_recv = passed_along(g_far, "seq", -1)
    g_kv, key_gain = pl.pallas_call(
        kv_back_kernel,
        grid=(seq_dev,),
        in_specs=[kv_spec, kv_spec, rows(block, head_dim), half_spec, half_spec, gain_h],
        out_specs=[rows(block, 2 * head_dim), whole((8, head_dim))],
        out_shape=[shaped((count, 2 * head_dim), bf16), shaped((8, head_dim), f32)],
        compiler_params=params(),
        name="key_value_back",
    )(g_near, g_recv, key_raw, own_cosine, own_sine, key_norm)

    each = head_dim // pieces
    column = jnp.arange(2 * head_dim, dtype=jnp.int32)
    inside = column % (2 * each)
    source = jnp.where(inside < each, inside, inside - each + head_dim)
    source = source + each * jnp.repeat(exchange.order[:pieces], 2 * each)
    sort = (column[:, None] == source[None, :]).astype(bf16)

    def attn_parts(base, extra):
        shape = (half, quarters, quarter, 128 + 2 * each)
        sent = (half // 2,) + shape[1:]
        outs = [shape] if base == 0 else [sent, sent]
        vmem = pl.BlockSpec(memory_space=pltpu.VMEM)
        chosen = sort[:, base * 2 * each : (base + half) * 2 * each]
        return pl.pallas_call(
            lambda *refs: attn_grad_kernel(base, *refs),
            in_specs=[smem] + [vmem] * (4 + len(extra)),
            out_specs=[vmem] * len(outs),
            out_shape=[shaped(o, bf16) for o in outs],
            scratch_shapes=[pltpu.VMEM((2, width, count), bf16)],
            compiler_params=params(),
            name="attn_gradients_kept" if base else "attn_gradients_sent",
        )(exchange.order, attn_low, g_query, g_kv, chosen, *extra)

    (attn_sent,) = attn_parts(0, [])
    attn_got = exchange.swap_cores(attn_sent) if exchange.direct else jnp.zeros_like(attn_sent)
    attn_parts_kept = attn_parts(half, [attn_got])
    g_res, attn_parts_kept = lax.optimization_barrier((g_res, attn_parts_kept))
    dtokens, attn_gain = pl.pallas_call(
        input_kernel,
        grid=(seq_dev,),
        in_specs=[rows(block, inner), rows(block, 2 * head_dim), wq_spec, wkv_spec]
        + [tok_spec, tok_spec, gain_w],
        out_specs=[tok_spec, whole((8, width))],
        out_shape=[shaped((count, width), bf16), shaped((8, width), f32)],
        compiler_params=params(),
        name="input_gradient",
    )(g_query, g_kv, full_q, full_kv, tokens_2d, g_res, pre_attn)

    if exchange.direct:
        weights = split_gradients(
            exchange.reduce(*ffn_parts_kept), exchange.reduce(*attn_parts_kept)
        )
    else:
        weights = plain_gradients(
            jnp.concatenate([ffn_sent, *ffn_parts_kept], axis=0),
            jnp.concatenate([attn_sent, *attn_parts_kept], axis=0),
        )
    sums = exchange.total(
        jnp.concatenate(
            [attn_gain[0], ffn_gains[2], ffn_gains[1], ffn_gains[0], query_gain[0], key_gain[0]]
        )
    )
    cuts = [0, width, 2 * width, 3 * width, 4 * width, 4 * width + head_dim]
    cuts.append(cuts[-1] + head_dim)
    gain_sums = tuple(sums[a:b] for a, b in zip(cuts[:-1], cuts[1:]))
    shape = (seq_dev, block, width)
    return (layer_out.reshape(shape), dtokens.reshape(shape)) + weights + gain_sums


def solution(mesh):
    sharded = P("fsdp", "seq", None)
    weight = P("fsdp", None)
    in_specs = (sharded, P("fsdp", "seq")) + (weight,) * 7 + (P(),) * 6 + (sharded,)
    out_specs = (sharded, sharded) + (P("fsdp", "seq"),) * 7 + (P(),) * 6
    return jax.shard_map(body, mesh=mesh, in_specs=in_specs, out_specs=out_specs, check_vma=False)
```

```python
import jax
import jax.numpy as jnp
import numpy as np
from jax import lax
from jax.experimental import pallas as pl
from jax.experimental.pallas import tpu as pltpu
from jax.sharding import PartitionSpec as P

WINDOW = 512
TILE = 128
FF_TILE = 256
FFN_ROWS = 256

epsilon = 1e-06
NEG_FILL = -1e30
ROPE_BASE = 10000.0
GELU_C = 0.7978845608028654
GELU_K = 0.044715

f32 = jnp.float32
bf16 = jnp.bfloat16

NN = (((1,), (0,)), ((), ()))
NT = (((1,), (1,)), ((), ()))
TN = (((0,), (0,)), ((), ()))


def mm(left, right, dims=NN):
    return lax.dot_general(left, right, dims, preferred_element_type=f32)


def inv_rms(vector):
    return lax.rsqrt(jnp.mean(vector * vector, axis=-1, keepdims=True) + epsilon)


def norm_back(vector, inv, gain, grad):
    unit = vector * inv
    scaled = gain * grad
    back = inv * (scaled - unit * jnp.mean(unit * scaled, axis=-1, keepdims=True))
    return back, grad * unit


def rope(vector, cosine, sine):
    half = vector.shape[-1] // 2
    one, two = vector[:, :half], vector[:, half:]
    return jnp.concatenate([one * cosine - two * sine, two * cosine + one * sine], axis=1)


def rope_back(vector, cosine, sine):
    half = vector.shape[-1] // 2
    one, two = vector[:, :half], vector[:, half:]
    return jnp.concatenate([one * cosine + two * sine, two * cosine - one * sine], axis=1)


def params(limit_mib=56):
    return pltpu.CompilerParams(vmem_limit_bytes=limit_mib * 1024 * 1024)


def cost(microseconds):
    return pl.CostEstimate(
        flops=int(microseconds * 1e9), bytes_accessed=int(microseconds * 3e6), transcendentals=0
    )


def whole(shape):
    return pl.BlockSpec(shape, lambda *_: (0,) * len(shape))


def rows(count, width):
    return pl.BlockSpec((count, width), lambda i: (i, 0))


def shaped(shape, dtype):
    return jax.ShapeDtypeStruct(shape, dtype)


def qkv_kernel(
    held_ref, tok_ref, far_ref, cos_ref, sin_ref, own_ref, got_ref, pre_ref, qn_ref, kn_ref,
    attn_ref, qraw_ref, qrot_ref, kraw_ref, key_ref, val_ref, wq_ref, wkv_ref, wot_ref,
):
    head_dim = kn_ref.shape[1]
    head_count = wq_ref.shape[1] // head_dim
    block, width = tok_ref.shape
    half, chunks, chunk_rows, _ = own_ref.shape
    pieces = 2 * half

    @pl.when(pl.program_id(0) == 0)
    def _():
        strip = chunk_rows // 2
        odd = held_ref[0] % 2 == 1

        def aligned(index, size):
            return pl.ds(pl.multiple_of(index * size, size), size)

        for c in range(chunks):
            z = held_ref[pieces + c]
            own = aligned(z, chunk_rows)
            for m in range(pieces):
                ref, s = (own_ref, got_ref)[m // half], held_ref[m]
                wq_ref[own, aligned(s, 128)] = ref[m % half, c, :, :128]
                turned = ref[m % half, c, :, 128:256]
                for i in range(2):
                    wot_ref[aligned(s, strip), aligned(2 * z + i, 128)] = turned[
                        i * strip : (i + 1) * strip
                    ]
            for m, mate in zip(range(half), (0, 2, 1, 3)):
                one, two = own_ref[m, c, :, 256:320], got_ref[mate, c, :, 256:320]
                wkv_ref[own, aligned(held_ref[m] // 2, 128)] = jnp.concatenate(
                    [jnp.where(odd, two, one), jnp.where(odd, one, two)], axis=1
                )

    pre = pre_ref[...]
    kgain = kn_ref[...]
    token = tok_ref[...].astype(f32)
    low = (token * inv_rms(token) * pre).astype(bf16)
    attn_ref[...] = low
    query = mm(low, wq_ref[...])
    qraw_ref[...] = query
    cosine, sine = cos_ref[block:, :], sin_ref[block:, :]
    scaling = head_dim ** (-0.5)
    for h in range(head_count):
        part = query[:, h * head_dim : (h + 1) * head_dim]
        normed = part * inv_rms(part) * qn_ref[...]
        qrot_ref[:, h * head_dim : (h + 1) * head_dim] = (
            rope(normed, cosine, sine).astype(bf16) * jnp.asarray(scaling, bf16)
        )
    both = mm(low, wkv_ref[...])
    key = both[:, :head_dim]
    kraw_ref[...] = key
    key_ref[0, block:, :] = rope(key * inv_rms(key) * kgain, cosine, sine).astype(bf16)
    val_ref[0, block:, :] = both[:, head_dim:].astype(bf16)
    token = far_ref[...].astype(f32)
    low = (token * inv_rms(token) * pre).astype(bf16)
    both = mm(low, wkv_ref[...])
    key = both[:, :head_dim]
    key_ref[0, :block, :] = rope(
        key * inv_rms(key) * kgain, cos_ref[:block, :], sin_ref[:block, :]
    ).astype(bf16)
    val_ref[0, :block, :] = both[:, head_dim:].astype(bf16)


def stacked(ref, tile, head_count, head_dim):
    return jnp.concatenate(
        [
            ref[tile * TILE : (tile + 1) * TILE, h * head_dim : (h + 1) * head_dim]
            for h in range(head_count)
        ],
        axis=0,
    )


def mask_of(pos_ref, tile, span):
    reach = pos_ref[tile * TILE : (tile + 1) * TILE, :]
    row = lax.broadcasted_iota(jnp.int32, (TILE, span), 0)
    col = lax.broadcasted_iota(jnp.int32, (TILE, span), 1)
    distance = WINDOW + row - col
    return jnp.where((distance >= 0) & (distance <= reach), 0.0, NEG_FILL)


def attn_kernel(
    q_ref, key_ref, val_ref, pos_ref, tok_ref, wot_ref, post_ref, pre_ref,
    ctx_ref, lse_ref, branch_ref, res_ref, fin_ref,
):
    head_dim = key_ref.shape[2]
    head_count = q_ref.shape[1] // head_dim
    span = WINDOW + TILE
    lane = lax.broadcasted_iota(jnp.int32, (TILE, 128), 1)
    for tile in range(q_ref.shape[0] // TILE):
        query = stacked(q_ref, tile, head_count, head_dim)
        key = key_ref[0, tile * TILE : tile * TILE + span, :]
        value = val_ref[0, tile * TILE : tile * TILE + span, :]
        score = mm(query, key, NT).reshape(head_count, TILE, span) + mask_of(pos_ref, tile, span)
        largest = jnp.max(score, axis=-1, keepdims=True)
        expo = jnp.exp(score - largest)
        total = jnp.sum(expo, axis=-1, keepdims=True)
        low = expo.astype(bf16).reshape(head_count * TILE, span)
        context = mm(low, value).reshape(head_count, TILE, head_dim) / total
        log_total = largest + jnp.log(total)
        kept = jnp.zeros((TILE, 128), f32)
        for h in range(head_count):
            ctx_ref[tile * TILE : (tile + 1) * TILE, h * head_dim : (h + 1) * head_dim] = context[
                h
            ].astype(bf16)
            kept = jnp.where(lane == h, log_total[h], kept)
        lse_ref[tile * TILE : (tile + 1) * TILE, :] = kept
    branch = mm(ctx_ref[...], wot_ref[...], NT)
    branch_ref[...] = branch
    residual = tok_ref[...].astype(f32) + branch * inv_rms(branch) * post_ref[...]
    res_ref[...] = residual
    fin_ref[...] = (residual * inv_rms(residual) * pre_ref[...]).astype(bf16)


def ffn_kernel(
    held_ref, res_ref, fin_ref, cot_ref, branch_ref, own_ref, got_ref, wot_ref,
    postf_ref, pref_ref, posta_ref,
    out_ref, hid_ref, gg_ref, gu_ref, gffn_ref, gres_ref, gattn_ref, gctx_ref, gain_ref,
    slope_ref, act_ref, wf_ref, copied,
):
    pieces, chunks, _, _ = wf_ref.shape
    width = res_ref.shape[1]
    quarter = width // chunks
    strip = width // pieces

    def gate_block(j):
        return wf_ref[j, :, :quarter, :].reshape(width, FF_TILE)

    def up_block(j):
        return wf_ref[j, :, quarter : 2 * quarter, :].reshape(width, FF_TILE)

    def down_block(j):
        start = 2 * quarter + (j % 2) * strip
        return wf_ref[:, j // 2, start : start + strip, :].reshape(width, FF_TILE)

    @pl.when(pl.program_id(0) == 0)
    def _():
        half = pieces // 2
        copies = [
            pltpu.make_async_copy(
                (own_ref, got_ref)[m // half].at[m % half, c],
                wf_ref.at[held_ref[m], held_ref[pieces + c]],
                copied.at[m, c],
            )
            for m in range(pieces)
            for c in range(chunks)
        ]
        for copy in copies:
            copy.start()
        gain_ref[...] = jnp.zeros_like(gain_ref)
        for copy in copies:
            copy.wait()

    ffn_in = fin_ref[...]
    branch = jnp.zeros(res_ref.shape, f32)
    for j in range(pieces):
        cols = slice(j * FF_TILE, (j + 1) * FF_TILE)
        gate = mm(ffn_in, gate_block(j))
        up = mm(ffn_in, up_block(j))
        square = gate * gate
        bent = jnp.tanh(GELU_C * gate * (1.0 + GELU_K * square))
        half = 0.5 * (1.0 + bent)
        act = gate * half
        slope = half + 0.5 * gate * (1.0 - bent * bent) * (
            GELU_C * (1.0 + 3.0 * GELU_K * square)
        )
        act_ref[:, cols] = act
        slope_ref[:, cols] = slope * up
        hidden = (act * up).astype(bf16)
        hid_ref[:, cols] = hidden
        branch += mm(hidden, down_block(j), NT)
    residual = res_ref[...]
    cot = cot_ref[...].astype(f32)
    inv = inv_rms(branch)
    out_ref[...] = (residual + branch * inv * postf_ref[...]).astype(bf16)
    g_ffn, gain_post = norm_back(branch, inv, postf_ref[...], cot)
    g_low = g_ffn.astype(bf16)
    gffn_ref[...] = g_low
    g_in = jnp.zeros(res_ref.shape, f32)
    for j in range(pieces):
        cols = slice(j * FF_TILE, (j + 1) * FF_TILE)
        g_hidden = mm(g_low, down_block(j))
        g_gate = (g_hidden * slope_ref[:, cols]).astype(bf16)
        g_up = (g_hidden * act_ref[:, cols]).astype(bf16)
        gg_ref[:, cols] = g_gate
        gu_ref[:, cols] = g_up
        g_in += mm(g_gate, gate_block(j), NT) + mm(g_up, up_block(j), NT)
    back, gain_pre = norm_back(residual, inv_rms(residual), pref_ref[...], g_in)
    g_res = cot + back
    gres_ref[...] = g_res
    attn_branch = branch_ref[...]
    g_attn, gain_attn = norm_back(attn_branch, inv_rms(attn_branch), posta_ref[...], g_res)
    g_attn = g_attn.astype(bf16)
    gattn_ref[...] = g_attn
    gctx_ref[...] = mm(g_attn, wot_ref[...]).astype(bf16)
    gain_ref[0:1, :] += jnp.sum(gain_post, axis=0, keepdims=True)
    gain_ref[1:2, :] += jnp.sum(gain_pre, axis=0, keepdims=True)
    gain_ref[2:3, :] += jnp.sum(gain_attn, axis=0, keepdims=True)


def turn_strips(left_ref, source, strip, where, count):
    left_ref[1] = source.T
    for m in range(count):
        begin = pl.multiple_of(where(m) * strip, 16)
        left_ref[0, m * strip : (m + 1) * strip, :] = left_ref[1, pl.ds(begin, strip), :]


def ffn_grad_kernel(
    base, order_ref, _, fin_ref, gffn_ref, gattn_ref, gg_ref, gu_ref, hid_ref, ctx_ref, *refs
):
    recv_ref = refs[0] if base else None
    outs = refs[1:3] if base else refs[:1]
    in_left, ffn_left, attn_left = refs[-3:]
    held, chunks, _, tile = outs[0].shape
    width = fin_ref.shape[1]
    pieces = order_ref.shape[0] - chunks
    quarter, strip = width // chunks, width // pieces
    half = pieces // 2
    j = pl.program_id(0)

    @pl.when(j == 0)
    def _():
        turn_strips(in_left, fin_ref[...], quarter, lambda m: order_ref[pieces + m], chunks)
        turn_strips(ffn_left, gffn_ref[...], strip, lambda m: order_ref[base + m], half)
        turn_strips(attn_left, gattn_ref[...], strip, lambda m: order_ref[base + m], half)

    def put(piece, chunk, begin, value):
        end = begin + value.shape[0]
        if base:
            value = value + recv_ref[piece, chunk, begin:end, :].astype(f32)
        for i, out in enumerate(outs):
            if len(outs) == 1:
                out[piece, chunk, begin:end, :] = value.astype(bf16)
            elif isinstance(piece, int):
                if piece // held == i:
                    out[piece % held, chunk, begin:end, :] = value.astype(bf16)
            else:

                @pl.when(piece // held == i)
                def _(out=out):
                    out[piece % held, chunk, begin:end, :] = value.astype(bf16)

    for i, ref in enumerate((gg_ref, gu_ref)):
        part = mm(in_left[0], ref[...])
        for z in range(chunks):
            put(j, z, i * quarter, part[z * quarter : (z + 1) * quarter])
    part = mm(ffn_left[0, : half * strip, :], hid_ref[...])
    for m in range(half):
        for i in range(2):
            put(
                m, j, 2 * quarter + i * strip,
                part[m * strip : (m + 1) * strip, i * tile : (i + 1) * tile],
            )
    part = mm(attn_left[0, : half * strip, :], ctx_ref[...])
    for m in range(half):
        put(m, j, 2 * quarter + 2 * strip, part[m * strip : (m + 1) * strip])


def attn_grad_kernel(base, order_ref, attn_ref, gq_ref, gkv_ref, sort_ref, *refs):
    recv_ref = refs[0] if base else None
    outs = refs[1:3] if base else refs[:1]
    left = refs[-1]
    held, chunks, quarter, _ = outs[0].shape
    width = attn_ref.shape[1]
    pieces = order_ref.shape[0] - chunks
    half = pieces // 2
    turn_strips(left, attn_ref[...], quarter, lambda m: order_ref[pieces + m], chunks)
    sorted_kv = mm(gkv_ref[...], sort_ref[...]).astype(bf16)
    part_kv = mm(left[0], sorted_kv)
    wide = part_kv.shape[1] // half
    for pair in range(0, half, 2):
        both = jnp.concatenate(
            [
                gq_ref[:, pl.ds(pl.multiple_of(order_ref[base + pair + i] * 128, 128), 128)]
                for i in range(2)
            ],
            axis=1,
        )
        part = mm(left[0], both)
        for i in range(2):
            m = pair + i
            value = part[:, i * 128 : (i + 1) * 128].reshape(chunks, quarter, 128)
            value_kv = part_kv[:, m * wide : (m + 1) * wide].reshape(chunks, quarter, wide)
            if base:
                value = value + recv_ref[m, :, :, :128].astype(f32)
                value_kv = value_kv + recv_ref[m, :, :, 128:].astype(f32)
            out = outs[m // held]
            out[m % held, :, :, :128] = value.astype(bf16)
            out[m % held, :, :, 128:] = value_kv.astype(bf16)


def attn_back_kernel(
    _, q_ref, gctx_ref, key_ref, val_ref, pos_ref, lse_ref, qraw_ref, cos_ref, sin_ref, qn_ref,
    gq_ref, far_ref, near_ref, gain_ref, gkey_ref, gval_ref,
):
    head_dim = key_ref.shape[2]
    head_count = q_ref.shape[1] // head_dim
    block = q_ref.shape[0]
    span = WINDOW + TILE
    scaling = head_dim ** (-0.5)

    @pl.when(pl.program_id(0) == 0)
    def _():
        gain_ref[...] = jnp.zeros_like(gain_ref)

    gkey_ref[...] = jnp.zeros_like(gkey_ref)
    gval_ref[...] = jnp.zeros_like(gval_ref)
    gain = jnp.zeros((1, head_dim), f32)
    for tile in range(block // TILE):
        own = slice(tile * TILE, (tile + 1) * TILE)
        reach = slice(tile * TILE, tile * TILE + span)
        query = stacked(q_ref, tile, head_count, head_dim)
        g_ctx = stacked(gctx_ref, tile, head_count, head_dim)
        key = key_ref[0, reach, :]
        value = val_ref[0, reach, :]
        log_total = jnp.stack([lse_ref[own, h : h + 1] for h in range(head_count)])
        score = mm(query, key, NT).reshape(head_count, TILE, span) + mask_of(pos_ref, tile, span)
        probs = jnp.exp(score - log_total)
        g_probs = mm(g_ctx, value, NT).reshape(head_count, TILE, span)
        spread = jnp.sum(g_probs * probs, axis=-1, keepdims=True)
        g_score = (probs * (g_probs - spread)).astype(bf16).reshape(head_count * TILE, span)
        low = probs.astype(bf16).reshape(head_count * TILE, span)
        gkey_ref[reach, :] += mm(g_score, query, TN)
        gval_ref[reach, :] += mm(low, g_ctx, TN)
        g_rot = mm(g_score, key) * scaling
        turned = slice(block + tile * TILE, block + (tile + 1) * TILE)
        cosine, sine = cos_ref[turned, :], sin_ref[turned, :]
        for h in range(head_count):
            cols = slice(h * head_dim, (h + 1) * head_dim)
            raw = qraw_ref[own, cols]
            back, share = norm_back(
                raw,
                inv_rms(raw),
                qn_ref[...],
                rope_back(g_rot[h * TILE : (h + 1) * TILE], cosine, sine),
            )
            gq_ref[own, cols] = back.astype(bf16)
            gain += jnp.sum(share, axis=0, keepdims=True)
    gain_ref[0:1, :] += gain
    far_ref[0, :, :head_dim] = rope_back(
        gkey_ref[:block, :], cos_ref[:block, :], sin_ref[:block, :]
    ).astype(bf16)
    far_ref[0, :, head_dim:] = gval_ref[:block, :].astype(bf16)
    near_ref[0, :, :head_dim] = gkey_ref[block:, :]
    near_ref[0, :, head_dim:] = gval_ref[block:, :]


def kv_back_kernel(
    _, near_ref, recv_ref, kraw_ref, cos_ref, sin_ref, kn_ref, gkv_ref, kgain_ref
):
    head_dim = kn_ref.shape[1]

    @pl.when(pl.program_id(0) == 0)
    def _():
        kgain_ref[...] = jnp.zeros_like(kgain_ref)

    near, far = near_ref[0], recv_ref[0].astype(f32)
    raw = kraw_ref[...]
    g_normed = rope_back(near[:, :head_dim], cos_ref[...], sin_ref[...]) + far[:, :head_dim]
    g_key, share = norm_back(raw, inv_rms(raw), kn_ref[...], g_normed)
    kgain_ref[0:1, :] += jnp.sum(share, axis=0, keepdims=True)
    gkv_ref[:, :head_dim] = g_key.astype(bf16)
    gkv_ref[:, head_dim:] = (near[:, head_dim:] + far[:, head_dim:]).astype(bf16)


def input_kernel(
    _, gq_ref, gkv_ref, wq_ref, wkv_ref, tok_ref, gres_ref, pre_ref, dtok_ref, gain_ref
):
    @pl.when(pl.program_id(0) == 0)
    def _():
        gain_ref[...] = jnp.zeros_like(gain_ref)

    g_in = mm(gq_ref[...], wq_ref[...], NT) + mm(gkv_ref[...], wkv_ref[...], NT)
    token = tok_ref[...].astype(f32)
    back, share = norm_back(token, inv_rms(token), pre_ref[...], g_in)
    dtok_ref[...] = (gres_ref[...] + back).astype(bf16)
    gain_ref[0:1, :] += jnp.sum(share, axis=0, keepdims=True)


def passed_along(shard, axis, by):
    length = lax.axis_size(axis)
    pairs = [(i, i + by) for i in range(length) if 0 <= i + by < length]
    return lax.ppermute(shard, axis, pairs)


def swapped(array, axis, even, odd):
    length = lax.axis_size(axis)
    return lax.ppermute(array, axis, [(i, i ^ (odd if i % 2 else even)) for i in range(length)])


def tables(block, head_dim):
    half_width = head_dim // 2
    frequency = ROPE_BASE ** (-(np.arange(half_width) * 2.0) / head_dim)
    angles = np.arange(-block, block)[:, None] * frequency
    return np.cos(angles).astype(np.float32), np.sin(angles).astype(np.float32)


def column_piece(array, axis_name, parts):
    wide = array.shape[1] // parts
    return lax.dynamic_slice_in_dim(array, lax.axis_index(axis_name) * wide, wide, 1)


def added(left, right):
    return left.astype(f32) + right.astype(f32)


HELD = [0, 4, 2, 6, 1, 3, 5, 7]
HELD_Z = [0, 2, 1, 3]


class Exchange:
    def __init__(self, seqs, chunks):
        self.direct = seqs == 8 and chunks == 4
        if not self.direct:
            self.order = jnp.arange(12, dtype=jnp.int32) % 8
            self.held = jnp.array(HELD + HELD_Z, jnp.int32)
            return
        s, z = lax.axis_index("seq"), lax.axis_index("fsdp")
        odd = s % 2 == 1
        one, two = jnp.where(odd, 4, 2), jnp.where(odd, 2, 4)
        zero = jnp.zeros_like(s)
        sent = [one | two | 1, two | 1, one | 1, zero | 1]
        kept = [one | two, one, two, zero]
        order = [s ^ k for k in sent + kept] + [z ^ k for k in (3, 1, 2, 0)]
        self.order = jnp.stack(order).astype(jnp.int32)
        held = [zero, two, one, one | two, zero | 1, one | 1, two | 1, one | two | 1]
        held = [s ^ k for k in held] + [z ^ k for k in HELD_Z]
        self.held = jnp.stack(held).astype(jnp.int32)

    def step(self, held, step):
        if step < 2:
            return held, swapped(held, "fsdp", 2 >> step, 2 >> step)
        return held, swapped(held, "seq", *((4, 2), (2, 4), (1, 1))[step - 2])

    def joined(self, held, got, step):
        held = jnp.concatenate([held, got], axis=0)
        return held[None] if step == 1 else held

    def swap_cores(self, parts):
        return swapped(parts, "seq", 1, 1)

    def fold(self, send, keep, step):
        if step < 2:
            got = swapped(send, "seq", *((2, 4), (4, 2))[step])
        else:
            got = swapped(send, "fsdp", step - 1, step - 1)
        if step == 3:
            return added(keep, got)
        if step == 1:
            return (
                added(keep[:2], got[:2]).astype(bf16),
                added(keep[2:], got[2:]).astype(bf16),
            )
        return added(keep[0], got[0]).astype(bf16), added(keep[1], got[1]).astype(bf16)

    def hop(self, value, axis, bits):
        return value + swapped(value, axis, bits, bits)


def scattered_plain(part):
    columns = lax.psum_scatter(part, "seq", scatter_dimension=1, tiled=True)
    return lax.psum_scatter(columns, "fsdp", scatter_dimension=0, tiled=True).astype(f32)


def gather_weights(w_query, w_key, w_value, w_out, w_gate, w_up, w_down, halo, exchange):
    pieces = w_gate.shape[1] // FF_TILE
    width = w_out.shape[1]
    if exchange.direct:
        down = column_piece(w_down, "seq", pieces).T
        ffn = jnp.concatenate(
            [
                column_piece(w_gate, "seq", pieces),
                column_piece(w_up, "seq", pieces),
                down[:, :FF_TILE],
                down[:, FF_TILE:],
            ],
            axis=0,
        )
        both = jnp.concatenate([w_key, w_value], axis=1)
        out = column_piece(w_out, "seq", pieces).T
        out = jnp.concatenate([out[:, :128], out[:, 128:]], axis=0)
        attn = jnp.concatenate(
            [column_piece(w_query, "seq", pieces), out, column_piece(both, "seq", pieces)], axis=1
        )
        def doubled(held, step):
            return exchange.joined(*exchange.step(held, step), step)

        attn = doubled(attn[None], 0)
        ffn = doubled(ffn[None], 0)
        attn = doubled(attn, 1)
        ffn, attn = lax.optimization_barrier((ffn, attn))
        ffn = doubled(ffn, 1)
        attn = doubled(attn, 2)
        attn, halo = lax.optimization_barrier((attn, halo))
        attn = doubled(attn, 3)
        attn, ffn = lax.optimization_barrier((attn, ffn))
        return exchange.step(attn, 4), ffn, halo
    w_query, w_key, w_value, w_out, w_gate, w_up, w_down = [
        lax.all_gather(w, "fsdp", axis=0, tiled=True)
        for w in (w_query, w_key, w_value, w_out, w_gate, w_up, w_down)
    ]
    chunks = w_down.shape[0] // (2 * FF_TILE)
    quarter, strip = width // chunks, width // pieces

    def columns(weight):
        return weight.reshape(chunks, quarter, pieces, -1).transpose(2, 0, 1, 3)

    def turned(weight):
        shape = (pieces, strip, chunks, 2, weight.shape[0] // (2 * chunks))
        turned_part = weight.T.reshape(shape).transpose(0, 2, 3, 1, 4)
        return turned_part.reshape(pieces, chunks, 2 * strip, -1)

    both = jnp.concatenate([w_key, w_value], axis=1)
    attn = jnp.concatenate([columns(w_query), turned(w_out), columns(both)], axis=3)
    ffn = jnp.concatenate([columns(w_gate), columns(w_up), turned(w_down)], axis=2)
    half = pieces // 2

    def listed(pack):
        pack = jnp.take(jnp.take(pack, np.array(HELD), axis=0), np.array(HELD_Z), axis=1)
        return pack[:half], pack[half:]

    return listed(attn), listed(ffn), halo


def plain_gradients(part_ffn, part_attn):
    pieces, quarters = part_ffn.shape[:2]
    quarter = part_attn.shape[2]
    width = quarters * quarter
    strip = width // pieces
    down_end = 2 * quarter + 2 * strip

    def columns(parts):
        return parts.transpose(1, 2, 0, 3).reshape(width, -1)

    def turned(parts):
        parts = parts.reshape(pieces, quarters, -1, strip, FF_TILE).transpose(1, 2, 4, 0, 3)
        return parts.reshape(-1, width)

    each = part_attn.shape[3] - (part_attn.shape[3] - 128) // 2
    return tuple(
        scattered_plain(part)
        for part in (
            columns(part_attn[..., :128]),
            columns(part_attn[..., 128:each]),
            columns(part_attn[..., each:]),
            turned(part_ffn[:, :, down_end:]),
            columns(part_ffn[:, :, :quarter]),
            columns(part_ffn[:, :, quarter : 2 * quarter]),
            turned(part_ffn[:, :, 2 * quarter : down_end]),
        )
    )


def split_gradients(ffn, attn):
    quarter = attn.shape[0]
    strip = (ffn.shape[0] - 2 * quarter) // 3
    each = attn.shape[1] - (attn.shape[1] - 128) // 2
    down = ffn[2 * quarter :]
    return (
        attn[:, :128],
        attn[:, 128:each],
        attn[:, each:],
        down[2 * strip :].T,
        ffn[:quarter],
        ffn[quarter : 2 * quarter],
        jnp.concatenate([down[:strip].T, down[strip : 2 * strip].T], axis=0),
    )


def body(
    tokens, doc_starts, w_query, w_key, w_value, w_out, w_gate, w_up, w_down,
    pre_attn, post_attn, pre_ffn, post_ffn, query_norm, key_norm, cotangent,
):
    seq_dev, block, width = tokens.shape
    head_dim = w_key.shape[1]
    inner = w_query.shape[1]
    hidden_dim = w_gate.shape[1]
    count = seq_dev * block
    seqs, chunks = lax.axis_size("seq"), lax.axis_size("fsdp")
    exchange = Exchange(seqs, chunks)
    far_tokens = passed_along(tokens, "seq", 1).reshape(count, width)
    starts = jnp.concatenate([passed_along(doc_starts, "seq", 1), doc_starts], axis=1)
    indices = jnp.arange(2 * block, dtype=jnp.int32)
    latest = lax.cummax(jnp.where(starts == 1, indices[None, :], -WINDOW), axis=1)
    reach = jnp.minimum(indices[None, :] - latest, WINDOW - 1)[:, block:]
    pos_column = reach.reshape(count, 1)
    cosine, sine = tables(block, head_dim)
    own_cosine, own_sine = cosine[block:], sine[block:]

    pack, ffn_pack, far_tokens = gather_weights(
        w_query, w_key, w_value, w_out, w_gate, w_up, w_down, far_tokens, exchange
    )
    pieces, quarters = 2 * pack[0].shape[0], pack[0].shape[1]
    quarter, strip = width // quarters, width // pieces
    gains = [g.reshape(1, -1) for g in (pre_attn, post_attn, pre_ffn, post_ffn)]
    pre_attn, post_attn, pre_ffn, post_ffn = gains
    query_norm, key_norm = query_norm.reshape(1, -1), key_norm.reshape(1, -1)
    tokens_2d = tokens.reshape(count, width)
    cot_2d = cotangent.reshape(count, width)

    tok_spec = rows(block, width)
    table_spec = whole((2 * block, head_dim // 2))
    half_spec = whole((block, head_dim // 2))
    key_spec = pl.BlockSpec((1, 2 * block, head_dim), lambda i: (i, 0, 0))
    gain_w, gain_h = whole((1, width)), whole((1, head_dim))
    wq_spec, wkv_spec, wot_spec = (
        whole((width, inner)),
        whole((width, 2 * head_dim)),
        whole((width, inner)),
    )
    smem = pl.BlockSpec(memory_space=pltpu.SMEM)
    remain = pl.BlockSpec(memory_space=pl.ANY)
    attn_low, query_raw, query_rot, key_raw, keys, values, full_q, full_kv, full_ot = (
        pl.pallas_call(
            qkv_kernel,
            grid=(seq_dev,),
            in_specs=[smem, tok_spec, tok_spec, table_spec, table_spec]
            + [whole(pack[0].shape)] * 2
            + [gain_w, gain_h, gain_h],
            out_specs=[
                tok_spec,
                rows(block, inner),
                rows(block, inner),
                rows(block, head_dim),
                key_spec,
                key_spec,
                wq_spec,
                wkv_spec,
                wot_spec,
            ],
            out_shape=[
                shaped((count, width), bf16),
                shaped((count, inner), f32),
                shaped((count, inner), bf16),
                shaped((count, head_dim), f32),
                shaped((seq_dev, 2 * block, head_dim), bf16),
                shaped((seq_dev, 2 * block, head_dim), bf16),
                shaped((width, inner), bf16),
                shaped((width, 2 * head_dim), bf16),
                shaped((width, inner), bf16),
            ],
            compiler_params=params(),
            name="project_rotate",
        cost_estimate=cost(11),
        )(
            exchange.held, tokens_2d, far_tokens, cosine, sine, *pack,
            pre_attn, query_norm, key_norm,
        )
    )
    if exchange.direct:
        own, got = exchange.step(ffn_pack, 2)
        got, keys = lax.optimization_barrier((got, keys))
        own, got = exchange.step(exchange.joined(own, got, 2), 3)
    context, log_total, attn_branch, residual, ffn_in = pl.pallas_call(
        attn_kernel,
        grid=(seq_dev,),
        in_specs=[rows(block, inner), key_spec, key_spec, rows(block, 1), tok_spec]
        + [wot_spec, gain_w, gain_w],
        out_specs=[rows(block, inner), rows(block, 128), tok_spec, tok_spec, tok_spec],
        out_shape=[
            shaped((count, inner), bf16),
            shaped((count, 128), f32),
            shaped((count, width), f32),
            shaped((count, width), f32),
            shaped((count, width), bf16),
        ],
        compiler_params=params(),
        name="window_attention",
        cost_estimate=cost(12),
    )(query_rot, keys, values, pos_column, tokens_2d, full_ot, post_attn, pre_ffn)

    if exchange.direct:
        got, ffn_in = lax.optimization_barrier((got, ffn_in))
        ffn_pack = exchange.step(exchange.joined(own, got, 3), 4)

    small = rows(FFN_ROWS, width)
    wide = rows(FFN_ROWS, hidden_dim)
    layer_out, hidden, g_gate, g_up, g_ffn, g_res, g_attn, g_ctx, ffn_gains = pl.pallas_call(
        ffn_kernel,
        grid=(count // FFN_ROWS,),
        in_specs=[smem, small, small, small, small, remain, remain, wot_spec]
        + [gain_w, gain_w, gain_w],
        out_specs=[small, wide, wide, wide, small, small, small, rows(FFN_ROWS, inner)]
        + [whole((8, width))],
        out_shape=[
            shaped((count, width), bf16),
            shaped((count, hidden_dim), bf16),
            shaped((count, hidden_dim), bf16),
            shaped((count, hidden_dim), bf16),
            shaped((count, width), bf16),
            shaped((count, width), f32),
            shaped((count, width), bf16),
            shaped((count, inner), bf16),
            shaped((8, width), f32),
        ],
        scratch_shapes=[
            pltpu.VMEM((FFN_ROWS, hidden_dim), f32),
            pltpu.VMEM((FFN_ROWS, hidden_dim), f32),
            pltpu.VMEM((pieces, quarters) + ffn_pack[0].shape[2:], bf16),
            pltpu.SemaphoreType.DMA((pieces, quarters)),
        ],
        compiler_params=params(),
        name="feed_forward",
        cost_estimate=cost(40),
    )(
        exchange.held, residual, ffn_in, cot_2d, attn_branch, *ffn_pack, full_ot,
        post_ffn, pre_ffn, post_attn,
    )

    half = pieces // 2
    full_rows = whole((count, width))

    def ffn_parts(base, before, extra):
        shape = (half, quarters, 2 * quarter + 3 * strip, FF_TILE)
        sent = (half // 2,) + shape[1:]
        outs = [shape] if base == 0 else [sent, sent]
        turned = pltpu.VMEM((2, width, count), bf16)
        by_piece = pl.BlockSpec((count, FF_TILE), lambda j, order: (0, order[base + j]))
        wide = pl.BlockSpec((count, 2 * FF_TILE), lambda j, order: (0, order[pieces + j]))
        by_chunk = pl.BlockSpec((count, FF_TILE), lambda j, order: (0, order[pieces + j]))
        return pl.pallas_call(
            lambda *refs: ffn_grad_kernel(base, *refs),
            grid_spec=pltpu.PrefetchScalarGridSpec(
                num_scalar_prefetch=1,
                grid=(half,),
                in_specs=[remain, full_rows, full_rows, full_rows, by_piece, by_piece, wide]
                + [by_chunk]
                + [whole(e.shape) for e in extra],
                out_specs=[whole(o) for o in outs],
                scratch_shapes=[turned, turned, turned],
            ),
            out_shape=[shaped(o, bf16) for o in outs],
            compiler_params=params(),
            cost_estimate=cost(15),
            name="ffn_gradients_kept" if base else "ffn_gradients_sent",
        )(exchange.order, before, ffn_in, g_ffn, g_attn, g_gate, g_up, hidden, context, *extra)

    (ffn_sent,) = ffn_parts(0, exchange.order, [])
    ffn_got = exchange.swap_cores(ffn_sent) if exchange.direct else jnp.zeros_like(ffn_sent)

    kv_spec = pl.BlockSpec((1, block, 2 * head_dim), lambda i: (i, 0, 0))
    g_query, g_far, g_near, query_gain = pl.pallas_call(
        attn_back_kernel,
        grid=(seq_dev,),
        in_specs=[remain, rows(block, inner), rows(block, inner), key_spec, key_spec]
        + [rows(block, 1), rows(block, 128), rows(block, inner), table_spec, table_spec, gain_h],
        out_specs=[rows(block, inner), kv_spec, kv_spec, whole((8, head_dim))],
        out_shape=[
            shaped((count, inner), bf16),
            shaped((seq_dev, block, 2 * head_dim), bf16),
            shaped((seq_dev, block, 2 * head_dim), f32),
            shaped((8, head_dim), f32),
        ],
        scratch_shapes=[
            pltpu.VMEM((2 * block, head_dim), f32),
            pltpu.VMEM((2 * block, head_dim), f32),
        ],
        compiler_params=params(),
        name="attention_gradient",
        cost_estimate=cost(16),
    )(
        ffn_sent, query_rot, g_ctx, keys, values, pos_column, log_total, query_raw, cosine, sine,
        query_norm,
    )
    g_recv = passed_along(g_far, "seq", -1)
    ffn_parts_kept = ffn_parts(half, g_far, [ffn_got])
    g_kv, key_gain = pl.pallas_call(
        kv_back_kernel,
        grid=(seq_dev,),
        in_specs=[remain, kv_spec, kv_spec, rows(block, head_dim), half_spec, half_spec, gain_h],
        out_specs=[rows(block, 2 * head_dim), whole((8, head_dim))],
        out_shape=[shaped((count, 2 * head_dim), bf16), shaped((8, head_dim), f32)],
        compiler_params=params(),
        name="key_value_back",
        cost_estimate=cost(4),
    )(ffn_parts_kept[0], g_near, g_recv, key_raw, own_cosine, own_sine, key_norm)

    each = head_dim // pieces
    column = jnp.arange(2 * head_dim, dtype=jnp.int32)
    inside = column % (2 * each)
    source = jnp.where(inside < each, inside, inside - each + head_dim)
    source = source + each * jnp.repeat(exchange.order[:pieces], 2 * each)
    sort = (column[:, None] == source[None, :]).astype(bf16)

    def attn_parts(base, extra):
        shape = (half, quarters, quarter, 128 + 2 * each)
        sent = (half // 2,) + shape[1:]
        outs = [shape] if base == 0 else [sent, sent]
        vmem = pl.BlockSpec(memory_space=pltpu.VMEM)
        chosen = sort[:, base * 2 * each : (base + half) * 2 * each]
        return pl.pallas_call(
            lambda *refs: attn_grad_kernel(base, *refs),
            in_specs=[smem] + [vmem] * (4 + len(extra)),
            out_specs=[vmem] * len(outs),
            out_shape=[shaped(o, bf16) for o in outs],
            scratch_shapes=[pltpu.VMEM((2, width, count), bf16)],
            compiler_params=params(),
            cost_estimate=cost(6),
            name="attn_gradients_kept" if base else "attn_gradients_sent",
        )(exchange.order, attn_low, g_query, g_kv, chosen, *extra)

    (attn_sent,) = attn_parts(0, [])
    attn_got = exchange.swap_cores(attn_sent) if exchange.direct else jnp.zeros_like(attn_sent)
    attn_parts_kept = attn_parts(half, [attn_got])
    dtokens, attn_gain = pl.pallas_call(
        input_kernel,
        grid=(seq_dev,),
        in_specs=[remain, rows(block, inner), rows(block, 2 * head_dim), wq_spec, wkv_spec]
        + [tok_spec, tok_spec, gain_w],
        out_specs=[tok_spec, whole((8, width))],
        out_shape=[shaped((count, width), bf16), shaped((8, width), f32)],
        compiler_params=params(),
        name="input_gradient",
        cost_estimate=cost(7),
    )(attn_parts_kept[0], g_query, g_kv, full_q, full_kv, tokens_2d, g_res, pre_attn)

    sums = jnp.concatenate(
        [attn_gain[0], ffn_gains[2], ffn_gains[1], ffn_gains[0], query_gain[0], key_gain[0]]
    )
    if exchange.direct:
        ffn, attn = ffn_parts_kept, attn_parts_kept
        ffn = exchange.fold(*ffn, 0)
        hops = (("seq", 1), ("seq", 2), ("seq", 4), ("fsdp", 1), ("fsdp", 2))
        for step in range(4):
            ffn = exchange.fold(*ffn, step + 1) if step < 3 else ffn
            attn = exchange.fold(*attn, step)
            sums = exchange.hop(sums, *hops[step])
            ffn, attn, sums = lax.optimization_barrier((ffn, attn, sums))
        sums = exchange.hop(sums, *hops[4])
        weights = split_gradients(ffn, attn)
    else:
        weights = plain_gradients(
            jnp.concatenate([ffn_sent, *ffn_parts_kept], axis=0),
            jnp.concatenate([attn_sent, *attn_parts_kept], axis=0),
        )
        sums = lax.psum(sums, ("seq", "fsdp"))
    cuts = [0, width, 2 * width, 3 * width, 4 * width, 4 * width + head_dim]
    cuts.append(cuts[-1] + head_dim)
    gain_sums = tuple(sums[a:b] for a, b in zip(cuts[:-1], cuts[1:]))
    shape = (seq_dev, block, width)
    return (layer_out.reshape(shape), dtokens.reshape(shape)) + weights + gain_sums


def solution(mesh):
    sharded = P("fsdp", "seq", None)
    weight = P("fsdp", None)
    in_specs = (sharded, P("fsdp", "seq")) + (weight,) * 7 + (P(),) * 6 + (sharded,)
    out_specs = (sharded, sharded) + (P("fsdp", "seq"),) * 7 + (P(),) * 6
    return jax.shard_map(body, mesh=mesh, in_specs=in_specs, out_specs=out_specs, check_vma=False)
```

```python
import jax
import jax.numpy as jnp
import numpy as np
from jax import lax
from jax.experimental import pallas as pl
from jax.experimental.pallas import tpu as pltpu
from jax.sharding import PartitionSpec as P

WINDOW = 512
TILE = 128
FF_TILE = 256
FFN_ROWS = 256

epsilon = 1e-06
NEG_FILL = -1e30
ROPE_BASE = 10000.0
GELU_C = 0.7978845608028654
GELU_K = 0.044715

f32 = jnp.float32
bf16 = jnp.bfloat16

NN = (((1,), (0,)), ((), ()))
NT = (((1,), (1,)), ((), ()))
TN = (((0,), (0,)), ((), ()))


def mm(left, right, dims=NN):
    return lax.dot_general(left, right, dims, preferred_element_type=f32)


def inv_rms(vector):
    return lax.rsqrt(jnp.mean(vector * vector, axis=-1, keepdims=True) + epsilon)


def norm_back(vector, inv, gain, grad):
    unit = vector * inv
    scaled = gain * grad
    back = inv * (scaled - unit * jnp.mean(unit * scaled, axis=-1, keepdims=True))
    return back, grad * unit


def rope(vector, cosine, sine):
    half = vector.shape[-1] // 2
    one, two = vector[:, :half], vector[:, half:]
    return jnp.concatenate([one * cosine - two * sine, two * cosine + one * sine], axis=1)


def rope_back(vector, cosine, sine):
    half = vector.shape[-1] // 2
    one, two = vector[:, :half], vector[:, half:]
    return jnp.concatenate([one * cosine + two * sine, two * cosine - one * sine], axis=1)


def params(limit_mib=58):
    return pltpu.CompilerParams(vmem_limit_bytes=limit_mib * 1024 * 1024)


def cost(microseconds):
    return pl.CostEstimate(
        flops=int(microseconds * 1e9), bytes_accessed=int(microseconds * 3e6), transcendentals=0
    )


def whole(shape):
    return pl.BlockSpec(shape, lambda *_: (0,) * len(shape))


def rows(count, width):
    return pl.BlockSpec((count, width), lambda i: (i, 0))


def shaped(shape, dtype):
    return jax.ShapeDtypeStruct(shape, dtype)


def qkv_kernel(
    held_ref, tok_ref, far_ref, cos_ref, sin_ref, own_ref, got_ref, gains_ref, head_ref,
    attn_ref, qraw_ref, qrot_ref, kraw_ref, key_ref, val_ref, wq_ref, wkv_ref, wot_ref,
):
    head_dim = head_ref.shape[1]
    head_count = wq_ref.shape[1] // head_dim
    block, width = tok_ref.shape
    half, chunks, chunk_rows, _ = own_ref.shape
    pieces = 2 * half

    @pl.when(pl.program_id(0) == 0)
    def _():
        strip = chunk_rows // 2
        odd = held_ref[0] % 2 == 1

        def aligned(index, size):
            return pl.ds(pl.multiple_of(index * size, size), size)

        for c in range(chunks):
            z = held_ref[pieces + c]
            own = aligned(z, chunk_rows)
            for m in range(pieces):
                ref, s = (own_ref, got_ref)[m // half], held_ref[m]
                wq_ref[own, aligned(s, 128)] = ref[m % half, c, :, :128]
                turned = ref[m % half, c, :, 128:256]
                for i in range(2):
                    wot_ref[aligned(s, strip), aligned(2 * z + i, 128)] = turned[
                        i * strip : (i + 1) * strip
                    ]
            for m, mate in zip(range(half), (0, 2, 1, 3)):
                one, two = own_ref[m, c, :, 256:320], got_ref[mate, c, :, 256:320]
                wkv_ref[own, aligned(held_ref[m] // 2, 128)] = jnp.concatenate(
                    [jnp.where(odd, two, one), jnp.where(odd, one, two)], axis=1
                )

    pre = gains_ref[0:1, :]
    qgain, kgain = head_ref[0:1, :], head_ref[1:2, :]
    token = tok_ref[...].astype(f32)
    low = (token * inv_rms(token) * pre).astype(bf16)
    attn_ref[...] = low
    query = mm(low, wq_ref[...])
    qraw_ref[...] = query
    cosine, sine = cos_ref[block:, :], sin_ref[block:, :]
    scaling = head_dim ** (-0.5)
    for h in range(head_count):
        part = query[:, h * head_dim : (h + 1) * head_dim]
        normed = part * inv_rms(part) * qgain
        qrot_ref[:, h * head_dim : (h + 1) * head_dim] = (
            rope(normed, cosine, sine).astype(bf16) * jnp.asarray(scaling, bf16)
        )
    both = mm(low, wkv_ref[...])
    key = both[:, :head_dim]
    kraw_ref[...] = key
    key_ref[0, block:, :] = rope(key * inv_rms(key) * kgain, cosine, sine).astype(bf16)
    val_ref[0, block:, :] = both[:, head_dim:].astype(bf16)
    token = far_ref[...].astype(f32)
    low = (token * inv_rms(token) * pre).astype(bf16)
    both = mm(low, wkv_ref[...])
    key = both[:, :head_dim]
    key_ref[0, :block, :] = rope(
        key * inv_rms(key) * kgain, cos_ref[:block, :], sin_ref[:block, :]
    ).astype(bf16)
    val_ref[0, :block, :] = both[:, head_dim:].astype(bf16)


def stacked(ref, tile, head_count, head_dim):
    return jnp.concatenate(
        [
            ref[tile * TILE : (tile + 1) * TILE, h * head_dim : (h + 1) * head_dim]
            for h in range(head_count)
        ],
        axis=0,
    )


def mask_of(pos_ref, tile, span):
    reach = pos_ref[tile * TILE : (tile + 1) * TILE, :]
    row = lax.broadcasted_iota(jnp.int32, (TILE, span), 0)
    col = lax.broadcasted_iota(jnp.int32, (TILE, span), 1)
    distance = WINDOW + row - col
    return jnp.where((distance >= 0) & (distance <= reach), 0.0, NEG_FILL)


def attn_kernel(
    q_ref, key_ref, val_ref, pos_ref, tok_ref, wot_ref, gains_ref,
    ctx_ref, lse_ref, branch_ref, res_ref, fin_ref,
):
    head_dim = key_ref.shape[2]
    head_count = q_ref.shape[1] // head_dim
    span = WINDOW + TILE
    lane = lax.broadcasted_iota(jnp.int32, (TILE, 128), 1)
    for tile in range(q_ref.shape[0] // TILE):
        query = stacked(q_ref, tile, head_count, head_dim)
        key = key_ref[0, tile * TILE : tile * TILE + span, :]
        value = val_ref[0, tile * TILE : tile * TILE + span, :]
        score = mm(query, key, NT).reshape(head_count, TILE, span) + mask_of(pos_ref, tile, span)
        largest = jnp.max(score, axis=-1, keepdims=True)
        expo = jnp.exp(score - largest)
        total = jnp.sum(expo, axis=-1, keepdims=True)
        low = expo.astype(bf16).reshape(head_count * TILE, span)
        context = mm(low, value).reshape(head_count, TILE, head_dim) / total
        log_total = largest + jnp.log(total)
        kept = jnp.zeros((TILE, 128), f32)
        for h in range(head_count):
            ctx_ref[tile * TILE : (tile + 1) * TILE, h * head_dim : (h + 1) * head_dim] = context[
                h
            ].astype(bf16)
            kept = jnp.where(lane == h, log_total[h], kept)
        lse_ref[tile * TILE : (tile + 1) * TILE, :] = kept
    branch = mm(ctx_ref[...], wot_ref[...], NT)
    branch_ref[...] = branch
    residual = tok_ref[...].astype(f32) + branch * inv_rms(branch) * gains_ref[1:2, :]
    res_ref[...] = residual
    fin_ref[...] = (residual * inv_rms(residual) * gains_ref[2:3, :]).astype(bf16)


def ffn_kernel(
    held_ref, res_ref, fin_ref, cot_ref, branch_ref, own_ref, got_ref, wot_ref, gains_ref,
    out_ref, hid_ref, gg_ref, gu_ref, gffn_ref, gres_ref, gattn_ref, gctx_ref, gain_ref,
    slope_ref, act_ref, gate_ref, up_ref, down_ref, stage_ref, copied,
):
    half, chunks, _, tile = own_ref.shape
    pieces = 2 * half
    width = res_ref.shape[1]
    quarter, strip = width // chunks, width // pieces
    post_attn, pre_ffn, post_ffn = [gains_ref[i : i + 1, :] for i in (1, 2, 3)]

    @pl.when(pl.program_id(0) == 0)
    def _():
        gain_ref[...] = jnp.zeros_like(gain_ref)

        def staged(m):
            source = (own_ref, got_ref)[m // half].at[m % half]
            return pltpu.make_async_copy(source, stage_ref.at[m % 2], copied.at[m % 2])

        def aligned(index, size):
            return pl.ds(pl.multiple_of(index * size, size), size)

        staged(0).start()
        for m in range(pieces):
            if m + 1 < pieces:
                staged(m + 1).start()
            staged(m).wait()
            s = held_ref[m]
            for c in range(chunks):
                z = held_ref[pieces + c]
                own, cols = aligned(z, quarter), aligned(s, tile)
                gate_ref[own, cols] = stage_ref[m % 2, c, :quarter, :]
                up_ref[own, cols] = stage_ref[m % 2, c, quarter : 2 * quarter, :]
                for i in range(2):
                    begin = 2 * quarter + i * strip
                    down_ref[aligned(s, strip), aligned(2 * z + i, tile)] = stage_ref[
                        m % 2, c, begin : begin + strip, :
                    ]

    ffn_in = fin_ref[...]
    gate = mm(ffn_in, gate_ref[...])
    up = mm(ffn_in, up_ref[...])
    square = gate * gate
    bent = jnp.tanh(GELU_C * gate * (1.0 + GELU_K * square))
    half_bent = 0.5 * (1.0 + bent)
    act = gate * half_bent
    slope = half_bent + 0.5 * gate * (1.0 - bent * bent) * (
        GELU_C * (1.0 + 3.0 * GELU_K * square)
    )
    act_ref[...] = act
    slope_ref[...] = slope * up
    hid_ref[...] = (act * up).astype(bf16)
    branch = mm(hid_ref[...], down_ref[...], NT)
    residual = res_ref[...]
    cot = cot_ref[...].astype(f32)
    inv = inv_rms(branch)
    out_ref[...] = (residual + branch * inv * post_ffn).astype(bf16)
    g_ffn, gain_post = norm_back(branch, inv, post_ffn, cot)
    g_low = g_ffn.astype(bf16)
    gffn_ref[...] = g_low
    g_hidden = mm(g_low, down_ref[...])
    gg_ref[...] = (g_hidden * slope_ref[...]).astype(bf16)
    gu_ref[...] = (g_hidden * act_ref[...]).astype(bf16)
    g_in = mm(gg_ref[...], gate_ref[...], NT) + mm(gu_ref[...], up_ref[...], NT)
    back, gain_pre = norm_back(residual, inv_rms(residual), pre_ffn, g_in)
    g_res = cot + back
    gres_ref[...] = g_res
    attn_branch = branch_ref[...]
    g_attn, gain_attn = norm_back(attn_branch, inv_rms(attn_branch), post_attn, g_res)
    g_attn = g_attn.astype(bf16)
    gattn_ref[...] = g_attn
    gctx_ref[...] = mm(g_attn, wot_ref[...]).astype(bf16)
    gain_ref[0:1, :] += jnp.sum(gain_post, axis=0, keepdims=True)
    gain_ref[1:2, :] += jnp.sum(gain_pre, axis=0, keepdims=True)
    gain_ref[2:3, :] += jnp.sum(gain_attn, axis=0, keepdims=True)


def turn_strips(left_ref, source, strip, where, count):
    left_ref[1] = source.T
    for m in range(count):
        begin = pl.multiple_of(where(m) * strip, 16)
        left_ref[0, m * strip : (m + 1) * strip, :] = left_ref[1, pl.ds(begin, strip), :]


def ffn_grad_kernel(
    base, order_ref, _, fin_ref, gffn_ref, gattn_ref, gg_ref, gu_ref, hid_ref, ctx_ref, *refs
):
    recv_ref, recv_down_ref = refs[:2] if base else (None, None)
    outs = refs[2:6] if base else refs[:2]
    in_left, ffn_left, attn_left = refs[-3:]
    gates, downs = outs[: len(outs) // 2], outs[len(outs) // 2 :]
    chunks, double, tile = gates[0].shape[1:]
    held = downs[0].shape[0]
    width = fin_ref.shape[1]
    pieces = order_ref.shape[0] - chunks
    quarter, strip, half = double // 2, width // pieces, pieces // 2
    j = pl.program_id(0)

    @pl.when(j == 0)
    def _():
        turn_strips(in_left, fin_ref[...], quarter, lambda m: order_ref[pieces + m], chunks)
        turn_strips(ffn_left, gffn_ref[...], strip, lambda m: order_ref[base + m], half)
        turn_strips(attn_left, gattn_ref[...], strip, lambda m: order_ref[base + m], half)

    both = mm(in_left[0], jnp.concatenate([gg_ref[...], gu_ref[...]], axis=1))
    for i in range(2):
        part = both[:, i * tile : (i + 1) * tile].reshape(chunks, quarter, tile)
        rows_of = slice(i * quarter, (i + 1) * quarter)
        if base:
            part = part + recv_ref[0, :, rows_of, :].astype(f32)
        for k, out in enumerate(gates):

            @pl.when(j // held == k)
            def _(out=out, rows_of=rows_of, part=part):
                out[0, :, rows_of, :] = part.astype(bf16)

    down = mm(ffn_left[0, : half * strip, :], hid_ref[...])
    turned = mm(attn_left[0, : half * strip, :], ctx_ref[...])
    for i, part in enumerate((down[:, :tile], down[:, tile:], turned)):
        part = part.reshape(half, strip, tile)
        rows_of = slice(i * strip, (i + 1) * strip)
        if base:
            part = part + recv_down_ref[:, 0, rows_of, :].astype(f32)
        for k, out in enumerate(downs):
            out[:, 0, rows_of, :] = part[k * held : (k + 1) * held].astype(bf16)


def attn_grad_kernel(base, order_ref, _, attn_ref, gq_ref, gkv_ref, sort_ref, *refs):
    recv_ref = refs[0] if base else None
    outs = refs[1:3] if base else refs[:1]
    left = refs[-1]
    held, chunks, quarter, _ = outs[0].shape
    width = attn_ref.shape[1]
    pieces = order_ref.shape[0] - chunks
    half = pieces // 2
    turn_strips(left, attn_ref[...], quarter, lambda m: order_ref[pieces + m], chunks)
    sorted_kv = mm(gkv_ref[...], sort_ref[...]).astype(bf16)
    part_kv = mm(left[0], sorted_kv)
    wide = part_kv.shape[1] // half
    for pair in range(0, half, 2):
        both = jnp.concatenate(
            [
                gq_ref[:, pl.ds(pl.multiple_of(order_ref[base + pair + i] * 128, 128), 128)]
                for i in range(2)
            ],
            axis=1,
        )
        part = mm(left[0], both)
        for i in range(2):
            m = pair + i
            value = part[:, i * 128 : (i + 1) * 128].reshape(chunks, quarter, 128)
            value_kv = part_kv[:, m * wide : (m + 1) * wide].reshape(chunks, quarter, wide)
            if base:
                value = value + recv_ref[m, :, :, :128].astype(f32)
                value_kv = value_kv + recv_ref[m, :, :, 128:].astype(f32)
            out = outs[m // held]
            out[m % held, :, :, :128] = value.astype(bf16)
            out[m % held, :, :, 128:] = value_kv.astype(bf16)


def attn_back_kernel(
    _, q_ref, gctx_ref, key_ref, val_ref, pos_ref, lse_ref, qraw_ref, cos_ref, sin_ref, head_ref,
    gq_ref, far_ref, near_ref, gain_ref, gkey_ref, gval_ref,
):
    head_dim = key_ref.shape[2]
    head_count = q_ref.shape[1] // head_dim
    block = q_ref.shape[0]
    span = WINDOW + TILE
    scaling = head_dim ** (-0.5)

    @pl.when(pl.program_id(0) == 0)
    def _():
        gain_ref[...] = jnp.zeros_like(gain_ref)

    gkey_ref[...] = jnp.zeros_like(gkey_ref)
    gval_ref[...] = jnp.zeros_like(gval_ref)
    gain = jnp.zeros((1, head_dim), f32)
    for tile in range(block // TILE):
        own = slice(tile * TILE, (tile + 1) * TILE)
        reach = slice(tile * TILE, tile * TILE + span)
        query = stacked(q_ref, tile, head_count, head_dim)
        g_ctx = stacked(gctx_ref, tile, head_count, head_dim)
        key = key_ref[0, reach, :]
        value = val_ref[0, reach, :]
        log_total = jnp.stack([lse_ref[own, h : h + 1] for h in range(head_count)])
        score = mm(query, key, NT).reshape(head_count, TILE, span) + mask_of(pos_ref, tile, span)
        probs = jnp.exp(score - log_total)
        g_probs = mm(g_ctx, value, NT).reshape(head_count, TILE, span)
        spread = jnp.sum(g_probs * probs, axis=-1, keepdims=True)
        g_score = (probs * (g_probs - spread)).astype(bf16).reshape(head_count * TILE, span)
        low = probs.astype(bf16).reshape(head_count * TILE, span)
        gkey_ref[reach, :] += mm(g_score, query, TN)
        gval_ref[reach, :] += mm(low, g_ctx, TN)
        g_rot = mm(g_score, key) * scaling
        turned = slice(block + tile * TILE, block + (tile + 1) * TILE)
        cosine, sine = cos_ref[turned, :], sin_ref[turned, :]
        for h in range(head_count):
            cols = slice(h * head_dim, (h + 1) * head_dim)
            raw = qraw_ref[own, cols]
            back, share = norm_back(
                raw,
                inv_rms(raw),
                head_ref[0:1, :],
                rope_back(g_rot[h * TILE : (h + 1) * TILE], cosine, sine),
            )
            gq_ref[own, cols] = back.astype(bf16)
            gain += jnp.sum(share, axis=0, keepdims=True)
    gain_ref[0:1, :] += gain
    far_ref[0, :, :head_dim] = rope_back(
        gkey_ref[:block, :], cos_ref[:block, :], sin_ref[:block, :]
    ).astype(bf16)
    far_ref[0, :, head_dim:] = gval_ref[:block, :].astype(bf16)
    near_ref[0, :, :head_dim] = gkey_ref[block:, :]
    near_ref[0, :, head_dim:] = gval_ref[block:, :]


def kv_back_kernel(
    _, near_ref, recv_ref, kraw_ref, cos_ref, sin_ref, head_ref, gkv_ref, kgain_ref
):
    head_dim = head_ref.shape[1]

    @pl.when(pl.program_id(0) == 0)
    def _():
        kgain_ref[...] = jnp.zeros_like(kgain_ref)

    near, far = near_ref[0], recv_ref[0].astype(f32)
    raw = kraw_ref[...]
    g_normed = rope_back(near[:, :head_dim], cos_ref[...], sin_ref[...]) + far[:, :head_dim]
    g_key, share = norm_back(raw, inv_rms(raw), head_ref[1:2, :], g_normed)
    kgain_ref[0:1, :] += jnp.sum(share, axis=0, keepdims=True)
    gkv_ref[:, :head_dim] = g_key.astype(bf16)
    gkv_ref[:, head_dim:] = (near[:, head_dim:] + far[:, head_dim:]).astype(bf16)


def input_kernel(
    _, __, gq_ref, gkv_ref, wq_ref, wkv_ref, tok_ref, gres_ref, gains_ref, dtok_ref, gain_ref
):
    @pl.when(pl.program_id(0) == 0)
    def _():
        gain_ref[...] = jnp.zeros_like(gain_ref)

    g_in = mm(gq_ref[...], wq_ref[...], NT) + mm(gkv_ref[...], wkv_ref[...], NT)
    token = tok_ref[...].astype(f32)
    back, share = norm_back(token, inv_rms(token), gains_ref[0:1, :], g_in)
    dtok_ref[...] = (gres_ref[...] + back).astype(bf16)
    gain_ref[0:1, :] += jnp.sum(share, axis=0, keepdims=True)


def passed_along(shard, axis, by):
    length = lax.axis_size(axis)
    pairs = [(i, i + by) for i in range(length) if 0 <= i + by < length]
    return lax.ppermute(shard, axis, pairs)


def swapped(array, axis, even, odd):
    length = lax.axis_size(axis)
    return lax.ppermute(array, axis, [(i, i ^ (odd if i % 2 else even)) for i in range(length)])


def tables(block, head_dim):
    half_width = head_dim // 2
    frequency = ROPE_BASE ** (-(np.arange(half_width) * 2.0) / head_dim)
    angles = np.arange(-block, block)[:, None] * frequency
    return np.cos(angles).astype(np.float32), np.sin(angles).astype(np.float32)


def column_piece(array, axis_name, parts):
    wide = array.shape[1] // parts
    return lax.dynamic_slice_in_dim(array, lax.axis_index(axis_name) * wide, wide, 1)


def added(left, right):
    return left.astype(f32) + right.astype(f32)


HELD = [0, 4, 2, 6, 1, 3, 5, 7]
HELD_Z = [0, 2, 1, 3]


class Exchange:
    def __init__(self, seqs, chunks):
        self.direct = seqs == 8 and chunks == 4
        if not self.direct:
            self.order = jnp.arange(12, dtype=jnp.int32) % 8
            self.held = jnp.array(HELD + HELD_Z, jnp.int32)
            return
        s, z = lax.axis_index("seq"), lax.axis_index("fsdp")
        odd = s % 2 == 1
        one, two = jnp.where(odd, 4, 2), jnp.where(odd, 2, 4)
        zero = jnp.zeros_like(s)
        sent = [one | two | 1, two | 1, one | 1, zero | 1]
        kept = [one | two, one, two, zero]
        order = [s ^ k for k in sent + kept] + [z ^ k for k in (3, 1, 2, 0)]
        self.order = jnp.stack(order).astype(jnp.int32)
        held = [zero, two, one, one | two, zero | 1, one | 1, two | 1, one | two | 1]
        held = [s ^ k for k in held] + [z ^ k for k in HELD_Z]
        self.held = jnp.stack(held).astype(jnp.int32)

    def step(self, held, step):
        if step < 2:
            return held, swapped(held, "fsdp", 2 >> step, 2 >> step)
        return held, swapped(held, "seq", *((4, 2), (2, 4), (1, 1))[step - 2])

    def joined(self, held, got, step):
        held = jnp.concatenate([held, got], axis=0)
        return held[None] if step == 1 else held

    def swap_cores(self, parts):
        return swapped(parts, "seq", 1, 1)

    def fold(self, send, keep, step):
        if step < 2:
            got = swapped(send, "seq", *((2, 4), (4, 2))[step])
        else:
            got = swapped(send, "fsdp", step - 1, step - 1)
        if step == 3:
            return added(keep, got)
        if step == 1:
            return (
                added(keep[:2], got[:2]).astype(bf16),
                added(keep[2:], got[2:]).astype(bf16),
            )
        return added(keep[0], got[0]).astype(bf16), added(keep[1], got[1]).astype(bf16)

    def hop(self, value, axis, bits):
        return value + swapped(value, axis, bits, bits)


def scattered_plain(part):
    columns = lax.psum_scatter(part, "seq", scatter_dimension=1, tiled=True)
    return lax.psum_scatter(columns, "fsdp", scatter_dimension=0, tiled=True).astype(f32)


def gather_weights(w_query, w_key, w_value, w_out, w_gate, w_up, w_down, halo, exchange):
    pieces = w_gate.shape[1] // FF_TILE
    width = w_out.shape[1]
    if exchange.direct:
        down = column_piece(w_down, "seq", pieces).T
        ffn = jnp.concatenate(
            [
                column_piece(w_gate, "seq", pieces),
                column_piece(w_up, "seq", pieces),
                down[:, :FF_TILE],
                down[:, FF_TILE:],
            ],
            axis=0,
        )
        both = jnp.concatenate([w_key, w_value], axis=1)
        out = column_piece(w_out, "seq", pieces).T
        out = jnp.concatenate([out[:, :128], out[:, 128:]], axis=0)
        attn = jnp.concatenate(
            [column_piece(w_query, "seq", pieces), out, column_piece(both, "seq", pieces)], axis=1
        )
        def doubled(held, step):
            return exchange.joined(*exchange.step(held, step), step)

        attn = doubled(attn[None], 0)
        attn = doubled(attn, 1)
        ffn, attn = lax.optimization_barrier((ffn, attn))
        ffn = doubled(doubled(ffn[None], 0), 1)
        attn = doubled(attn, 2)
        attn, halo = lax.optimization_barrier((attn, halo))
        attn = doubled(attn, 3)
        attn, ffn = lax.optimization_barrier((attn, ffn))
        return exchange.step(attn, 4), ffn, halo
    w_query, w_key, w_value, w_out, w_gate, w_up, w_down = [
        lax.all_gather(w, "fsdp", axis=0, tiled=True)
        for w in (w_query, w_key, w_value, w_out, w_gate, w_up, w_down)
    ]
    chunks = w_down.shape[0] // (2 * FF_TILE)
    quarter, strip = width // chunks, width // pieces

    def columns(weight):
        return weight.reshape(chunks, quarter, pieces, -1).transpose(2, 0, 1, 3)

    def turned(weight):
        shape = (pieces, strip, chunks, 2, weight.shape[0] // (2 * chunks))
        turned_part = weight.T.reshape(shape).transpose(0, 2, 3, 1, 4)
        return turned_part.reshape(pieces, chunks, 2 * strip, -1)

    both = jnp.concatenate([w_key, w_value], axis=1)
    attn = jnp.concatenate([columns(w_query), turned(w_out), columns(both)], axis=3)
    ffn = jnp.concatenate([columns(w_gate), columns(w_up), turned(w_down)], axis=2)
    half = pieces // 2

    def listed(pack):
        pack = jnp.take(jnp.take(pack, np.array(HELD), axis=0), np.array(HELD_Z), axis=1)
        return pack[:half], pack[half:]

    return listed(attn), listed(ffn), halo


def plain_gradients(part_gate, part_down, part_attn):
    pieces, quarters, double, _ = part_gate.shape
    width = quarters * double // 2
    strip = width // pieces

    def columns(parts):
        return parts.transpose(1, 2, 0, 3).reshape(width, -1)

    def turned(parts):
        parts = parts.reshape(pieces, quarters, -1, strip, FF_TILE).transpose(1, 2, 4, 0, 3)
        return parts.reshape(-1, width)

    each = part_attn.shape[3] - (part_attn.shape[3] - 128) // 2
    return tuple(
        scattered_plain(part)
        for part in (
            columns(part_attn[..., :128]),
            columns(part_attn[..., 128:each]),
            columns(part_attn[..., each:]),
            turned(part_down[:, :, 2 * strip :]),
            columns(part_gate[:, :, : double // 2]),
            columns(part_gate[:, :, double // 2 :]),
            turned(part_down[:, :, : 2 * strip]),
        )
    )


def split_gradients(gate, down, attn):
    quarter = attn.shape[0]
    strip = down.shape[0] // 3
    each = attn.shape[1] - (attn.shape[1] - 128) // 2
    return (
        attn[:, :128],
        attn[:, 128:each],
        attn[:, each:],
        down[2 * strip :].T,
        gate[:quarter],
        gate[quarter:],
        jnp.concatenate([down[:strip].T, down[strip : 2 * strip].T], axis=0),
    )


def body(
    tokens, doc_starts, w_query, w_key, w_value, w_out, w_gate, w_up, w_down,
    pre_attn, post_attn, pre_ffn, post_ffn, query_norm, key_norm, cotangent,
):
    seq_dev, block, width = tokens.shape
    head_dim = w_key.shape[1]
    inner = w_query.shape[1]
    hidden_dim = w_gate.shape[1]
    count = seq_dev * block
    seqs, chunks = lax.axis_size("seq"), lax.axis_size("fsdp")
    exchange = Exchange(seqs, chunks)
    far_tokens = passed_along(tokens, "seq", 1).reshape(count, width)
    starts = jnp.concatenate([passed_along(doc_starts, "seq", 1), doc_starts], axis=1)
    indices = jnp.arange(2 * block, dtype=jnp.int32)
    latest = lax.cummax(jnp.where(starts == 1, indices[None, :], -WINDOW), axis=1)
    reach = jnp.minimum(indices[None, :] - latest, WINDOW - 1)[:, block:]
    pos_column = reach.reshape(count, 1)
    cosine, sine = tables(block, head_dim)
    own_cosine, own_sine = cosine[block:], sine[block:]

    pack, ffn_pack, far_tokens = gather_weights(
        w_query, w_key, w_value, w_out, w_gate, w_up, w_down, far_tokens, exchange
    )
    pieces, quarters = 2 * pack[0].shape[0], pack[0].shape[1]
    quarter, strip = width // quarters, width // pieces
    gains = jnp.stack([pre_attn, post_attn, pre_ffn, post_ffn])
    head_gains = jnp.stack([query_norm, key_norm])
    tokens_2d = tokens.reshape(count, width)
    cot_2d = cotangent.reshape(count, width)

    tok_spec = rows(block, width)
    table_spec = whole((2 * block, head_dim // 2))
    half_spec = whole((block, head_dim // 2))
    key_spec = pl.BlockSpec((1, 2 * block, head_dim), lambda i: (i, 0, 0))
    gains_spec, head_spec = whole((4, width)), whole((2, head_dim))
    wq_spec, wkv_spec, wot_spec = (
        whole((width, inner)),
        whole((width, 2 * head_dim)),
        whole((width, inner)),
    )
    smem = pl.BlockSpec(memory_space=pltpu.SMEM)
    remain = pl.BlockSpec(memory_space=pl.ANY)
    attn_low, query_raw, query_rot, key_raw, keys, values, full_q, full_kv, full_ot = (
        pl.pallas_call(
            qkv_kernel,
            grid=(seq_dev,),
            in_specs=[smem, tok_spec, tok_spec, table_spec, table_spec]
            + [whole(pack[0].shape)] * 2
            + [gains_spec, head_spec],
            out_specs=[
                tok_spec,
                rows(block, inner),
                rows(block, inner),
                rows(block, head_dim),
                key_spec,
                key_spec,
                wq_spec,
                wkv_spec,
                wot_spec,
            ],
            out_shape=[
                shaped((count, width), bf16),
                shaped((count, inner), f32),
                shaped((count, inner), bf16),
                shaped((count, head_dim), f32),
                shaped((seq_dev, 2 * block, head_dim), bf16),
                shaped((seq_dev, 2 * block, head_dim), bf16),
                shaped((width, inner), bf16),
                shaped((width, 2 * head_dim), bf16),
                shaped((width, inner), bf16),
            ],
            compiler_params=params(),
            name="project_rotate",
        cost_estimate=cost(11),
        )(
            exchange.held, tokens_2d, far_tokens, cosine, sine, *pack,
            gains, head_gains,
        )
    )
    if exchange.direct:
        own, got = exchange.step(ffn_pack, 2)
        got, keys = lax.optimization_barrier((got, keys))
        own, got = exchange.step(exchange.joined(own, got, 2), 3)
    context, log_total, attn_branch, residual, ffn_in = pl.pallas_call(
        attn_kernel,
        grid=(seq_dev,),
        in_specs=[rows(block, inner), key_spec, key_spec, rows(block, 1), tok_spec]
        + [wot_spec, gains_spec],
        out_specs=[rows(block, inner), rows(block, 128), tok_spec, tok_spec, tok_spec],
        out_shape=[
            shaped((count, inner), bf16),
            shaped((count, 128), f32),
            shaped((count, width), f32),
            shaped((count, width), f32),
            shaped((count, width), bf16),
        ],
        compiler_params=params(),
        name="window_attention",
        cost_estimate=cost(12),
    )(query_rot, keys, values, pos_column, tokens_2d, full_ot, gains)

    if exchange.direct:
        got, ffn_in = lax.optimization_barrier((got, ffn_in))
        ffn_pack = exchange.step(exchange.joined(own, got, 3), 4)

    small = rows(FFN_ROWS, width)
    wide = rows(FFN_ROWS, hidden_dim)
    layer_out, hidden, g_gate, g_up, g_ffn, g_res, g_attn, g_ctx, ffn_gains = pl.pallas_call(
        ffn_kernel,
        grid=(count // FFN_ROWS,),
        in_specs=[smem, small, small, small, small, remain, remain, wot_spec, gains_spec],
        out_specs=[small, wide, wide, wide, small, small, small, rows(FFN_ROWS, inner)]
        + [whole((8, width))],
        out_shape=[
            shaped((count, width), bf16),
            shaped((count, hidden_dim), bf16),
            shaped((count, hidden_dim), bf16),
            shaped((count, hidden_dim), bf16),
            shaped((count, width), bf16),
            shaped((count, width), f32),
            shaped((count, width), bf16),
            shaped((count, inner), bf16),
            shaped((8, width), f32),
        ],
        scratch_shapes=[
            pltpu.VMEM((FFN_ROWS, hidden_dim), f32),
            pltpu.VMEM((FFN_ROWS, hidden_dim), f32),
            pltpu.VMEM((width, hidden_dim), bf16),
            pltpu.VMEM((width, hidden_dim), bf16),
            pltpu.VMEM((width, hidden_dim), bf16),
            pltpu.VMEM((2,) + ffn_pack[0].shape[1:], bf16),
            pltpu.SemaphoreType.DMA((2,)),
        ],
        compiler_params=params(),
        name="feed_forward",
        cost_estimate=cost(40),
    )(
        exchange.held, residual, ffn_in, cot_2d, attn_branch, *ffn_pack, full_ot, gains,
    )

    half = pieces // 2
    full_rows = whole((count, width))

    def ffn_parts(base, before, extra):
        count_out = half // 2 if base else half
        gate_shape = (count_out, quarters, 2 * quarter, FF_TILE)
        down_shape = (count_out, quarters, 3 * strip, FF_TILE)
        gate_block, down_block = (1,) + gate_shape[1:], (count_out, 1) + down_shape[2:]

        def gate_spec(first):
            end = count_out - 1
            return pl.BlockSpec(
                gate_block, lambda j, order: (jnp.clip(j - first, 0, end), 0, 0, 0)
            )

        firsts = (0, count_out) if base else (0,)
        down_spec = pl.BlockSpec(down_block, lambda j, order: (0, j, 0, 0))
        got_specs = [
            pl.BlockSpec(gate_block, lambda j, order: (j, 0, 0, 0)),
            pl.BlockSpec((half, 1) + down_shape[2:], lambda j, order: (0, j, 0, 0)),
        ]
        turned = pltpu.VMEM((2, width, count), bf16)
        by_piece = pl.BlockSpec((count, FF_TILE), lambda j, order: (0, order[base + j]))
        wide = pl.BlockSpec((count, 2 * FF_TILE), lambda j, order: (0, order[pieces + j]))
        by_chunk = pl.BlockSpec((count, FF_TILE), lambda j, order: (0, order[pieces + j]))
        return pl.pallas_call(
            lambda *refs: ffn_grad_kernel(base, *refs),
            grid_spec=pltpu.PrefetchScalarGridSpec(
                num_scalar_prefetch=1,
                grid=(half,),
                in_specs=[remain, full_rows, full_rows, full_rows, by_piece, by_piece, wide]
                + [by_chunk]
                + got_specs[: len(extra)],
                out_specs=[gate_spec(f) for f in firsts] + [down_spec for f in firsts],
                scratch_shapes=[turned, turned, turned],
            ),
            out_shape=[shaped(gate_shape, bf16) for f in firsts]
            + [shaped(down_shape, bf16) for f in firsts],
            compiler_params=params(),
            cost_estimate=cost(11),
            name="ffn_gradients_kept" if base else "ffn_gradients_sent",
        )(exchange.order, before, ffn_in, g_ffn, g_attn, g_gate, g_up, hidden, context, *extra)

    ffn_sent = ffn_parts(0, exchange.order, [])
    ffn_got = [
        exchange.swap_cores(part) if exchange.direct else jnp.zeros_like(part)
        for part in ffn_sent
    ]

    kv_spec = pl.BlockSpec((1, block, 2 * head_dim), lambda i: (i, 0, 0))
    g_query, g_far, g_near, query_gain = pl.pallas_call(
        attn_back_kernel,
        grid=(seq_dev,),
        in_specs=[remain, rows(block, inner), rows(block, inner), key_spec, key_spec]
        + [rows(block, 1), rows(block, 128), rows(block, inner), table_spec, table_spec, head_spec],
        out_specs=[rows(block, inner), kv_spec, kv_spec, whole((8, head_dim))],
        out_shape=[
            shaped((count, inner), bf16),
            shaped((seq_dev, block, 2 * head_dim), bf16),
            shaped((seq_dev, block, 2 * head_dim), f32),
            shaped((8, head_dim), f32),
        ],
        scratch_shapes=[
            pltpu.VMEM((2 * block, head_dim), f32),
            pltpu.VMEM((2 * block, head_dim), f32),
        ],
        compiler_params=params(),
        name="attention_gradient",
        cost_estimate=cost(16),
    )(
        ffn_sent[0], query_rot, g_ctx, keys, values, pos_column, log_total, query_raw, cosine, sine,
        head_gains,
    )
    g_recv = passed_along(g_far, "seq", -1)
    gate_send, gate_keep, down_send, down_keep = ffn_parts(half, g_far, ffn_got)
    g_kv, key_gain = pl.pallas_call(
        kv_back_kernel,
        grid=(seq_dev,),
        in_specs=[remain, kv_spec, kv_spec, rows(block, head_dim), half_spec, half_spec, head_spec],
        out_specs=[rows(block, 2 * head_dim), whole((8, head_dim))],
        out_shape=[shaped((count, 2 * head_dim), bf16), shaped((8, head_dim), f32)],
        compiler_params=params(),
        name="key_value_back",
        cost_estimate=cost(4),
    )(gate_send, g_near, g_recv, key_raw, own_cosine, own_sine, head_gains)

    each = head_dim // pieces
    column = jnp.arange(2 * head_dim, dtype=jnp.int32)
    inside = column % (2 * each)
    source = jnp.where(inside < each, inside, inside - each + head_dim)
    source = source + each * jnp.repeat(exchange.order[:pieces], 2 * each)
    sort = (column[:, None] == source[None, :]).astype(bf16)

    def attn_parts(base, before, extra):
        shape = (half, quarters, quarter, 128 + 2 * each)
        sent = (half // 2,) + shape[1:]
        outs = [shape] if base == 0 else [sent, sent]
        vmem = pl.BlockSpec(memory_space=pltpu.VMEM)
        chosen = sort[:, base * 2 * each : (base + half) * 2 * each]
        return pl.pallas_call(
            lambda *refs: attn_grad_kernel(base, *refs),
            in_specs=[smem, remain] + [vmem] * (4 + len(extra)),
            out_specs=[vmem] * len(outs),
            out_shape=[shaped(o, bf16) for o in outs],
            scratch_shapes=[pltpu.VMEM((2, width, count), bf16)],
            compiler_params=params(),
            cost_estimate=cost(6),
            name="attn_gradients_kept" if base else "attn_gradients_sent",
        )(exchange.order, before, attn_low, g_query, g_kv, chosen, *extra)

    (attn_sent,) = attn_parts(0, exchange.order, [])
    attn_got = exchange.swap_cores(attn_sent) if exchange.direct else jnp.zeros_like(attn_sent)
    gate, down = (gate_send, gate_keep), (down_send, down_keep)
    if exchange.direct:
        gate = exchange.fold(*gate, 0)
        down, gate = lax.optimization_barrier((down, gate))
    attn_parts_kept = attn_parts(half, gate[0], [attn_got])
    if exchange.direct:
        gate = exchange.fold(*gate, 1)
        down = exchange.fold(*down, 0)
    dtokens, attn_gain = pl.pallas_call(
        input_kernel,
        grid=(seq_dev,),
        in_specs=[remain, remain, rows(block, inner), rows(block, 2 * head_dim)]
        + [wq_spec, wkv_spec]
        + [tok_spec, tok_spec, gains_spec],
        out_specs=[tok_spec, whole((8, width))],
        out_shape=[shaped((count, width), bf16), shaped((8, width), f32)],
        compiler_params=params(),
        name="input_gradient",
        cost_estimate=cost(7),
    )(attn_parts_kept[0], down[0], g_query, g_kv, full_q, full_kv, tokens_2d, g_res, gains)

    sums = jnp.concatenate(
        [attn_gain[0], ffn_gains[2], ffn_gains[1], ffn_gains[0], query_gain[0], key_gain[0]]
    )
    if exchange.direct:
        attn = attn_parts_kept
        hops = (("seq", 1), ("seq", 2), ("seq", 4), ("fsdp", 1), ("fsdp", 2))
        for step in range(4):
            gate = exchange.fold(*gate, step + 2) if step < 2 else gate
            down = exchange.fold(*down, step + 1) if step < 3 else down
            attn = exchange.fold(*attn, step)
            sums = exchange.hop(sums, *hops[step])
            gate, down, attn, sums = lax.optimization_barrier((gate, down, attn, sums))
        sums = exchange.hop(sums, *hops[4])
        weights = split_gradients(gate, down, attn)
    else:
        weights = plain_gradients(
            jnp.concatenate([ffn_sent[0], gate_send, gate_keep], axis=0),
            jnp.concatenate([ffn_sent[1], down_send, down_keep], axis=0),
            jnp.concatenate([attn_sent, *attn_parts_kept], axis=0),
        )
        sums = lax.psum(sums, ("seq", "fsdp"))
    cuts = [0, width, 2 * width, 3 * width, 4 * width, 4 * width + head_dim]
    cuts.append(cuts[-1] + head_dim)
    gain_sums = tuple(sums[a:b] for a, b in zip(cuts[:-1], cuts[1:]))
    shape = (seq_dev, block, width)
    return (layer_out.reshape(shape), dtokens.reshape(shape)) + weights + gain_sums


def solution(mesh):
    sharded = P("fsdp", "seq", None)
    weight = P("fsdp", None)
    in_specs = (sharded, P("fsdp", "seq")) + (weight,) * 7 + (P(),) * 6 + (sharded,)
    out_specs = (sharded, sharded) + (P("fsdp", "seq"),) * 7 + (P(),) * 6
    return jax.shard_map(body, mesh=mesh, in_specs=in_specs, out_specs=out_specs, check_vma=False)
```

```python
import jax
import jax.numpy as jnp
import numpy as np
from jax import lax
from jax.experimental import pallas as pl
from jax.experimental.pallas import tpu as pltpu
from jax.sharding import PartitionSpec as P

WINDOW = 512
TILE = 128
FF_TILE = 256
FFN_ROWS = 256

epsilon = 1e-06
NEG_FILL = -1e30
ROPE_BASE = 10000.0
GELU_C = 0.7978845608028654
GELU_K = 0.044715

f32 = jnp.float32
bf16 = jnp.bfloat16

NN = (((1,), (0,)), ((), ()))
NT = (((1,), (1,)), ((), ()))
TN = (((0,), (0,)), ((), ()))


def mm(left, right, dims=NN):
    return lax.dot_general(left, right, dims, preferred_element_type=f32)


def inv_rms(vector):
    return lax.rsqrt(jnp.mean(vector * vector, axis=-1, keepdims=True) + epsilon)


def norm_back(vector, inv, gain, grad):
    unit = vector * inv
    scaled = gain * grad
    back = inv * (scaled - unit * jnp.mean(unit * scaled, axis=-1, keepdims=True))
    return back, grad * unit


def rope(vector, cosine, sine):
    half = vector.shape[-1] // 2
    one, two = vector[:, :half], vector[:, half:]
    return jnp.concatenate([one * cosine - two * sine, two * cosine + one * sine], axis=1)


def rope_back(vector, cosine, sine):
    half = vector.shape[-1] // 2
    one, two = vector[:, :half], vector[:, half:]
    return jnp.concatenate([one * cosine + two * sine, two * cosine - one * sine], axis=1)


def params(limit_mib=58):
    return pltpu.CompilerParams(vmem_limit_bytes=limit_mib * 1024 * 1024)


def cost(microseconds):
    return pl.CostEstimate(
        flops=int(microseconds * 1e9), bytes_accessed=int(microseconds * 3e6), transcendentals=0
    )


def whole(shape):
    return pl.BlockSpec(shape, lambda *_: (0,) * len(shape))


def rows(count, width):
    return pl.BlockSpec((count, width), lambda i: (i, 0))


def shaped(shape, dtype):
    return jax.ShapeDtypeStruct(shape, dtype)


def qkv_kernel(
    held_ref, tok_ref, far_ref, cos_ref, sin_ref, gains_ref, head_ref, *refs
):
    packs = refs[:-9]
    attn_ref, qraw_ref, qrot_ref, kraw_ref, key_ref, val_ref, wq_ref, wkv_ref, wot_ref = refs[-9:]
    head_dim = head_ref.shape[1]
    head_count = wq_ref.shape[1] // head_dim
    block, width = tok_ref.shape
    chunks, chunk_rows, _ = packs[0].shape
    pieces = len(packs)
    half = pieces // 2

    @pl.when(pl.program_id(0) == 0)
    def _():
        strip = chunk_rows // 2
        odd = held_ref[0] % 2 == 1

        def aligned(index, size):
            return pl.ds(pl.multiple_of(index * size, size), size)

        for c in range(chunks):
            z = held_ref[pieces + c]
            own = aligned(z, chunk_rows)
            for m in range(pieces):
                s = held_ref[m]
                wq_ref[own, aligned(s, 128)] = packs[m][c, :, :128]
                turned = packs[m][c, :, 128:256]
                for i in range(2):
                    wot_ref[aligned(s, strip), aligned(2 * z + i, 128)] = turned[
                        i * strip : (i + 1) * strip
                    ]
            for m, mate in zip(range(half), (0, 2, 1, 3)):
                one, two = packs[m][c, :, 256:320], packs[half + mate][c, :, 256:320]
                wkv_ref[own, aligned(held_ref[m] // 2, 128)] = jnp.concatenate(
                    [jnp.where(odd, two, one), jnp.where(odd, one, two)], axis=1
                )

    pre = gains_ref[0:1, :]
    qgain, kgain = head_ref[0:1, :], head_ref[1:2, :]
    token = tok_ref[...].astype(f32)
    low = (token * inv_rms(token) * pre).astype(bf16)
    attn_ref[...] = low
    query = mm(low, wq_ref[...])
    qraw_ref[...] = query
    cosine, sine = cos_ref[block:, :], sin_ref[block:, :]
    scaling = head_dim ** (-0.5)
    for h in range(head_count):
        part = query[:, h * head_dim : (h + 1) * head_dim]
        normed = part * inv_rms(part) * qgain
        qrot_ref[:, h * head_dim : (h + 1) * head_dim] = (
            rope(normed, cosine, sine).astype(bf16) * jnp.asarray(scaling, bf16)
        )
    both = mm(low, wkv_ref[...])
    key = both[:, :head_dim]
    kraw_ref[...] = key
    key_ref[0, block:, :] = rope(key * inv_rms(key) * kgain, cosine, sine).astype(bf16)
    val_ref[0, block:, :] = both[:, head_dim:].astype(bf16)
    token = far_ref[...].astype(f32)
    low = (token * inv_rms(token) * pre).astype(bf16)
    both = mm(low, wkv_ref[...])
    key = both[:, :head_dim]
    key_ref[0, :block, :] = rope(
        key * inv_rms(key) * kgain, cos_ref[:block, :], sin_ref[:block, :]
    ).astype(bf16)
    val_ref[0, :block, :] = both[:, head_dim:].astype(bf16)


def stacked(ref, tile, head_count, head_dim):
    return jnp.concatenate(
        [
            ref[tile * TILE : (tile + 1) * TILE, h * head_dim : (h + 1) * head_dim]
            for h in range(head_count)
        ],
        axis=0,
    )


def mask_of(pos_ref, tile, span):
    reach = pos_ref[tile * TILE : (tile + 1) * TILE, :]
    row = lax.broadcasted_iota(jnp.int32, (TILE, span), 0)
    col = lax.broadcasted_iota(jnp.int32, (TILE, span), 1)
    distance = WINDOW + row - col
    return jnp.where((distance >= 0) & (distance <= reach), 0.0, NEG_FILL)


def attn_kernel(
    q_ref, key_ref, val_ref, pos_ref, tok_ref, wot_ref, gains_ref,
    ctx_ref, lse_ref, branch_ref, res_ref, fin_ref,
):
    head_dim = key_ref.shape[2]
    head_count = q_ref.shape[1] // head_dim
    span = WINDOW + TILE
    lane = lax.broadcasted_iota(jnp.int32, (TILE, 128), 1)
    for tile in range(q_ref.shape[0] // TILE):
        query = stacked(q_ref, tile, head_count, head_dim)
        key = key_ref[0, tile * TILE : tile * TILE + span, :]
        value = val_ref[0, tile * TILE : tile * TILE + span, :]
        score = mm(query, key, NT).reshape(head_count, TILE, span) + mask_of(pos_ref, tile, span)
        largest = jnp.max(score, axis=-1, keepdims=True)
        expo = jnp.exp(score - largest)
        total = jnp.sum(expo, axis=-1, keepdims=True)
        low = expo.astype(bf16).reshape(head_count * TILE, span)
        context = mm(low, value).reshape(head_count, TILE, head_dim) / total
        log_total = largest + jnp.log(total)
        kept = jnp.zeros((TILE, 128), f32)
        for h in range(head_count):
            ctx_ref[tile * TILE : (tile + 1) * TILE, h * head_dim : (h + 1) * head_dim] = context[
                h
            ].astype(bf16)
            kept = jnp.where(lane == h, log_total[h], kept)
        lse_ref[tile * TILE : (tile + 1) * TILE, :] = kept
    branch = mm(ctx_ref[...], wot_ref[...], NT)
    branch_ref[...] = branch
    residual = tok_ref[...].astype(f32) + branch * inv_rms(branch) * gains_ref[1:2, :]
    res_ref[...] = residual
    fin_ref[...] = (residual * inv_rms(residual) * gains_ref[2:3, :]).astype(bf16)


def ffn_kernel(
    held_ref, order_ref, res_ref, fin_ref, cot_ref, branch_ref, ctx_ref, wot_ref, gains_ref, *refs
):
    pieces = order_ref.shape[0] - refs[0].shape[0]
    packs, refs = refs[:pieces], refs[pieces:]
    out_ref, gres_ref, gctx_ref, gain_ref = refs[:4]
    gate_sent, gate_kept, down_sent, down_kept = refs[4:8]
    slope_ref, act_ref, gate_ref, up_ref, down_ref, stage_ref, copied = refs[8:15]
    hid_ref, gg_ref, gu_ref, in_left, ffn_left, attn_left, turn_ref = refs[15:]
    chunks, _, tile = packs[0].shape
    width = res_ref.shape[1]
    count = hid_ref.shape[0]
    quarter, strip, half = width // chunks, width // pieces, pieces // 2
    step = pl.program_id(0)
    tiles = count // FFN_ROWS
    post_attn, pre_ffn, post_ffn = [gains_ref[i : i + 1, :] for i in (1, 2, 3)]

    def aligned(index, size):
        return pl.ds(pl.multiple_of(index * size, size), size)

    @pl.when(step == 0)
    def _():
        gain_ref[...] = jnp.zeros_like(gain_ref)

        def staged(m):
            return pltpu.make_async_copy(packs[m], stage_ref.at[m % 2], copied.at[m % 2])

        staged(0).start()
        for m in range(pieces):
            if m + 1 < pieces:
                staged(m + 1).start()
            staged(m).wait()
            s = held_ref[m]
            for c in range(chunks):
                z = held_ref[pieces + c]
                own, cols = aligned(z, quarter), aligned(s, tile)
                gate_ref[own, cols] = stage_ref[m % 2, c, :quarter, :]
                up_ref[own, cols] = stage_ref[m % 2, c, quarter : 2 * quarter, :]
                for i in range(2):
                    begin = 2 * quarter + i * strip
                    down_ref[aligned(s, strip), aligned(2 * z + i, tile)] = stage_ref[
                        m % 2, c, begin : begin + strip, :
                    ]

    @pl.when(step < tiles)
    def _():
        own = aligned(step, FFN_ROWS)

        def turn(left_ref, source, size, first, number):
            turn_ref[...] = source.T
            for m in range(number):
                left_ref[m * size : (m + 1) * size, own] = turn_ref[
                    aligned(order_ref[first + m], size), :
                ]

        ffn_in = fin_ref[...]
        turn(in_left, ffn_in, quarter, pieces, chunks)
        gate = mm(ffn_in, gate_ref[...])
        up = mm(ffn_in, up_ref[...])
        square = gate * gate
        bent = jnp.tanh(GELU_C * gate * (1.0 + GELU_K * square))
        half_bent = 0.5 * (1.0 + bent)
        act = gate * half_bent
        slope = half_bent + 0.5 * gate * (1.0 - bent * bent) * (
            GELU_C * (1.0 + 3.0 * GELU_K * square)
        )
        act_ref[...] = act
        slope_ref[...] = slope * up
        hidden = (act * up).astype(bf16)
        hid_ref[own, :] = hidden
        branch = mm(hidden, down_ref[...], NT)
        residual = res_ref[...]
        cot = cot_ref[...].astype(f32)
        inv = inv_rms(branch)
        out_ref[...] = (residual + branch * inv * post_ffn).astype(bf16)
        g_ffn, gain_post = norm_back(branch, inv, post_ffn, cot)
        g_low = g_ffn.astype(bf16)
        turn(ffn_left, g_low, strip, 0, pieces)
        g_hidden = mm(g_low, down_ref[...])
        g_gate = (g_hidden * slope_ref[...]).astype(bf16)
        g_up = (g_hidden * act_ref[...]).astype(bf16)
        gg_ref[own, :] = g_gate
        gu_ref[own, :] = g_up
        g_in = mm(g_gate, gate_ref[...], NT) + mm(g_up, up_ref[...], NT)
        back, gain_pre = norm_back(residual, inv_rms(residual), pre_ffn, g_in)
        g_res = cot + back
        gres_ref[...] = g_res
        attn_branch = branch_ref[...]
        g_attn, gain_attn = norm_back(attn_branch, inv_rms(attn_branch), post_attn, g_res)
        g_attn = g_attn.astype(bf16)
        turn(attn_left, g_attn, strip, 0, pieces)
        gctx_ref[...] = mm(g_attn, wot_ref[...]).astype(bf16)
        gain_ref[0:1, :] += jnp.sum(gain_post, axis=0, keepdims=True)
        gain_ref[1:2, :] += jnp.sum(gain_pre, axis=0, keepdims=True)
        gain_ref[2:3, :] += jnp.sum(gain_attn, axis=0, keepdims=True)

    @pl.when(step >= tiles)
    def _():
        k = step - tiles
        cols = aligned(order_ref[k], tile)
        z = order_ref[pieces + k // 2]
        both = mm(in_left[...], jnp.concatenate([gg_ref[:, cols], gu_ref[:, cols]], axis=1))
        both = both.astype(bf16)
        for i in range(2):
            part = both[:, i * tile : (i + 1) * tile].reshape(chunks, quarter, tile)
            for inside, out in ((k < half, gate_sent), (k >= half, gate_kept)):

                @pl.when(inside)
                def _(out=out, part=part, i=i):
                    out[0, :, i * quarter : (i + 1) * quarter, :] = part

        def put(begin, part):
            part = part.astype(bf16).reshape(pieces, strip, tile)
            down_sent[:, 0, pl.ds(begin, strip), :] = part[:half]
            down_kept[:, 0, pl.ds(begin, strip), :] = part[half:]

        put(
            pl.multiple_of(k % 2 * strip, strip),
            mm(ffn_left[...], hid_ref[:, aligned(2 * z + k % 2, tile)]),
        )

        @pl.when(k % 2 == 0)
        def _():
            put(2 * strip, mm(attn_left[...], ctx_ref[:, aligned(z, tile)]))


def turn_strips(left_ref, source, strip, where, count):
    left_ref[1] = source.T
    for m in range(count):
        begin = pl.multiple_of(where(m) * strip, 16)
        left_ref[0, m * strip : (m + 1) * strip, :] = left_ref[1, pl.ds(begin, strip), :]


def attn_grad_kernel(base, order_ref, _, attn_ref, gq_ref, gkv_ref, sort_ref, *refs):
    recv_ref = refs[0] if base else None
    outs = refs[1:3] if base else refs[:1]
    left = refs[-1]
    held, chunks, quarter, _ = outs[0].shape
    width = attn_ref.shape[1]
    pieces = order_ref.shape[0] - chunks
    half = pieces // 2
    turn_strips(left, attn_ref[...], quarter, lambda m: order_ref[pieces + m], chunks)
    sorted_kv = mm(gkv_ref[...], sort_ref[...]).astype(bf16)
    part_kv = mm(left[0], sorted_kv)
    wide = part_kv.shape[1] // half
    for pair in range(0, half, 2):
        both = jnp.concatenate(
            [
                gq_ref[:, pl.ds(pl.multiple_of(order_ref[base + pair + i] * 128, 128), 128)]
                for i in range(2)
            ],
            axis=1,
        )
        part = mm(left[0], both)
        for i in range(2):
            m = pair + i
            value = part[:, i * 128 : (i + 1) * 128].reshape(chunks, quarter, 128)
            value_kv = part_kv[:, m * wide : (m + 1) * wide].reshape(chunks, quarter, wide)
            if base:
                value = value + recv_ref[m, :, :, :128].astype(f32)
                value_kv = value_kv + recv_ref[m, :, :, 128:].astype(f32)
            out = outs[m // held]
            out[m % held, :, :, :128] = value.astype(bf16)
            out[m % held, :, :, 128:] = value_kv.astype(bf16)


def attn_back_kernel(
    q_ref, gctx_ref, key_ref, val_ref, pos_ref, lse_ref, qraw_ref, cos_ref, sin_ref, head_ref,
    gq_ref, far_ref, near_ref, gain_ref, gkey_ref, gval_ref,
):
    head_dim = key_ref.shape[2]
    head_count = q_ref.shape[1] // head_dim
    block = q_ref.shape[0]
    span = WINDOW + TILE
    scaling = head_dim ** (-0.5)

    @pl.when(pl.program_id(0) == 0)
    def _():
        gain_ref[...] = jnp.zeros_like(gain_ref)

    gkey_ref[...] = jnp.zeros_like(gkey_ref)
    gval_ref[...] = jnp.zeros_like(gval_ref)
    gain = jnp.zeros((1, head_dim), f32)
    for tile in range(block // TILE):
        own = slice(tile * TILE, (tile + 1) * TILE)
        reach = slice(tile * TILE, tile * TILE + span)
        query = stacked(q_ref, tile, head_count, head_dim)
        g_ctx = stacked(gctx_ref, tile, head_count, head_dim)
        key = key_ref[0, reach, :]
        value = val_ref[0, reach, :]
        log_total = jnp.stack([lse_ref[own, h : h + 1] for h in range(head_count)])
        score = mm(query, key, NT).reshape(head_count, TILE, span) + mask_of(pos_ref, tile, span)
        probs = jnp.exp(score - log_total)
        g_probs = mm(g_ctx, value, NT).reshape(head_count, TILE, span)
        spread = jnp.sum(g_probs * probs, axis=-1, keepdims=True)
        g_score = (probs * (g_probs - spread)).astype(bf16).reshape(head_count * TILE, span)
        low = probs.astype(bf16).reshape(head_count * TILE, span)
        gkey_ref[reach, :] += mm(g_score, query, TN)
        gval_ref[reach, :] += mm(low, g_ctx, TN)
        g_rot = mm(g_score, key) * scaling
        turned = slice(block + tile * TILE, block + (tile + 1) * TILE)
        cosine, sine = cos_ref[turned, :], sin_ref[turned, :]
        for h in range(head_count):
            cols = slice(h * head_dim, (h + 1) * head_dim)
            raw = qraw_ref[own, cols]
            back, share = norm_back(
                raw,
                inv_rms(raw),
                head_ref[0:1, :],
                rope_back(g_rot[h * TILE : (h + 1) * TILE], cosine, sine),
            )
            gq_ref[own, cols] = back.astype(bf16)
            gain += jnp.sum(share, axis=0, keepdims=True)
    gain_ref[0:1, :] += gain
    far_ref[0, :, :head_dim] = rope_back(
        gkey_ref[:block, :], cos_ref[:block, :], sin_ref[:block, :]
    ).astype(bf16)
    far_ref[0, :, head_dim:] = gval_ref[:block, :].astype(bf16)
    near_ref[0, :, :head_dim] = gkey_ref[block:, :]
    near_ref[0, :, head_dim:] = gval_ref[block:, :]


def kv_back_kernel(
    _, near_ref, recv_ref, kraw_ref, cos_ref, sin_ref, head_ref, gkv_ref, kgain_ref
):
    head_dim = head_ref.shape[1]

    @pl.when(pl.program_id(0) == 0)
    def _():
        kgain_ref[...] = jnp.zeros_like(kgain_ref)

    near, far = near_ref[0], recv_ref[0].astype(f32)
    raw = kraw_ref[...]
    g_normed = rope_back(near[:, :head_dim], cos_ref[...], sin_ref[...]) + far[:, :head_dim]
    g_key, share = norm_back(raw, inv_rms(raw), head_ref[1:2, :], g_normed)
    kgain_ref[0:1, :] += jnp.sum(share, axis=0, keepdims=True)
    gkv_ref[:, :head_dim] = g_key.astype(bf16)
    gkv_ref[:, head_dim:] = (near[:, head_dim:] + far[:, head_dim:]).astype(bf16)


def input_kernel(
    _, __, gq_ref, gkv_ref, wq_ref, wkv_ref, tok_ref, gres_ref, gains_ref, dtok_ref, gain_ref
):
    @pl.when(pl.program_id(0) == 0)
    def _():
        gain_ref[...] = jnp.zeros_like(gain_ref)

    g_in = mm(gq_ref[...], wq_ref[...], NT) + mm(gkv_ref[...], wkv_ref[...], NT)
    token = tok_ref[...].astype(f32)
    back, share = norm_back(token, inv_rms(token), gains_ref[0:1, :], g_in)
    dtok_ref[...] = (gres_ref[...] + back).astype(bf16)
    gain_ref[0:1, :] += jnp.sum(share, axis=0, keepdims=True)


def passed_along(shard, axis, by):
    length = lax.axis_size(axis)
    pairs = [(i, i + by) for i in range(length) if 0 <= i + by < length]
    return lax.ppermute(shard, axis, pairs)


def swapped(array, axis, even, odd):
    length = lax.axis_size(axis)
    return lax.ppermute(array, axis, [(i, i ^ (odd if i % 2 else even)) for i in range(length)])


def tables(block, head_dim):
    half_width = head_dim // 2
    frequency = ROPE_BASE ** (-(np.arange(half_width) * 2.0) / head_dim)
    angles = np.arange(-block, block)[:, None] * frequency
    return np.cos(angles).astype(np.float32), np.sin(angles).astype(np.float32)


def column_piece(array, axis_name, parts):
    wide = array.shape[1] // parts
    return lax.dynamic_slice_in_dim(array, lax.axis_index(axis_name) * wide, wide, 1)


def added(left, right):
    return left.astype(f32) + right.astype(f32)


HELD = [0, 4, 2, 6, 1, 3, 5, 7]
HELD_Z = [0, 2, 1, 3]


class Exchange:
    def __init__(self, seqs, chunks):
        self.direct = seqs == 8 and chunks == 4
        if not self.direct:
            self.order = jnp.arange(12, dtype=jnp.int32) % 8
            self.held = jnp.array(HELD + HELD_Z, jnp.int32)
            return
        s, z = lax.axis_index("seq"), lax.axis_index("fsdp")
        odd = s % 2 == 1
        one, two = jnp.where(odd, 4, 2), jnp.where(odd, 2, 4)
        zero = jnp.zeros_like(s)
        sent = [one | two | 1, two | 1, one | 1, zero | 1]
        kept = [one | two, one, two, zero]
        order = [s ^ k for k in sent + kept] + [z ^ k for k in (3, 1, 2, 0)]
        self.order = jnp.stack(order).astype(jnp.int32)
        held = [zero, two, one, one | two, zero | 1, one | 1, two | 1, one | two | 1]
        held = [s ^ k for k in held] + [z ^ k for k in HELD_Z]
        self.held = jnp.stack(held).astype(jnp.int32)

    def along_step(self, held, bits):
        return jnp.concatenate([held, swapped(held, "fsdp", bits, bits)], axis=0)

    def second(self, piece):
        return swapped(piece, "seq", 4, 2)

    def first(self, piece):
        return swapped(piece, "seq", 2, 4)

    def swap_cores(self, parts):
        return swapped(parts, "seq", 1, 1)

    def fold(self, send, keep, step):
        if step < 2:
            got = swapped(send, "seq", *((2, 4), (4, 2))[step])
        else:
            got = swapped(send, "fsdp", step - 1, step - 1)
        if step == 3:
            return added(keep, got)
        if step == 1:
            return self.fold_got(keep, got)
        return added(keep[0], got[0]).astype(bf16), added(keep[1], got[1]).astype(bf16)

    def fold_got(self, keep, got):
        half = keep.shape[0] // 2
        sums = added(keep, got).astype(bf16)
        return sums[:half], sums[half:]

    def hop(self, value, axis, bits):
        return value + swapped(value, axis, bits, bits)


def scattered_plain(part):
    columns = lax.psum_scatter(part, "seq", scatter_dimension=1, tiled=True)
    return lax.psum_scatter(columns, "fsdp", scatter_dimension=0, tiled=True).astype(f32)


def gather_weights(w_query, w_key, w_value, w_out, w_gate, w_up, w_down, halo, exchange):
    pieces = w_gate.shape[1] // FF_TILE
    width = w_out.shape[1]
    if exchange.direct:
        down = column_piece(w_down, "seq", pieces).T
        ffn = jnp.concatenate(
            [
                column_piece(w_gate, "seq", pieces),
                column_piece(w_up, "seq", pieces),
                down[:, :FF_TILE],
                down[:, FF_TILE:],
            ],
            axis=0,
        )
        both = jnp.concatenate([w_key, w_value], axis=1)
        out = column_piece(w_out, "seq", pieces).T
        out = jnp.concatenate([out[:, :128], out[:, 128:]], axis=0)
        attn = jnp.concatenate(
            [column_piece(w_query, "seq", pieces), out, column_piece(both, "seq", pieces)], axis=1
        )
        attn = exchange.along_step(exchange.along_step(attn[None], 2), 1)
        ffn, attn = lax.optimization_barrier((ffn, attn))
        ffn = exchange.along_step(ffn[None], 2)
        attn, halo = lax.optimization_barrier((attn, halo))
        two, one = exchange.second(attn), exchange.first(attn)
        ffn, two = lax.optimization_barrier((ffn, two))
        ffn = exchange.along_step(ffn, 1)
        attn = [attn, two, one, exchange.first(two)]
        attn[3], ffn = lax.optimization_barrier((attn[3], ffn))
        return attn + [exchange.swap_cores(held) for held in attn], ffn, halo
    w_query, w_key, w_value, w_out, w_gate, w_up, w_down = [
        lax.all_gather(w, "fsdp", axis=0, tiled=True)
        for w in (w_query, w_key, w_value, w_out, w_gate, w_up, w_down)
    ]
    chunks = w_down.shape[0] // (2 * FF_TILE)
    quarter, strip = width // chunks, width // pieces

    def columns(weight):
        return weight.reshape(chunks, quarter, pieces, -1).transpose(2, 0, 1, 3)

    def turned(weight):
        shape = (pieces, strip, chunks, 2, weight.shape[0] // (2 * chunks))
        turned_part = weight.T.reshape(shape).transpose(0, 2, 3, 1, 4)
        return turned_part.reshape(pieces, chunks, 2 * strip, -1)

    both = jnp.concatenate([w_key, w_value], axis=1)
    attn = jnp.concatenate([columns(w_query), turned(w_out), columns(both)], axis=3)
    ffn = jnp.concatenate([columns(w_gate), columns(w_up), turned(w_down)], axis=2)
    def listed(pack):
        pack = jnp.take(jnp.take(pack, np.array(HELD), axis=0), np.array(HELD_Z), axis=1)
        return [pack[m] for m in range(pieces)]

    return listed(attn), listed(ffn), halo


def plain_gradients(part_gate, part_down, part_attn):
    pieces, quarters, double, _ = part_gate.shape
    width = quarters * double // 2
    strip = width // pieces

    def columns(parts):
        return parts.transpose(1, 2, 0, 3).reshape(width, -1)

    def turned(parts):
        parts = parts.reshape(pieces, quarters, -1, strip, FF_TILE).transpose(1, 2, 4, 0, 3)
        return parts.reshape(-1, width)

    each = part_attn.shape[3] - (part_attn.shape[3] - 128) // 2
    return tuple(
        scattered_plain(part)
        for part in (
            columns(part_attn[..., :128]),
            columns(part_attn[..., 128:each]),
            columns(part_attn[..., each:]),
            turned(part_down[:, :, 2 * strip :]),
            columns(part_gate[:, :, : double // 2]),
            columns(part_gate[:, :, double // 2 :]),
            turned(part_down[:, :, : 2 * strip]),
        )
    )


def split_gradients(gate, down, attn):
    quarter = attn.shape[0]
    strip = down.shape[0] // 3
    each = attn.shape[1] - (attn.shape[1] - 128) // 2
    return (
        attn[:, :128],
        attn[:, 128:each],
        attn[:, each:],
        down[2 * strip :].T,
        gate[:quarter],
        gate[quarter:],
        jnp.concatenate([down[:strip].T, down[strip : 2 * strip].T], axis=0),
    )


def body(
    tokens, doc_starts, w_query, w_key, w_value, w_out, w_gate, w_up, w_down,
    pre_attn, post_attn, pre_ffn, post_ffn, query_norm, key_norm, cotangent,
):
    seq_dev, block, width = tokens.shape
    head_dim = w_key.shape[1]
    inner = w_query.shape[1]
    hidden_dim = w_gate.shape[1]
    count = seq_dev * block
    seqs, chunks = lax.axis_size("seq"), lax.axis_size("fsdp")
    exchange = Exchange(seqs, chunks)
    far_tokens = passed_along(tokens, "seq", 1).reshape(count, width)
    far_starts = passed_along(doc_starts, "seq", 1)
    pack, ffn_pack, (far_tokens, far_starts) = gather_weights(
        w_query, w_key, w_value, w_out, w_gate, w_up, w_down, (far_tokens, far_starts), exchange
    )
    starts = jnp.concatenate([far_starts, doc_starts], axis=1)
    indices = jnp.arange(2 * block, dtype=jnp.int32)
    latest = lax.cummax(jnp.where(starts == 1, indices[None, :], -WINDOW), axis=1)
    reach = jnp.minimum(indices[None, :] - latest, WINDOW - 1)[:, block:]
    pos_column = reach.reshape(count, 1)
    cosine, sine = tables(block, head_dim)
    own_cosine, own_sine = cosine[block:], sine[block:]

    pieces, quarters = len(pack), pack[0].shape[0]
    quarter, strip = width // quarters, width // pieces
    gains = jnp.stack([pre_attn, post_attn, pre_ffn, post_ffn])
    head_gains = jnp.stack([query_norm, key_norm])
    tokens_2d = tokens.reshape(count, width)
    cot_2d = cotangent.reshape(count, width)

    tok_spec = rows(block, width)
    table_spec = whole((2 * block, head_dim // 2))
    half_spec = whole((block, head_dim // 2))
    key_spec = pl.BlockSpec((1, 2 * block, head_dim), lambda i: (i, 0, 0))
    gains_spec, head_spec = whole((4, width)), whole((2, head_dim))
    wq_spec, wkv_spec, wot_spec = (
        whole((width, inner)),
        whole((width, 2 * head_dim)),
        whole((width, inner)),
    )
    smem = pl.BlockSpec(memory_space=pltpu.SMEM)
    remain = pl.BlockSpec(memory_space=pl.ANY)
    attn_low, query_raw, query_rot, key_raw, keys, values, full_q, full_kv, full_ot = (
        pl.pallas_call(
            qkv_kernel,
            grid=(seq_dev,),
            in_specs=[smem, tok_spec, tok_spec, table_spec, table_spec]
            + [gains_spec, head_spec]
            + [whole(pack[0].shape)] * pieces,
            out_specs=[
                tok_spec,
                rows(block, inner),
                rows(block, inner),
                rows(block, head_dim),
                key_spec,
                key_spec,
                wq_spec,
                wkv_spec,
                wot_spec,
            ],
            out_shape=[
                shaped((count, width), bf16),
                shaped((count, inner), f32),
                shaped((count, inner), bf16),
                shaped((count, head_dim), f32),
                shaped((seq_dev, 2 * block, head_dim), bf16),
                shaped((seq_dev, 2 * block, head_dim), bf16),
                shaped((width, inner), bf16),
                shaped((width, 2 * head_dim), bf16),
                shaped((width, inner), bf16),
            ],
            compiler_params=params(),
            name="project_rotate",
        cost_estimate=cost(11),
        )(
            exchange.held, tokens_2d, far_tokens, cosine, sine, gains, head_gains,
            *pack,
        )
    )
    if exchange.direct:
        own, two, one = ffn_pack, exchange.second(ffn_pack), exchange.first(ffn_pack)
        own_swapped = exchange.swap_cores(own)
        two, keys = lax.optimization_barrier((two, keys))
        both, two_swapped = exchange.first(two), exchange.swap_cores(two)
    context, log_total, attn_branch, residual, ffn_in = pl.pallas_call(
        attn_kernel,
        grid=(seq_dev,),
        in_specs=[rows(block, inner), key_spec, key_spec, rows(block, 1), tok_spec]
        + [wot_spec, gains_spec],
        out_specs=[rows(block, inner), rows(block, 128), tok_spec, tok_spec, tok_spec],
        out_shape=[
            shaped((count, inner), bf16),
            shaped((count, 128), f32),
            shaped((count, width), f32),
            shaped((count, width), f32),
            shaped((count, width), bf16),
        ],
        compiler_params=params(),
        name="window_attention",
        cost_estimate=cost(12),
    )(query_rot, keys, values, pos_column, tokens_2d, full_ot, gains)

    if exchange.direct:
        one, both, ffn_in = lax.optimization_barrier((one, both, ffn_in))
        ffn_pack = [own, two, one, both, own_swapped, two_swapped]
        ffn_pack += [exchange.swap_cores(one), exchange.swap_cores(both)]

    half = pieces // 2
    tiles = count // FFN_ROWS

    def small(wide):
        return pl.BlockSpec((FFN_ROWS, wide), lambda i: (jnp.minimum(i, tiles - 1), 0))

    def once(shape):
        return pl.BlockSpec(
            shape, lambda *_: (0,) * len(shape), pipeline_mode=pl.Buffered(buffer_count=1)
        )

    gate_shape = (half, quarters, 2 * quarter, FF_TILE)
    down_shape = (half, quarters, 3 * strip, FF_TILE)

    def gate_spec(first):
        return pl.BlockSpec(
            (1,) + gate_shape[1:],
            lambda i: (jnp.clip(i - tiles - first, 0, half - 1), 0, 0, 0),
        )

    down_spec = pl.BlockSpec(
        (half, 1) + down_shape[2:], lambda i: (0, jnp.clip(i - tiles, 0, pieces - 1) // 2, 0, 0)
    )
    turned = pltpu.VMEM((width, count), bf16)
    weight = pltpu.VMEM((width, hidden_dim), bf16)
    middle = pltpu.VMEM((count, hidden_dim), bf16)
    gelu_parts = pltpu.VMEM((FFN_ROWS, hidden_dim), f32)
    layer_out, g_res, g_ctx, ffn_gains, *ffn_parts = pl.pallas_call(
        ffn_kernel,
        grid=(tiles + pieces,),
        in_specs=[smem, smem, small(width), small(width), small(width), small(width)]
        + [once((count, inner)), once((width, inner)), gains_spec]
        + [remain] * pieces,
        out_specs=[small(width), small(width), small(inner), whole((8, width))]
        + [gate_spec(0), gate_spec(half), down_spec, down_spec],
        out_shape=[
            shaped((count, width), bf16),
            shaped((count, width), f32),
            shaped((count, inner), bf16),
            shaped((8, width), f32),
            shaped(gate_shape, bf16),
            shaped(gate_shape, bf16),
            shaped(down_shape, bf16),
            shaped(down_shape, bf16),
        ],
        scratch_shapes=[gelu_parts, gelu_parts, weight, weight, weight]
        + [pltpu.VMEM((2,) + ffn_pack[0].shape, bf16), pltpu.SemaphoreType.DMA((2,))]
        + [middle, middle, middle, turned, turned, turned]
        + [pltpu.VMEM((width, FFN_ROWS), bf16)],
        compiler_params=params(62),
        name="feed_forward",
        cost_estimate=cost(60),
    )(
        exchange.held, exchange.order, residual, ffn_in, cot_2d, attn_branch, context, full_ot,
        gains, *ffn_pack,
    )
    gate_sent, gate_kept, down_sent, down_kept = ffn_parts
    gate, down = (gate_sent, gate_kept), (down_sent, down_kept)
    if exchange.direct:
        gate_got, down_got = swapped(gate_sent, "seq", 1, 1), swapped(down_sent, "seq", 1, 1)

    kv_spec = pl.BlockSpec((1, block, 2 * head_dim), lambda i: (i, 0, 0))
    g_query, g_far, g_near, query_gain = pl.pallas_call(
        attn_back_kernel,
        grid=(seq_dev,),
        in_specs=[rows(block, inner), rows(block, inner), key_spec, key_spec]
        + [rows(block, 1), rows(block, 128), rows(block, inner), table_spec, table_spec, head_spec],
        out_specs=[rows(block, inner), kv_spec, kv_spec, whole((8, head_dim))],
        out_shape=[
            shaped((count, inner), bf16),
            shaped((seq_dev, block, 2 * head_dim), bf16),
            shaped((seq_dev, block, 2 * head_dim), f32),
            shaped((8, head_dim), f32),
        ],
        scratch_shapes=[
            pltpu.VMEM((2 * block, head_dim), f32),
            pltpu.VMEM((2 * block, head_dim), f32),
        ],
        compiler_params=params(),
        name="attention_gradient",
        cost_estimate=cost(16),
    )(
        query_rot, g_ctx, keys, values, pos_column, log_total, query_raw, cosine, sine,
        head_gains,
    )
    g_recv = passed_along(g_far, "seq", -1)
    if exchange.direct:
        gate_got, down_got, g_query = lax.optimization_barrier((gate_got, down_got, g_query))
        gate = exchange.fold_got(gate_kept, gate_got)
        down = exchange.fold_got(down_kept, down_got)
    g_kv, key_gain = pl.pallas_call(
        kv_back_kernel,
        grid=(seq_dev,),
        in_specs=[remain, kv_spec, kv_spec, rows(block, head_dim), half_spec, half_spec, head_spec],
        out_specs=[rows(block, 2 * head_dim), whole((8, head_dim))],
        out_shape=[shaped((count, 2 * head_dim), bf16), shaped((8, head_dim), f32)],
        compiler_params=params(),
        name="key_value_back",
        cost_estimate=cost(4),
    )(gate[0], g_near, g_recv, key_raw, own_cosine, own_sine, head_gains)

    each = head_dim // pieces
    column = jnp.arange(2 * head_dim, dtype=jnp.int32)
    inside = column % (2 * each)
    source = jnp.where(inside < each, inside, inside - each + head_dim)
    source = source + each * jnp.repeat(exchange.order[:pieces], 2 * each)
    sort = (column[:, None] == source[None, :]).astype(bf16)

    def attn_parts(base, before, extra):
        shape = (half, quarters, quarter, 128 + 2 * each)
        sent = (half // 2,) + shape[1:]
        outs = [shape] if base == 0 else [sent, sent]
        vmem = pl.BlockSpec(memory_space=pltpu.VMEM)
        chosen = sort[:, base * 2 * each : (base + half) * 2 * each]
        return pl.pallas_call(
            lambda *refs: attn_grad_kernel(base, *refs),
            in_specs=[smem, remain] + [vmem] * (4 + len(extra)),
            out_specs=[vmem] * len(outs),
            out_shape=[shaped(o, bf16) for o in outs],
            scratch_shapes=[pltpu.VMEM((2, width, count), bf16)],
            compiler_params=params(),
            cost_estimate=cost(6),
            name="attn_gradients_kept" if base else "attn_gradients_sent",
        )(exchange.order, before, attn_low, g_query, g_kv, chosen, *extra)

    (attn_sent,) = attn_parts(0, exchange.order, [])
    attn_got = exchange.swap_cores(attn_sent) if exchange.direct else jnp.zeros_like(attn_sent)
    if exchange.direct:
        gate = exchange.fold(*gate, 0)
        down, gate = lax.optimization_barrier((down, gate))
    attn_parts_kept = attn_parts(half, gate[0], [attn_got])
    if exchange.direct:
        gate = exchange.fold(*gate, 1)
        down = exchange.fold(*down, 0)
    dtokens, attn_gain = pl.pallas_call(
        input_kernel,
        grid=(seq_dev,),
        in_specs=[remain, remain, rows(block, inner), rows(block, 2 * head_dim)]
        + [wq_spec, wkv_spec]
        + [tok_spec, tok_spec, gains_spec],
        out_specs=[tok_spec, whole((8, width))],
        out_shape=[shaped((count, width), bf16), shaped((8, width), f32)],
        compiler_params=params(),
        name="input_gradient",
        cost_estimate=cost(7),
    )(attn_parts_kept[0], down[0], g_query, g_kv, full_q, full_kv, tokens_2d, g_res, gains)

    sums = jnp.concatenate(
        [attn_gain[0], ffn_gains[2], ffn_gains[1], ffn_gains[0], query_gain[0], key_gain[0]]
    )
    if exchange.direct:
        attn = attn_parts_kept
        hops = (("seq", 1), ("seq", 2), ("seq", 4), ("fsdp", 1), ("fsdp", 2))
        for step in range(4):
            gate = exchange.fold(*gate, step + 2) if step < 2 else gate
            down = exchange.fold(*down, step + 1) if step < 3 else down
            attn = exchange.fold(*attn, step)
            sums = exchange.hop(sums, *hops[step])
            gate, down, attn, sums = lax.optimization_barrier((gate, down, attn, sums))
        sums = exchange.hop(sums, *hops[4])
        weights = split_gradients(gate, down, attn)
    else:
        weights = plain_gradients(
            jnp.concatenate(gate, axis=0),
            jnp.concatenate(down, axis=0),
            jnp.concatenate([attn_sent, *attn_parts_kept], axis=0),
        )
        sums = lax.psum(sums, ("seq", "fsdp"))
    cuts = [0, width, 2 * width, 3 * width, 4 * width, 4 * width + head_dim]
    cuts.append(cuts[-1] + head_dim)
    gain_sums = tuple(sums[a:b] for a, b in zip(cuts[:-1], cuts[1:]))
    shape = (seq_dev, block, width)
    return (layer_out.reshape(shape), dtokens.reshape(shape)) + weights + gain_sums


def solution(mesh):
    sharded = P("fsdp", "seq", None)
    weight = P("fsdp", None)
    in_specs = (sharded, P("fsdp", "seq")) + (weight,) * 7 + (P(),) * 6 + (sharded,)
    out_specs = (sharded, sharded) + (P("fsdp", "seq"),) * 7 + (P(),) * 6
    return jax.shard_map(body, mesh=mesh, in_specs=in_specs, out_specs=out_specs, check_vma=False)
```

```python
import jax
import jax.numpy as jnp
import numpy as np
from jax import lax
from jax.experimental import pallas as pl
from jax.experimental.pallas import tpu as pltpu
from jax.sharding import PartitionSpec as P

WINDOW = 512
TILE = 128
FF_TILE = 256
FFN_ROWS = 256

epsilon = 1e-06
NEG_FILL = -1e30
ROPE_BASE = 10000.0
GELU_C = 0.7978845608028654
GELU_K = 0.044715

f32 = jnp.float32
bf16 = jnp.bfloat16

NN = (((1,), (0,)), ((), ()))
NT = (((1,), (1,)), ((), ()))
TN = (((0,), (0,)), ((), ()))


def mm(left, right, dims=NN):
    return lax.dot_general(left, right, dims, preferred_element_type=f32)


def inv_rms(vector):
    return lax.rsqrt(jnp.mean(vector * vector, axis=-1, keepdims=True) + epsilon)


def norm_back(vector, inv, gain, grad):
    unit = vector * inv
    scaled = gain * grad
    back = inv * (scaled - unit * jnp.mean(unit * scaled, axis=-1, keepdims=True))
    return back, grad * unit


def rope(vector, cosine, sine):
    half = vector.shape[-1] // 2
    one, two = vector[:, :half], vector[:, half:]
    return jnp.concatenate([one * cosine - two * sine, two * cosine + one * sine], axis=1)


def rope_back(vector, cosine, sine):
    half = vector.shape[-1] // 2
    one, two = vector[:, :half], vector[:, half:]
    return jnp.concatenate([one * cosine + two * sine, two * cosine - one * sine], axis=1)


def params(limit_mib=58):
    return pltpu.CompilerParams(vmem_limit_bytes=limit_mib * 1024 * 1024)


def cost(microseconds):
    return pl.CostEstimate(
        flops=int(microseconds * 1e9), bytes_accessed=int(microseconds * 3e6), transcendentals=0
    )


def whole(shape):
    return pl.BlockSpec(shape, lambda *_: (0,) * len(shape))


def rows(count, width):
    return pl.BlockSpec((count, width), lambda i: (i, 0))


def shaped(shape, dtype):
    return jax.ShapeDtypeStruct(shape, dtype)


def qkv_kernel(
    held_ref, tok_ref, far_ref, cos_ref, sin_ref, gains_ref, head_ref, *refs
):
    packs = refs[:-9]
    attn_ref, qraw_ref, qrot_ref, kraw_ref, key_ref, val_ref, wq_ref, wkv_ref, wot_ref = refs[-9:]
    head_dim = head_ref.shape[1]
    head_count = wq_ref.shape[1] // head_dim
    block, width = tok_ref.shape
    chunks, chunk_rows, _ = packs[0].shape
    pieces = len(packs)
    half = pieces // 2

    @pl.when(pl.program_id(0) == 0)
    def _():
        strip = chunk_rows // 2
        odd = held_ref[0] % 2 == 1

        def aligned(index, size):
            return pl.ds(pl.multiple_of(index * size, size), size)

        for c in range(chunks):
            z = held_ref[pieces + c]
            own = aligned(z, chunk_rows)
            for m in range(pieces):
                s = held_ref[m]
                wq_ref[own, aligned(s, 128)] = packs[m][c, :, :128]
                turned = packs[m][c, :, 128:256]
                for i in range(2):
                    wot_ref[aligned(s, strip), aligned(2 * z + i, 128)] = turned[
                        i * strip : (i + 1) * strip
                    ]
            for m, mate in zip(range(half), (0, 2, 1, 3)):
                one, two = packs[m][c, :, 256:320], packs[half + mate][c, :, 256:320]
                wkv_ref[own, aligned(held_ref[m] // 2, 128)] = jnp.concatenate(
                    [jnp.where(odd, two, one), jnp.where(odd, one, two)], axis=1
                )

    pre = gains_ref[0:1, :]
    qgain, kgain = head_ref[0:1, :], head_ref[1:2, :]
    token = tok_ref[...].astype(f32)
    low = (token * inv_rms(token) * pre).astype(bf16)
    attn_ref[...] = low
    query = mm(low, wq_ref[...])
    qraw_ref[...] = query
    cosine, sine = cos_ref[block:, :], sin_ref[block:, :]
    scaling = head_dim ** (-0.5)
    for h in range(head_count):
        part = query[:, h * head_dim : (h + 1) * head_dim]
        normed = part * inv_rms(part) * qgain
        qrot_ref[:, h * head_dim : (h + 1) * head_dim] = (
            rope(normed, cosine, sine).astype(bf16) * jnp.asarray(scaling, bf16)
        )
    both = mm(low, wkv_ref[...])
    key = both[:, :head_dim]
    kraw_ref[...] = key
    key_ref[0, block:, :] = rope(key * inv_rms(key) * kgain, cosine, sine).astype(bf16)
    val_ref[0, block:, :] = both[:, head_dim:].astype(bf16)
    token = far_ref[...].astype(f32)
    low = (token * inv_rms(token) * pre).astype(bf16)
    both = mm(low, wkv_ref[...])
    key = both[:, :head_dim]
    key_ref[0, :block, :] = rope(
        key * inv_rms(key) * kgain, cos_ref[:block, :], sin_ref[:block, :]
    ).astype(bf16)
    val_ref[0, :block, :] = both[:, head_dim:].astype(bf16)


def stacked(ref, tile, head_count, head_dim):
    return jnp.concatenate(
        [
            ref[tile * TILE : (tile + 1) * TILE, h * head_dim : (h + 1) * head_dim]
            for h in range(head_count)
        ],
        axis=0,
    )


def mask_of(pos_ref, tile, span):
    reach = pos_ref[tile * TILE : (tile + 1) * TILE, :]
    row = lax.broadcasted_iota(jnp.int32, (TILE, span), 0)
    col = lax.broadcasted_iota(jnp.int32, (TILE, span), 1)
    distance = WINDOW + row - col
    return jnp.where((distance >= 0) & (distance <= reach), 0.0, NEG_FILL)


def attn_kernel(
    q_ref, key_ref, val_ref, pos_ref, tok_ref, wot_ref, gains_ref,
    ctx_ref, lse_ref, branch_ref, res_ref, fin_ref,
):
    head_dim = key_ref.shape[2]
    head_count = q_ref.shape[1] // head_dim
    span = WINDOW + TILE
    lane = lax.broadcasted_iota(jnp.int32, (TILE, 128), 1)
    for tile in range(q_ref.shape[0] // TILE):
        query = stacked(q_ref, tile, head_count, head_dim)
        key = key_ref[0, tile * TILE : tile * TILE + span, :]
        value = val_ref[0, tile * TILE : tile * TILE + span, :]
        score = mm(query, key, NT).reshape(head_count, TILE, span) + mask_of(pos_ref, tile, span)
        largest = jnp.max(score, axis=-1, keepdims=True)
        expo = jnp.exp(score - largest)
        total = jnp.sum(expo, axis=-1, keepdims=True)
        low = expo.astype(bf16).reshape(head_count * TILE, span)
        context = mm(low, value).reshape(head_count, TILE, head_dim) / total
        log_total = largest + jnp.log(total)
        kept = jnp.zeros((TILE, 128), f32)
        for h in range(head_count):
            ctx_ref[tile * TILE : (tile + 1) * TILE, h * head_dim : (h + 1) * head_dim] = context[
                h
            ].astype(bf16)
            kept = jnp.where(lane == h, log_total[h], kept)
        lse_ref[tile * TILE : (tile + 1) * TILE, :] = kept
    branch = mm(ctx_ref[...], wot_ref[...], NT)
    branch_ref[...] = branch
    residual = tok_ref[...].astype(f32) + branch * inv_rms(branch) * gains_ref[1:2, :]
    res_ref[...] = residual
    fin_ref[...] = (residual * inv_rms(residual) * gains_ref[2:3, :]).astype(bf16)


def ffn_kernel(
    held_ref, order_ref, res_ref, fin_ref, cot_ref, branch_ref, ctx_ref, wot_ref, gains_ref, *refs
):
    pieces = order_ref.shape[0] - refs[0].shape[0]
    packs, refs = refs[:pieces], refs[pieces:]
    out_ref, gres_ref, gctx_ref, gain_ref = refs[:4]
    gate_sent, gate_kept, down_sent, down_kept = refs[4:8]
    slope_ref, act_ref, gate_ref, up_ref, down_ref, stage_ref, copied = refs[8:15]
    hid_ref, gg_ref, gu_ref, in_left, ffn_left, attn_left, turn_ref = refs[15:]
    chunks, _, tile = packs[0].shape
    width = res_ref.shape[1]
    count = hid_ref.shape[0]
    quarter, strip, half = width // chunks, width // pieces, pieces // 2
    step = pl.program_id(0)
    tiles = count // FFN_ROWS
    post_attn, pre_ffn, post_ffn = [gains_ref[i : i + 1, :] for i in (1, 2, 3)]

    def aligned(index, size):
        return pl.ds(pl.multiple_of(index * size, size), size)

    @pl.when(step == 0)
    def _():
        gain_ref[...] = jnp.zeros_like(gain_ref)

        def staged(m):
            return pltpu.make_async_copy(packs[m], stage_ref.at[m % 2], copied.at[m % 2])

        staged(0).start()
        for m in range(pieces):
            if m + 1 < pieces:
                staged(m + 1).start()
            staged(m).wait()
            s = held_ref[m]
            for c in range(chunks):
                z = held_ref[pieces + c]
                own, cols = aligned(z, quarter), aligned(s, tile)
                gate_ref[own, cols] = stage_ref[m % 2, c, :quarter, :]
                up_ref[own, cols] = stage_ref[m % 2, c, quarter : 2 * quarter, :]
                for i in range(2):
                    begin = 2 * quarter + i * strip
                    down_ref[aligned(s, strip), aligned(2 * z + i, tile)] = stage_ref[
                        m % 2, c, begin : begin + strip, :
                    ]

    @pl.when(step < tiles)
    def _():
        own = aligned(step, FFN_ROWS)

        def turn(left_ref, source, size, first, number):
            turn_ref[...] = source.T
            for m in range(number):
                left_ref[m * size : (m + 1) * size, own] = turn_ref[
                    aligned(order_ref[first + m], size), :
                ]

        ffn_in = fin_ref[...]
        turn(in_left, ffn_in, quarter, pieces, chunks)
        gate = mm(ffn_in, gate_ref[...])
        up = mm(ffn_in, up_ref[...])
        square = gate * gate
        bent = jnp.tanh(GELU_C * gate * (1.0 + GELU_K * square))
        half_bent = 0.5 * (1.0 + bent)
        act = gate * half_bent
        slope = half_bent + 0.5 * gate * (1.0 - bent * bent) * (
            GELU_C * (1.0 + 3.0 * GELU_K * square)
        )
        act_ref[...] = act
        slope_ref[...] = slope * up
        hidden = (act * up).astype(bf16)
        hid_ref[own, :] = hidden
        branch = mm(hidden, down_ref[...], NT)
        residual = res_ref[...]
        cot = cot_ref[...].astype(f32)
        inv = inv_rms(branch)
        out_ref[...] = (residual + branch * inv * post_ffn).astype(bf16)
        g_ffn, gain_post = norm_back(branch, inv, post_ffn, cot)
        g_low = g_ffn.astype(bf16)
        turn(ffn_left, g_low, strip, 0, pieces)
        g_hidden = mm(g_low, down_ref[...])
        g_gate = (g_hidden * slope_ref[...]).astype(bf16)
        g_up = (g_hidden * act_ref[...]).astype(bf16)
        gg_ref[own, :] = g_gate
        gu_ref[own, :] = g_up
        g_in = mm(g_gate, gate_ref[...], NT) + mm(g_up, up_ref[...], NT)
        back, gain_pre = norm_back(residual, inv_rms(residual), pre_ffn, g_in)
        g_res = cot + back
        gres_ref[...] = g_res
        attn_branch = branch_ref[...]
        g_attn, gain_attn = norm_back(attn_branch, inv_rms(attn_branch), post_attn, g_res)
        g_attn = g_attn.astype(bf16)
        turn(attn_left, g_attn, strip, 0, pieces)
        gctx_ref[...] = mm(g_attn, wot_ref[...]).astype(bf16)
        gain_ref[0:1, :] += jnp.sum(gain_post, axis=0, keepdims=True)
        gain_ref[1:2, :] += jnp.sum(gain_pre, axis=0, keepdims=True)
        gain_ref[2:3, :] += jnp.sum(gain_attn, axis=0, keepdims=True)

    @pl.when(step >= tiles)
    def _():
        k = step - tiles
        cols = aligned(order_ref[k], tile)
        z = order_ref[pieces + k // 2]
        both = mm(in_left[...], jnp.concatenate([gg_ref[:, cols], gu_ref[:, cols]], axis=1))
        both = both.astype(bf16)
        for i in range(2):
            part = both[:, i * tile : (i + 1) * tile].reshape(chunks, quarter, tile)
            for inside, out in ((k < half, gate_sent), (k >= half, gate_kept)):

                @pl.when(inside)
                def _(out=out, part=part, i=i):
                    out[0, :, i * quarter : (i + 1) * quarter, :] = part

        def put(begin, part):
            part = part.astype(bf16).reshape(pieces, strip, tile)
            down_sent[:, 0, pl.ds(begin, strip), :] = part[:half]
            down_kept[:, 0, pl.ds(begin, strip), :] = part[half:]

        put(
            pl.multiple_of(k % 2 * strip, strip),
            mm(ffn_left[...], hid_ref[:, aligned(2 * z + k % 2, tile)]),
        )

        @pl.when(k % 2 == 0)
        def _():
            put(2 * strip, mm(attn_left[...], ctx_ref[:, aligned(z, tile)]))


def turn_strips(left_ref, source, strip, where, count):
    left_ref[1] = source.T
    for m in range(count):
        begin = pl.multiple_of(where(m) * strip, 16)
        left_ref[0, m * strip : (m + 1) * strip, :] = left_ref[1, pl.ds(begin, strip), :]


def attn_grad_kernel(base, order_ref, _, attn_ref, gq_ref, gkv_ref, sort_ref, *refs):
    recv_ref = refs[0] if base else None
    outs = refs[1:3] if base else refs[:1]
    left = refs[-1]
    held, chunks, quarter, _ = outs[0].shape
    width = attn_ref.shape[1]
    pieces = order_ref.shape[0] - chunks
    half = pieces // 2
    turn_strips(left, attn_ref[...], quarter, lambda m: order_ref[pieces + m], chunks)
    sorted_kv = mm(gkv_ref[...], sort_ref[...]).astype(bf16)
    part_kv = mm(left[0], sorted_kv)
    wide = part_kv.shape[1] // half
    for pair in range(0, half, 2):
        both = jnp.concatenate(
            [
                gq_ref[:, pl.ds(pl.multiple_of(order_ref[base + pair + i] * 128, 128), 128)]
                for i in range(2)
            ],
            axis=1,
        )
        part = mm(left[0], both)
        for i in range(2):
            m = pair + i
            value = part[:, i * 128 : (i + 1) * 128].reshape(chunks, quarter, 128)
            value_kv = part_kv[:, m * wide : (m + 1) * wide].reshape(chunks, quarter, wide)
            if base:
                value = value + recv_ref[m, :, :, :128].astype(f32)
                value_kv = value_kv + recv_ref[m, :, :, 128:].astype(f32)
            out = outs[m // held]
            out[m % held, :, :, :128] = value.astype(bf16)
            out[m % held, :, :, 128:] = value_kv.astype(bf16)


def attn_back_kernel(
    q_ref, gctx_ref, key_ref, val_ref, pos_ref, lse_ref, qraw_ref, cos_ref, sin_ref, head_ref,
    *refs,
):
    gq_ref, far_ref, near_ref, gain_ref, gkey_ref, gval_ref = refs[-6:]
    head_dim = key_ref.shape[2]
    head_count = q_ref.shape[1] // head_dim
    block = q_ref.shape[0]
    span = WINDOW + TILE
    scaling = head_dim ** (-0.5)

    @pl.when(pl.program_id(0) == 0)
    def _():
        gain_ref[...] = jnp.zeros_like(gain_ref)

    gkey_ref[...] = jnp.zeros_like(gkey_ref)
    gval_ref[...] = jnp.zeros_like(gval_ref)
    gain = jnp.zeros((1, head_dim), f32)
    for tile in range(block // TILE):
        own = slice(tile * TILE, (tile + 1) * TILE)
        reach = slice(tile * TILE, tile * TILE + span)
        query = stacked(q_ref, tile, head_count, head_dim)
        g_ctx = stacked(gctx_ref, tile, head_count, head_dim)
        key = key_ref[0, reach, :]
        value = val_ref[0, reach, :]
        log_total = jnp.stack([lse_ref[own, h : h + 1] for h in range(head_count)])
        score = mm(query, key, NT).reshape(head_count, TILE, span) + mask_of(pos_ref, tile, span)
        probs = jnp.exp(score - log_total)
        g_probs = mm(g_ctx, value, NT).reshape(head_count, TILE, span)
        spread = jnp.sum(g_probs * probs, axis=-1, keepdims=True)
        g_score = (probs * (g_probs - spread)).astype(bf16).reshape(head_count * TILE, span)
        low = probs.astype(bf16).reshape(head_count * TILE, span)
        gkey_ref[reach, :] += mm(g_score, query, TN)
        gval_ref[reach, :] += mm(low, g_ctx, TN)
        g_rot = mm(g_score, key) * scaling
        turned = slice(block + tile * TILE, block + (tile + 1) * TILE)
        cosine, sine = cos_ref[turned, :], sin_ref[turned, :]
        for h in range(head_count):
            cols = slice(h * head_dim, (h + 1) * head_dim)
            raw = qraw_ref[own, cols]
            back, share = norm_back(
                raw,
                inv_rms(raw),
                head_ref[0:1, :],
                rope_back(g_rot[h * TILE : (h + 1) * TILE], cosine, sine),
            )
            gq_ref[own, cols] = back.astype(bf16)
            gain += jnp.sum(share, axis=0, keepdims=True)
    gain_ref[0:1, :] += gain
    far_ref[0, :, :head_dim] = rope_back(
        gkey_ref[:block, :], cos_ref[:block, :], sin_ref[:block, :]
    ).astype(bf16)
    far_ref[0, :, head_dim:] = gval_ref[:block, :].astype(bf16)
    near_ref[0, :, :head_dim] = gkey_ref[block:, :]
    near_ref[0, :, head_dim:] = gval_ref[block:, :]


def kv_back_kernel(
    kraw_ref, cos_ref, sin_ref, head_ref, *refs
):
    gkv_ref, kgain_ref = refs[-2:]
    sequences = (len(refs) - 2) // 2
    head_dim = head_ref.shape[1]

    @pl.when(pl.program_id(0) == 0)
    def _():
        kgain_ref[...] = jnp.zeros_like(kgain_ref)

    near, far = refs[0][0], refs[sequences][0]
    for index in range(1, sequences):
        mine = pl.program_id(0) == index
        near = jnp.where(mine, refs[index][0], near)
        far = jnp.where(mine, refs[sequences + index][0], far)
    far = far.astype(f32)
    raw = kraw_ref[...]
    g_normed = rope_back(near[:, :head_dim], cos_ref[...], sin_ref[...]) + far[:, :head_dim]
    g_key, share = norm_back(raw, inv_rms(raw), head_ref[1:2, :], g_normed)
    kgain_ref[0:1, :] += jnp.sum(share, axis=0, keepdims=True)
    gkv_ref[:, :head_dim] = g_key.astype(bf16)
    gkv_ref[:, head_dim:] = (near[:, head_dim:] + far[:, head_dim:]).astype(bf16)


def input_kernel(
    _, gq_ref, gkv_ref, wq_ref, wkv_ref, tok_ref, gres_ref, gains_ref, ffn_gain_ref, kgain_ref,
    *refs
):
    dtok_ref, gain_ref = refs[-2:]
    @pl.when(pl.program_id(0) == 0)
    def _():
        gain_ref[...] = jnp.zeros_like(gain_ref)
        head_dim = kgain_ref.shape[1]
        gain_ref[1:4, :] = ffn_gain_ref[0:3, :]
        gain_ref[4:5, :head_dim] = sum(ref[0:1, :] for ref in refs[:-2])
        gain_ref[4:5, head_dim : 2 * head_dim] = kgain_ref[0:1, :]

    g_in = mm(gq_ref[...], wq_ref[...], NT) + mm(gkv_ref[...], wkv_ref[...], NT)
    token = tok_ref[...].astype(f32)
    back, share = norm_back(token, inv_rms(token), gains_ref[0:1, :], g_in)
    dtok_ref[...] = (gres_ref[...] + back).astype(bf16)
    gain_ref[0:1, :] += jnp.sum(share, axis=0, keepdims=True)


def passed_along(shard, axis, by):
    length = lax.axis_size(axis)
    pairs = [(i, i + by) for i in range(length) if 0 <= i + by < length]
    return lax.ppermute(shard, axis, pairs)


def swapped(array, axis, even, odd):
    length = lax.axis_size(axis)
    return lax.ppermute(array, axis, [(i, i ^ (odd if i % 2 else even)) for i in range(length)])


def tables(block, head_dim):
    half_width = head_dim // 2
    frequency = ROPE_BASE ** (-(np.arange(half_width) * 2.0) / head_dim)
    angles = np.arange(-block, block)[:, None] * frequency
    return np.cos(angles).astype(np.float32), np.sin(angles).astype(np.float32)


def column_piece(array, axis_name, parts):
    wide = array.shape[1] // parts
    return lax.dynamic_slice_in_dim(array, lax.axis_index(axis_name) * wide, wide, 1)


def halves(array):
    half = array.shape[0] // 2
    return (array[:half], array[half:]) if half > 1 else (array[0], array[1])


def total(terms):
    result = terms[0].astype(f32)
    for term in terms[1:]:
        result = result + term.astype(f32)
    return result


HELD = [0, 4, 2, 6, 1, 3, 5, 7]
HELD_Z = [0, 2, 1, 3]


def linked(*chains):
    arrays, steps = [], []
    for chain in chains:
        send, keep = chain if isinstance(chain, tuple) else (chain, [])
        arrays.append([send] + [array for array, _ in keep])
        steps.append([begin for _, begin in keep])
    arrays = lax.optimization_barrier(arrays)
    result = []
    for chain, (send, *keep), begins in zip(chains, arrays, steps):
        result.append((send, list(zip(keep, begins))) if isinstance(chain, tuple) else send)
    return result


class Exchange:
    def __init__(self, seqs, chunks):
        self.direct = seqs == 8 and chunks == 4
        if not self.direct:
            self.order = jnp.arange(12, dtype=jnp.int32) % 8
            self.held = jnp.array(HELD + HELD_Z, jnp.int32)
            return
        s, z = lax.axis_index("seq"), lax.axis_index("fsdp")
        odd = s % 2 == 1
        one, two = jnp.where(odd, 4, 2), jnp.where(odd, 2, 4)
        zero = jnp.zeros_like(s)
        sent = [one | two | 1, two | 1, one | 1, zero | 1]
        kept = [one | two, one, two, zero]
        order = [s ^ k for k in sent + kept] + [z ^ k for k in (3, 1, 2, 0)]
        self.order = jnp.stack(order).astype(jnp.int32)
        held = [zero, two, one, one | two, zero | 1, one | 1, two | 1, one | two | 1]
        held = [s ^ k for k in held] + [z ^ k for k in HELD_Z]
        self.held = jnp.stack(held).astype(jnp.int32)

    def along_step(self, held, bits):
        return jnp.concatenate([held, swapped(held, "fsdp", bits, bits)], axis=0)

    def second(self, piece):
        return swapped(piece, "seq", 4, 2)

    def first(self, piece):
        return swapped(piece, "seq", 2, 4)

    def swap_cores(self, parts):
        return swapped(parts, "seq", 1, 1)

    def fold(self, send, keep, step):
        if step < 3:
            got = swapped(send, "seq", *((1, 1), (2, 4), (4, 2))[step])
        else:
            got = swapped(send, "fsdp", step - 2, step - 2)
        return self.split(keep + [(got, step)], step)

    def split(self, terms, step):
        rest = []
        for array, begin in terms:
            for done in range(begin, step):
                array = halves(array)[1]
            rest.append(array)
        if step == 4:
            return total(rest)
        return total([halves(array)[0] for array in rest]).astype(bf16), terms

    def hop(self, value, axis, bits):
        return value + swapped(value, axis, bits, bits)


def scattered_plain(part):
    columns = lax.psum_scatter(part, "seq", scatter_dimension=1, tiled=True)
    return lax.psum_scatter(columns, "fsdp", scatter_dimension=0, tiled=True).astype(f32)


def gather_weights(w_query, w_key, w_value, w_out, w_gate, w_up, w_down, halo, exchange):
    pieces = w_gate.shape[1] // FF_TILE
    width = w_out.shape[1]
    if exchange.direct:
        down = column_piece(w_down, "seq", pieces).T
        ffn = jnp.concatenate(
            [
                column_piece(w_gate, "seq", pieces),
                column_piece(w_up, "seq", pieces),
                down[:, :FF_TILE],
                down[:, FF_TILE:],
            ],
            axis=0,
        )
        both = jnp.concatenate([w_key, w_value], axis=1)
        out = column_piece(w_out, "seq", pieces).T
        out = jnp.concatenate([out[:, :128], out[:, 128:]], axis=0)
        attn = jnp.concatenate(
            [column_piece(w_query, "seq", pieces), out, column_piece(both, "seq", pieces)], axis=1
        )
        attn = exchange.along_step(exchange.along_step(attn[None], 2), 1)
        ffn, attn = lax.optimization_barrier((ffn, attn))
        ffn = exchange.along_step(ffn[None], 2)
        attn, halo = lax.optimization_barrier((attn, halo))
        two, one = exchange.second(attn), exchange.first(attn)
        ffn, two = lax.optimization_barrier((ffn, two))
        ffn = exchange.along_step(ffn, 1)
        attn = [attn, two, one, exchange.first(two)]
        attn[3], ffn = lax.optimization_barrier((attn[3], ffn))
        return attn + [exchange.swap_cores(held) for held in attn], ffn, halo
    w_query, w_key, w_value, w_out, w_gate, w_up, w_down = [
        lax.all_gather(w, "fsdp", axis=0, tiled=True)
        for w in (w_query, w_key, w_value, w_out, w_gate, w_up, w_down)
    ]
    chunks = w_down.shape[0] // (2 * FF_TILE)
    quarter, strip = width // chunks, width // pieces

    def columns(weight):
        return weight.reshape(chunks, quarter, pieces, -1).transpose(2, 0, 1, 3)

    def turned(weight):
        shape = (pieces, strip, chunks, 2, weight.shape[0] // (2 * chunks))
        turned_part = weight.T.reshape(shape).transpose(0, 2, 3, 1, 4)
        return turned_part.reshape(pieces, chunks, 2 * strip, -1)

    both = jnp.concatenate([w_key, w_value], axis=1)
    attn = jnp.concatenate([columns(w_query), turned(w_out), columns(both)], axis=3)
    ffn = jnp.concatenate([columns(w_gate), columns(w_up), turned(w_down)], axis=2)
    def listed(pack):
        pack = jnp.take(jnp.take(pack, np.array(HELD), axis=0), np.array(HELD_Z), axis=1)
        return [pack[m] for m in range(pieces)]

    return listed(attn), listed(ffn), halo


def plain_gradients(part_gate, part_down, part_attn):
    pieces, quarters, double, _ = part_gate.shape
    width = quarters * double // 2
    strip = width // pieces

    def columns(parts):
        return parts.transpose(1, 2, 0, 3).reshape(width, -1)

    def turned(parts):
        parts = parts.reshape(pieces, quarters, -1, strip, FF_TILE).transpose(1, 2, 4, 0, 3)
        return parts.reshape(-1, width)

    each = part_attn.shape[3] - (part_attn.shape[3] - 128) // 2
    return tuple(
        scattered_plain(part)
        for part in (
            columns(part_attn[..., :128]),
            columns(part_attn[..., 128:each]),
            columns(part_attn[..., each:]),
            turned(part_down[:, :, 2 * strip :]),
            columns(part_gate[:, :, : double // 2]),
            columns(part_gate[:, :, double // 2 :]),
            turned(part_down[:, :, : 2 * strip]),
        )
    )


def split_gradients(gate, down, attn):
    quarter = attn.shape[0]
    strip = down.shape[0] // 3
    each = attn.shape[1] - (attn.shape[1] - 128) // 2
    return (
        attn[:, :128],
        attn[:, 128:each],
        attn[:, each:],
        down[2 * strip :].T,
        gate[:quarter],
        gate[quarter:],
        jnp.concatenate([down[:strip].T, down[strip : 2 * strip].T], axis=0),
    )


def body(
    tokens, doc_starts, w_query, w_key, w_value, w_out, w_gate, w_up, w_down,
    pre_attn, post_attn, pre_ffn, post_ffn, query_norm, key_norm, cotangent,
):
    seq_dev, block, width = tokens.shape
    head_dim = w_key.shape[1]
    inner = w_query.shape[1]
    hidden_dim = w_gate.shape[1]
    count = seq_dev * block
    seqs, chunks = lax.axis_size("seq"), lax.axis_size("fsdp")
    exchange = Exchange(seqs, chunks)
    far_tokens = passed_along(tokens, "seq", 1).reshape(count, width)
    far_starts = passed_along(doc_starts, "seq", 1)
    pack, ffn_pack, (far_tokens, far_starts) = gather_weights(
        w_query, w_key, w_value, w_out, w_gate, w_up, w_down, (far_tokens, far_starts), exchange
    )
    starts = jnp.concatenate([far_starts, doc_starts], axis=1)
    indices = jnp.arange(2 * block, dtype=jnp.int32)
    latest = lax.cummax(jnp.where(starts == 1, indices[None, :], -WINDOW), axis=1)
    reach = jnp.minimum(indices[None, :] - latest, WINDOW - 1)[:, block:]
    pos_column = reach.reshape(count, 1)
    cosine, sine = tables(block, head_dim)
    own_cosine, own_sine = cosine[block:], sine[block:]

    pieces, quarters = len(pack), pack[0].shape[0]
    quarter, strip = width // quarters, width // pieces
    gains = jnp.stack([pre_attn, post_attn, pre_ffn, post_ffn])
    head_gains = jnp.stack([query_norm, key_norm])
    tokens_2d = tokens.reshape(count, width)
    cot_2d = cotangent.reshape(count, width)

    tok_spec = rows(block, width)
    table_spec = whole((2 * block, head_dim // 2))
    half_spec = whole((block, head_dim // 2))
    key_spec = pl.BlockSpec((1, 2 * block, head_dim), lambda i: (i, 0, 0))
    gains_spec, head_spec = whole((4, width)), whole((2, head_dim))
    wq_spec, wkv_spec, wot_spec = (
        whole((width, inner)),
        whole((width, 2 * head_dim)),
        whole((width, inner)),
    )
    smem = pl.BlockSpec(memory_space=pltpu.SMEM)
    remain = pl.BlockSpec(memory_space=pl.ANY)
    attn_low, query_raw, query_rot, key_raw, keys, values, full_q, full_kv, full_ot = (
        pl.pallas_call(
            qkv_kernel,
            grid=(seq_dev,),
            in_specs=[smem, tok_spec, tok_spec, table_spec, table_spec]
            + [gains_spec, head_spec]
            + [whole(pack[0].shape)] * pieces,
            out_specs=[
                tok_spec,
                rows(block, inner),
                rows(block, inner),
                rows(block, head_dim),
                key_spec,
                key_spec,
                wq_spec,
                wkv_spec,
                wot_spec,
            ],
            out_shape=[
                shaped((count, width), bf16),
                shaped((count, inner), f32),
                shaped((count, inner), bf16),
                shaped((count, head_dim), f32),
                shaped((seq_dev, 2 * block, head_dim), bf16),
                shaped((seq_dev, 2 * block, head_dim), bf16),
                shaped((width, inner), bf16),
                shaped((width, 2 * head_dim), bf16),
                shaped((width, inner), bf16),
            ],
            compiler_params=params(),
            name="project_rotate",
        cost_estimate=cost(11),
        )(
            exchange.held, tokens_2d, far_tokens, cosine, sine, gains, head_gains,
            *pack,
        )
    )
    if exchange.direct:
        own, two, one = ffn_pack, exchange.second(ffn_pack), exchange.first(ffn_pack)
        own_swapped = exchange.swap_cores(own)
        two, keys = lax.optimization_barrier((two, keys))
        both, two_swapped = exchange.first(two), exchange.swap_cores(two)
    context, log_total, attn_branch, residual, ffn_in = pl.pallas_call(
        attn_kernel,
        grid=(seq_dev,),
        in_specs=[rows(block, inner), key_spec, key_spec, rows(block, 1), tok_spec]
        + [wot_spec, gains_spec],
        out_specs=[rows(block, inner), rows(block, 128), tok_spec, tok_spec, tok_spec],
        out_shape=[
            shaped((count, inner), bf16),
            shaped((count, 128), f32),
            shaped((count, width), f32),
            shaped((count, width), f32),
            shaped((count, width), bf16),
        ],
        compiler_params=params(),
        name="window_attention",
        cost_estimate=cost(12),
    )(query_rot, keys, values, pos_column, tokens_2d, full_ot, gains)

    if exchange.direct:
        one, both, ffn_in = lax.optimization_barrier((one, both, ffn_in))
        ffn_pack = [own, two, one, both, own_swapped, two_swapped]
        ffn_pack += [exchange.swap_cores(one), exchange.swap_cores(both)]

    half = pieces // 2
    tiles = count // FFN_ROWS

    def small(wide):
        return pl.BlockSpec((FFN_ROWS, wide), lambda i: (jnp.minimum(i, tiles - 1), 0))

    def once(shape):
        return pl.BlockSpec(
            shape, lambda *_: (0,) * len(shape), pipeline_mode=pl.Buffered(buffer_count=1)
        )

    gate_shape = (half, quarters, 2 * quarter, FF_TILE)
    down_shape = (half, quarters, 3 * strip, FF_TILE)

    def gate_spec(first):
        return pl.BlockSpec(
            (1,) + gate_shape[1:],
            lambda i: (jnp.clip(i - tiles - first, 0, half - 1), 0, 0, 0),
        )

    down_spec = pl.BlockSpec(
        (half, 1) + down_shape[2:], lambda i: (0, jnp.clip(i - tiles, 0, pieces - 1) // 2, 0, 0)
    )
    turned = pltpu.VMEM((width, count), bf16)
    weight = pltpu.VMEM((width, hidden_dim), bf16)
    middle = pltpu.VMEM((count, hidden_dim), bf16)
    gelu_parts = pltpu.VMEM((FFN_ROWS, hidden_dim), f32)
    layer_out, g_res, g_ctx, ffn_gains, *ffn_parts = pl.pallas_call(
        ffn_kernel,
        grid=(tiles + pieces,),
        in_specs=[smem, smem, small(width), small(width), small(width), small(width)]
        + [once((count, inner)), once((width, inner)), gains_spec]
        + [remain] * pieces,
        out_specs=[small(width), small(width), small(inner), whole((8, width))]
        + [gate_spec(0), gate_spec(half), down_spec, down_spec],
        out_shape=[
            shaped((count, width), bf16),
            shaped((count, width), f32),
            shaped((count, inner), bf16),
            shaped((8, width), f32),
            shaped(gate_shape, bf16),
            shaped(gate_shape, bf16),
            shaped(down_shape, bf16),
            shaped(down_shape, bf16),
        ],
        scratch_shapes=[gelu_parts, gelu_parts, weight, weight, weight]
        + [pltpu.VMEM((2,) + ffn_pack[0].shape, bf16), pltpu.SemaphoreType.DMA((2,))]
        + [middle, middle, middle, turned, turned, turned]
        + [pltpu.VMEM((width, FFN_ROWS), bf16)],
        compiler_params=params(62),
        name="feed_forward",
        cost_estimate=cost(60),
    )(
        exchange.held, exchange.order, residual, ffn_in, cot_2d, attn_branch, context, full_ot,
        gains, *ffn_pack,
    )
    gate_sent, gate_kept, down_sent, down_kept = ffn_parts
    gate, down = (gate_sent, gate_kept), (down_sent, down_kept)
    if exchange.direct:
        gate_got, down_got = swapped(gate_sent, "seq", 1, 1), swapped(down_sent, "seq", 1, 1)


    def attn_back(index, before):
        def at(count, wide):
            return pl.BlockSpec((count, wide), lambda *_: (index, 0))

        own_keys = pl.BlockSpec((1, 2 * block, head_dim), lambda *_: (index, 0, 0))
        pair = whole((1, block, 2 * head_dim))
        in_specs = [at(block, inner), at(block, inner), own_keys, own_keys, at(block, 1)]
        in_specs += [at(block, 128), at(block, inner), table_spec, table_spec, head_spec]
        return pl.pallas_call(
            attn_back_kernel,
            grid=(1,),
            in_specs=in_specs + [remain] * len(before),
            out_specs=[at(block, inner), pair, pair, whole((8, head_dim))],
            out_shape=[
                shaped((count, inner), bf16),
                shaped((1, block, 2 * head_dim), bf16),
                shaped((1, block, 2 * head_dim), f32),
                shaped((8, head_dim), f32),
            ],
            input_output_aliases={len(in_specs): 0} if before else {},
            scratch_shapes=[
                pltpu.VMEM((2 * block, head_dim), f32),
                pltpu.VMEM((2 * block, head_dim), f32),
            ],
            compiler_params=params(),
            name="attention_gradient",
            cost_estimate=cost(8),
        )(
            query_rot, g_ctx, keys, values, pos_column, log_total, query_raw, cosine, sine,
            head_gains, *before,
        )

    g_nears, g_recvs, query_gains, before = [], [], [], ()
    for index in range(seq_dev):
        g_query, g_far, g_near, part_gain = attn_back(index, before)
        query_gains.append(part_gain)
        g_nears.append(g_near)
        g_recvs.append(passed_along(g_far, "seq", -1))
        before = (g_query,)
        if index == 0 and exchange.direct:
            gate_got, down_got, g_query = lax.optimization_barrier((gate_got, down_got, g_query))
            gate = exchange.split([(gate_kept, 0), (gate_got, 0)], 0)
            down = exchange.split([(down_kept, 0), (down_got, 0)], 0)
            before = (g_query, gate[0], down[0])

    g_kv, key_gain = pl.pallas_call(
        kv_back_kernel,
        grid=(seq_dev,),
        in_specs=[rows(block, head_dim), half_spec, half_spec, head_spec]
        + [whole((1, block, 2 * head_dim))] * (2 * seq_dev),
        out_specs=[rows(block, 2 * head_dim), whole((8, head_dim))],
        out_shape=[shaped((count, 2 * head_dim), bf16), shaped((8, head_dim), f32)],
        compiler_params=params(),
        name="key_value_back",
        cost_estimate=cost(4),
    )(key_raw, own_cosine, own_sine, head_gains, *g_nears, *g_recvs)

    each = head_dim // pieces
    column = jnp.arange(2 * head_dim, dtype=jnp.int32)
    inside = column % (2 * each)
    source = jnp.where(inside < each, inside, inside - each + head_dim)
    source = source + each * jnp.repeat(exchange.order[:pieces], 2 * each)
    sort = (column[:, None] == source[None, :]).astype(bf16)

    def attn_parts(base, before, extra):
        shape = (half, quarters, quarter, 128 + 2 * each)
        sent = (half // 2,) + shape[1:]
        outs = [shape] if base == 0 else [sent, sent]
        vmem = pl.BlockSpec(memory_space=pltpu.VMEM)
        chosen = sort[:, base * 2 * each : (base + half) * 2 * each]
        return pl.pallas_call(
            lambda *refs: attn_grad_kernel(base, *refs),
            in_specs=[smem, remain] + [vmem] * (4 + len(extra)),
            out_specs=[vmem] * len(outs),
            out_shape=[shaped(o, bf16) for o in outs],
            scratch_shapes=[pltpu.VMEM((2, width, count), bf16)],
            compiler_params=params(),
            cost_estimate=cost(6),
            name="attn_gradients_kept" if base else "attn_gradients_sent",
        )(exchange.order, before, attn_low, g_query, g_kv, chosen, *extra)

    if exchange.direct:
        gate, down = exchange.fold(*gate, 1), exchange.fold(*down, 1)
        down, gate = linked(down, gate)
    (attn_sent,) = attn_parts(0, gate[0], [])
    attn_got = exchange.swap_cores(attn_sent) if exchange.direct else jnp.zeros_like(attn_sent)
    attn_parts_kept = attn_parts(half, gate[0], [attn_got])
    dtokens, sums = pl.pallas_call(
        input_kernel,
        grid=(seq_dev,),
        in_specs=[remain, rows(block, inner), rows(block, 2 * head_dim)]
        + [wq_spec, wkv_spec]
        + [tok_spec, tok_spec, gains_spec, whole((8, width))]
        + [whole((8, head_dim))] * (1 + seq_dev),
        out_specs=[tok_spec, whole((8, width))],
        out_shape=[shaped((count, width), bf16), shaped((8, width), f32)],
        compiler_params=params(),
        name="input_gradient",
        cost_estimate=cost(7),
    )(attn_parts_kept[0], g_query, g_kv, full_q, full_kv, tokens_2d, g_res, gains, ffn_gains, key_gain, *query_gains)

    if exchange.direct:
        attn = exchange.fold(attn_parts_kept[0], [(attn_parts_kept[1], 1)], 1)
        attn, sums = linked(attn, sums)
        hops = (("seq", 1), ("seq", 2), ("seq", 4), ("fsdp", 1), ("fsdp", 2))
        for step in range(2, 5):
            gate, down = exchange.fold(*gate, step), exchange.fold(*down, step)
            attn = exchange.fold(*attn, step - 1) if step > 2 else attn
            for hop in hops[2 * step - 4 : 2 * step - 2]:
                sums = exchange.hop(sums, *hop)
            gate, down, attn, sums = linked(gate, down, attn, sums)
        attn = exchange.fold(*attn, 4)
        weights = split_gradients(gate, down, attn)
    else:
        weights = plain_gradients(
            jnp.concatenate(gate, axis=0),
            jnp.concatenate(down, axis=0),
            jnp.concatenate([attn_sent, *attn_parts_kept], axis=0),
        )
        sums = lax.psum(sums, ("seq", "fsdp"))
    gain_sums = (sums[0], sums[3], sums[2], sums[1])
    gain_sums += (sums[4, :head_dim], sums[4, head_dim : 2 * head_dim])
    shape = (seq_dev, block, width)
    return (layer_out.reshape(shape), dtokens.reshape(shape)) + weights + gain_sums


def solution(mesh):
    sharded = P("fsdp", "seq", None)
    weight = P("fsdp", None)
    in_specs = (sharded, P("fsdp", "seq")) + (weight,) * 7 + (P(),) * 6 + (sharded,)
    out_specs = (sharded, sharded) + (P("fsdp", "seq"),) * 7 + (P(),) * 6
    return jax.shard_map(body, mesh=mesh, in_specs=in_specs, out_specs=out_specs, check_vma=False)
```

```python
import jax
import jax.numpy as jnp
import numpy as np
from jax import lax
from jax.experimental import pallas as pl
from jax.experimental.pallas import tpu as pltpu
from jax.sharding import PartitionSpec as P

WINDOW = 512
TILE = 128
FF_TILE = 256
FFN_ROWS = 256

epsilon = 1e-06
NEG_FILL = -1e30
ROPE_BASE = 10000.0
GELU_C = 0.7978845608028654
GELU_K = 0.044715

f32 = jnp.float32
bf16 = jnp.bfloat16

NN = (((1,), (0,)), ((), ()))
NT = (((1,), (1,)), ((), ()))
TN = (((0,), (0,)), ((), ()))


def mm(left, right, dims=NN):
    return lax.dot_general(left, right, dims, preferred_element_type=f32)


def inv_rms(vector):
    return lax.rsqrt(jnp.mean(vector * vector, axis=-1, keepdims=True) + epsilon)


def norm_back(vector, inv, gain, grad):
    unit = vector * inv
    scaled = gain * grad
    back = inv * (scaled - unit * jnp.mean(unit * scaled, axis=-1, keepdims=True))
    return back, grad * unit


def rope(vector, cosine, sine):
    half = vector.shape[-1] // 2
    one, two = vector[:, :half], vector[:, half:]
    return jnp.concatenate([one * cosine - two * sine, two * cosine + one * sine], axis=1)


def rope_back(vector, cosine, sine):
    half = vector.shape[-1] // 2
    one, two = vector[:, :half], vector[:, half:]
    return jnp.concatenate([one * cosine + two * sine, two * cosine - one * sine], axis=1)


def params(limit_mib=58):
    return pltpu.CompilerParams(vmem_limit_bytes=limit_mib * 1024 * 1024)


def cost(microseconds):
    return pl.CostEstimate(
        flops=int(microseconds * 1e9), bytes_accessed=int(microseconds * 3e6), transcendentals=0
    )


def whole(shape):
    return pl.BlockSpec(shape, lambda *_: (0,) * len(shape))


def rows(count, width):
    return pl.BlockSpec((count, width), lambda i: (i, 0))


def shaped(shape, dtype):
    return jax.ShapeDtypeStruct(shape, dtype)


def qkv_kernel(
    held_ref, tok_ref, far_ref, cos_ref, sin_ref, gains_ref, head_ref, *refs
):
    packs = refs[:-9]
    attn_ref, qraw_ref, qrot_ref, kraw_ref, key_ref, val_ref, wq_ref, wkv_ref, wot_ref = refs[-9:]
    head_dim = head_ref.shape[1]
    head_count = wq_ref.shape[1] // head_dim
    block, width = tok_ref.shape
    chunks, chunk_rows, _ = packs[0].shape
    pieces = len(packs)
    half = pieces // 2

    @pl.when(pl.program_id(0) == 0)
    def _():
        strip = chunk_rows // 2
        odd = held_ref[0] % 2 == 1

        def aligned(index, size):
            return pl.ds(pl.multiple_of(index * size, size), size)

        for c in range(chunks):
            z = held_ref[pieces + c]
            own = aligned(z, chunk_rows)
            for m in range(pieces):
                s = held_ref[m]
                wq_ref[own, aligned(s, 128)] = packs[m][c, :, :128]
                turned = packs[m][c, :, 128:256]
                for i in range(2):
                    wot_ref[aligned(s, strip), aligned(2 * z + i, 128)] = turned[
                        i * strip : (i + 1) * strip
                    ]
            for m, mate in zip(range(half), (0, 2, 1, 3)):
                one, two = packs[m][c, :, 256:320], packs[half + mate][c, :, 256:320]
                wkv_ref[own, aligned(held_ref[m] // 2, 128)] = jnp.concatenate(
                    [jnp.where(odd, two, one), jnp.where(odd, one, two)], axis=1
                )

    pre = gains_ref[0:1, :]
    qgain, kgain = head_ref[0:1, :], head_ref[1:2, :]
    token = tok_ref[...].astype(f32)
    low = (token * inv_rms(token) * pre).astype(bf16)
    attn_ref[...] = low
    query = mm(low, wq_ref[...])
    qraw_ref[...] = query
    cosine, sine = cos_ref[block:, :], sin_ref[block:, :]
    scaling = head_dim ** (-0.5)
    for h in range(head_count):
        part = query[:, h * head_dim : (h + 1) * head_dim]
        normed = part * inv_rms(part) * qgain
        qrot_ref[:, h * head_dim : (h + 1) * head_dim] = (
            rope(normed, cosine, sine).astype(bf16) * jnp.asarray(scaling, bf16)
        )
    both = mm(low, wkv_ref[...])
    key = both[:, :head_dim]
    kraw_ref[...] = key
    key_ref[0, block:, :] = rope(key * inv_rms(key) * kgain, cosine, sine).astype(bf16)
    val_ref[0, block:, :] = both[:, head_dim:].astype(bf16)
    token = far_ref[...].astype(f32)
    low = (token * inv_rms(token) * pre).astype(bf16)
    both = mm(low, wkv_ref[...])
    key = both[:, :head_dim]
    key_ref[0, :block, :] = rope(
        key * inv_rms(key) * kgain, cos_ref[:block, :], sin_ref[:block, :]
    ).astype(bf16)
    val_ref[0, :block, :] = both[:, head_dim:].astype(bf16)


def stacked(ref, tile, head_count, head_dim):
    return jnp.concatenate(
        [
            ref[tile * TILE : (tile + 1) * TILE, h * head_dim : (h + 1) * head_dim]
            for h in range(head_count)
        ],
        axis=0,
    )


def mask_of(pos_ref, tile, span):
    reach = pos_ref[tile * TILE : (tile + 1) * TILE, :]
    row = lax.broadcasted_iota(jnp.int32, (TILE, span), 0)
    col = lax.broadcasted_iota(jnp.int32, (TILE, span), 1)
    distance = WINDOW + row - col
    return jnp.where((distance >= 0) & (distance <= reach), 0.0, NEG_FILL)


def attn_kernel(
    q_ref, key_ref, val_ref, pos_ref, tok_ref, wot_ref, gains_ref,
    ctx_ref, lse_ref, branch_ref, res_ref, fin_ref,
):
    head_dim = key_ref.shape[2]
    head_count = q_ref.shape[1] // head_dim
    span = WINDOW + TILE
    lane = lax.broadcasted_iota(jnp.int32, (TILE, 128), 1)
    for tile in range(q_ref.shape[0] // TILE):
        query = stacked(q_ref, tile, head_count, head_dim)
        key = key_ref[0, tile * TILE : tile * TILE + span, :]
        value = val_ref[0, tile * TILE : tile * TILE + span, :]
        score = mm(query, key, NT).reshape(head_count, TILE, span) + mask_of(pos_ref, tile, span)
        largest = jnp.max(score, axis=-1, keepdims=True)
        expo = jnp.exp(score - largest)
        total = jnp.sum(expo, axis=-1, keepdims=True)
        low = expo.astype(bf16).reshape(head_count * TILE, span)
        context = mm(low, value).reshape(head_count, TILE, head_dim) / total
        log_total = largest + jnp.log(total)
        kept = jnp.zeros((TILE, 128), f32)
        for h in range(head_count):
            ctx_ref[tile * TILE : (tile + 1) * TILE, h * head_dim : (h + 1) * head_dim] = context[
                h
            ].astype(bf16)
            kept = jnp.where(lane == h, log_total[h], kept)
        lse_ref[tile * TILE : (tile + 1) * TILE, :] = kept
    branch = mm(ctx_ref[...], wot_ref[...], NT)
    branch_ref[...] = branch
    residual = tok_ref[...].astype(f32) + branch * inv_rms(branch) * gains_ref[1:2, :]
    res_ref[...] = residual
    fin_ref[...] = (residual * inv_rms(residual) * gains_ref[2:3, :]).astype(bf16)


def ffn_kernel(
    held_ref, order_ref, res_ref, fin_ref, cot_ref, branch_ref, ctx_ref, wot_ref, gains_ref, *refs
):
    pieces = order_ref.shape[0] - refs[0].shape[0]
    packs, refs = (refs[:pieces], refs[pieces : 2 * pieces]), refs[2 * pieces :]
    out_ref, gres_ref, gctx_ref, gain_ref = refs[:4]
    gate_sent, gate_kept, down_sent, down_kept = refs[4:8]
    slope_ref, act_ref, gate_ref, up_ref, down_ref, stage_ref, copied = refs[8:15]
    hid_ref, gg_ref, gu_ref, in_left, ffn_left, attn_left, turn_ref = refs[15:]
    chunks, middle, tile = packs[0][0].shape
    width = res_ref.shape[1]
    count = hid_ref.shape[0]
    quarter, strip, half = width // chunks, width // pieces, pieces // 2
    step = pl.program_id(0)
    tiles = count // FFN_ROWS
    post_attn, pre_ffn, post_ffn = [gains_ref[i : i + 1, :] for i in (1, 2, 3)]

    def aligned(index, size):
        return pl.ds(pl.multiple_of(index * size, size), size)

    @pl.when(step == 0)
    def _():
        gain_ref[...] = jnp.zeros_like(gain_ref)

        def staged(m):
            return [
                pltpu.make_async_copy(
                    packs[i][m],
                    stage_ref.at[m % 2, :, pl.ds(i * middle, middle), :],
                    copied.at[m % 2, i],
                )
                for i in range(2)
            ]

        for copy in staged(0):
            copy.start()
        for m in range(pieces):
            if m + 1 < pieces:
                for copy in staged(m + 1):
                    copy.start()
            for copy in staged(m):
                copy.wait()
            s = held_ref[m]
            for c in range(chunks):
                z = held_ref[pieces + c]
                own, cols = aligned(z, quarter), aligned(s, tile)
                gate_ref[own, cols] = stage_ref[m % 2, c, :quarter, :]
                up_ref[own, cols] = stage_ref[m % 2, c, quarter : 2 * quarter, :]
                for i in range(2):
                    begin = 2 * quarter + i * strip
                    down_ref[aligned(s, strip), aligned(2 * z + i, tile)] = stage_ref[
                        m % 2, c, begin : begin + strip, :
                    ]

    @pl.when(step < tiles)
    def _():
        own = aligned(step, FFN_ROWS)

        def turn(left_ref, source, size, first, number):
            turn_ref[...] = source.T
            for m in range(number):
                left_ref[m * size : (m + 1) * size, own] = turn_ref[
                    aligned(order_ref[first + m], size), :
                ]

        ffn_in = fin_ref[...]
        turn(in_left, ffn_in, quarter, pieces, chunks)
        gate = mm(ffn_in, gate_ref[...])
        up = mm(ffn_in, up_ref[...])
        square = gate * gate
        bent = jnp.tanh(GELU_C * gate * (1.0 + GELU_K * square))
        half_bent = 0.5 * (1.0 + bent)
        act = gate * half_bent
        slope = half_bent + 0.5 * gate * (1.0 - bent * bent) * (
            GELU_C * (1.0 + 3.0 * GELU_K * square)
        )
        act_ref[...] = act
        slope_ref[...] = slope * up
        hidden = (act * up).astype(bf16)
        hid_ref[own, :] = hidden
        branch = mm(hidden, down_ref[...], NT)
        residual = res_ref[...]
        cot = cot_ref[...].astype(f32)
        inv = inv_rms(branch)
        out_ref[...] = (residual + branch * inv * post_ffn).astype(bf16)
        g_ffn, gain_post = norm_back(branch, inv, post_ffn, cot)
        g_low = g_ffn.astype(bf16)
        turn(ffn_left, g_low, strip, 0, pieces)
        g_hidden = mm(g_low, down_ref[...])
        g_gate = (g_hidden * slope_ref[...]).astype(bf16)
        g_up = (g_hidden * act_ref[...]).astype(bf16)
        gg_ref[own, :] = g_gate
        gu_ref[own, :] = g_up
        g_in = mm(g_gate, gate_ref[...], NT) + mm(g_up, up_ref[...], NT)
        back, gain_pre = norm_back(residual, inv_rms(residual), pre_ffn, g_in)
        g_res = cot + back
        gres_ref[...] = g_res
        attn_branch = branch_ref[...]
        g_attn, gain_attn = norm_back(attn_branch, inv_rms(attn_branch), post_attn, g_res)
        g_attn = g_attn.astype(bf16)
        turn(attn_left, g_attn, strip, 0, pieces)
        gctx_ref[...] = mm(g_attn, wot_ref[...]).astype(bf16)
        gain_ref[0:1, :] += jnp.sum(gain_post, axis=0, keepdims=True)
        gain_ref[1:2, :] += jnp.sum(gain_pre, axis=0, keepdims=True)
        gain_ref[2:3, :] += jnp.sum(gain_attn, axis=0, keepdims=True)

    @pl.when(step >= tiles)
    def _():
        k = step - tiles
        cols = aligned(order_ref[k], tile)
        z = order_ref[pieces + k // 2]
        both = mm(in_left[...], jnp.concatenate([gg_ref[:, cols], gu_ref[:, cols]], axis=1))
        both = both.astype(bf16)
        for i in range(2):
            part = both[:, i * tile : (i + 1) * tile].reshape(chunks, quarter, tile)
            for inside, out in ((k < half, gate_sent), (k >= half, gate_kept)):

                @pl.when(inside)
                def _(out=out, part=part, i=i):
                    out[0, :, i * quarter : (i + 1) * quarter, :] = part

        def put(begin, part):
            part = part.astype(bf16).reshape(pieces, strip, tile)
            down_sent[:, 0, pl.ds(begin, strip), :] = part[:half]
            down_kept[:, 0, pl.ds(begin, strip), :] = part[half:]

        put(
            pl.multiple_of(k % 2 * strip, strip),
            mm(ffn_left[...], hid_ref[:, aligned(2 * z + k % 2, tile)]),
        )

        @pl.when(k % 2 == 0)
        def _():
            put(2 * strip, mm(attn_left[...], ctx_ref[:, aligned(z, tile)]))


def turn_strips(left_ref, source, strip, where, count):
    left_ref[1] = source.T
    for m in range(count):
        begin = pl.multiple_of(where(m) * strip, 16)
        left_ref[0, m * strip : (m + 1) * strip, :] = left_ref[1, pl.ds(begin, strip), :]


def attn_grad_kernel(base, order_ref, _, attn_ref, gq_ref, gkv_ref, sort_ref, *refs):
    recv_ref = refs[0] if base else None
    outs = refs[1:3] if base else refs[:1]
    left = refs[-1]
    held, chunks, quarter, _ = outs[0].shape
    width = attn_ref.shape[1]
    pieces = order_ref.shape[0] - chunks
    half = pieces // 2
    turn_strips(left, attn_ref[...], quarter, lambda m: order_ref[pieces + m], chunks)
    sorted_kv = mm(gkv_ref[...], sort_ref[...]).astype(bf16)
    part_kv = mm(left[0], sorted_kv)
    wide = part_kv.shape[1] // half
    for pair in range(0, half, 2):
        both = jnp.concatenate(
            [
                gq_ref[:, pl.ds(pl.multiple_of(order_ref[base + pair + i] * 128, 128), 128)]
                for i in range(2)
            ],
            axis=1,
        )
        part = mm(left[0], both)
        for i in range(2):
            m = pair + i
            value = part[:, i * 128 : (i + 1) * 128].reshape(chunks, quarter, 128)
            value_kv = part_kv[:, m * wide : (m + 1) * wide].reshape(chunks, quarter, wide)
            if base:
                value = value + recv_ref[m, :, :, :128].astype(f32)
                value_kv = value_kv + recv_ref[m, :, :, 128:].astype(f32)
            out = outs[m // held]
            out[m % held, :, :, :128] = value.astype(bf16)
            out[m % held, :, :, 128:] = value_kv.astype(bf16)


def attn_back_kernel(
    q_ref, gctx_ref, key_ref, val_ref, pos_ref, lse_ref, qraw_ref, cos_ref, sin_ref, head_ref,
    *refs,
):
    gq_ref, far_ref, near_ref, gain_ref, gkey_ref, gval_ref = refs[-6:]
    head_dim = key_ref.shape[2]
    head_count = q_ref.shape[1] // head_dim
    block = q_ref.shape[0]
    span = WINDOW + TILE
    scaling = head_dim ** (-0.5)

    @pl.when(pl.program_id(0) == 0)
    def _():
        gain_ref[...] = jnp.zeros_like(gain_ref)

    gkey_ref[...] = jnp.zeros_like(gkey_ref)
    gval_ref[...] = jnp.zeros_like(gval_ref)
    gain = jnp.zeros((1, head_dim), f32)
    for tile in range(block // TILE):
        own = slice(tile * TILE, (tile + 1) * TILE)
        reach = slice(tile * TILE, tile * TILE + span)
        query = stacked(q_ref, tile, head_count, head_dim)
        g_ctx = stacked(gctx_ref, tile, head_count, head_dim)
        key = key_ref[0, reach, :]
        value = val_ref[0, reach, :]
        log_total = jnp.stack([lse_ref[own, h : h + 1] for h in range(head_count)])
        score = mm(query, key, NT).reshape(head_count, TILE, span) + mask_of(pos_ref, tile, span)
        probs = jnp.exp(score - log_total)
        g_probs = mm(g_ctx, value, NT).reshape(head_count, TILE, span)
        spread = jnp.sum(g_probs * probs, axis=-1, keepdims=True)
        g_score = (probs * (g_probs - spread)).astype(bf16).reshape(head_count * TILE, span)
        low = probs.astype(bf16).reshape(head_count * TILE, span)
        gkey_ref[reach, :] += mm(g_score, query, TN)
        gval_ref[reach, :] += mm(low, g_ctx, TN)
        g_rot = mm(g_score, key) * scaling
        turned = slice(block + tile * TILE, block + (tile + 1) * TILE)
        cosine, sine = cos_ref[turned, :], sin_ref[turned, :]
        for h in range(head_count):
            cols = slice(h * head_dim, (h + 1) * head_dim)
            raw = qraw_ref[own, cols]
            back, share = norm_back(
                raw,
                inv_rms(raw),
                head_ref[0:1, :],
                rope_back(g_rot[h * TILE : (h + 1) * TILE], cosine, sine),
            )
            gq_ref[own, cols] = back.astype(bf16)
            gain += jnp.sum(share, axis=0, keepdims=True)
    gain_ref[0:1, :] += gain
    far_ref[0, :, :head_dim] = rope_back(
        gkey_ref[:block, :], cos_ref[:block, :], sin_ref[:block, :]
    ).astype(bf16)
    far_ref[0, :, head_dim:] = gval_ref[:block, :].astype(bf16)
    near_ref[0, :, :head_dim] = gkey_ref[block:, :]
    near_ref[0, :, head_dim:] = gval_ref[block:, :]


def kv_back_kernel(
    kraw_ref, cos_ref, sin_ref, head_ref, *refs
):
    gkv_ref, kgain_ref = refs[-2:]
    sequences = (len(refs) - 2) // 2
    head_dim = head_ref.shape[1]

    @pl.when(pl.program_id(0) == 0)
    def _():
        kgain_ref[...] = jnp.zeros_like(kgain_ref)

    near, far = refs[0][0], refs[sequences][0]
    for index in range(1, sequences):
        mine = pl.program_id(0) == index
        near = jnp.where(mine, refs[index][0], near)
        far = jnp.where(mine, refs[sequences + index][0], far)
    far = far.astype(f32)
    raw = kraw_ref[...]
    g_normed = rope_back(near[:, :head_dim], cos_ref[...], sin_ref[...]) + far[:, :head_dim]
    g_key, share = norm_back(raw, inv_rms(raw), head_ref[1:2, :], g_normed)
    kgain_ref[0:1, :] += jnp.sum(share, axis=0, keepdims=True)
    gkv_ref[:, :head_dim] = g_key.astype(bf16)
    gkv_ref[:, head_dim:] = (near[:, head_dim:] + far[:, head_dim:]).astype(bf16)


def input_kernel(
    _, __, gq_ref, gkv_ref, wq_ref, wkv_ref, tok_ref, gres_ref, gains_ref, ffn_gain_ref, kgain_ref,
    *refs
):
    dtok_ref, gain_ref = refs[-2:]
    @pl.when(pl.program_id(0) == 0)
    def _():
        gain_ref[...] = jnp.zeros_like(gain_ref)
        head_dim = kgain_ref.shape[1]
        gain_ref[1:4, :] = ffn_gain_ref[0:3, :]
        gain_ref[4:5, :head_dim] = sum(ref[0:1, :] for ref in refs[:-2])
        gain_ref[4:5, head_dim : 2 * head_dim] = kgain_ref[0:1, :]

    g_in = mm(gq_ref[...], wq_ref[...], NT) + mm(gkv_ref[...], wkv_ref[...], NT)
    token = tok_ref[...].astype(f32)
    back, share = norm_back(token, inv_rms(token), gains_ref[0:1, :], g_in)
    dtok_ref[...] = (gres_ref[...] + back).astype(bf16)
    gain_ref[0:1, :] += jnp.sum(share, axis=0, keepdims=True)


def passed_along(shard, axis, by):
    length = lax.axis_size(axis)
    pairs = [(i, i + by) for i in range(length) if 0 <= i + by < length]
    return lax.ppermute(shard, axis, pairs)


def swapped(array, axis, even, odd):
    length = lax.axis_size(axis)
    return lax.ppermute(array, axis, [(i, i ^ (odd if i % 2 else even)) for i in range(length)])


def tables(block, head_dim):
    half_width = head_dim // 2
    frequency = ROPE_BASE ** (-(np.arange(half_width) * 2.0) / head_dim)
    angles = np.arange(-block, block)[:, None] * frequency
    return np.cos(angles).astype(np.float32), np.sin(angles).astype(np.float32)


def column_piece(array, axis_name, parts):
    wide = array.shape[1] // parts
    return lax.dynamic_slice_in_dim(array, lax.axis_index(axis_name) * wide, wide, 1)


def halves(array):
    if isinstance(array, tuple):
        return tuple(zip(*(halves(part) for part in array)))
    half = array.shape[0] // 2
    return (array[:half], array[half:]) if half > 1 else (array[0], array[1])


def total(terms):
    laid = [term for term in terms if isinstance(term, tuple)]
    terms = [term for term in terms if not isinstance(term, tuple)]
    if laid:
        terms.insert(0, jnp.concatenate([total(list(parts)) for parts in zip(*laid)], axis=-2))
    result = terms[0].astype(f32)
    for term in terms[1:]:
        result = result + term.astype(f32)
    return result


HELD = [0, 4, 2, 6, 1, 3, 5, 7]
HELD_Z = [0, 2, 1, 3]


def linked(*chains):
    arrays, steps = [], []
    for chain in chains:
        send, keep = chain if isinstance(chain, tuple) else (chain, [])
        arrays.append([send] + [array for array, _ in keep])
        steps.append([begin for _, begin in keep])
    arrays = lax.optimization_barrier(arrays)
    result = []
    for chain, (send, *keep), begins in zip(chains, arrays, steps):
        result.append((send, list(zip(keep, begins))) if isinstance(chain, tuple) else send)
    return result


class Exchange:
    def __init__(self, seqs, chunks):
        self.direct = seqs == 8 and chunks == 4
        if not self.direct:
            self.order = jnp.arange(12, dtype=jnp.int32) % 8
            self.held = jnp.array(HELD + HELD_Z, jnp.int32)
            return
        s, z = lax.axis_index("seq"), lax.axis_index("fsdp")
        odd = s % 2 == 1
        one, two = jnp.where(odd, 4, 2), jnp.where(odd, 2, 4)
        zero = jnp.zeros_like(s)
        sent = [one | two | 1, two | 1, one | 1, zero | 1]
        kept = [one | two, one, two, zero]
        order = [s ^ k for k in sent + kept] + [z ^ k for k in (3, 1, 2, 0)]
        self.order = jnp.stack(order).astype(jnp.int32)
        held = [zero, two, one, one | two, zero | 1, one | 1, two | 1, one | two | 1]
        held = [s ^ k for k in held] + [z ^ k for k in HELD_Z]
        self.held = jnp.stack(held).astype(jnp.int32)

    def along_step(self, held, bits):
        return jnp.concatenate([held, swapped(held, "fsdp", bits, bits)], axis=0)

    def second(self, piece):
        return swapped(piece, "seq", 4, 2)

    def first(self, piece):
        return swapped(piece, "seq", 2, 4)

    def swap_cores(self, parts):
        return swapped(parts, "seq", 1, 1)

    def fold(self, send, keep, step):
        if step < 3:
            got = swapped(send, "seq", *((1, 1), (2, 4), (4, 2))[step])
        else:
            got = swapped(send, "fsdp", step - 2, step - 2)
        return self.split(keep + [(got, step)], step)

    def split(self, terms, step):
        rest = []
        for array, begin in terms:
            for done in range(begin, step):
                array = halves(array)[1]
            rest.append(array)
        if step == 4:
            return total(rest)
        return total([halves(array)[0] for array in rest]).astype(bf16), terms

    def hop_terms(self, send, keep):
        keep = keep + [(swapped(send, "seq", 4, 2), 2)]
        rest = []
        for array, begin in keep:
            for done in range(begin, 2):
                array = halves(array)[1]
            rest.append(array)
        parts = [total([array[p] for array in rest]) for p in range(4)]
        return [part.astype(bf16) for part in parts[:3]] + [parts[3]]

    def last(self, *parts):
        got = [swapped(part, "fsdp", bits, bits) for part, bits in zip(parts, (3, 1, 2))]
        return total([parts[3]] + got)

    def hop(self, value, axis, bits):
        got = [swapped(value, axis, b, b) for b in bits]
        if len(bits) == 1:
            return value + got[0]
        both = bits[0] | bits[1]
        return (value + got[0]) + (got[1] + swapped(value, axis, both, both))


def scattered_plain(part):
    columns = lax.psum_scatter(part, "seq", scatter_dimension=1, tiled=True)
    return lax.psum_scatter(columns, "fsdp", scatter_dimension=0, tiled=True).astype(f32)


def gather_weights(w_query, w_key, w_value, w_out, w_gate, w_up, w_down, halo, exchange):
    pieces = w_gate.shape[1] // FF_TILE
    width = w_out.shape[1]
    if exchange.direct:
        down = column_piece(w_down, "seq", pieces).T
        ffn = jnp.concatenate(
            [
                column_piece(w_gate, "seq", pieces),
                column_piece(w_up, "seq", pieces),
                down[:, :FF_TILE],
                down[:, FF_TILE:],
            ],
            axis=0,
        )
        both = jnp.concatenate([w_key, w_value], axis=1)
        out = column_piece(w_out, "seq", pieces).T
        out = jnp.concatenate([out[:, :128], out[:, 128:]], axis=0)
        attn = jnp.concatenate(
            [column_piece(w_query, "seq", pieces), out, column_piece(both, "seq", pieces)], axis=1
        )
        attn = exchange.along_step(exchange.along_step(attn[None], 2), 1)
        middle = ffn.shape[0] // 2
        one_ffn, two_ffn, attn = lax.optimization_barrier((ffn[:middle], ffn[middle:], attn))
        one_ffn = exchange.along_step(one_ffn[None], 2)
        attn, halo = lax.optimization_barrier((attn, halo))
        two = exchange.second(attn)
        one_ffn, two_ffn, two = lax.optimization_barrier((one_ffn, two_ffn, two))
        one_ffn = exchange.along_step(one_ffn, 1)
        two_ffn = exchange.along_step(two_ffn[None], 2)
        attn = [attn, two, exchange.first(attn), exchange.first(two)]
        attn[3], one_ffn, two_ffn = lax.optimization_barrier((attn[3], one_ffn, two_ffn))
        two_ffn = exchange.along_step(two_ffn, 1)
        attn += [exchange.swap_cores(held) for held in attn]
        return attn, (one_ffn, two_ffn), halo
    w_query, w_key, w_value, w_out, w_gate, w_up, w_down = [
        lax.all_gather(w, "fsdp", axis=0, tiled=True)
        for w in (w_query, w_key, w_value, w_out, w_gate, w_up, w_down)
    ]
    chunks = w_down.shape[0] // (2 * FF_TILE)
    quarter, strip = width // chunks, width // pieces

    def columns(weight):
        return weight.reshape(chunks, quarter, pieces, -1).transpose(2, 0, 1, 3)

    def turned(weight):
        shape = (pieces, strip, chunks, 2, weight.shape[0] // (2 * chunks))
        turned_part = weight.T.reshape(shape).transpose(0, 2, 3, 1, 4)
        return turned_part.reshape(pieces, chunks, 2 * strip, -1)

    both = jnp.concatenate([w_key, w_value], axis=1)
    attn = jnp.concatenate([columns(w_query), turned(w_out), columns(both)], axis=3)
    ffn = jnp.concatenate([columns(w_gate), columns(w_up), turned(w_down)], axis=2)
    def listed(pack):
        pack = jnp.take(jnp.take(pack, np.array(HELD), axis=0), np.array(HELD_Z), axis=1)
        return [pack[m] for m in range(pieces)]

    middle = ffn.shape[2] // 2
    return listed(attn), [listed(ffn[:, :, :middle]), listed(ffn[:, :, middle:])], halo


def plain_gradients(part_gate, part_down, part_attn):
    pieces, quarters, double, _ = part_gate.shape
    width = quarters * double // 2
    strip = width // pieces

    def columns(parts):
        return parts.transpose(1, 2, 0, 3).reshape(width, -1)

    def turned(parts):
        parts = parts.reshape(pieces, quarters, -1, strip, FF_TILE).transpose(1, 2, 4, 0, 3)
        return parts.reshape(-1, width)

    each = part_attn.shape[3] - (part_attn.shape[3] - 128) // 2
    return tuple(
        scattered_plain(part)
        for part in (
            columns(part_attn[..., :128]),
            columns(part_attn[..., 128:each]),
            columns(part_attn[..., each:]),
            turned(part_down[:, :, 2 * strip :]),
            columns(part_gate[:, :, : double // 2]),
            columns(part_gate[:, :, double // 2 :]),
            turned(part_down[:, :, : 2 * strip]),
        )
    )


def split_gradients(ffn, attn):
    quarter = attn.shape[0]
    gate, down = ffn[: 2 * quarter], ffn[2 * quarter :]
    strip = down.shape[0] // 3
    each = attn.shape[1] - (attn.shape[1] - 128) // 2
    return (
        attn[:, :128],
        attn[:, 128:each],
        attn[:, each:],
        down[2 * strip :].T,
        gate[:quarter],
        gate[quarter:],
        jnp.concatenate([down[:strip].T, down[strip : 2 * strip].T], axis=0),
    )


def body(
    tokens, doc_starts, w_query, w_key, w_value, w_out, w_gate, w_up, w_down,
    pre_attn, post_attn, pre_ffn, post_ffn, query_norm, key_norm, cotangent,
):
    seq_dev, block, width = tokens.shape
    head_dim = w_key.shape[1]
    inner = w_query.shape[1]
    hidden_dim = w_gate.shape[1]
    count = seq_dev * block
    seqs, chunks = lax.axis_size("seq"), lax.axis_size("fsdp")
    exchange = Exchange(seqs, chunks)
    far_tokens = passed_along(tokens, "seq", 1).reshape(count, width)
    far_starts = passed_along(doc_starts, "seq", 1)
    pack, ffn_pack, (far_tokens, far_starts) = gather_weights(
        w_query, w_key, w_value, w_out, w_gate, w_up, w_down, (far_tokens, far_starts), exchange
    )
    starts = jnp.concatenate([far_starts, doc_starts], axis=1)
    indices = jnp.arange(2 * block, dtype=jnp.int32)
    latest = lax.cummax(jnp.where(starts == 1, indices[None, :], -WINDOW), axis=1)
    reach = jnp.minimum(indices[None, :] - latest, WINDOW - 1)[:, block:]
    pos_column = reach.reshape(count, 1)
    cosine, sine = tables(block, head_dim)
    own_cosine, own_sine = cosine[block:], sine[block:]

    pieces, quarters = len(pack), pack[0].shape[0]
    quarter, strip = width // quarters, width // pieces
    gains = jnp.stack([pre_attn, post_attn, pre_ffn, post_ffn])
    head_gains = jnp.stack([query_norm, key_norm])
    tokens_2d = tokens.reshape(count, width)
    cot_2d = cotangent.reshape(count, width)

    tok_spec = rows(block, width)
    table_spec = whole((2 * block, head_dim // 2))
    half_spec = whole((block, head_dim // 2))
    key_spec = pl.BlockSpec((1, 2 * block, head_dim), lambda i: (i, 0, 0))
    gains_spec, head_spec = whole((4, width)), whole((2, head_dim))
    wq_spec, wkv_spec, wot_spec = (
        whole((width, inner)),
        whole((width, 2 * head_dim)),
        whole((width, inner)),
    )
    smem = pl.BlockSpec(memory_space=pltpu.SMEM)
    remain = pl.BlockSpec(memory_space=pl.ANY)
    attn_low, query_raw, query_rot, key_raw, keys, values, full_q, full_kv, full_ot = (
        pl.pallas_call(
            qkv_kernel,
            grid=(seq_dev,),
            in_specs=[smem, tok_spec, tok_spec, table_spec, table_spec]
            + [gains_spec, head_spec]
            + [whole(pack[0].shape)] * pieces,
            out_specs=[
                tok_spec,
                rows(block, inner),
                rows(block, inner),
                rows(block, head_dim),
                key_spec,
                key_spec,
                wq_spec,
                wkv_spec,
                wot_spec,
            ],
            out_shape=[
                shaped((count, width), bf16),
                shaped((count, inner), f32),
                shaped((count, inner), bf16),
                shaped((count, head_dim), f32),
                shaped((seq_dev, 2 * block, head_dim), bf16),
                shaped((seq_dev, 2 * block, head_dim), bf16),
                shaped((width, inner), bf16),
                shaped((width, 2 * head_dim), bf16),
                shaped((width, inner), bf16),
            ],
            compiler_params=params(),
            name="project_rotate",
        cost_estimate=cost(11),
        )(
            exchange.held, tokens_2d, far_tokens, cosine, sine, gains, head_gains,
            *pack,
        )
    )
    if exchange.direct:
        held = [[own, exchange.second(own), exchange.first(own)] for own in ffn_pack]
        swaps = [[exchange.swap_cores(pack[0])] for pack in held]
        held[0][1], held[1][1], keys = lax.optimization_barrier((held[0][1], held[1][1], keys))
        for pack, swap in zip(held, swaps):
            pack.append(exchange.first(pack[1]))
            swap.append(exchange.swap_cores(pack[1]))
    context, log_total, attn_branch, residual, ffn_in = pl.pallas_call(
        attn_kernel,
        grid=(seq_dev,),
        in_specs=[rows(block, inner), key_spec, key_spec, rows(block, 1), tok_spec]
        + [wot_spec, gains_spec],
        out_specs=[rows(block, inner), rows(block, 128), tok_spec, tok_spec, tok_spec],
        out_shape=[
            shaped((count, inner), bf16),
            shaped((count, 128), f32),
            shaped((count, width), f32),
            shaped((count, width), f32),
            shaped((count, width), bf16),
        ],
        compiler_params=params(),
        name="window_attention",
        cost_estimate=cost(12),
    )(query_rot, keys, values, pos_column, tokens_2d, full_ot, gains)

    if exchange.direct:
        *late, ffn_in = lax.optimization_barrier((*held[0][2:], *held[1][2:], ffn_in))
        ffn_pack = []
        for pack, swap, rest in zip(held, swaps, (late[:2], late[2:])):
            ffn_pack.append(pack[:2] + rest + swap + [exchange.swap_cores(r) for r in rest])

    half = pieces // 2
    tiles = count // FFN_ROWS

    def small(wide):
        return pl.BlockSpec((FFN_ROWS, wide), lambda i: (jnp.minimum(i, tiles - 1), 0))

    def once(shape):
        return pl.BlockSpec(
            shape, lambda *_: (0,) * len(shape), pipeline_mode=pl.Buffered(buffer_count=1)
        )

    gate_shape = (half, quarters, 2 * quarter, FF_TILE)
    down_shape = (half, quarters, 3 * strip, FF_TILE)

    def gate_spec(first):
        return pl.BlockSpec(
            (1,) + gate_shape[1:],
            lambda i: (jnp.clip(i - tiles - first, 0, half - 1), 0, 0, 0),
        )

    down_spec = pl.BlockSpec(
        (half, 1) + down_shape[2:], lambda i: (0, jnp.clip(i - tiles, 0, pieces - 1) // 2, 0, 0)
    )
    turned = pltpu.VMEM((width, count), bf16)
    weight = pltpu.VMEM((width, hidden_dim), bf16)
    middle = pltpu.VMEM((count, hidden_dim), bf16)
    gelu_parts = pltpu.VMEM((FFN_ROWS, hidden_dim), f32)
    layer_out, g_res, g_ctx, ffn_gains, *ffn_parts = pl.pallas_call(
        ffn_kernel,
        grid=(tiles + pieces,),
        in_specs=[smem, smem, small(width), small(width), small(width), small(width)]
        + [once((count, inner)), once((width, inner)), gains_spec]
        + [remain] * (2 * pieces),
        out_specs=[small(width), small(width), small(inner), whole((8, width))]
        + [gate_spec(0), gate_spec(half), down_spec, down_spec],
        out_shape=[
            shaped((count, width), bf16),
            shaped((count, width), f32),
            shaped((count, inner), bf16),
            shaped((8, width), f32),
            shaped(gate_shape, bf16),
            shaped(gate_shape, bf16),
            shaped(down_shape, bf16),
            shaped(down_shape, bf16),
        ],
        scratch_shapes=[gelu_parts, gelu_parts, weight, weight, weight]
        + [pltpu.VMEM((2, quarters, 2 * ffn_pack[0][0].shape[1], FF_TILE), bf16)]
        + [pltpu.SemaphoreType.DMA((2, 2))]
        + [middle, middle, middle, turned, turned, turned]
        + [pltpu.VMEM((width, FFN_ROWS), bf16)],
        compiler_params=params(62),
        name="feed_forward",
        cost_estimate=cost(60),
    )(
        exchange.held, exchange.order, residual, ffn_in, cot_2d, attn_branch, context, full_ot,
        gains, *ffn_pack[0], *ffn_pack[1],
    )
    gate_sent, gate_kept, down_sent, down_kept = ffn_parts
    gate, down = (gate_sent, gate_kept), (down_sent, down_kept)
    if exchange.direct:
        gate_got, down_got = swapped(gate_sent, "seq", 1, 1), swapped(down_sent, "seq", 1, 1)


    def attn_back(index, before):
        def at(count, wide):
            return pl.BlockSpec((count, wide), lambda *_: (index, 0))

        own_keys = pl.BlockSpec((1, 2 * block, head_dim), lambda *_: (index, 0, 0))
        pair = whole((1, block, 2 * head_dim))
        in_specs = [at(block, inner), at(block, inner), own_keys, own_keys, at(block, 1)]
        in_specs += [at(block, 128), at(block, inner), table_spec, table_spec, head_spec]
        return pl.pallas_call(
            attn_back_kernel,
            grid=(1,),
            in_specs=in_specs + [remain] * len(before),
            out_specs=[at(block, inner), pair, pair, whole((8, head_dim))],
            out_shape=[
                shaped((count, inner), bf16),
                shaped((1, block, 2 * head_dim), bf16),
                shaped((1, block, 2 * head_dim), f32),
                shaped((8, head_dim), f32),
            ],
            input_output_aliases={len(in_specs): 0} if before else {},
            scratch_shapes=[
                pltpu.VMEM((2 * block, head_dim), f32),
                pltpu.VMEM((2 * block, head_dim), f32),
            ],
            compiler_params=params(),
            name="attention_gradient",
            cost_estimate=cost(8),
        )(
            query_rot, g_ctx, keys, values, pos_column, log_total, query_raw, cosine, sine,
            head_gains, *before,
        )

    g_nears, g_recvs, query_gains, before = [], [], [], ()
    for index in range(seq_dev):
        g_query, g_far, g_near, part_gain = attn_back(index, before)
        query_gains.append(part_gain)
        g_nears.append(g_near)
        g_recvs.append(passed_along(g_far, "seq", -1))
        before = (g_query,)
        if index == 0 and exchange.direct:
            gate_got, down_got, g_query = lax.optimization_barrier((gate_got, down_got, g_query))
            kept, got = (gate_kept, down_kept), (gate_got, down_got)
            ffn = exchange.split([(kept, 0), (got, 0)], 0)
            before = (g_query, ffn[0])

    g_kv, key_gain = pl.pallas_call(
        kv_back_kernel,
        grid=(seq_dev,),
        in_specs=[rows(block, head_dim), half_spec, half_spec, head_spec]
        + [whole((1, block, 2 * head_dim))] * (2 * seq_dev),
        out_specs=[rows(block, 2 * head_dim), whole((8, head_dim))],
        out_shape=[shaped((count, 2 * head_dim), bf16), shaped((8, head_dim), f32)],
        compiler_params=params(),
        name="key_value_back",
        cost_estimate=cost(4),
    )(key_raw, own_cosine, own_sine, head_gains, *g_nears, *g_recvs)

    each = head_dim // pieces
    column = jnp.arange(2 * head_dim, dtype=jnp.int32)
    inside = column % (2 * each)
    source = jnp.where(inside < each, inside, inside - each + head_dim)
    source = source + each * jnp.repeat(exchange.order[:pieces], 2 * each)
    sort = (column[:, None] == source[None, :]).astype(bf16)

    def attn_parts(base, before, extra):
        shape = (half, quarters, quarter, 128 + 2 * each)
        sent = (half // 2,) + shape[1:]
        outs = [shape] if base == 0 else [sent, sent]
        vmem = pl.BlockSpec(memory_space=pltpu.VMEM)
        chosen = sort[:, base * 2 * each : (base + half) * 2 * each]
        return pl.pallas_call(
            lambda *refs: attn_grad_kernel(base, *refs),
            in_specs=[smem, remain] + [vmem] * (4 + len(extra)),
            out_specs=[vmem] * len(outs),
            out_shape=[shaped(o, bf16) for o in outs],
            scratch_shapes=[pltpu.VMEM((2, width, count), bf16)],
            compiler_params=params(),
            cost_estimate=cost(6),
            name="attn_gradients_kept" if base else "attn_gradients_sent",
        )(exchange.order, before, attn_low, g_query, g_kv, chosen, *extra)

    if exchange.direct:
        ffn = exchange.fold(*ffn, 1)
    else:
        ffn = ffn_parts
    (attn_sent,) = attn_parts(0, ffn[0], [])
    attn_got = exchange.swap_cores(attn_sent) if exchange.direct else jnp.zeros_like(attn_sent)
    if exchange.direct:
        ffn = exchange.fold(*ffn, 2)
    attn_parts_kept = attn_parts(half, ffn[0], [attn_got])
    attn = attn_parts_kept[0], [(attn_parts_kept[1], 1)]
    if exchange.direct:
        ffn, attn = linked(exchange.fold(*ffn, 3), exchange.fold(*attn, 1))
    dtokens, sums = pl.pallas_call(
        input_kernel,
        grid=(seq_dev,),
        in_specs=[remain, remain, rows(block, inner), rows(block, 2 * head_dim)]
        + [wq_spec, wkv_spec]
        + [tok_spec, tok_spec, gains_spec, whole((8, width))]
        + [whole((8, head_dim))] * (1 + seq_dev),
        out_specs=[tok_spec, whole((8, width))],
        out_shape=[shaped((count, width), bf16), shaped((8, width), f32)],
        compiler_params=params(),
        name="input_gradient",
        cost_estimate=cost(7),
    )(ffn[0], attn[0], g_query, g_kv, full_q, full_kv, tokens_2d, g_res, gains, ffn_gains, key_gain, *query_gains)

    if exchange.direct:
        sums = exchange.hop(sums, "seq", (1,))
        attn = exchange.hop_terms(*attn)
        *attn, sums = linked(*attn, sums)
        sums = exchange.hop(sums, "seq", (2, 4))
        attn = exchange.last(*attn)
        ffn = exchange.fold(*ffn, 4)
        ffn, sums = lax.optimization_barrier((ffn, sums))
        sums = exchange.hop(sums, "fsdp", (1, 2))
        weights = split_gradients(ffn, attn)
    else:
        weights = plain_gradients(
            jnp.concatenate(gate, axis=0),
            jnp.concatenate(down, axis=0),
            jnp.concatenate([attn_sent, *attn_parts_kept], axis=0),
        )
        sums = lax.psum(sums, ("seq", "fsdp"))
    gain_sums = (sums[0], sums[3], sums[2], sums[1])
    gain_sums += (sums[4, :head_dim], sums[4, head_dim : 2 * head_dim])
    shape = (seq_dev, block, width)
    return (layer_out.reshape(shape), dtokens.reshape(shape)) + weights + gain_sums


def solution(mesh):
    sharded = P("fsdp", "seq", None)
    weight = P("fsdp", None)
    in_specs = (sharded, P("fsdp", "seq")) + (weight,) * 7 + (P(),) * 6 + (sharded,)
    out_specs = (sharded, sharded) + (P("fsdp", "seq"),) * 7 + (P(),) * 6
    return jax.shard_map(body, mesh=mesh, in_specs=in_specs, out_specs=out_specs, check_vma=False)
```

```python
import jax
import jax.numpy as jnp
import numpy as np
from jax import lax
from jax.experimental import pallas as pl
from jax.experimental.pallas import tpu as pltpu
from jax.sharding import PartitionSpec as P

WINDOW = 512
TILE = 128
FF_TILE = 256
FFN_ROWS = 256

epsilon = 1e-06
NEG_FILL = -1e30
ROPE_BASE = 10000.0
GELU_C = 0.7978845608028654
GELU_K = 0.044715

f32 = jnp.float32
bf16 = jnp.bfloat16

NN = (((1,), (0,)), ((), ()))
NT = (((1,), (1,)), ((), ()))
TN = (((0,), (0,)), ((), ()))


def mm(left, right, dims=NN):
    return lax.dot_general(left, right, dims, preferred_element_type=f32)


def inv_rms(vector):
    return lax.rsqrt(jnp.mean(vector * vector, axis=-1, keepdims=True) + epsilon)


def norm_back(vector, inv, gain, grad):
    unit = vector * inv
    scaled = gain * grad
    back = inv * (scaled - unit * jnp.mean(unit * scaled, axis=-1, keepdims=True))
    return back, grad * unit


def rope(vector, cosine, sine):
    half = vector.shape[-1] // 2
    one, two = vector[:, :half], vector[:, half:]
    return jnp.concatenate([one * cosine - two * sine, two * cosine + one * sine], axis=1)


def rope_back(vector, cosine, sine):
    half = vector.shape[-1] // 2
    one, two = vector[:, :half], vector[:, half:]
    return jnp.concatenate([one * cosine + two * sine, two * cosine - one * sine], axis=1)


def params(limit_mib=58):
    return pltpu.CompilerParams(vmem_limit_bytes=limit_mib * 1024 * 1024)


def cost(microseconds):
    return pl.CostEstimate(
        flops=int(microseconds * 1e9), bytes_accessed=int(microseconds * 3e6), transcendentals=0
    )


def whole(shape):
    return pl.BlockSpec(shape, lambda *_: (0,) * len(shape))


def rows(count, width):
    return pl.BlockSpec((count, width), lambda i: (i, 0))


def shaped(shape, dtype):
    return jax.ShapeDtypeStruct(shape, dtype)


def qkv_kernel(
    held_ref, tok_ref, far_ref, cos_ref, sin_ref, gains_ref, head_ref, *refs
):
    packs = refs[:-9]
    attn_ref, qraw_ref, qrot_ref, kraw_ref, key_ref, val_ref, wq_ref, wkv_ref, wot_ref = refs[-9:]
    head_dim = head_ref.shape[1]
    head_count = wq_ref.shape[1] // head_dim
    block, width = tok_ref.shape
    chunks, chunk_rows, _ = packs[0].shape
    pieces = len(packs)
    half = pieces // 2

    @pl.when(pl.program_id(0) == 0)
    def _():
        strip = chunk_rows // 2
        odd = held_ref[0] % 2 == 1

        def aligned(index, size):
            return pl.ds(pl.multiple_of(index * size, size), size)

        for c in range(chunks):
            z = held_ref[pieces + c]
            own = aligned(z, chunk_rows)
            for m in range(pieces):
                s = held_ref[m]
                wq_ref[own, aligned(s, 128)] = packs[m][c, :, :128]
                turned = packs[m][c, :, 128:256]
                for i in range(2):
                    wot_ref[aligned(s, strip), aligned(2 * z + i, 128)] = turned[
                        i * strip : (i + 1) * strip
                    ]
            for m, mate in zip(range(half), (0, 2, 1, 3)):
                one, two = packs[m][c, :, 256:320], packs[half + mate][c, :, 256:320]
                wkv_ref[own, aligned(held_ref[m] // 2, 128)] = jnp.concatenate(
                    [jnp.where(odd, two, one), jnp.where(odd, one, two)], axis=1
                )

    pre = gains_ref[0:1, :]
    qgain, kgain = head_ref[0:1, :], head_ref[1:2, :]
    token = tok_ref[...].astype(f32)
    low = (token * inv_rms(token) * pre).astype(bf16)
    attn_ref[...] = low
    query = mm(low, wq_ref[...])
    qraw_ref[...] = query
    cosine, sine = cos_ref[block:, :], sin_ref[block:, :]
    scaling = head_dim ** (-0.5)
    for h in range(head_count):
        part = query[:, h * head_dim : (h + 1) * head_dim]
        normed = part * inv_rms(part) * qgain
        qrot_ref[:, h * head_dim : (h + 1) * head_dim] = (
            rope(normed, cosine, sine).astype(bf16) * jnp.asarray(scaling, bf16)
        )
    both = mm(low, wkv_ref[...])
    key = both[:, :head_dim]
    kraw_ref[...] = key
    key_ref[0, block:, :] = rope(key * inv_rms(key) * kgain, cosine, sine).astype(bf16)
    val_ref[0, block:, :] = both[:, head_dim:].astype(bf16)
    token = far_ref[...].astype(f32)
    low = (token * inv_rms(token) * pre).astype(bf16)
    both = mm(low, wkv_ref[...])
    key = both[:, :head_dim]
    key_ref[0, :block, :] = rope(
        key * inv_rms(key) * kgain, cos_ref[:block, :], sin_ref[:block, :]
    ).astype(bf16)
    val_ref[0, :block, :] = both[:, head_dim:].astype(bf16)


def stacked(ref, tile, head_count, head_dim):
    return jnp.concatenate(
        [
            ref[tile * TILE : (tile + 1) * TILE, h * head_dim : (h + 1) * head_dim]
            for h in range(head_count)
        ],
        axis=0,
    )


def mask_of(pos_ref, tile, span):
    reach = pos_ref[tile * TILE : (tile + 1) * TILE, :]
    row = lax.broadcasted_iota(jnp.int32, (TILE, span), 0)
    col = lax.broadcasted_iota(jnp.int32, (TILE, span), 1)
    distance = WINDOW + row - col
    return jnp.where((distance >= 0) & (distance <= reach), 0.0, NEG_FILL)


def attn_kernel(
    q_ref, key_ref, val_ref, pos_ref, tok_ref, wot_ref, gains_ref,
    ctx_ref, lse_ref, branch_ref, res_ref, fin_ref,
):
    head_dim = key_ref.shape[2]
    head_count = q_ref.shape[1] // head_dim
    span = WINDOW + TILE
    lane = lax.broadcasted_iota(jnp.int32, (TILE, 128), 1)
    for tile in range(q_ref.shape[0] // TILE):
        query = stacked(q_ref, tile, head_count, head_dim)
        key = key_ref[0, tile * TILE : tile * TILE + span, :]
        value = val_ref[0, tile * TILE : tile * TILE + span, :]
        score = mm(query, key, NT).reshape(head_count, TILE, span) + mask_of(pos_ref, tile, span)
        largest = jnp.max(score, axis=-1, keepdims=True)
        expo = jnp.exp(score - largest)
        total = jnp.sum(expo, axis=-1, keepdims=True)
        low = expo.astype(bf16).reshape(head_count * TILE, span)
        context = mm(low, value).reshape(head_count, TILE, head_dim) / total
        log_total = largest + jnp.log(total)
        kept = jnp.zeros((TILE, 128), f32)
        for h in range(head_count):
            ctx_ref[tile * TILE : (tile + 1) * TILE, h * head_dim : (h + 1) * head_dim] = context[
                h
            ].astype(bf16)
            kept = jnp.where(lane == h, log_total[h], kept)
        lse_ref[tile * TILE : (tile + 1) * TILE, :] = kept
    branch = mm(ctx_ref[...], wot_ref[...], NT)
    branch_ref[...] = branch
    residual = tok_ref[...].astype(f32) + branch * inv_rms(branch) * gains_ref[1:2, :]
    res_ref[...] = residual
    fin_ref[...] = (residual * inv_rms(residual) * gains_ref[2:3, :]).astype(bf16)


def ffn_kernel(
    held_ref, order_ref, res_ref, fin_ref, cot_ref, branch_ref, ctx_ref, wot_ref, gains_ref, *refs
):
    pieces = order_ref.shape[0] - refs[0].shape[0]
    packs, refs = refs[:pieces], refs[pieces:]
    out_ref, gres_ref, gctx_ref, gain_ref = refs[:4]
    gate_sent, gate_kept, down_sent, down_kept = refs[4:8]
    slope_ref, act_ref, gate_ref, up_ref, down_ref, stage_ref, copied = refs[8:15]
    hid_ref, gg_ref, gu_ref, in_left, ffn_left, attn_left, turn_ref = refs[15:]
    chunks, _, tile = packs[0].shape
    width = res_ref.shape[1]
    count = hid_ref.shape[0]
    quarter, strip, half = width // chunks, width // pieces, pieces // 2
    step = pl.program_id(0)
    tiles = count // FFN_ROWS
    post_attn, pre_ffn, post_ffn = [gains_ref[i : i + 1, :] for i in (1, 2, 3)]

    def aligned(index, size):
        return pl.ds(pl.multiple_of(index * size, size), size)

    @pl.when(step == 0)
    def _():
        gain_ref[...] = jnp.zeros_like(gain_ref)

        def staged(m):
            return pltpu.make_async_copy(packs[m], stage_ref.at[m % 2], copied.at[m % 2])

        staged(0).start()
        for m in range(pieces):
            if m + 1 < pieces:
                staged(m + 1).start()
            staged(m).wait()
            s = held_ref[m]
            for c in range(chunks):
                z = held_ref[pieces + c]
                own, cols = aligned(z, quarter), aligned(s, tile)
                gate_ref[own, cols] = stage_ref[m % 2, c, :quarter, :]
                up_ref[own, cols] = stage_ref[m % 2, c, quarter : 2 * quarter, :]
                for i in range(2):
                    begin = 2 * quarter + i * strip
                    down_ref[aligned(s, strip), aligned(2 * z + i, tile)] = stage_ref[
                        m % 2, c, begin : begin + strip, :
                    ]

    @pl.when(step < tiles)
    def _():
        own = aligned(step, FFN_ROWS)

        def turn(left_ref, source, size, first, number):
            turn_ref[...] = source.T
            for m in range(number):
                left_ref[m * size : (m + 1) * size, own] = turn_ref[
                    aligned(order_ref[first + m], size), :
                ]

        ffn_in = fin_ref[...]
        turn(in_left, ffn_in, quarter, pieces, chunks)
        gate = mm(ffn_in, gate_ref[...])
        up = mm(ffn_in, up_ref[...])
        square = gate * gate
        bent = jnp.tanh(GELU_C * gate * (1.0 + GELU_K * square))
        half_bent = 0.5 * (1.0 + bent)
        act = gate * half_bent
        slope = half_bent + 0.5 * gate * (1.0 - bent * bent) * (
            GELU_C * (1.0 + 3.0 * GELU_K * square)
        )
        act_ref[...] = act
        slope_ref[...] = slope * up
        hidden = (act * up).astype(bf16)
        hid_ref[own, :] = hidden
        branch = mm(hidden, down_ref[...], NT)
        residual = res_ref[...]
        cot = cot_ref[...].astype(f32)
        inv = inv_rms(branch)
        out_ref[...] = (residual + branch * inv * post_ffn).astype(bf16)
        g_ffn, gain_post = norm_back(branch, inv, post_ffn, cot)
        g_low = g_ffn.astype(bf16)
        turn(ffn_left, g_low, strip, 0, pieces)
        g_hidden = mm(g_low, down_ref[...])
        g_gate = (g_hidden * slope_ref[...]).astype(bf16)
        g_up = (g_hidden * act_ref[...]).astype(bf16)
        gg_ref[own, :] = g_gate
        gu_ref[own, :] = g_up
        g_in = mm(g_gate, gate_ref[...], NT) + mm(g_up, up_ref[...], NT)
        back, gain_pre = norm_back(residual, inv_rms(residual), pre_ffn, g_in)
        g_res = cot + back
        gres_ref[...] = g_res
        attn_branch = branch_ref[...]
        g_attn, gain_attn = norm_back(attn_branch, inv_rms(attn_branch), post_attn, g_res)
        g_attn = g_attn.astype(bf16)
        turn(attn_left, g_attn, strip, 0, pieces)
        gctx_ref[...] = mm(g_attn, wot_ref[...]).astype(bf16)
        gain_ref[0:1, :] += jnp.sum(gain_post, axis=0, keepdims=True)
        gain_ref[1:2, :] += jnp.sum(gain_pre, axis=0, keepdims=True)
        gain_ref[2:3, :] += jnp.sum(gain_attn, axis=0, keepdims=True)

    @pl.when(step >= tiles)
    def _():
        k = step - tiles
        cols = aligned(order_ref[k], tile)
        z = order_ref[pieces + k // 2]
        both = mm(in_left[...], jnp.concatenate([gg_ref[:, cols], gu_ref[:, cols]], axis=1))
        both = both.astype(bf16)
        for i in range(2):
            part = both[:, i * tile : (i + 1) * tile].reshape(chunks, quarter, tile)
            for inside, out in ((k < half, gate_sent), (k >= half, gate_kept)):

                @pl.when(inside)
                def _(out=out, part=part, i=i):
                    out[0, :, i * quarter : (i + 1) * quarter, :] = part

        def put(begin, part):
            part = part.astype(bf16).reshape(pieces, strip, tile)
            down_sent[:, 0, pl.ds(begin, strip), :] = part[:half]
            down_kept[:, 0, pl.ds(begin, strip), :] = part[half:]

        put(
            pl.multiple_of(k % 2 * strip, strip),
            mm(ffn_left[...], hid_ref[:, aligned(2 * z + k % 2, tile)]),
        )

        @pl.when(k % 2 == 0)
        def _():
            put(2 * strip, mm(attn_left[...], ctx_ref[:, aligned(z, tile)]))


def turn_strips(left_ref, source, strip, where, count):
    left_ref[1] = source.T
    for m in range(count):
        begin = pl.multiple_of(where(m) * strip, 16)
        left_ref[0, m * strip : (m + 1) * strip, :] = left_ref[1, pl.ds(begin, strip), :]


def attn_grad_kernel(base, order_ref, _, attn_ref, gq_ref, gkv_ref, sort_ref, *refs):
    recv_ref = refs[0] if base else None
    outs = refs[1:3] if base else refs[:1]
    left = refs[-1]
    held, chunks, quarter, _ = outs[0].shape
    width = attn_ref.shape[1]
    pieces = order_ref.shape[0] - chunks
    half = pieces // 2
    turn_strips(left, attn_ref[...], quarter, lambda m: order_ref[pieces + m], chunks)
    sorted_kv = mm(gkv_ref[...], sort_ref[...]).astype(bf16)
    part_kv = mm(left[0], sorted_kv)
    wide = part_kv.shape[1] // half
    for pair in range(0, half, 2):
        both = jnp.concatenate(
            [
                gq_ref[:, pl.ds(pl.multiple_of(order_ref[base + pair + i] * 128, 128), 128)]
                for i in range(2)
            ],
            axis=1,
        )
        part = mm(left[0], both)
        for i in range(2):
            m = pair + i
            value = part[:, i * 128 : (i + 1) * 128].reshape(chunks, quarter, 128)
            value_kv = part_kv[:, m * wide : (m + 1) * wide].reshape(chunks, quarter, wide)
            if base:
                value = value + recv_ref[m, :, :, :128].astype(f32)
                value_kv = value_kv + recv_ref[m, :, :, 128:].astype(f32)
            out = outs[m // held]
            out[m % held, :, :, :128] = value.astype(bf16)
            out[m % held, :, :, 128:] = value_kv.astype(bf16)


def attn_back_kernel(
    q_ref, gctx_ref, key_ref, val_ref, pos_ref, lse_ref, qraw_ref, cos_ref, sin_ref, head_ref,
    gq_ref, far_ref, near_ref, gain_ref, gkey_ref, gval_ref,
):
    head_dim = key_ref.shape[2]
    head_count = q_ref.shape[1] // head_dim
    block = q_ref.shape[0]
    span = WINDOW + TILE
    scaling = head_dim ** (-0.5)

    @pl.when(pl.program_id(0) == 0)
    def _():
        gain_ref[...] = jnp.zeros_like(gain_ref)

    gkey_ref[...] = jnp.zeros_like(gkey_ref)
    gval_ref[...] = jnp.zeros_like(gval_ref)
    gain = jnp.zeros((1, head_dim), f32)
    for tile in range(block // TILE):
        own = slice(tile * TILE, (tile + 1) * TILE)
        reach = slice(tile * TILE, tile * TILE + span)
        query = stacked(q_ref, tile, head_count, head_dim)
        g_ctx = stacked(gctx_ref, tile, head_count, head_dim)
        key = key_ref[0, reach, :]
        value = val_ref[0, reach, :]
        log_total = jnp.stack([lse_ref[own, h : h + 1] for h in range(head_count)])
        score = mm(query, key, NT).reshape(head_count, TILE, span) + mask_of(pos_ref, tile, span)
        probs = jnp.exp(score - log_total)
        g_probs = mm(g_ctx, value, NT).reshape(head_count, TILE, span)
        spread = jnp.sum(g_probs * probs, axis=-1, keepdims=True)
        g_score = (probs * (g_probs - spread)).astype(bf16).reshape(head_count * TILE, span)
        low = probs.astype(bf16).reshape(head_count * TILE, span)
        gkey_ref[reach, :] += mm(g_score, query, TN)
        gval_ref[reach, :] += mm(low, g_ctx, TN)
        g_rot = mm(g_score, key) * scaling
        turned = slice(block + tile * TILE, block + (tile + 1) * TILE)
        cosine, sine = cos_ref[turned, :], sin_ref[turned, :]
        for h in range(head_count):
            cols = slice(h * head_dim, (h + 1) * head_dim)
            raw = qraw_ref[own, cols]
            back, share = norm_back(
                raw,
                inv_rms(raw),
                head_ref[0:1, :],
                rope_back(g_rot[h * TILE : (h + 1) * TILE], cosine, sine),
            )
            gq_ref[own, cols] = back.astype(bf16)
            gain += jnp.sum(share, axis=0, keepdims=True)
    gain_ref[0:1, :] += gain
    far_ref[0, :, :head_dim] = rope_back(
        gkey_ref[:block, :], cos_ref[:block, :], sin_ref[:block, :]
    ).astype(bf16)
    far_ref[0, :, head_dim:] = gval_ref[:block, :].astype(bf16)
    near_ref[0, :, :head_dim] = gkey_ref[block:, :]
    near_ref[0, :, head_dim:] = gval_ref[block:, :]


def kv_back_kernel(
    kraw_ref, cos_ref, sin_ref, head_ref, near_ref, recv_ref, _, gkv_ref, kgain_ref
):
    head_dim = head_ref.shape[1]

    @pl.when(pl.program_id(0) == 0)
    def _():
        kgain_ref[...] = jnp.zeros_like(kgain_ref)

    near, far = near_ref[0], recv_ref[0].astype(f32)
    raw = kraw_ref[...]
    g_normed = rope_back(near[:, :head_dim], cos_ref[...], sin_ref[...]) + far[:, :head_dim]
    g_key, share = norm_back(raw, inv_rms(raw), head_ref[1:2, :], g_normed)
    kgain_ref[0:1, :] += jnp.sum(share, axis=0, keepdims=True)
    gkv_ref[:, :head_dim] = g_key.astype(bf16)
    gkv_ref[:, head_dim:] = (near[:, head_dim:] + far[:, head_dim:]).astype(bf16)


def input_kernel(
    _, __, gq_ref, gkv_ref, wq_ref, wkv_ref, tok_ref, gres_ref, gains_ref, ffn_gain_ref, kgain_ref,
    qgain_ref, dtok_ref, gain_ref
):
    @pl.when(pl.program_id(0) == 0)
    def _():
        gain_ref[...] = jnp.zeros_like(gain_ref)
        head_dim = kgain_ref.shape[1]
        gain_ref[1:4, :] = ffn_gain_ref[0:3, :]
        gain_ref[4:5, :head_dim] = qgain_ref[0:1, :]
        gain_ref[4:5, head_dim : 2 * head_dim] = kgain_ref[0:1, :]

    g_in = mm(gq_ref[...], wq_ref[...], NT) + mm(gkv_ref[...], wkv_ref[...], NT)
    token = tok_ref[...].astype(f32)
    back, share = norm_back(token, inv_rms(token), gains_ref[0:1, :], g_in)
    dtok_ref[...] = (gres_ref[...] + back).astype(bf16)
    gain_ref[0:1, :] += jnp.sum(share, axis=0, keepdims=True)


def passed_along(shard, axis, by):
    length = lax.axis_size(axis)
    pairs = [(i, i + by) for i in range(length) if 0 <= i + by < length]
    return lax.ppermute(shard, axis, pairs)


def swapped(array, axis, even, odd):
    length = lax.axis_size(axis)
    return lax.ppermute(array, axis, [(i, i ^ (odd if i % 2 else even)) for i in range(length)])


def tables(block, head_dim):
    half_width = head_dim // 2
    frequency = ROPE_BASE ** (-(np.arange(half_width) * 2.0) / head_dim)
    angles = np.arange(-block, block)[:, None] * frequency
    return np.cos(angles).astype(np.float32), np.sin(angles).astype(np.float32)


def column_piece(array, axis_name, parts):
    wide = array.shape[1] // parts
    return lax.dynamic_slice_in_dim(array, lax.axis_index(axis_name) * wide, wide, 1)


def halves(array):
    if isinstance(array, tuple):
        return tuple(zip(*(halves(part) for part in array)))
    half = array.shape[0] // 2
    return (array[:half], array[half:]) if half > 1 else (array[0], array[1])


def total(terms):
    laid = [term for term in terms if isinstance(term, tuple)]
    terms = [term for term in terms if not isinstance(term, tuple)]
    if laid:
        terms.insert(0, jnp.concatenate([total(list(parts)) for parts in zip(*laid)], axis=-2))
    result = terms[0].astype(f32)
    for term in terms[1:]:
        result = result + term.astype(f32)
    return result


HELD = [0, 4, 2, 6, 1, 3, 5, 7]
HELD_Z = [0, 2, 1, 3]


def linked(*chains):
    arrays, steps = [], []
    for chain in chains:
        send, keep = chain if isinstance(chain, tuple) else (chain, [])
        arrays.append([send] + [array for array, _ in keep])
        steps.append([begin for _, begin in keep])
    arrays = lax.optimization_barrier(arrays)
    result = []
    for chain, (send, *keep), begins in zip(chains, arrays, steps):
        result.append((send, list(zip(keep, begins))) if isinstance(chain, tuple) else send)
    return result


class Exchange:
    def __init__(self, seqs, chunks):
        self.direct = seqs == 8 and chunks == 4
        if not self.direct:
            self.order = jnp.arange(12, dtype=jnp.int32) % 8
            self.held = jnp.array(HELD + HELD_Z, jnp.int32)
            return
        s, z = lax.axis_index("seq"), lax.axis_index("fsdp")
        odd = s % 2 == 1
        one, two = jnp.where(odd, 4, 2), jnp.where(odd, 2, 4)
        zero = jnp.zeros_like(s)
        sent = [one | two | 1, two | 1, one | 1, zero | 1]
        kept = [one | two, one, two, zero]
        order = [s ^ k for k in sent + kept] + [z ^ k for k in (3, 1, 2, 0)]
        self.order = jnp.stack(order).astype(jnp.int32)
        held = [zero, two, one, one | two, zero | 1, one | 1, two | 1, one | two | 1]
        held = [s ^ k for k in held] + [z ^ k for k in HELD_Z]
        self.held = jnp.stack(held).astype(jnp.int32)

    def along_step(self, held, bits):
        return jnp.concatenate([held, swapped(held, "fsdp", bits, bits)], axis=0)

    def second(self, piece):
        return swapped(piece, "seq", 4, 2)

    def first(self, piece):
        return swapped(piece, "seq", 2, 4)

    def swap_cores(self, parts):
        return swapped(parts, "seq", 1, 1)

    def fold(self, send, keep, step):
        if step < 3:
            got = swapped(send, "seq", *((1, 1), (2, 4), (4, 2))[step])
        else:
            got = swapped(send, "fsdp", step - 2, step - 2)
        return self.split(keep + [(got, step)], step)

    def split(self, terms, step):
        rest = []
        for array, begin in terms:
            for done in range(begin, step):
                array = halves(array)[1]
            rest.append(array)
        if step == 4:
            return total(rest)
        return total([halves(array)[0] for array in rest]).astype(bf16), terms

    def hop_terms(self, send, keep):
        keep = keep + [(swapped(send, "seq", 4, 2), 2)]
        rest = []
        for array, begin in keep:
            for done in range(begin, 2):
                array = halves(array)[1]
            rest.append(array)
        parts = [total([array[p] for array in rest]) for p in range(4)]
        return [part.astype(bf16) for part in parts[:3]] + [parts[3]]

    def last(self, *parts):
        got = [swapped(part, "fsdp", bits, bits) for part, bits in zip(parts, (3, 1, 2))]
        return total([parts[3]] + got)

    def hop(self, value, axis, bits):
        got = [swapped(value, axis, b, b) for b in bits]
        if len(bits) == 1:
            return value + got[0]
        both = bits[0] | bits[1]
        return (value + got[0]) + (got[1] + swapped(value, axis, both, both))


def scattered_plain(part):
    columns = lax.psum_scatter(part, "seq", scatter_dimension=1, tiled=True)
    return lax.psum_scatter(columns, "fsdp", scatter_dimension=0, tiled=True).astype(f32)


def gather_weights(w_query, w_key, w_value, w_out, w_gate, w_up, w_down, halo, exchange):
    pieces = w_gate.shape[1] // FF_TILE
    width = w_out.shape[1]
    if exchange.direct:
        down = column_piece(w_down, "seq", pieces).T
        ffn = jnp.concatenate(
            [
                column_piece(w_gate, "seq", pieces),
                column_piece(w_up, "seq", pieces),
                down[:, :FF_TILE],
                down[:, FF_TILE:],
            ],
            axis=0,
        )
        both = jnp.concatenate([w_key, w_value], axis=1)
        out = column_piece(w_out, "seq", pieces).T
        out = jnp.concatenate([out[:, :128], out[:, 128:]], axis=0)
        attn = jnp.concatenate(
            [column_piece(w_query, "seq", pieces), out, column_piece(both, "seq", pieces)], axis=1
        )
        attn = exchange.along_step(exchange.along_step(attn[None], 2), 1)
        ffn, attn = lax.optimization_barrier((ffn, attn))
        ffn = exchange.along_step(ffn[None], 2)
        attn, halo = lax.optimization_barrier((attn, halo))
        two, one = exchange.second(attn), exchange.first(attn)
        ffn, two = lax.optimization_barrier((ffn, two))
        ffn = exchange.along_step(ffn, 1)
        attn = [attn, two, one, exchange.first(two)]
        attn[3], ffn = lax.optimization_barrier((attn[3], ffn))
        return attn + [exchange.swap_cores(held) for held in attn], ffn, halo
    w_query, w_key, w_value, w_out, w_gate, w_up, w_down = [
        lax.all_gather(w, "fsdp", axis=0, tiled=True)
        for w in (w_query, w_key, w_value, w_out, w_gate, w_up, w_down)
    ]
    chunks = w_down.shape[0] // (2 * FF_TILE)
    quarter, strip = width // chunks, width // pieces

    def columns(weight):
        return weight.reshape(chunks, quarter, pieces, -1).transpose(2, 0, 1, 3)

    def turned(weight):
        shape = (pieces, strip, chunks, 2, weight.shape[0] // (2 * chunks))
        turned_part = weight.T.reshape(shape).transpose(0, 2, 3, 1, 4)
        return turned_part.reshape(pieces, chunks, 2 * strip, -1)

    both = jnp.concatenate([w_key, w_value], axis=1)
    attn = jnp.concatenate([columns(w_query), turned(w_out), columns(both)], axis=3)
    ffn = jnp.concatenate([columns(w_gate), columns(w_up), turned(w_down)], axis=2)
    def listed(pack):
        pack = jnp.take(jnp.take(pack, np.array(HELD), axis=0), np.array(HELD_Z), axis=1)
        return [pack[m] for m in range(pieces)]

    return listed(attn), listed(ffn), halo


def plain_gradients(part_gate, part_down, part_attn):
    pieces, quarters, double, _ = part_gate.shape
    width = quarters * double // 2
    strip = width // pieces

    def columns(parts):
        return parts.transpose(1, 2, 0, 3).reshape(width, -1)

    def turned(parts):
        parts = parts.reshape(pieces, quarters, -1, strip, FF_TILE).transpose(1, 2, 4, 0, 3)
        return parts.reshape(-1, width)

    each = part_attn.shape[3] - (part_attn.shape[3] - 128) // 2
    return tuple(
        scattered_plain(part)
        for part in (
            columns(part_attn[..., :128]),
            columns(part_attn[..., 128:each]),
            columns(part_attn[..., each:]),
            turned(part_down[:, :, 2 * strip :]),
            columns(part_gate[:, :, : double // 2]),
            columns(part_gate[:, :, double // 2 :]),
            turned(part_down[:, :, : 2 * strip]),
        )
    )


def split_gradients(ffn, attn):
    quarter = attn.shape[0]
    gate, down = ffn[: 2 * quarter], ffn[2 * quarter :]
    strip = down.shape[0] // 3
    each = attn.shape[1] - (attn.shape[1] - 128) // 2
    return (
        attn[:, :128],
        attn[:, 128:each],
        attn[:, each:],
        down[2 * strip :].T,
        gate[:quarter],
        gate[quarter:],
        jnp.concatenate([down[:strip].T, down[strip : 2 * strip].T], axis=0),
    )


def body(
    tokens, doc_starts, w_query, w_key, w_value, w_out, w_gate, w_up, w_down,
    pre_attn, post_attn, pre_ffn, post_ffn, query_norm, key_norm, cotangent,
):
    seq_dev, block, width = tokens.shape
    head_dim = w_key.shape[1]
    inner = w_query.shape[1]
    hidden_dim = w_gate.shape[1]
    count = seq_dev * block
    seqs, chunks = lax.axis_size("seq"), lax.axis_size("fsdp")
    exchange = Exchange(seqs, chunks)
    far_tokens = passed_along(tokens, "seq", 1).reshape(count, width)
    far_starts = passed_along(doc_starts, "seq", 1)
    pack, ffn_pack, (far_tokens, far_starts) = gather_weights(
        w_query, w_key, w_value, w_out, w_gate, w_up, w_down, (far_tokens, far_starts), exchange
    )
    starts = jnp.concatenate([far_starts, doc_starts], axis=1)
    indices = jnp.arange(2 * block, dtype=jnp.int32)
    latest = lax.cummax(jnp.where(starts == 1, indices[None, :], -WINDOW), axis=1)
    reach = jnp.minimum(indices[None, :] - latest, WINDOW - 1)[:, block:]
    pos_column = reach.reshape(count, 1)
    cosine, sine = tables(block, head_dim)
    own_cosine, own_sine = cosine[block:], sine[block:]

    pieces, quarters = len(pack), pack[0].shape[0]
    quarter, strip = width // quarters, width // pieces
    gains = jnp.stack([pre_attn, post_attn, pre_ffn, post_ffn])
    head_gains = jnp.stack([query_norm, key_norm])
    tokens_2d = tokens.reshape(count, width)
    cot_2d = cotangent.reshape(count, width)

    tok_spec = rows(block, width)
    table_spec = whole((2 * block, head_dim // 2))
    half_spec = whole((block, head_dim // 2))
    key_spec = pl.BlockSpec((1, 2 * block, head_dim), lambda i: (i, 0, 0))
    gains_spec, head_spec = whole((4, width)), whole((2, head_dim))
    wq_spec, wkv_spec, wot_spec = (
        whole((width, inner)),
        whole((width, 2 * head_dim)),
        whole((width, inner)),
    )
    smem = pl.BlockSpec(memory_space=pltpu.SMEM)
    remain = pl.BlockSpec(memory_space=pl.ANY)
    attn_low, query_raw, query_rot, key_raw, keys, values, full_q, full_kv, full_ot = (
        pl.pallas_call(
            qkv_kernel,
            grid=(seq_dev,),
            in_specs=[smem, tok_spec, tok_spec, table_spec, table_spec]
            + [gains_spec, head_spec]
            + [whole(pack[0].shape)] * pieces,
            out_specs=[
                tok_spec,
                rows(block, inner),
                rows(block, inner),
                rows(block, head_dim),
                key_spec,
                key_spec,
                wq_spec,
                wkv_spec,
                wot_spec,
            ],
            out_shape=[
                shaped((count, width), bf16),
                shaped((count, inner), f32),
                shaped((count, inner), bf16),
                shaped((count, head_dim), f32),
                shaped((seq_dev, 2 * block, head_dim), bf16),
                shaped((seq_dev, 2 * block, head_dim), bf16),
                shaped((width, inner), bf16),
                shaped((width, 2 * head_dim), bf16),
                shaped((width, inner), bf16),
            ],
            compiler_params=params(),
            name="project_rotate",
        cost_estimate=cost(11),
        )(
            exchange.held, tokens_2d, far_tokens, cosine, sine, gains, head_gains,
            *pack,
        )
    )
    if exchange.direct:
        own, two = ffn_pack, exchange.second(ffn_pack)
        own_swapped = exchange.swap_cores(own)
        again, two, keys = lax.optimization_barrier((own, two, keys))
        one, both, two_swapped = exchange.first(again), exchange.first(two), exchange.swap_cores(two)
    context, log_total, attn_branch, residual, ffn_in = pl.pallas_call(
        attn_kernel,
        grid=(seq_dev,),
        in_specs=[rows(block, inner), key_spec, key_spec, rows(block, 1), tok_spec]
        + [wot_spec, gains_spec],
        out_specs=[rows(block, inner), rows(block, 128), tok_spec, tok_spec, tok_spec],
        out_shape=[
            shaped((count, inner), bf16),
            shaped((count, 128), f32),
            shaped((count, width), f32),
            shaped((count, width), f32),
            shaped((count, width), bf16),
        ],
        compiler_params=params(),
        name="window_attention",
        cost_estimate=cost(12),
    )(query_rot, keys, values, pos_column, tokens_2d, full_ot, gains)

    if exchange.direct:
        one, both, ffn_in = lax.optimization_barrier((one, both, ffn_in))
        ffn_pack = [own, two, one, both, own_swapped, two_swapped]
        ffn_pack += [exchange.swap_cores(one), exchange.swap_cores(both)]

    half = pieces // 2
    tiles = count // FFN_ROWS

    def small(wide):
        return pl.BlockSpec((FFN_ROWS, wide), lambda i: (jnp.minimum(i, tiles - 1), 0))

    def once(shape):
        return pl.BlockSpec(
            shape, lambda *_: (0,) * len(shape), pipeline_mode=pl.Buffered(buffer_count=1)
        )

    gate_shape = (half, quarters, 2 * quarter, FF_TILE)
    down_shape = (half, quarters, 3 * strip, FF_TILE)

    def gate_spec(first):
        return pl.BlockSpec(
            (1,) + gate_shape[1:],
            lambda i: (jnp.clip(i - tiles - first, 0, half - 1), 0, 0, 0),
        )

    down_spec = pl.BlockSpec(
        (half, 1) + down_shape[2:], lambda i: (0, jnp.clip(i - tiles, 0, pieces - 1) // 2, 0, 0)
    )
    turned = pltpu.VMEM((width, count), bf16)
    weight = pltpu.VMEM((width, hidden_dim), bf16)
    middle = pltpu.VMEM((count, hidden_dim), bf16)
    gelu_parts = pltpu.VMEM((FFN_ROWS, hidden_dim), f32)
    layer_out, g_res, g_ctx, ffn_gains, *ffn_parts = pl.pallas_call(
        ffn_kernel,
        grid=(tiles + pieces,),
        in_specs=[smem, smem, small(width), small(width), small(width), small(width)]
        + [once((count, inner)), once((width, inner)), gains_spec]
        + [remain] * pieces,
        out_specs=[small(width), small(width), small(inner), whole((8, width))]
        + [gate_spec(0), gate_spec(half), down_spec, down_spec],
        out_shape=[
            shaped((count, width), bf16),
            shaped((count, width), f32),
            shaped((count, inner), bf16),
            shaped((8, width), f32),
            shaped(gate_shape, bf16),
            shaped(gate_shape, bf16),
            shaped(down_shape, bf16),
            shaped(down_shape, bf16),
        ],
        scratch_shapes=[gelu_parts, gelu_parts, weight, weight, weight]
        + [pltpu.VMEM((2,) + ffn_pack[0].shape, bf16), pltpu.SemaphoreType.DMA((2,))]
        + [middle, middle, middle, turned, turned, turned]
        + [pltpu.VMEM((width, FFN_ROWS), bf16)],
        compiler_params=params(62),
        name="feed_forward",
        cost_estimate=cost(60),
    )(
        exchange.held, exchange.order, residual, ffn_in, cot_2d, attn_branch, context, full_ot,
        gains, *ffn_pack,
    )
    gate_sent, gate_kept, down_sent, down_kept = ffn_parts
    gate, down = (gate_sent, gate_kept), (down_sent, down_kept)
    if exchange.direct:
        gate_got, down_got = swapped(gate_sent, "seq", 1, 1), swapped(down_sent, "seq", 1, 1)


    pair = pl.BlockSpec((1, block, 2 * head_dim), lambda i: (i, 0, 0))
    g_query, g_far, g_near, query_gain = pl.pallas_call(
        attn_back_kernel,
        grid=(seq_dev,),
        in_specs=[rows(block, inner), rows(block, inner), key_spec, key_spec]
        + [rows(block, 1), rows(block, 128), rows(block, inner), table_spec, table_spec]
        + [head_spec],
        out_specs=[rows(block, inner), pair, pair, whole((8, head_dim))],
        out_shape=[
            shaped((count, inner), bf16),
            shaped((seq_dev, block, 2 * head_dim), bf16),
            shaped((seq_dev, block, 2 * head_dim), f32),
            shaped((8, head_dim), f32),
        ],
        scratch_shapes=[
            pltpu.VMEM((2 * block, head_dim), f32),
            pltpu.VMEM((2 * block, head_dim), f32),
        ],
        compiler_params=params(),
        name="attention_gradient",
        cost_estimate=cost(16),
    )(
        query_rot, g_ctx, keys, values, pos_column, log_total, query_raw, cosine, sine,
        head_gains,
    )
    g_recv = passed_along(g_far, "seq", -1)
    ffn = ffn_parts
    if exchange.direct:
        gate_got, down_got, g_query = lax.optimization_barrier((gate_got, down_got, g_query))
        kept, got = (gate_kept, down_kept), (gate_got, down_got)
        ffn = exchange.split([(kept, 0), (got, 0)], 0)
    g_kv, key_gain = pl.pallas_call(
        kv_back_kernel,
        grid=(seq_dev,),
        in_specs=[rows(block, head_dim), half_spec, half_spec, head_spec]
        + [pair, pair, remain],
        out_specs=[rows(block, 2 * head_dim), whole((8, head_dim))],
        out_shape=[shaped((count, 2 * head_dim), bf16), shaped((8, head_dim), f32)],
        compiler_params=params(),
        name="key_value_back",
        cost_estimate=cost(4),
    )(key_raw, own_cosine, own_sine, head_gains, g_near, g_recv, ffn[0])

    each = head_dim // pieces
    column = jnp.arange(2 * head_dim, dtype=jnp.int32)
    inside = column % (2 * each)
    source = jnp.where(inside < each, inside, inside - each + head_dim)
    source = source + each * jnp.repeat(exchange.order[:pieces], 2 * each)
    sort = (column[:, None] == source[None, :]).astype(bf16)

    def attn_parts(base, before, extra):
        shape = (half, quarters, quarter, 128 + 2 * each)
        sent = (half // 2,) + shape[1:]
        outs = [shape] if base == 0 else [sent, sent]
        vmem = pl.BlockSpec(memory_space=pltpu.VMEM)
        chosen = sort[:, base * 2 * each : (base + half) * 2 * each]
        return pl.pallas_call(
            lambda *refs: attn_grad_kernel(base, *refs),
            in_specs=[smem, remain] + [vmem] * (4 + len(extra)),
            out_specs=[vmem] * len(outs),
            out_shape=[shaped(o, bf16) for o in outs],
            scratch_shapes=[pltpu.VMEM((2, width, count), bf16)],
            compiler_params=params(),
            cost_estimate=cost(6),
            name="attn_gradients_kept" if base else "attn_gradients_sent",
        )(exchange.order, before, attn_low, g_query, g_kv, chosen, *extra)

    early = ffn
    if exchange.direct:
        ffn = early = exchange.fold(*ffn, 1)
    (attn_sent,) = attn_parts(0, early[0], [])
    attn_got = exchange.swap_cores(attn_sent) if exchange.direct else jnp.zeros_like(attn_sent)
    if exchange.direct:
        ffn = exchange.fold(*ffn, 2)
    attn_parts_kept = attn_parts(half, ffn[0], [attn_got])
    attn = attn_parts_kept[0], [(attn_parts_kept[1], 1)]
    if exchange.direct:
        ffn, attn = linked(exchange.fold(*ffn, 3), exchange.fold(*attn, 1))
    dtokens, sums = pl.pallas_call(
        input_kernel,
        grid=(seq_dev,),
        in_specs=[remain, remain, rows(block, inner), rows(block, 2 * head_dim)]
        + [wq_spec, wkv_spec]
        + [tok_spec, tok_spec, gains_spec, whole((8, width))]
        + [whole((8, head_dim))] * 2,
        out_specs=[tok_spec, whole((8, width))],
        out_shape=[shaped((count, width), bf16), shaped((8, width), f32)],
        compiler_params=params(),
        name="input_gradient",
        cost_estimate=cost(7),
    )(ffn[0], attn[0], g_query, g_kv, full_q, full_kv, tokens_2d, g_res, gains, ffn_gains, key_gain, query_gain)

    if exchange.direct:
        attn = exchange.hop_terms(*attn)
        sums = exchange.hop(sums, "seq", (1,))
        *attn, sums = linked(*attn, sums)
        attn = exchange.last(*attn)
        sums = exchange.hop(sums, "seq", (2, 4))
        ffn = exchange.fold(*ffn, 4)
        ffn, attn, sums = linked(ffn, attn, sums)
        sums = exchange.hop(sums, "fsdp", (1, 2))
        weights = split_gradients(ffn, attn)
    else:
        weights = plain_gradients(
            jnp.concatenate(gate, axis=0),
            jnp.concatenate(down, axis=0),
            jnp.concatenate([attn_sent, *attn_parts_kept], axis=0),
        )
        sums = lax.psum(sums, ("seq", "fsdp"))
    gain_sums = (sums[0], sums[3], sums[2], sums[1])
    gain_sums += (sums[4, :head_dim], sums[4, head_dim : 2 * head_dim])
    shape = (seq_dev, block, width)
    return (layer_out.reshape(shape), dtokens.reshape(shape)) + weights + gain_sums


def solution(mesh):
    sharded = P("fsdp", "seq", None)
    weight = P("fsdp", None)
    in_specs = (sharded, P("fsdp", "seq")) + (weight,) * 7 + (P(),) * 6 + (sharded,)
    out_specs = (sharded, sharded) + (P("fsdp", "seq"),) * 7 + (P(),) * 6
    return jax.shard_map(body, mesh=mesh, in_specs=in_specs, out_specs=out_specs, check_vma=False)
```

```python
import jax
import jax.numpy as jnp
import numpy as np
from jax import lax
from jax.experimental import pallas as pl
from jax.experimental.pallas import tpu as pltpu
from jax.sharding import PartitionSpec as P

WINDOW = 512
TILE = 128
FF_TILE = 256
FFN_ROWS = 256

epsilon = 1e-06
NEG_FILL = -1e30
ROPE_BASE = 10000.0
GELU_C = 0.7978845608028654
GELU_K = 0.044715

f32 = jnp.float32
bf16 = jnp.bfloat16

NN = (((1,), (0,)), ((), ()))
NT = (((1,), (1,)), ((), ()))
TN = (((0,), (0,)), ((), ()))


def mm(left, right, dims=NN):
    return lax.dot_general(left, right, dims, preferred_element_type=f32)


def inv_rms(vector):
    return lax.rsqrt(jnp.mean(vector * vector, axis=-1, keepdims=True) + epsilon)


def norm_back(vector, inv, gain, grad):
    unit = vector * inv
    scaled = gain * grad
    back = inv * (scaled - unit * jnp.mean(unit * scaled, axis=-1, keepdims=True))
    return back, grad * unit


def rope(vector, cosine, sine):
    half = vector.shape[-1] // 2
    one, two = vector[:, :half], vector[:, half:]
    return jnp.concatenate([one * cosine - two * sine, two * cosine + one * sine], axis=1)


def rope_back(vector, cosine, sine):
    half = vector.shape[-1] // 2
    one, two = vector[:, :half], vector[:, half:]
    return jnp.concatenate([one * cosine + two * sine, two * cosine - one * sine], axis=1)


def params(limit_mib=58):
    return pltpu.CompilerParams(vmem_limit_bytes=limit_mib * 1024 * 1024)


def cost(microseconds):
    return pl.CostEstimate(
        flops=int(microseconds * 1e9), bytes_accessed=int(microseconds * 3e6), transcendentals=0
    )


def whole(shape):
    return pl.BlockSpec(shape, lambda *_: (0,) * len(shape))


def rows(count, width):
    return pl.BlockSpec((count, width), lambda i: (i, 0))


def shaped(shape, dtype):
    return jax.ShapeDtypeStruct(shape, dtype)


def qkv_kernel(
    held_ref, tok_ref, far_ref, cos_ref, sin_ref, gains_ref, head_ref, *refs
):
    packs = refs[:-9]
    attn_ref, qraw_ref, qrot_ref, kraw_ref, key_ref, val_ref, wq_ref, wkv_ref, wot_ref = refs[-9:]
    head_dim = head_ref.shape[1]
    head_count = wq_ref.shape[1] // head_dim
    block, width = tok_ref.shape
    chunks, chunk_rows, _ = packs[0].shape
    pieces = len(packs)
    half = pieces // 2

    @pl.when(pl.program_id(0) == 0)
    def _():
        strip = chunk_rows // 2
        odd = held_ref[0] % 2 == 1

        def aligned(index, size):
            return pl.ds(pl.multiple_of(index * size, size), size)

        for c in range(chunks):
            z = held_ref[pieces + c]
            own = aligned(z, chunk_rows)
            for m in range(pieces):
                s = held_ref[m]
                wq_ref[own, aligned(s, 128)] = packs[m][c, :, :128]
                turned = packs[m][c, :, 128:256]
                for i in range(2):
                    wot_ref[aligned(s, strip), aligned(2 * z + i, 128)] = turned[
                        i * strip : (i + 1) * strip
                    ]
            for m, mate in zip(range(half), (0, 2, 1, 3)):
                one, two = packs[m][c, :, 256:320], packs[half + mate][c, :, 256:320]
                wkv_ref[own, aligned(held_ref[m] // 2, 128)] = jnp.concatenate(
                    [jnp.where(odd, two, one), jnp.where(odd, one, two)], axis=1
                )

    pre = gains_ref[0:1, :]
    qgain, kgain = head_ref[0:1, :], head_ref[1:2, :]
    token = tok_ref[...].astype(f32)
    low = (token * inv_rms(token) * pre).astype(bf16)
    attn_ref[...] = low
    query = mm(low, wq_ref[...])
    qraw_ref[...] = query
    cosine, sine = cos_ref[block:, :], sin_ref[block:, :]
    scaling = head_dim ** (-0.5)
    for h in range(head_count):
        part = query[:, h * head_dim : (h + 1) * head_dim]
        normed = part * inv_rms(part) * qgain
        qrot_ref[:, h * head_dim : (h + 1) * head_dim] = (
            rope(normed, cosine, sine).astype(bf16) * jnp.asarray(scaling, bf16)
        )
    both = mm(low, wkv_ref[...])
    key = both[:, :head_dim]
    kraw_ref[...] = key
    key_ref[0, block:, :] = rope(key * inv_rms(key) * kgain, cosine, sine).astype(bf16)
    val_ref[0, block:, :] = both[:, head_dim:].astype(bf16)
    token = far_ref[...].astype(f32)
    low = (token * inv_rms(token) * pre).astype(bf16)
    both = mm(low, wkv_ref[...])
    key = both[:, :head_dim]
    key_ref[0, :block, :] = rope(
        key * inv_rms(key) * kgain, cos_ref[:block, :], sin_ref[:block, :]
    ).astype(bf16)
    val_ref[0, :block, :] = both[:, head_dim:].astype(bf16)


def stacked(ref, tile, head_count, head_dim):
    return jnp.concatenate(
        [
            ref[tile * TILE : (tile + 1) * TILE, h * head_dim : (h + 1) * head_dim]
            for h in range(head_count)
        ],
        axis=0,
    )


def mask_of(pos_ref, tile, span):
    reach = pos_ref[tile * TILE : (tile + 1) * TILE, :]
    row = lax.broadcasted_iota(jnp.int32, (TILE, span), 0)
    col = lax.broadcasted_iota(jnp.int32, (TILE, span), 1)
    distance = WINDOW + row - col
    return jnp.where((distance >= 0) & (distance <= reach), 0.0, NEG_FILL)


def attn_kernel(
    q_ref, key_ref, val_ref, pos_ref, tok_ref, wot_ref, gains_ref,
    ctx_ref, lse_ref, branch_ref, res_ref, fin_ref,
):
    head_dim = key_ref.shape[2]
    head_count = q_ref.shape[1] // head_dim
    span = WINDOW + TILE
    lane = lax.broadcasted_iota(jnp.int32, (TILE, 128), 1)
    for tile in range(q_ref.shape[0] // TILE):
        query = stacked(q_ref, tile, head_count, head_dim)
        key = key_ref[0, tile * TILE : tile * TILE + span, :]
        value = val_ref[0, tile * TILE : tile * TILE + span, :]
        score = mm(query, key, NT).reshape(head_count, TILE, span) + mask_of(pos_ref, tile, span)
        largest = jnp.max(score, axis=-1, keepdims=True)
        expo = jnp.exp(score - largest)
        total = jnp.sum(expo, axis=-1, keepdims=True)
        low = expo.astype(bf16).reshape(head_count * TILE, span)
        context = mm(low, value).reshape(head_count, TILE, head_dim) / total
        log_total = largest + jnp.log(total)
        kept = jnp.zeros((TILE, 128), f32)
        for h in range(head_count):
            ctx_ref[tile * TILE : (tile + 1) * TILE, h * head_dim : (h + 1) * head_dim] = context[
                h
            ].astype(bf16)
            kept = jnp.where(lane == h, log_total[h], kept)
        lse_ref[tile * TILE : (tile + 1) * TILE, :] = kept
    branch = mm(ctx_ref[...], wot_ref[...], NT)
    branch_ref[...] = branch
    residual = tok_ref[...].astype(f32) + branch * inv_rms(branch) * gains_ref[1:2, :]
    res_ref[...] = residual
    fin_ref[...] = (residual * inv_rms(residual) * gains_ref[2:3, :]).astype(bf16)


def ffn_kernel(
    held_ref, order_ref, res_ref, fin_ref, cot_ref, branch_ref, ctx_ref, wot_ref, gains_ref, *refs
):
    pieces = order_ref.shape[0] - refs[0].shape[0]
    packs, refs = refs[:pieces], refs[pieces:]
    out_ref, gres_ref, gctx_ref, gain_ref = refs[:4]
    gate_sent, gate_kept, down_sent, down_kept = refs[4:8]
    slope_ref, act_ref, gate_ref, up_ref, down_ref, stage_ref, copied = refs[8:15]
    hid_ref, gg_ref, gu_ref, in_left, ffn_left, attn_left, turn_ref = refs[15:]
    chunks, _, tile = packs[0].shape
    width = res_ref.shape[1]
    count = hid_ref.shape[0]
    quarter, strip, half = width // chunks, width // pieces, pieces // 2
    step = pl.program_id(0)
    tiles = count // FFN_ROWS
    post_attn, pre_ffn, post_ffn = [gains_ref[i : i + 1, :] for i in (1, 2, 3)]

    def aligned(index, size):
        return pl.ds(pl.multiple_of(index * size, size), size)

    @pl.when(step == 0)
    def _():
        gain_ref[...] = jnp.zeros_like(gain_ref)

        def staged(m):
            return pltpu.make_async_copy(packs[m], stage_ref.at[m % 2], copied.at[m % 2])

        staged(0).start()
        for m in range(pieces):
            if m + 1 < pieces:
                staged(m + 1).start()
            staged(m).wait()
            s = held_ref[m]
            for c in range(chunks):
                z = held_ref[pieces + c]
                own, cols = aligned(z, quarter), aligned(s, tile)
                gate_ref[own, cols] = stage_ref[m % 2, c, :quarter, :]
                up_ref[own, cols] = stage_ref[m % 2, c, quarter : 2 * quarter, :]
                for i in range(2):
                    begin = 2 * quarter + i * strip
                    down_ref[aligned(s, strip), aligned(2 * z + i, tile)] = stage_ref[
                        m % 2, c, begin : begin + strip, :
                    ]

    @pl.when(step < tiles)
    def _():
        own = aligned(step, FFN_ROWS)

        def turn(left_ref, source, size, first, number):
            turn_ref[...] = source.T
            for m in range(number):
                left_ref[m * size : (m + 1) * size, own] = turn_ref[
                    aligned(order_ref[first + m], size), :
                ]

        ffn_in = fin_ref[...]
        turn(in_left, ffn_in, quarter, pieces, chunks)
        gate = mm(ffn_in, gate_ref[...])
        up = mm(ffn_in, up_ref[...])
        square = gate * gate
        bent = jnp.tanh(GELU_C * gate * (1.0 + GELU_K * square))
        half_bent = 0.5 * (1.0 + bent)
        act = gate * half_bent
        slope = half_bent + 0.5 * gate * (1.0 - bent * bent) * (
            GELU_C * (1.0 + 3.0 * GELU_K * square)
        )
        act_ref[...] = act
        slope_ref[...] = slope * up
        hidden = (act * up).astype(bf16)
        hid_ref[own, :] = hidden
        branch = mm(hidden, down_ref[...], NT)
        residual = res_ref[...]
        cot = cot_ref[...].astype(f32)
        inv = inv_rms(branch)
        out_ref[...] = (residual + branch * inv * post_ffn).astype(bf16)
        g_ffn, gain_post = norm_back(branch, inv, post_ffn, cot)
        g_low = g_ffn.astype(bf16)
        turn(ffn_left, g_low, strip, 0, pieces)
        g_hidden = mm(g_low, down_ref[...])
        g_gate = (g_hidden * slope_ref[...]).astype(bf16)
        g_up = (g_hidden * act_ref[...]).astype(bf16)
        gg_ref[own, :] = g_gate
        gu_ref[own, :] = g_up
        g_in = mm(g_gate, gate_ref[...], NT) + mm(g_up, up_ref[...], NT)
        back, gain_pre = norm_back(residual, inv_rms(residual), pre_ffn, g_in)
        g_res = cot + back
        gres_ref[...] = g_res
        attn_branch = branch_ref[...]
        g_attn, gain_attn = norm_back(attn_branch, inv_rms(attn_branch), post_attn, g_res)
        g_attn = g_attn.astype(bf16)
        turn(attn_left, g_attn, strip, 0, pieces)
        gctx_ref[...] = mm(g_attn, wot_ref[...]).astype(bf16)
        gain_ref[0:1, :] += jnp.sum(gain_post, axis=0, keepdims=True)
        gain_ref[1:2, :] += jnp.sum(gain_pre, axis=0, keepdims=True)
        gain_ref[2:3, :] += jnp.sum(gain_attn, axis=0, keepdims=True)

    @pl.when(step >= tiles)
    def _():
        k = step - tiles
        cols = aligned(order_ref[k], tile)
        z = order_ref[pieces + k // 2]
        both = mm(in_left[...], jnp.concatenate([gg_ref[:, cols], gu_ref[:, cols]], axis=1))
        both = both.astype(bf16)
        for i in range(2):
            part = both[:, i * tile : (i + 1) * tile].reshape(chunks, quarter, tile)
            for inside, out in ((k < half, gate_sent), (k >= half, gate_kept)):

                @pl.when(inside)
                def _(out=out, part=part, i=i):
                    out[0, :, i * quarter : (i + 1) * quarter, :] = part

        def put(begin, part):
            part = part.astype(bf16).reshape(pieces, strip, tile)
            down_sent[:, 0, pl.ds(begin, strip), :] = part[:half]
            down_kept[:, 0, pl.ds(begin, strip), :] = part[half:]

        put(
            pl.multiple_of(k % 2 * strip, strip),
            mm(ffn_left[...], hid_ref[:, aligned(2 * z + k % 2, tile)]),
        )

        @pl.when(k % 2 == 0)
        def _():
            put(2 * strip, mm(attn_left[...], ctx_ref[:, aligned(z, tile)]))


def turn_strips(left_ref, source, strip, where, count):
    left_ref[1] = source.T
    for m in range(count):
        begin = pl.multiple_of(where(m) * strip, 16)
        left_ref[0, m * strip : (m + 1) * strip, :] = left_ref[1, pl.ds(begin, strip), :]


def attn_grad_kernel(base, order_ref, _, attn_ref, gq_ref, gkv_ref, sort_ref, *refs):
    recv_ref = refs[0] if base else None
    outs = refs[1:3] if base else refs[:1]
    left = refs[-1]
    held, chunks, quarter, _ = outs[0].shape
    width = attn_ref.shape[1]
    pieces = order_ref.shape[0] - chunks
    half = pieces // 2
    turn_strips(left, attn_ref[...], quarter, lambda m: order_ref[pieces + m], chunks)
    sorted_kv = mm(gkv_ref[...], sort_ref[...]).astype(bf16)
    part_kv = mm(left[0], sorted_kv)
    wide = part_kv.shape[1] // half
    for pair in range(0, half, 2):
        both = jnp.concatenate(
            [
                gq_ref[:, pl.ds(pl.multiple_of(order_ref[base + pair + i] * 128, 128), 128)]
                for i in range(2)
            ],
            axis=1,
        )
        part = mm(left[0], both)
        for i in range(2):
            m = pair + i
            value = part[:, i * 128 : (i + 1) * 128].reshape(chunks, quarter, 128)
            value_kv = part_kv[:, m * wide : (m + 1) * wide].reshape(chunks, quarter, wide)
            if base:
                value = value + recv_ref[m, :, :, :128].astype(f32)
                value_kv = value_kv + recv_ref[m, :, :, 128:].astype(f32)
            out = outs[m // held]
            out[m % held, :, :, :128] = value.astype(bf16)
            out[m % held, :, :, 128:] = value_kv.astype(bf16)


def attn_back_kernel(
    _, q_ref, gctx_ref, key_ref, val_ref, pos_ref, lse_ref, qraw_ref, cos_ref, sin_ref, head_ref,
    gq_ref, far_ref, near_ref, gain_ref, gkey_ref, gval_ref,
):
    head_dim = key_ref.shape[2]
    head_count = q_ref.shape[1] // head_dim
    block = q_ref.shape[0]
    span = WINDOW + TILE
    scaling = head_dim ** (-0.5)

    @pl.when(pl.program_id(0) == 0)
    def _():
        gain_ref[...] = jnp.zeros_like(gain_ref)

    gkey_ref[...] = jnp.zeros_like(gkey_ref)
    gval_ref[...] = jnp.zeros_like(gval_ref)
    gain = jnp.zeros((1, head_dim), f32)
    for tile in range(block // TILE):
        own = slice(tile * TILE, (tile + 1) * TILE)
        reach = slice(tile * TILE, tile * TILE + span)
        query = stacked(q_ref, tile, head_count, head_dim)
        g_ctx = stacked(gctx_ref, tile, head_count, head_dim)
        key = key_ref[0, reach, :]
        value = val_ref[0, reach, :]
        log_total = jnp.stack([lse_ref[own, h : h + 1] for h in range(head_count)])
        score = mm(query, key, NT).reshape(head_count, TILE, span) + mask_of(pos_ref, tile, span)
        probs = jnp.exp(score - log_total)
        g_probs = mm(g_ctx, value, NT).reshape(head_count, TILE, span)
        spread = jnp.sum(g_probs * probs, axis=-1, keepdims=True)
        g_score = (probs * (g_probs - spread)).astype(bf16).reshape(head_count * TILE, span)
        low = probs.astype(bf16).reshape(head_count * TILE, span)
        gkey_ref[reach, :] += mm(g_score, query, TN)
        gval_ref[reach, :] += mm(low, g_ctx, TN)
        g_rot = mm(g_score, key) * scaling
        turned = slice(block + tile * TILE, block + (tile + 1) * TILE)
        cosine, sine = cos_ref[turned, :], sin_ref[turned, :]
        for h in range(head_count):
            cols = slice(h * head_dim, (h + 1) * head_dim)
            raw = qraw_ref[own, cols]
            back, share = norm_back(
                raw,
                inv_rms(raw),
                head_ref[0:1, :],
                rope_back(g_rot[h * TILE : (h + 1) * TILE], cosine, sine),
            )
            gq_ref[own, cols] = back.astype(bf16)
            gain += jnp.sum(share, axis=0, keepdims=True)
    gain_ref[0:1, :] += gain
    far_ref[0, :, :head_dim] = rope_back(
        gkey_ref[:block, :], cos_ref[:block, :], sin_ref[:block, :]
    ).astype(bf16)
    far_ref[0, :, head_dim:] = gval_ref[:block, :].astype(bf16)
    near_ref[0, :, :head_dim] = gkey_ref[block:, :]
    near_ref[0, :, head_dim:] = gval_ref[block:, :]


def kv_back_kernel(
    kraw_ref, cos_ref, sin_ref, head_ref, near_ref, recv_ref, _, gkv_ref, kgain_ref
):
    head_dim = head_ref.shape[1]

    @pl.when(pl.program_id(0) == 0)
    def _():
        kgain_ref[...] = jnp.zeros_like(kgain_ref)

    near, far = near_ref[0], recv_ref[0].astype(f32)
    raw = kraw_ref[...]
    g_normed = rope_back(near[:, :head_dim], cos_ref[...], sin_ref[...]) + far[:, :head_dim]
    g_key, share = norm_back(raw, inv_rms(raw), head_ref[1:2, :], g_normed)
    kgain_ref[0:1, :] += jnp.sum(share, axis=0, keepdims=True)
    gkv_ref[:, :head_dim] = g_key.astype(bf16)
    gkv_ref[:, head_dim:] = (near[:, head_dim:] + far[:, head_dim:]).astype(bf16)


def input_kernel(
    _, __, gq_ref, gkv_ref, wq_ref, wkv_ref, tok_ref, gres_ref, gains_ref, ffn_gain_ref, kgain_ref,
    qgain_ref, dtok_ref, gain_ref
):
    @pl.when(pl.program_id(0) == 0)
    def _():
        gain_ref[...] = jnp.zeros_like(gain_ref)
        head_dim = kgain_ref.shape[1]
        gain_ref[1:4, :] = ffn_gain_ref[0:3, :]
        gain_ref[4:5, :head_dim] = qgain_ref[0:1, :]
        gain_ref[4:5, head_dim : 2 * head_dim] = kgain_ref[0:1, :]

    g_in = mm(gq_ref[...], wq_ref[...], NT) + mm(gkv_ref[...], wkv_ref[...], NT)
    token = tok_ref[...].astype(f32)
    back, share = norm_back(token, inv_rms(token), gains_ref[0:1, :], g_in)
    dtok_ref[...] = (gres_ref[...] + back).astype(bf16)
    gain_ref[0:1, :] += jnp.sum(share, axis=0, keepdims=True)


def passed_along(shard, axis, by):
    length = lax.axis_size(axis)
    pairs = [(i, i + by) for i in range(length) if 0 <= i + by < length]
    return lax.ppermute(shard, axis, pairs)


def swapped(array, axis, even, odd):
    length = lax.axis_size(axis)
    return lax.ppermute(array, axis, [(i, i ^ (odd if i % 2 else even)) for i in range(length)])


def tables(block, head_dim):
    half_width = head_dim // 2
    frequency = ROPE_BASE ** (-(np.arange(half_width) * 2.0) / head_dim)
    angles = np.arange(-block, block)[:, None] * frequency
    return np.cos(angles).astype(np.float32), np.sin(angles).astype(np.float32)


def column_piece(array, axis_name, parts):
    wide = array.shape[1] // parts
    return lax.dynamic_slice_in_dim(array, lax.axis_index(axis_name) * wide, wide, 1)


def halves(array):
    if isinstance(array, tuple):
        return tuple(zip(*(halves(part) for part in array)))
    half = array.shape[0] // 2
    return (array[:half], array[half:]) if half > 1 else (array[0], array[1])


def total(terms):
    laid = [term for term in terms if isinstance(term, tuple)]
    terms = [term for term in terms if not isinstance(term, tuple)]
    if laid:
        terms.insert(0, jnp.concatenate([total(list(parts)) for parts in zip(*laid)], axis=-2))
    result = terms[0].astype(f32)
    for term in terms[1:]:
        result = result + term.astype(f32)
    return result


HELD = [0, 4, 2, 6, 1, 3, 5, 7]
HELD_Z = [0, 2, 1, 3]


def linked(*chains):
    arrays, steps = [], []
    for chain in chains:
        send, keep = chain if isinstance(chain, tuple) else (chain, [])
        arrays.append([send] + [array for array, _ in keep])
        steps.append([begin for _, begin in keep])
    arrays = lax.optimization_barrier(arrays)
    result = []
    for chain, (send, *keep), begins in zip(chains, arrays, steps):
        result.append((send, list(zip(keep, begins))) if isinstance(chain, tuple) else send)
    return result


class Exchange:
    def __init__(self, seqs, chunks):
        self.direct = seqs == 8 and chunks == 4
        if not self.direct:
            self.order = jnp.arange(12, dtype=jnp.int32) % 8
            self.held = jnp.array(HELD + HELD_Z, jnp.int32)
            return
        s, z = lax.axis_index("seq"), lax.axis_index("fsdp")
        odd = s % 2 == 1
        one, two = jnp.where(odd, 4, 2), jnp.where(odd, 2, 4)
        zero = jnp.zeros_like(s)
        sent = [one | two | 1, two | 1, one | 1, zero | 1]
        kept = [one | two, one, two, zero]
        order = [s ^ k for k in sent + kept] + [z ^ k for k in (3, 1, 2, 0)]
        self.order = jnp.stack(order).astype(jnp.int32)
        held = [zero, two, one, one | two, zero | 1, one | 1, two | 1, one | two | 1]
        held = [s ^ k for k in held] + [z ^ k for k in HELD_Z]
        self.held = jnp.stack(held).astype(jnp.int32)

    def along_step(self, held, bits):
        return jnp.concatenate([held, swapped(held, "fsdp", bits, bits)], axis=0)

    def second(self, piece):
        return swapped(piece, "seq", 4, 2)

    def first(self, piece):
        return swapped(piece, "seq", 2, 4)

    def swap_cores(self, parts):
        return swapped(parts, "seq", 1, 1)

    def fold(self, send, keep, step):
        if step < 3:
            got = swapped(send, "seq", *((1, 1), (2, 4), (4, 2))[step])
        else:
            got = swapped(send, "fsdp", step - 2, step - 2)
        return self.split(keep + [(got, step)], step)

    def split(self, terms, step):
        rest = []
        for array, begin in terms:
            for done in range(begin, step):
                array = halves(array)[1]
            rest.append(array)
        if step == 4:
            return total(rest)
        return total([halves(array)[0] for array in rest]).astype(bf16), terms

    def hop_terms(self, send, keep):
        keep = keep + [(swapped(send, "seq", 4, 2), 2)]
        rest = []
        for array, begin in keep:
            for done in range(begin, 2):
                array = halves(array)[1]
            rest.append(array)
        parts = [total([array[p] for array in rest]) for p in range(4)]
        return [part.astype(bf16) for part in parts[:3]] + [parts[3]]

    def last(self, *parts):
        got = [swapped(part, "fsdp", bits, bits) for part, bits in zip(parts, (3, 1, 2))]
        return total([parts[3]] + got)

    def hop(self, value, axis, bits):
        got = [swapped(value, axis, b, b) for b in bits]
        if len(bits) == 1:
            return value + got[0]
        both = bits[0] | bits[1]
        return (value + got[0]) + (got[1] + swapped(value, axis, both, both))


def scattered_plain(part):
    columns = lax.psum_scatter(part, "seq", scatter_dimension=1, tiled=True)
    return lax.psum_scatter(columns, "fsdp", scatter_dimension=0, tiled=True).astype(f32)


def gather_weights(w_query, w_key, w_value, w_out, w_gate, w_up, w_down, halo, exchange):
    pieces = w_gate.shape[1] // FF_TILE
    width = w_out.shape[1]
    if exchange.direct:
        down = column_piece(w_down, "seq", pieces).T
        ffn = jnp.concatenate(
            [
                column_piece(w_gate, "seq", pieces),
                column_piece(w_up, "seq", pieces),
                down[:, :FF_TILE],
                down[:, FF_TILE:],
            ],
            axis=0,
        )
        both = jnp.concatenate([w_key, w_value], axis=1)
        out = column_piece(w_out, "seq", pieces).T
        out = jnp.concatenate([out[:, :128], out[:, 128:]], axis=0)
        attn = jnp.concatenate(
            [column_piece(w_query, "seq", pieces), out, column_piece(both, "seq", pieces)], axis=1
        )
        attn = exchange.along_step(exchange.along_step(attn[None], 2), 1)
        ffn, attn = lax.optimization_barrier((ffn, attn))
        ffn = exchange.along_step(ffn[None], 2)
        attn, halo = lax.optimization_barrier((attn, halo))
        two, one = exchange.second(attn), exchange.first(attn)
        ffn, two = lax.optimization_barrier((ffn, two))
        ffn = exchange.along_step(ffn, 1)
        attn = [attn, two, one, exchange.first(two)]
        attn[3], ffn = lax.optimization_barrier((attn[3], ffn))
        return attn + [exchange.swap_cores(held) for held in attn], ffn, halo
    w_query, w_key, w_value, w_out, w_gate, w_up, w_down = [
        lax.all_gather(w, "fsdp", axis=0, tiled=True)
        for w in (w_query, w_key, w_value, w_out, w_gate, w_up, w_down)
    ]
    chunks = w_down.shape[0] // (2 * FF_TILE)
    quarter, strip = width // chunks, width // pieces

    def columns(weight):
        return weight.reshape(chunks, quarter, pieces, -1).transpose(2, 0, 1, 3)

    def turned(weight):
        shape = (pieces, strip, chunks, 2, weight.shape[0] // (2 * chunks))
        turned_part = weight.T.reshape(shape).transpose(0, 2, 3, 1, 4)
        return turned_part.reshape(pieces, chunks, 2 * strip, -1)

    both = jnp.concatenate([w_key, w_value], axis=1)
    attn = jnp.concatenate([columns(w_query), turned(w_out), columns(both)], axis=3)
    ffn = jnp.concatenate([columns(w_gate), columns(w_up), turned(w_down)], axis=2)
    def listed(pack):
        pack = jnp.take(jnp.take(pack, np.array(HELD), axis=0), np.array(HELD_Z), axis=1)
        return [pack[m] for m in range(pieces)]

    return listed(attn), listed(ffn), halo


def plain_gradients(part_gate, part_down, part_attn):
    pieces, quarters, double, _ = part_gate.shape
    width = quarters * double // 2
    strip = width // pieces

    def columns(parts):
        return parts.transpose(1, 2, 0, 3).reshape(width, -1)

    def turned(parts):
        parts = parts.reshape(pieces, quarters, -1, strip, FF_TILE).transpose(1, 2, 4, 0, 3)
        return parts.reshape(-1, width)

    each = part_attn.shape[3] - (part_attn.shape[3] - 128) // 2
    return tuple(
        scattered_plain(part)
        for part in (
            columns(part_attn[..., :128]),
            columns(part_attn[..., 128:each]),
            columns(part_attn[..., each:]),
            turned(part_down[:, :, 2 * strip :]),
            columns(part_gate[:, :, : double // 2]),
            columns(part_gate[:, :, double // 2 :]),
            turned(part_down[:, :, : 2 * strip]),
        )
    )


def split_gradients(ffn, attn):
    quarter = attn.shape[0]
    gate, down = ffn[: 2 * quarter], ffn[2 * quarter :]
    strip = down.shape[0] // 3
    each = attn.shape[1] - (attn.shape[1] - 128) // 2
    return (
        attn[:, :128],
        attn[:, 128:each],
        attn[:, each:],
        down[2 * strip :].T,
        gate[:quarter],
        gate[quarter:],
        jnp.concatenate([down[:strip].T, down[strip : 2 * strip].T], axis=0),
    )


def body(
    tokens, doc_starts, w_query, w_key, w_value, w_out, w_gate, w_up, w_down,
    pre_attn, post_attn, pre_ffn, post_ffn, query_norm, key_norm, cotangent,
):
    seq_dev, block, width = tokens.shape
    head_dim = w_key.shape[1]
    inner = w_query.shape[1]
    hidden_dim = w_gate.shape[1]
    count = seq_dev * block
    seqs, chunks = lax.axis_size("seq"), lax.axis_size("fsdp")
    exchange = Exchange(seqs, chunks)
    far_tokens = passed_along(tokens, "seq", 1).reshape(count, width)
    far_starts = passed_along(doc_starts, "seq", 1)
    pack, ffn_pack, (far_tokens, far_starts) = gather_weights(
        w_query, w_key, w_value, w_out, w_gate, w_up, w_down, (far_tokens, far_starts), exchange
    )
    starts = jnp.concatenate([far_starts, doc_starts], axis=1)
    indices = jnp.arange(2 * block, dtype=jnp.int32)
    latest = lax.cummax(jnp.where(starts == 1, indices[None, :], -WINDOW), axis=1)
    reach = jnp.minimum(indices[None, :] - latest, WINDOW - 1)[:, block:]
    pos_column = reach.reshape(count, 1)
    cosine, sine = tables(block, head_dim)
    own_cosine, own_sine = cosine[block:], sine[block:]

    pieces, quarters = len(pack), pack[0].shape[0]
    quarter, strip = width // quarters, width // pieces
    gains = jnp.stack([pre_attn, post_attn, pre_ffn, post_ffn])
    head_gains = jnp.stack([query_norm, key_norm])
    tokens_2d = tokens.reshape(count, width)
    cot_2d = cotangent.reshape(count, width)

    tok_spec = rows(block, width)
    table_spec = whole((2 * block, head_dim // 2))
    half_spec = whole((block, head_dim // 2))
    key_spec = pl.BlockSpec((1, 2 * block, head_dim), lambda i: (i, 0, 0))
    gains_spec, head_spec = whole((4, width)), whole((2, head_dim))
    wq_spec, wkv_spec, wot_spec = (
        whole((width, inner)),
        whole((width, 2 * head_dim)),
        whole((width, inner)),
    )
    smem = pl.BlockSpec(memory_space=pltpu.SMEM)
    remain = pl.BlockSpec(memory_space=pl.ANY)
    attn_low, query_raw, query_rot, key_raw, keys, values, full_q, full_kv, full_ot = (
        pl.pallas_call(
            qkv_kernel,
            grid=(seq_dev,),
            in_specs=[smem, tok_spec, tok_spec, table_spec, table_spec]
            + [gains_spec, head_spec]
            + [whole(pack[0].shape)] * pieces,
            out_specs=[
                tok_spec,
                rows(block, inner),
                rows(block, inner),
                rows(block, head_dim),
                key_spec,
                key_spec,
                wq_spec,
                wkv_spec,
                wot_spec,
            ],
            out_shape=[
                shaped((count, width), bf16),
                shaped((count, inner), f32),
                shaped((count, inner), bf16),
                shaped((count, head_dim), f32),
                shaped((seq_dev, 2 * block, head_dim), bf16),
                shaped((seq_dev, 2 * block, head_dim), bf16),
                shaped((width, inner), bf16),
                shaped((width, 2 * head_dim), bf16),
                shaped((width, inner), bf16),
            ],
            compiler_params=params(),
            name="project_rotate",
        cost_estimate=cost(11),
        )(
            exchange.held, tokens_2d, far_tokens, cosine, sine, gains, head_gains,
            *pack,
        )
    )
    if exchange.direct:
        own, two = ffn_pack, exchange.second(ffn_pack)
        own_swapped = exchange.swap_cores(own)
        again, two, keys = lax.optimization_barrier((own, two, keys))
        one, both, two_swapped = exchange.first(again), exchange.first(two), exchange.swap_cores(two)
    context, log_total, attn_branch, residual, ffn_in = pl.pallas_call(
        attn_kernel,
        grid=(seq_dev,),
        in_specs=[rows(block, inner), key_spec, key_spec, rows(block, 1), tok_spec]
        + [wot_spec, gains_spec],
        out_specs=[rows(block, inner), rows(block, 128), tok_spec, tok_spec, tok_spec],
        out_shape=[
            shaped((count, inner), bf16),
            shaped((count, 128), f32),
            shaped((count, width), f32),
            shaped((count, width), f32),
            shaped((count, width), bf16),
        ],
        compiler_params=params(),
        name="window_attention",
        cost_estimate=cost(12),
    )(query_rot, keys, values, pos_column, tokens_2d, full_ot, gains)

    if exchange.direct:
        one, both, ffn_in = lax.optimization_barrier((one, both, ffn_in))
        ffn_pack = [own, two, one, both, own_swapped, two_swapped]
        ffn_pack += [exchange.swap_cores(one), exchange.swap_cores(both)]

    half = pieces // 2
    tiles = count // FFN_ROWS

    def small(wide):
        return pl.BlockSpec((FFN_ROWS, wide), lambda i: (jnp.minimum(i, tiles - 1), 0))

    def once(shape):
        return pl.BlockSpec(
            shape, lambda *_: (0,) * len(shape), pipeline_mode=pl.Buffered(buffer_count=1)
        )

    gate_shape = (half, quarters, 2 * quarter, FF_TILE)
    down_shape = (half, quarters, 3 * strip, FF_TILE)

    def gate_spec(first):
        return pl.BlockSpec(
            (1,) + gate_shape[1:],
            lambda i: (jnp.clip(i - tiles - first, 0, half - 1), 0, 0, 0),
        )

    down_spec = pl.BlockSpec(
        (half, 1) + down_shape[2:], lambda i: (0, jnp.clip(i - tiles, 0, pieces - 1) // 2, 0, 0)
    )
    turned = pltpu.VMEM((width, count), bf16)
    weight = pltpu.VMEM((width, hidden_dim), bf16)
    middle = pltpu.VMEM((count, hidden_dim), bf16)
    gelu_parts = pltpu.VMEM((FFN_ROWS, hidden_dim), f32)
    layer_out, g_res, g_ctx, ffn_gains, *ffn_parts = pl.pallas_call(
        ffn_kernel,
        grid=(tiles + pieces,),
        in_specs=[smem, smem, small(width), small(width), small(width), small(width)]
        + [once((count, inner)), once((width, inner)), gains_spec]
        + [remain] * pieces,
        out_specs=[small(width), small(width), small(inner), whole((8, width))]
        + [gate_spec(0), gate_spec(half), down_spec, down_spec],
        out_shape=[
            shaped((count, width), bf16),
            shaped((count, width), f32),
            shaped((count, inner), bf16),
            shaped((8, width), f32),
            shaped(gate_shape, bf16),
            shaped(gate_shape, bf16),
            shaped(down_shape, bf16),
            shaped(down_shape, bf16),
        ],
        scratch_shapes=[gelu_parts, gelu_parts, weight, weight, weight]
        + [pltpu.VMEM((2,) + ffn_pack[0].shape, bf16), pltpu.SemaphoreType.DMA((2,))]
        + [middle, middle, middle, turned, turned, turned]
        + [pltpu.VMEM((width, FFN_ROWS), bf16)],
        compiler_params=params(62),
        name="feed_forward",
        cost_estimate=cost(60),
    )(
        exchange.held, exchange.order, residual, ffn_in, cot_2d, attn_branch, context, full_ot,
        gains, *ffn_pack,
    )
    gate_sent, gate_kept, down_sent, down_kept = ffn_parts
    gate, down = (gate_sent, gate_kept), (down_sent, down_kept)
    if exchange.direct:
        gate_got, down_got = swapped(gate_sent, "seq", 1, 1), swapped(down_sent, "seq", 1, 1)


    ffn = ffn_parts
    if exchange.direct:
        kept, got = (gate_kept, down_kept), (gate_got, down_got)
        ffn = exchange.split([(kept, 0), (got, 0)], 0)

    pair = pl.BlockSpec((1, block, 2 * head_dim), lambda i: (i, 0, 0))
    g_query, g_far, g_near, query_gain = pl.pallas_call(
        attn_back_kernel,
        grid=(seq_dev,),
        in_specs=[remain, rows(block, inner), rows(block, inner), key_spec, key_spec]
        + [rows(block, 1), rows(block, 128), rows(block, inner), table_spec, table_spec]
        + [head_spec],
        out_specs=[rows(block, inner), pair, pair, whole((8, head_dim))],
        out_shape=[
            shaped((count, inner), bf16),
            shaped((seq_dev, block, 2 * head_dim), bf16),
            shaped((seq_dev, block, 2 * head_dim), f32),
            shaped((8, head_dim), f32),
        ],
        scratch_shapes=[
            pltpu.VMEM((2 * block, head_dim), f32),
            pltpu.VMEM((2 * block, head_dim), f32),
        ],
        compiler_params=params(),
        name="attention_gradient",
        cost_estimate=cost(16),
    )(
        ffn[0], query_rot, g_ctx, keys, values, pos_column, log_total, query_raw, cosine, sine,
        head_gains,
    )
    g_recv = passed_along(g_far, "seq", -1)
    early = ffn
    if exchange.direct:
        ffn = early = exchange.fold(*ffn, 1)
    g_kv, key_gain = pl.pallas_call(
        kv_back_kernel,
        grid=(seq_dev,),
        in_specs=[rows(block, head_dim), half_spec, half_spec, head_spec]
        + [pair, pair, remain],
        out_specs=[rows(block, 2 * head_dim), whole((8, head_dim))],
        out_shape=[shaped((count, 2 * head_dim), bf16), shaped((8, head_dim), f32)],
        compiler_params=params(),
        name="key_value_back",
        cost_estimate=cost(4),
    )(key_raw, own_cosine, own_sine, head_gains, g_near, g_recv, early[0])

    each = head_dim // pieces
    column = jnp.arange(2 * head_dim, dtype=jnp.int32)
    inside = column % (2 * each)
    source = jnp.where(inside < each, inside, inside - each + head_dim)
    source = source + each * jnp.repeat(exchange.order[:pieces], 2 * each)
    sort = (column[:, None] == source[None, :]).astype(bf16)

    def attn_parts(base, before, extra):
        shape = (half, quarters, quarter, 128 + 2 * each)
        sent = (half // 2,) + shape[1:]
        outs = [shape] if base == 0 else [sent, sent]
        vmem = pl.BlockSpec(memory_space=pltpu.VMEM)
        chosen = sort[:, base * 2 * each : (base + half) * 2 * each]
        return pl.pallas_call(
            lambda *refs: attn_grad_kernel(base, *refs),
            in_specs=[smem, remain] + [vmem] * (4 + len(extra)),
            out_specs=[vmem] * len(outs),
            out_shape=[shaped(o, bf16) for o in outs],
            scratch_shapes=[pltpu.VMEM((2, width, count), bf16)],
            compiler_params=params(),
            cost_estimate=cost(6),
            name="attn_gradients_kept" if base else "attn_gradients_sent",
        )(exchange.order, before, attn_low, g_query, g_kv, chosen, *extra)

    (attn_sent,) = attn_parts(0, early[0], [])
    attn_got = exchange.swap_cores(attn_sent) if exchange.direct else jnp.zeros_like(attn_sent)
    if exchange.direct:
        ffn = exchange.fold(*ffn, 2)
    attn_parts_kept = attn_parts(half, ffn[0], [attn_got])
    attn = attn_parts_kept[0], [(attn_parts_kept[1], 1)]
    if exchange.direct:
        ffn, attn = linked(exchange.fold(*ffn, 3), exchange.fold(*attn, 1))
    dtokens, sums = pl.pallas_call(
        input_kernel,
        grid=(seq_dev,),
        in_specs=[remain, remain, rows(block, inner), rows(block, 2 * head_dim)]
        + [wq_spec, wkv_spec]
        + [tok_spec, tok_spec, gains_spec, whole((8, width))]
        + [whole((8, head_dim))] * 2,
        out_specs=[tok_spec, whole((8, width))],
        out_shape=[shaped((count, width), bf16), shaped((8, width), f32)],
        compiler_params=params(),
        name="input_gradient",
        cost_estimate=cost(7),
    )(ffn[0], attn[0], g_query, g_kv, full_q, full_kv, tokens_2d, g_res, gains, ffn_gains, key_gain, query_gain)

    if exchange.direct:
        attn = exchange.hop_terms(*attn)
        sums = exchange.hop(sums, "seq", (1,))
        *attn, sums = linked(*attn, sums)
        attn = exchange.last(*attn)
        sums = exchange.hop(sums, "seq", (2, 4))
        ffn = exchange.fold(*ffn, 4)
        ffn, attn, sums = linked(ffn, attn, sums)
        sums = exchange.hop(sums, "fsdp", (1, 2))
        weights = split_gradients(ffn, attn)
    else:
        weights = plain_gradients(
            jnp.concatenate(gate, axis=0),
            jnp.concatenate(down, axis=0),
            jnp.concatenate([attn_sent, *attn_parts_kept], axis=0),
        )
        sums = lax.psum(sums, ("seq", "fsdp"))
    gain_sums = (sums[0], sums[3], sums[2], sums[1])
    gain_sums += (sums[4, :head_dim], sums[4, head_dim : 2 * head_dim])
    shape = (seq_dev, block, width)
    return (layer_out.reshape(shape), dtokens.reshape(shape)) + weights + gain_sums


def solution(mesh):
    sharded = P("fsdp", "seq", None)
    weight = P("fsdp", None)
    in_specs = (sharded, P("fsdp", "seq")) + (weight,) * 7 + (P(),) * 6 + (sharded,)
    out_specs = (sharded, sharded) + (P("fsdp", "seq"),) * 7 + (P(),) * 6
    return jax.shard_map(body, mesh=mesh, in_specs=in_specs, out_specs=out_specs, check_vma=False)
```

```python
import jax
import jax.numpy as jnp
import numpy as np
from jax import lax
from jax.experimental import pallas as pl
from jax.experimental.pallas import tpu as pltpu
from jax.sharding import PartitionSpec as P

WINDOW = 512
TILE = 128
FF_TILE = 256
FFN_ROWS = 256

epsilon = 1e-06
NEG_FILL = -1e30
ROPE_BASE = 10000.0
GELU_C = 0.7978845608028654
GELU_K = 0.044715

f32 = jnp.float32
bf16 = jnp.bfloat16

NN = (((1,), (0,)), ((), ()))
NT = (((1,), (1,)), ((), ()))
TN = (((0,), (0,)), ((), ()))


def mm(left, right, dims=NN):
    return lax.dot_general(left, right, dims, preferred_element_type=f32)


def inv_rms(vector):
    return lax.rsqrt(jnp.mean(vector * vector, axis=-1, keepdims=True) + epsilon)


def norm_back(vector, inv, gain, grad):
    unit = vector * inv
    scaled = gain * grad
    back = inv * (scaled - unit * jnp.mean(unit * scaled, axis=-1, keepdims=True))
    return back, grad * unit


def rope(vector, cosine, sine):
    half = vector.shape[-1] // 2
    one, two = vector[:, :half], vector[:, half:]
    return jnp.concatenate([one * cosine - two * sine, two * cosine + one * sine], axis=1)


def rope_back(vector, cosine, sine):
    half = vector.shape[-1] // 2
    one, two = vector[:, :half], vector[:, half:]
    return jnp.concatenate([one * cosine + two * sine, two * cosine - one * sine], axis=1)


def params(limit_mib=58):
    return pltpu.CompilerParams(vmem_limit_bytes=limit_mib * 1024 * 1024)


def cost(microseconds):
    return pl.CostEstimate(
        flops=int(microseconds * 1e9), bytes_accessed=int(microseconds * 3e6), transcendentals=0
    )


def whole(shape):
    return pl.BlockSpec(shape, lambda *_: (0,) * len(shape))


def rows(count, width):
    return pl.BlockSpec((count, width), lambda i: (i, 0))


def shaped(shape, dtype):
    return jax.ShapeDtypeStruct(shape, dtype)


def qkv_kernel(
    held_ref, tok_ref, far_ref, cos_ref, sin_ref, gains_ref, head_ref, *refs
):
    packs = refs[:-9]
    attn_ref, qraw_ref, qrot_ref, kraw_ref, key_ref, val_ref, wq_ref, wkv_ref, wot_ref = refs[-9:]
    head_dim = head_ref.shape[1]
    head_count = wq_ref.shape[1] // head_dim
    block, width = tok_ref.shape
    chunks, chunk_rows, _ = packs[0].shape
    pieces = len(packs)
    half = pieces // 2

    @pl.when(pl.program_id(0) == 0)
    def _():
        strip = chunk_rows // 2
        odd = held_ref[0] % 2 == 1

        def aligned(index, size):
            return pl.ds(pl.multiple_of(index * size, size), size)

        for c in range(chunks):
            z = held_ref[pieces + c]
            own = aligned(z, chunk_rows)
            for m in range(pieces):
                s = held_ref[m]
                wq_ref[own, aligned(s, 128)] = packs[m][c, :, :128]
                turned = packs[m][c, :, 128:256]
                for i in range(2):
                    wot_ref[aligned(s, strip), aligned(2 * z + i, 128)] = turned[
                        i * strip : (i + 1) * strip
                    ]
            for m, mate in zip(range(half), (0, 2, 1, 3)):
                one, two = packs[m][c, :, 256:320], packs[half + mate][c, :, 256:320]
                wkv_ref[own, aligned(held_ref[m] // 2, 128)] = jnp.concatenate(
                    [jnp.where(odd, two, one), jnp.where(odd, one, two)], axis=1
                )

    pre = gains_ref[0:1, :]
    qgain, kgain = head_ref[0:1, :], head_ref[1:2, :]
    token = tok_ref[...].astype(f32)
    low = (token * inv_rms(token) * pre).astype(bf16)
    attn_ref[...] = low
    query = mm(low, wq_ref[...])
    qraw_ref[...] = query
    cosine, sine = cos_ref[block:, :], sin_ref[block:, :]
    scaling = head_dim ** (-0.5)
    for h in range(head_count):
        part = query[:, h * head_dim : (h + 1) * head_dim]
        normed = part * inv_rms(part) * qgain
        qrot_ref[:, h * head_dim : (h + 1) * head_dim] = (
            rope(normed, cosine, sine).astype(bf16) * jnp.asarray(scaling, bf16)
        )
    both = mm(low, wkv_ref[...])
    key = both[:, :head_dim]
    kraw_ref[...] = key
    key_ref[0, block:, :] = rope(key * inv_rms(key) * kgain, cosine, sine).astype(bf16)
    val_ref[0, block:, :] = both[:, head_dim:].astype(bf16)
    token = far_ref[...].astype(f32)
    low = (token * inv_rms(token) * pre).astype(bf16)
    both = mm(low, wkv_ref[...])
    key = both[:, :head_dim]
    key_ref[0, :block, :] = rope(
        key * inv_rms(key) * kgain, cos_ref[:block, :], sin_ref[:block, :]
    ).astype(bf16)
    val_ref[0, :block, :] = both[:, head_dim:].astype(bf16)


def stacked(ref, tile, head_count, head_dim):
    return jnp.concatenate(
        [
            ref[tile * TILE : (tile + 1) * TILE, h * head_dim : (h + 1) * head_dim]
            for h in range(head_count)
        ],
        axis=0,
    )


def mask_of(pos_ref, tile, span):
    reach = pos_ref[tile * TILE : (tile + 1) * TILE, :]
    row = lax.broadcasted_iota(jnp.int32, (TILE, span), 0)
    col = lax.broadcasted_iota(jnp.int32, (TILE, span), 1)
    distance = WINDOW + row - col
    return jnp.where((distance >= 0) & (distance <= reach), 0.0, NEG_FILL)


def attn_kernel(
    q_ref, key_ref, val_ref, pos_ref, tok_ref, wot_ref, gains_ref,
    ctx_ref, lse_ref, branch_ref, res_ref, fin_ref,
):
    head_dim = key_ref.shape[2]
    head_count = q_ref.shape[1] // head_dim
    span = WINDOW + TILE
    lane = lax.broadcasted_iota(jnp.int32, (TILE, 128), 1)
    for tile in range(q_ref.shape[0] // TILE):
        query = stacked(q_ref, tile, head_count, head_dim)
        key = key_ref[0, tile * TILE : tile * TILE + span, :]
        value = val_ref[0, tile * TILE : tile * TILE + span, :]
        score = mm(query, key, NT).reshape(head_count, TILE, span) + mask_of(pos_ref, tile, span)
        largest = jnp.max(score, axis=-1, keepdims=True)
        expo = jnp.exp(score - largest)
        total = jnp.sum(expo, axis=-1, keepdims=True)
        low = expo.astype(bf16).reshape(head_count * TILE, span)
        context = mm(low, value).reshape(head_count, TILE, head_dim) / total
        log_total = largest + jnp.log(total)
        kept = jnp.zeros((TILE, 128), f32)
        for h in range(head_count):
            ctx_ref[tile * TILE : (tile + 1) * TILE, h * head_dim : (h + 1) * head_dim] = context[
                h
            ].astype(bf16)
            kept = jnp.where(lane == h, log_total[h], kept)
        lse_ref[tile * TILE : (tile + 1) * TILE, :] = kept
    branch = mm(ctx_ref[...], wot_ref[...], NT)
    branch_ref[...] = branch
    residual = tok_ref[...].astype(f32) + branch * inv_rms(branch) * gains_ref[1:2, :]
    res_ref[...] = residual
    fin_ref[...] = (residual * inv_rms(residual) * gains_ref[2:3, :]).astype(bf16)


def ffn_kernel(
    held_ref, order_ref, res_ref, fin_ref, cot_ref, branch_ref, ctx_ref, wot_ref, gains_ref, *refs
):
    pieces = order_ref.shape[0] - refs[0].shape[0]
    packs, refs = refs[:pieces], refs[pieces:]
    out_ref, gres_ref, gctx_ref, gain_ref = refs[:4]
    gate_sent, gate_kept, down_sent, down_kept = refs[4:8]
    slope_ref, act_ref, gate_ref, up_ref, down_ref, stage_ref, copied = refs[8:15]
    hid_ref, gg_ref, gu_ref, in_left, ffn_left, attn_left, turn_ref = refs[15:]
    chunks, _, tile = packs[0].shape
    width = res_ref.shape[1]
    count = hid_ref.shape[0]
    quarter, strip, half = width // chunks, width // pieces, pieces // 2
    step = pl.program_id(0)
    tiles = count // FFN_ROWS
    post_attn, pre_ffn, post_ffn = [gains_ref[i : i + 1, :] for i in (1, 2, 3)]

    def aligned(index, size):
        return pl.ds(pl.multiple_of(index * size, size), size)

    @pl.when(step == 0)
    def _():
        gain_ref[...] = jnp.zeros_like(gain_ref)

        def staged(m):
            return pltpu.make_async_copy(packs[m], stage_ref.at[m % 2], copied.at[m % 2])

        staged(0).start()
        for m in range(pieces):
            if m + 1 < pieces:
                staged(m + 1).start()
            staged(m).wait()
            s = held_ref[m]
            for c in range(chunks):
                z = held_ref[pieces + c]
                own, cols = aligned(z, quarter), aligned(s, tile)
                gate_ref[own, cols] = stage_ref[m % 2, c, :quarter, :]
                up_ref[own, cols] = stage_ref[m % 2, c, quarter : 2 * quarter, :]
                for i in range(2):
                    begin = 2 * quarter + i * strip
                    down_ref[aligned(s, strip), aligned(2 * z + i, tile)] = stage_ref[
                        m % 2, c, begin : begin + strip, :
                    ]

    @pl.when(step < tiles)
    def _():
        own = aligned(step, FFN_ROWS)

        def turn(left_ref, source, size, first, number):
            turn_ref[...] = source.T
            for m in range(number):
                left_ref[m * size : (m + 1) * size, own] = turn_ref[
                    aligned(order_ref[first + m], size), :
                ]

        ffn_in = fin_ref[...]
        turn(in_left, ffn_in, quarter, pieces, chunks)
        gate = mm(ffn_in, gate_ref[...])
        up = mm(ffn_in, up_ref[...])
        square = gate * gate
        bent = jnp.tanh(GELU_C * gate * (1.0 + GELU_K * square))
        half_bent = 0.5 * (1.0 + bent)
        act = gate * half_bent
        slope = half_bent + 0.5 * gate * (1.0 - bent * bent) * (
            GELU_C * (1.0 + 3.0 * GELU_K * square)
        )
        act_ref[...] = act
        slope_ref[...] = slope * up
        hidden = (act * up).astype(bf16)
        hid_ref[own, :] = hidden
        branch = mm(hidden, down_ref[...], NT)
        residual = res_ref[...]
        cot = cot_ref[...].astype(f32)
        inv = inv_rms(branch)
        out_ref[...] = (residual + branch * inv * post_ffn).astype(bf16)
        g_ffn, gain_post = norm_back(branch, inv, post_ffn, cot)
        g_low = g_ffn.astype(bf16)
        turn(ffn_left, g_low, strip, 0, pieces)
        g_hidden = mm(g_low, down_ref[...])
        g_gate = (g_hidden * slope_ref[...]).astype(bf16)
        g_up = (g_hidden * act_ref[...]).astype(bf16)
        gg_ref[own, :] = g_gate
        gu_ref[own, :] = g_up
        g_in = mm(g_gate, gate_ref[...], NT) + mm(g_up, up_ref[...], NT)
        back, gain_pre = norm_back(residual, inv_rms(residual), pre_ffn, g_in)
        g_res = cot + back
        gres_ref[...] = g_res
        attn_branch = branch_ref[...]
        g_attn, gain_attn = norm_back(attn_branch, inv_rms(attn_branch), post_attn, g_res)
        g_attn = g_attn.astype(bf16)
        turn(attn_left, g_attn, strip, 0, pieces)
        gctx_ref[...] = mm(g_attn, wot_ref[...]).astype(bf16)
        gain_ref[0:1, :] += jnp.sum(gain_post, axis=0, keepdims=True)
        gain_ref[1:2, :] += jnp.sum(gain_pre, axis=0, keepdims=True)
        gain_ref[2:3, :] += jnp.sum(gain_attn, axis=0, keepdims=True)

    @pl.when(step >= tiles)
    def _():
        k = step - tiles
        cols = aligned(order_ref[k], tile)
        z = order_ref[pieces + k // 2]
        both = mm(in_left[...], jnp.concatenate([gg_ref[:, cols], gu_ref[:, cols]], axis=1))
        both = both.astype(bf16)
        for i in range(2):
            part = both[:, i * tile : (i + 1) * tile].reshape(chunks, quarter, tile)
            for inside, out in ((k < half, gate_sent), (k >= half, gate_kept)):

                @pl.when(inside)
                def _(out=out, part=part, i=i):
                    out[0, :, i * quarter : (i + 1) * quarter, :] = part

        def put(begin, part):
            part = part.astype(bf16).reshape(pieces, strip, tile)
            down_sent[:, 0, pl.ds(begin, strip), :] = part[:half]
            down_kept[:, 0, pl.ds(begin, strip), :] = part[half:]

        put(
            pl.multiple_of(k % 2 * strip, strip),
            mm(ffn_left[...], hid_ref[:, aligned(2 * z + k % 2, tile)]),
        )

        @pl.when(k % 2 == 0)
        def _():
            put(2 * strip, mm(attn_left[...], ctx_ref[:, aligned(z, tile)]))


def turn_strips(left_ref, source, strip, where, count):
    left_ref[1] = source.T
    for m in range(count):
        begin = pl.multiple_of(where(m) * strip, 16)
        left_ref[0, m * strip : (m + 1) * strip, :] = left_ref[1, pl.ds(begin, strip), :]


def attn_grad_kernel(base, order_ref, _, attn_ref, gq_ref, gkv_ref, sort_ref, *refs):
    recv_ref = refs[0] if base else None
    outs = refs[1:3] if base else refs[:1]
    left = refs[-1]
    held, chunks, quarter, _ = outs[0].shape
    width = attn_ref.shape[1]
    pieces = order_ref.shape[0] - chunks
    half = pieces // 2
    turn_strips(left, attn_ref[...], quarter, lambda m: order_ref[pieces + m], chunks)
    sorted_kv = mm(gkv_ref[...], sort_ref[...]).astype(bf16)
    part_kv = mm(left[0], sorted_kv)
    wide = part_kv.shape[1] // half
    for pair in range(0, half, 2):
        both = jnp.concatenate(
            [
                gq_ref[:, pl.ds(pl.multiple_of(order_ref[base + pair + i] * 128, 128), 128)]
                for i in range(2)
            ],
            axis=1,
        )
        part = mm(left[0], both)
        for i in range(2):
            m = pair + i
            value = part[:, i * 128 : (i + 1) * 128].reshape(chunks, quarter, 128)
            value_kv = part_kv[:, m * wide : (m + 1) * wide].reshape(chunks, quarter, wide)
            if base:
                value = value + recv_ref[m, :, :, :128].astype(f32)
                value_kv = value_kv + recv_ref[m, :, :, 128:].astype(f32)
            out = outs[m // held]
            out[m % held, :, :, :128] = value.astype(bf16)
            out[m % held, :, :, 128:] = value_kv.astype(bf16)


def attn_back_kernel(
    _, q_ref, gctx_ref, key_ref, val_ref, pos_ref, lse_ref, qraw_ref, cos_ref, sin_ref, head_ref,
    gq_ref, far_ref, near_ref, gain_ref, gkey_ref, gval_ref,
):
    head_dim = key_ref.shape[2]
    head_count = q_ref.shape[1] // head_dim
    block = q_ref.shape[0]
    span = WINDOW + TILE
    scaling = head_dim ** (-0.5)

    @pl.when(pl.program_id(0) == 0)
    def _():
        gain_ref[...] = jnp.zeros_like(gain_ref)

    gkey_ref[...] = jnp.zeros_like(gkey_ref)
    gval_ref[...] = jnp.zeros_like(gval_ref)
    gain = jnp.zeros((1, head_dim), f32)
    for tile in range(block // TILE):
        own = slice(tile * TILE, (tile + 1) * TILE)
        reach = slice(tile * TILE, tile * TILE + span)
        query = stacked(q_ref, tile, head_count, head_dim)
        g_ctx = stacked(gctx_ref, tile, head_count, head_dim)
        key = key_ref[0, reach, :]
        value = val_ref[0, reach, :]
        log_total = jnp.stack([lse_ref[own, h : h + 1] for h in range(head_count)])
        score = mm(query, key, NT).reshape(head_count, TILE, span) + mask_of(pos_ref, tile, span)
        probs = jnp.exp(score - log_total)
        g_probs = mm(g_ctx, value, NT).reshape(head_count, TILE, span)
        spread = jnp.sum(g_probs * probs, axis=-1, keepdims=True)
        g_score = (probs * (g_probs - spread)).astype(bf16).reshape(head_count * TILE, span)
        low = probs.astype(bf16).reshape(head_count * TILE, span)
        gkey_ref[reach, :] += mm(g_score, query, TN)
        gval_ref[reach, :] += mm(low, g_ctx, TN)
        g_rot = mm(g_score, key) * scaling
        turned = slice(block + tile * TILE, block + (tile + 1) * TILE)
        cosine, sine = cos_ref[turned, :], sin_ref[turned, :]
        for h in range(head_count):
            cols = slice(h * head_dim, (h + 1) * head_dim)
            raw = qraw_ref[own, cols]
            back, share = norm_back(
                raw,
                inv_rms(raw),
                head_ref[0:1, :],
                rope_back(g_rot[h * TILE : (h + 1) * TILE], cosine, sine),
            )
            gq_ref[own, cols] = back.astype(bf16)
            gain += jnp.sum(share, axis=0, keepdims=True)
    gain_ref[0:1, :] += gain
    far_ref[0, :, :head_dim] = rope_back(
        gkey_ref[:block, :], cos_ref[:block, :], sin_ref[:block, :]
    ).astype(bf16)
    far_ref[0, :, head_dim:] = gval_ref[:block, :].astype(bf16)
    near_ref[0, :, :head_dim] = gkey_ref[block:, :]
    near_ref[0, :, head_dim:] = gval_ref[block:, :]


def kv_back_kernel(
    kraw_ref, cos_ref, sin_ref, head_ref, near_ref, recv_ref, _, gkv_ref, kgain_ref
):
    head_dim = head_ref.shape[1]

    @pl.when(pl.program_id(0) == 0)
    def _():
        kgain_ref[...] = jnp.zeros_like(kgain_ref)

    near, far = near_ref[0], recv_ref[0].astype(f32)
    raw = kraw_ref[...]
    g_normed = rope_back(near[:, :head_dim], cos_ref[...], sin_ref[...]) + far[:, :head_dim]
    g_key, share = norm_back(raw, inv_rms(raw), head_ref[1:2, :], g_normed)
    kgain_ref[0:1, :] += jnp.sum(share, axis=0, keepdims=True)
    gkv_ref[:, :head_dim] = g_key.astype(bf16)
    gkv_ref[:, head_dim:] = (near[:, head_dim:] + far[:, head_dim:]).astype(bf16)


def input_kernel(
    _, gq_ref, gkv_ref, wq_ref, wkv_ref, tok_ref, gres_ref, gains_ref, ffn_gain_ref, kgain_ref,
    qgain_ref, dtok_ref, gain_ref
):
    @pl.when(pl.program_id(0) == 0)
    def _():
        gain_ref[...] = jnp.zeros_like(gain_ref)
        head_dim = kgain_ref.shape[1]
        gain_ref[1:4, :] = ffn_gain_ref[0:3, :]
        gain_ref[4:5, :head_dim] = qgain_ref[0:1, :]
        gain_ref[4:5, head_dim : 2 * head_dim] = kgain_ref[0:1, :]

    g_in = mm(gq_ref[...], wq_ref[...], NT) + mm(gkv_ref[...], wkv_ref[...], NT)
    token = tok_ref[...].astype(f32)
    back, share = norm_back(token, inv_rms(token), gains_ref[0:1, :], g_in)
    dtok_ref[...] = (gres_ref[...] + back).astype(bf16)
    gain_ref[0:1, :] += jnp.sum(share, axis=0, keepdims=True)


def passed_along(shard, axis, by):
    length = lax.axis_size(axis)
    pairs = [(i, i + by) for i in range(length) if 0 <= i + by < length]
    return lax.ppermute(shard, axis, pairs)


def swapped(array, axis, even, odd):
    length = lax.axis_size(axis)
    return lax.ppermute(array, axis, [(i, i ^ (odd if i % 2 else even)) for i in range(length)])


def tables(block, head_dim):
    half_width = head_dim // 2
    frequency = ROPE_BASE ** (-(np.arange(half_width) * 2.0) / head_dim)
    angles = np.arange(-block, block)[:, None] * frequency
    return np.cos(angles).astype(np.float32), np.sin(angles).astype(np.float32)


def column_piece(array, axis_name, parts):
    wide = array.shape[1] // parts
    return lax.dynamic_slice_in_dim(array, lax.axis_index(axis_name) * wide, wide, 1)


def halves(array):
    if isinstance(array, tuple):
        return tuple(zip(*(halves(part) for part in array)))
    half = array.shape[0] // 2
    return (array[:half], array[half:]) if half > 1 else (array[0], array[1])


def total(terms):
    laid = [term for term in terms if isinstance(term, tuple)]
    terms = [term for term in terms if not isinstance(term, tuple)]
    if laid:
        terms.insert(0, jnp.concatenate([total(list(parts)) for parts in zip(*laid)], axis=-2))
    result = terms[0].astype(f32)
    for term in terms[1:]:
        result = result + term.astype(f32)
    return result


HELD = [0, 4, 2, 6, 1, 3, 5, 7]
HELD_Z = [0, 2, 1, 3]


def linked(*chains):
    arrays, steps = [], []
    for chain in chains:
        send, keep = chain if isinstance(chain, tuple) else (chain, [])
        arrays.append([send] + [array for array, _ in keep])
        steps.append([begin for _, begin in keep])
    arrays = lax.optimization_barrier(arrays)
    result = []
    for chain, (send, *keep), begins in zip(chains, arrays, steps):
        result.append((send, list(zip(keep, begins))) if isinstance(chain, tuple) else send)
    return result


class Exchange:
    def __init__(self, seqs, chunks):
        self.direct = seqs == 8 and chunks == 4
        if not self.direct:
            self.order = jnp.arange(12, dtype=jnp.int32) % 8
            self.held = jnp.array(HELD + HELD_Z, jnp.int32)
            return
        s, z = lax.axis_index("seq"), lax.axis_index("fsdp")
        odd = s % 2 == 1
        one, two = jnp.where(odd, 4, 2), jnp.where(odd, 2, 4)
        zero = jnp.zeros_like(s)
        sent = [one | two | 1, two | 1, one | 1, zero | 1]
        kept = [one | two, one, two, zero]
        order = [s ^ k for k in sent + kept] + [z ^ k for k in (3, 1, 2, 0)]
        self.order = jnp.stack(order).astype(jnp.int32)
        held = [zero, two, one, one | two, zero | 1, one | 1, two | 1, one | two | 1]
        held = [s ^ k for k in held] + [z ^ k for k in HELD_Z]
        self.held = jnp.stack(held).astype(jnp.int32)

    def along_step(self, held, bits):
        return jnp.concatenate([held, swapped(held, "fsdp", bits, bits)], axis=0)

    def second(self, piece):
        return swapped(piece, "seq", 4, 2)

    def first(self, piece):
        return swapped(piece, "seq", 2, 4)

    def swap_cores(self, parts):
        return swapped(parts, "seq", 1, 1)

    def fold(self, send, keep, step):
        if step < 3:
            got = swapped(send, "seq", *((1, 1), (2, 4), (4, 2))[step])
        else:
            got = swapped(send, "fsdp", step - 2, step - 2)
        return self.split(keep + [(got, step)], step)

    def split(self, terms, step):
        rest = []
        for array, begin in terms:
            for done in range(begin, step):
                array = halves(array)[1]
            rest.append(array)
        if step == 4:
            return total(rest)
        return total([halves(array)[0] for array in rest]).astype(bf16), terms

    def hop_terms(self, send, keep):
        keep = keep + [(swapped(send, "seq", 4, 2), 2)]
        rest = []
        for array, begin in keep:
            for done in range(begin, 2):
                array = halves(array)[1]
            rest.append(array)
        parts = [total([array[p] for array in rest]) for p in range(4)]
        return [part.astype(bf16) for part in parts[:3]] + [parts[3]]

    def last(self, *parts):
        got = [swapped(part, "fsdp", bits, bits) for part, bits in zip(parts, (3, 1, 2))]
        return total([parts[3]] + got)

    def hop(self, value, axis, bits):
        got = [swapped(value, axis, b, b) for b in bits]
        if len(bits) == 1:
            return value + got[0]
        both = bits[0] | bits[1]
        return (value + got[0]) + (got[1] + swapped(value, axis, both, both))


def scattered_plain(part):
    columns = lax.psum_scatter(part, "seq", scatter_dimension=1, tiled=True)
    return lax.psum_scatter(columns, "fsdp", scatter_dimension=0, tiled=True).astype(f32)


def gather_weights(w_query, w_key, w_value, w_out, w_gate, w_up, w_down, halo, exchange):
    pieces = w_gate.shape[1] // FF_TILE
    width = w_out.shape[1]
    if exchange.direct:
        down = column_piece(w_down, "seq", pieces).T
        ffn = jnp.concatenate(
            [
                column_piece(w_gate, "seq", pieces),
                column_piece(w_up, "seq", pieces),
                down[:, :FF_TILE],
                down[:, FF_TILE:],
            ],
            axis=0,
        )
        both = jnp.concatenate([w_key, w_value], axis=1)
        out = column_piece(w_out, "seq", pieces).T
        out = jnp.concatenate([out[:, :128], out[:, 128:]], axis=0)
        attn = jnp.concatenate(
            [column_piece(w_query, "seq", pieces), out, column_piece(both, "seq", pieces)], axis=1
        )
        attn = exchange.along_step(exchange.along_step(attn[None], 2), 1)
        ffn, attn = lax.optimization_barrier((ffn, attn))
        ffn = exchange.along_step(ffn[None], 2)
        attn, halo = lax.optimization_barrier((attn, halo))
        two, one = exchange.second(attn), exchange.first(attn)
        ffn, two = lax.optimization_barrier((ffn, two))
        ffn = exchange.along_step(ffn, 1)
        attn = [attn, two, one, exchange.first(two)]
        attn[3], ffn = lax.optimization_barrier((attn[3], ffn))
        return attn + [exchange.swap_cores(held) for held in attn], ffn, halo
    w_query, w_key, w_value, w_out, w_gate, w_up, w_down = [
        lax.all_gather(w, "fsdp", axis=0, tiled=True)
        for w in (w_query, w_key, w_value, w_out, w_gate, w_up, w_down)
    ]
    chunks = w_down.shape[0] // (2 * FF_TILE)
    quarter, strip = width // chunks, width // pieces

    def columns(weight):
        return weight.reshape(chunks, quarter, pieces, -1).transpose(2, 0, 1, 3)

    def turned(weight):
        shape = (pieces, strip, chunks, 2, weight.shape[0] // (2 * chunks))
        turned_part = weight.T.reshape(shape).transpose(0, 2, 3, 1, 4)
        return turned_part.reshape(pieces, chunks, 2 * strip, -1)

    both = jnp.concatenate([w_key, w_value], axis=1)
    attn = jnp.concatenate([columns(w_query), turned(w_out), columns(both)], axis=3)
    ffn = jnp.concatenate([columns(w_gate), columns(w_up), turned(w_down)], axis=2)
    def listed(pack):
        pack = jnp.take(jnp.take(pack, np.array(HELD), axis=0), np.array(HELD_Z), axis=1)
        return [pack[m] for m in range(pieces)]

    return listed(attn), listed(ffn), halo


def plain_gradients(part_gate, part_down, part_attn):
    pieces, quarters, double, _ = part_gate.shape
    width = quarters * double // 2
    strip = width // pieces

    def columns(parts):
        return parts.transpose(1, 2, 0, 3).reshape(width, -1)

    def turned(parts):
        parts = parts.reshape(pieces, quarters, -1, strip, FF_TILE).transpose(1, 2, 4, 0, 3)
        return parts.reshape(-1, width)

    each = part_attn.shape[3] - (part_attn.shape[3] - 128) // 2
    return tuple(
        scattered_plain(part)
        for part in (
            columns(part_attn[..., :128]),
            columns(part_attn[..., 128:each]),
            columns(part_attn[..., each:]),
            turned(part_down[:, :, 2 * strip :]),
            columns(part_gate[:, :, : double // 2]),
            columns(part_gate[:, :, double // 2 :]),
            turned(part_down[:, :, : 2 * strip]),
        )
    )


def split_gradients(ffn, attn):
    quarter = attn.shape[0]
    gate, down = ffn[: 2 * quarter], ffn[2 * quarter :]
    strip = down.shape[0] // 3
    each = attn.shape[1] - (attn.shape[1] - 128) // 2
    return (
        attn[:, :128],
        attn[:, 128:each],
        attn[:, each:],
        down[2 * strip :].T,
        gate[:quarter],
        gate[quarter:],
        jnp.concatenate([down[:strip].T, down[strip : 2 * strip].T], axis=0),
    )


def body(
    tokens, doc_starts, w_query, w_key, w_value, w_out, w_gate, w_up, w_down,
    pre_attn, post_attn, pre_ffn, post_ffn, query_norm, key_norm, cotangent,
):
    seq_dev, block, width = tokens.shape
    head_dim = w_key.shape[1]
    inner = w_query.shape[1]
    hidden_dim = w_gate.shape[1]
    count = seq_dev * block
    seqs, chunks = lax.axis_size("seq"), lax.axis_size("fsdp")
    exchange = Exchange(seqs, chunks)
    far_tokens = passed_along(tokens, "seq", 1).reshape(count, width)
    far_starts = passed_along(doc_starts, "seq", 1)
    pack, ffn_pack, (far_tokens, far_starts) = gather_weights(
        w_query, w_key, w_value, w_out, w_gate, w_up, w_down, (far_tokens, far_starts), exchange
    )
    starts = jnp.concatenate([far_starts, doc_starts], axis=1)
    indices = jnp.arange(2 * block, dtype=jnp.int32)
    latest = lax.cummax(jnp.where(starts == 1, indices[None, :], -WINDOW), axis=1)
    reach = jnp.minimum(indices[None, :] - latest, WINDOW - 1)[:, block:]
    pos_column = reach.reshape(count, 1)
    cosine, sine = tables(block, head_dim)
    own_cosine, own_sine = cosine[block:], sine[block:]

    pieces, quarters = len(pack), pack[0].shape[0]
    quarter, strip = width // quarters, width // pieces
    gains = jnp.stack([pre_attn, post_attn, pre_ffn, post_ffn])
    head_gains = jnp.stack([query_norm, key_norm])
    tokens_2d = tokens.reshape(count, width)
    cot_2d = cotangent.reshape(count, width)

    tok_spec = rows(block, width)
    table_spec = whole((2 * block, head_dim // 2))
    half_spec = whole((block, head_dim // 2))
    key_spec = pl.BlockSpec((1, 2 * block, head_dim), lambda i: (i, 0, 0))
    gains_spec, head_spec = whole((4, width)), whole((2, head_dim))
    wq_spec, wkv_spec, wot_spec = (
        whole((width, inner)),
        whole((width, 2 * head_dim)),
        whole((width, inner)),
    )
    smem = pl.BlockSpec(memory_space=pltpu.SMEM)
    remain = pl.BlockSpec(memory_space=pl.ANY)
    attn_low, query_raw, query_rot, key_raw, keys, values, full_q, full_kv, full_ot = (
        pl.pallas_call(
            qkv_kernel,
            grid=(seq_dev,),
            in_specs=[smem, tok_spec, tok_spec, table_spec, table_spec]
            + [gains_spec, head_spec]
            + [whole(pack[0].shape)] * pieces,
            out_specs=[
                tok_spec,
                rows(block, inner),
                rows(block, inner),
                rows(block, head_dim),
                key_spec,
                key_spec,
                wq_spec,
                wkv_spec,
                wot_spec,
            ],
            out_shape=[
                shaped((count, width), bf16),
                shaped((count, inner), f32),
                shaped((count, inner), bf16),
                shaped((count, head_dim), f32),
                shaped((seq_dev, 2 * block, head_dim), bf16),
                shaped((seq_dev, 2 * block, head_dim), bf16),
                shaped((width, inner), bf16),
                shaped((width, 2 * head_dim), bf16),
                shaped((width, inner), bf16),
            ],
            compiler_params=params(),
            name="project_rotate",
        cost_estimate=cost(11),
        )(
            exchange.held, tokens_2d, far_tokens, cosine, sine, gains, head_gains,
            *pack,
        )
    )
    if exchange.direct:
        own, two = ffn_pack, exchange.second(ffn_pack)
        own_swapped = exchange.swap_cores(own)
        again, two, keys = lax.optimization_barrier((own, two, keys))
        one, both, two_swapped = exchange.first(again), exchange.first(two), exchange.swap_cores(two)
    context, log_total, attn_branch, residual, ffn_in = pl.pallas_call(
        attn_kernel,
        grid=(seq_dev,),
        in_specs=[rows(block, inner), key_spec, key_spec, rows(block, 1), tok_spec]
        + [wot_spec, gains_spec],
        out_specs=[rows(block, inner), rows(block, 128), tok_spec, tok_spec, tok_spec],
        out_shape=[
            shaped((count, inner), bf16),
            shaped((count, 128), f32),
            shaped((count, width), f32),
            shaped((count, width), f32),
            shaped((count, width), bf16),
        ],
        compiler_params=params(),
        name="window_attention",
        cost_estimate=cost(12),
    )(query_rot, keys, values, pos_column, tokens_2d, full_ot, gains)

    if exchange.direct:
        one, both, ffn_in = lax.optimization_barrier((one, both, ffn_in))
        ffn_pack = [own, two, one, both, own_swapped, two_swapped]
        ffn_pack += [exchange.swap_cores(one), exchange.swap_cores(both)]

    half = pieces // 2
    tiles = count // FFN_ROWS

    def small(wide):
        return pl.BlockSpec((FFN_ROWS, wide), lambda i: (jnp.minimum(i, tiles - 1), 0))

    def once(shape):
        return pl.BlockSpec(
            shape, lambda *_: (0,) * len(shape), pipeline_mode=pl.Buffered(buffer_count=1)
        )

    gate_shape = (half, quarters, 2 * quarter, FF_TILE)
    down_shape = (half, quarters, 3 * strip, FF_TILE)

    def gate_spec(first):
        return pl.BlockSpec(
            (1,) + gate_shape[1:],
            lambda i: (jnp.clip(i - tiles - first, 0, half - 1), 0, 0, 0),
        )

    down_spec = pl.BlockSpec(
        (half, 1) + down_shape[2:], lambda i: (0, jnp.clip(i - tiles, 0, pieces - 1) // 2, 0, 0)
    )
    turned = pltpu.VMEM((width, count), bf16)
    weight = pltpu.VMEM((width, hidden_dim), bf16)
    middle = pltpu.VMEM((count, hidden_dim), bf16)
    gelu_parts = pltpu.VMEM((FFN_ROWS, hidden_dim), f32)
    layer_out, g_res, g_ctx, ffn_gains, *ffn_parts = pl.pallas_call(
        ffn_kernel,
        grid=(tiles + pieces,),
        in_specs=[smem, smem, small(width), small(width), small(width), small(width)]
        + [once((count, inner)), once((width, inner)), gains_spec]
        + [remain] * pieces,
        out_specs=[small(width), small(width), small(inner), whole((8, width))]
        + [gate_spec(0), gate_spec(half), down_spec, down_spec],
        out_shape=[
            shaped((count, width), bf16),
            shaped((count, width), f32),
            shaped((count, inner), bf16),
            shaped((8, width), f32),
            shaped(gate_shape, bf16),
            shaped(gate_shape, bf16),
            shaped(down_shape, bf16),
            shaped(down_shape, bf16),
        ],
        scratch_shapes=[gelu_parts, gelu_parts, weight, weight, weight]
        + [pltpu.VMEM((2,) + ffn_pack[0].shape, bf16), pltpu.SemaphoreType.DMA((2,))]
        + [middle, middle, middle, turned, turned, turned]
        + [pltpu.VMEM((width, FFN_ROWS), bf16)],
        compiler_params=params(62),
        name="feed_forward",
        cost_estimate=cost(60),
    )(
        exchange.held, exchange.order, residual, ffn_in, cot_2d, attn_branch, context, full_ot,
        gains, *ffn_pack,
    )
    gate_sent, gate_kept, down_sent, down_kept = ffn_parts
    gate, down = (gate_sent, gate_kept), (down_sent, down_kept)
    if exchange.direct:
        gate_got, down_got = swapped(gate_sent, "seq", 1, 1), swapped(down_sent, "seq", 1, 1)


    ffn = ffn_parts
    if exchange.direct:
        kept, got = (gate_kept, down_kept), (gate_got, down_got)
        ffn = exchange.split([(kept, 0), (got, 0)], 0)

    pair = pl.BlockSpec((1, block, 2 * head_dim), lambda i: (i, 0, 0))
    g_query, g_far, g_near, query_gain = pl.pallas_call(
        attn_back_kernel,
        grid=(seq_dev,),
        in_specs=[remain, rows(block, inner), rows(block, inner), key_spec, key_spec]
        + [rows(block, 1), rows(block, 128), rows(block, inner), table_spec, table_spec]
        + [head_spec],
        out_specs=[rows(block, inner), pair, pair, whole((8, head_dim))],
        out_shape=[
            shaped((count, inner), bf16),
            shaped((seq_dev, block, 2 * head_dim), bf16),
            shaped((seq_dev, block, 2 * head_dim), f32),
            shaped((8, head_dim), f32),
        ],
        scratch_shapes=[
            pltpu.VMEM((2 * block, head_dim), f32),
            pltpu.VMEM((2 * block, head_dim), f32),
        ],
        compiler_params=params(),
        name="attention_gradient",
        cost_estimate=cost(16),
    )(
        ffn[0], query_rot, g_ctx, keys, values, pos_column, log_total, query_raw, cosine, sine,
        head_gains,
    )
    g_recv = passed_along(g_far, "seq", -1)
    early = ffn
    if exchange.direct:
        ffn, g_recv = linked(exchange.fold(*ffn, 1), g_recv)
        early = ffn
    g_kv, key_gain = pl.pallas_call(
        kv_back_kernel,
        grid=(seq_dev,),
        in_specs=[rows(block, head_dim), half_spec, half_spec, head_spec]
        + [pair, pair, remain],
        out_specs=[rows(block, 2 * head_dim), whole((8, head_dim))],
        out_shape=[shaped((count, 2 * head_dim), bf16), shaped((8, head_dim), f32)],
        compiler_params=params(),
        name="key_value_back",
        cost_estimate=cost(4),
    )(key_raw, own_cosine, own_sine, head_gains, g_near, g_recv, early[0])

    each = head_dim // pieces
    column = jnp.arange(2 * head_dim, dtype=jnp.int32)
    inside = column % (2 * each)
    source = jnp.where(inside < each, inside, inside - each + head_dim)
    source = source + each * jnp.repeat(exchange.order[:pieces], 2 * each)
    sort = (column[:, None] == source[None, :]).astype(bf16)

    def attn_parts(base, before, extra):
        shape = (half, quarters, quarter, 128 + 2 * each)
        sent = (half // 2,) + shape[1:]
        outs = [shape] if base == 0 else [sent, sent]
        vmem = pl.BlockSpec(memory_space=pltpu.VMEM)
        chosen = sort[:, base * 2 * each : (base + half) * 2 * each]
        return pl.pallas_call(
            lambda *refs: attn_grad_kernel(base, *refs),
            in_specs=[smem, remain] + [vmem] * (4 + len(extra)),
            out_specs=[vmem] * len(outs),
            out_shape=[shaped(o, bf16) for o in outs],
            scratch_shapes=[pltpu.VMEM((2, width, count), bf16)],
            compiler_params=params(),
            cost_estimate=cost(6),
            name="attn_gradients_kept" if base else "attn_gradients_sent",
        )(exchange.order, before, attn_low, g_query, g_kv, chosen, *extra)

    (attn_sent,) = attn_parts(0, early[0], [])
    attn_got = exchange.swap_cores(attn_sent) if exchange.direct else jnp.zeros_like(attn_sent)
    if exchange.direct:
        ffn = exchange.fold(*ffn, 2)
    attn_parts_kept = attn_parts(half, ffn[0], [attn_got])
    attn = attn_parts_kept[0], [(attn_parts_kept[1], 1)]
    dtokens, sums = pl.pallas_call(
        input_kernel,
        grid=(seq_dev,),
        in_specs=[remain, rows(block, inner), rows(block, 2 * head_dim)]
        + [wq_spec, wkv_spec]
        + [tok_spec, tok_spec, gains_spec, whole((8, width))]
        + [whole((8, head_dim))] * 2,
        out_specs=[tok_spec, whole((8, width))],
        out_shape=[shaped((count, width), bf16), shaped((8, width), f32)],
        compiler_params=params(),
        name="input_gradient",
        cost_estimate=cost(7),
    )(attn_parts_kept[0], g_query, g_kv, full_q, full_kv, tokens_2d, g_res, gains, ffn_gains, key_gain, query_gain)

    if exchange.direct:
        ffn, attn = exchange.fold(*ffn, 3), exchange.fold(*attn, 1)
        sums = exchange.hop(sums, "seq", (1,))
        ffn, attn, sums = linked(ffn, attn, sums)
        ffn, attn = exchange.fold(*ffn, 4), exchange.hop_terms(*attn)
        sums = exchange.hop(sums, "seq", (2, 4))
        *attn, sums = linked(*attn, sums)
        attn = exchange.last(*attn)
        sums = exchange.hop(sums, "fsdp", (1, 2))
        weights = split_gradients(ffn, attn)
    else:
        weights = plain_gradients(
            jnp.concatenate(gate, axis=0),
            jnp.concatenate(down, axis=0),
            jnp.concatenate([attn_sent, *attn_parts_kept], axis=0),
        )
        sums = lax.psum(sums, ("seq", "fsdp"))
    gain_sums = (sums[0], sums[3], sums[2], sums[1])
    gain_sums += (sums[4, :head_dim], sums[4, head_dim : 2 * head_dim])
    shape = (seq_dev, block, width)
    return (layer_out.reshape(shape), dtokens.reshape(shape)) + weights + gain_sums


def solution(mesh):
    sharded = P("fsdp", "seq", None)
    weight = P("fsdp", None)
    in_specs = (sharded, P("fsdp", "seq")) + (weight,) * 7 + (P(),) * 6 + (sharded,)
    out_specs = (sharded, sharded) + (P("fsdp", "seq"),) * 7 + (P(),) * 6
    return jax.shard_map(body, mesh=mesh, in_specs=in_specs, out_specs=out_specs, check_vma=False)
```
